32 devices in a mesh: dp: 8 (over z, y), segment: 4 (over x, core).
Axes of the slice: x: 2, y: 2, z: 4, core: 2. Of those that a mesh axis runs over, the one named last changes fastest.
Arguments:
- images: bfloat16 [32, 16, 16, 384], P('dp'), may hold values from -6 to 6
- cotangent: bfloat16 [32, 16, 16, 384], P('dp'), may hold values from -0.09375 to 0.09375
- kernels: float32 [4, 49, 384], P('segment'), may hold values from -0.875 to 0.875
- norm_gains: float32 [4, 384], P('segment'), may hold values from 0.25 to 1.75
- w_in: bfloat16 [4, 384, 768], P('segment'), may hold values from -0.3125 to 0.3125
- w_out: bfloat16 [4, 768, 384], P('segment'), may hold values from -0.21875 to 0.21875
- scales: float32 [4, 384], P('segment'), may hold values from 0.3 to 1
Outputs:
- grad_kernels: float32 [4, 49, 384], P('segment', None, 'dp')
- grad_gains: float32 [4, 384], P('segment', 'dp')
- grad_w_in: float32 [4, 384, 768], P('segment', 'dp')
- grad_w_out: float32 [4, 768, 384], P('segment', None, 'dp')
- grad_scales: float32 [4, 384], P('segment', 'dp')
The draws below stay inside these ranges and needn't reach their ends.
All inputs are finite; a program needn't handle non-finite values.
Results may differ from the reference program's by a relative error of at most 0.034.
Values may be sent and summed in bfloat16 or wider, within the bound.
No kernel may reach another device: no remote copies, remote signals or barrier semaphores. Data moves between devices by JAX's collectives and lax.ppermute only.
A program may use at most 64 MiB of HBM per device.

```python
import math
import jax
import jax.numpy as jnp
from jax import lax

C = 384
FF = 768
HH = 16
WW = 16
IMAGES = 32
N_SEGMENT = 4


def strengthened(values, key, source, target, shards_of, factor):
    def block_of(position):
        return (jnp.arange(values.shape[position]) // (values.shape[position] // shards_of)).reshape((-1,) + (1,) * (values.ndim - 1 - position))

    one_side = jax.random.permutation(key, shards_of)[block_of(target)]
    second = (block_of(target) + shards_of // 2) % shards_of
    return jnp.where((block_of(source) == one_side) | (block_of(source) == second), factor * values, values)


def shard_levels(stream_key, dims, split, least, high):
    def one(dim, blocks):
        heights = jax.random.uniform(jax.random.fold_in(jax.random.fold_in(stream_key, 6), dim), (blocks,), jnp.float32, least / len(split), high / len(split))
        return jnp.repeat(jnp.exp(heights), dims[dim] // blocks).reshape((-1,) + (1,) * (len(dims) - dim - 1))

    loudness = one(*split[0])
    for cut in split[1:]:
        loudness = loudness * one(*cut)
    return loudness


def centred(key, extent, scale, most, cuts=(), kind=jnp.bfloat16):
    factor_of = shard_levels(key, extent, cuts, -0.22, 0.18) if cuts else 1.0
    array = jax.random.normal(key, extent, jnp.float32) * scale * factor_of
    return jnp.minimum(jnp.maximum(array, -most), most).astype(kind)


def bell_draw_with(rng, dims, width, most, split, heavy, dtype=jnp.bfloat16):
    entries = width * jax.random.normal(rng, dims, jnp.float32)
    if split:
        entries = entries * shard_levels(rng, dims, split, -0.22, 0.18)
    return jnp.clip(strengthened(entries, jax.random.fold_in(rng, 3), *heavy), -most, most).astype(dtype)


def setup_inputs(seed: int = 0) -> dict:
    keys = jax.random.split(jax.random.key(seed), 8)
    return {
        "images": centred(keys[0], (IMAGES, HH, WW, C), 1.0, 6.0, ((0, 8),)),
        "cotangent": bell_draw_with(keys[1], (IMAGES, HH, WW, C), ((IMAGES * HH * WW) ** -0.5), 0.09375, ((0, 8),), (0, 3, 8, 2.0)),
        "kernels": centred(keys[2], (N_SEGMENT, 49, C), 49 ** -0.5, 0.875, ((0, 4),), jnp.float32),
        "norm_gains": jnp.clip(1.0 + 0.15 * jax.random.normal(keys[3], (N_SEGMENT, C), jnp.float32), 0.25, 1.75),
        "w_in": centred(keys[4], (N_SEGMENT, C, FF), C ** -0.5, 0.3125, ((0, 4),)),
        "w_out": centred(keys[5], (N_SEGMENT, FF, C), FF ** -0.5, 0.21875, ((0, 4),)),
        "scales": jnp.clip(jnp.exp(math.log(1.0) - 1.2039728 * jax.random.uniform(keys[6], (N_SEGMENT, C), jnp.float32) ** shard_levels(keys[6], (N_SEGMENT, C), ((0, 4),), -0.2, 0.2)), 0.3, 1.0),
    }


EPS = 1e-06

def depthwise(padded, kernel, map_rows, map_cols):
    running = jnp.zeros((padded.shape[0], map_rows, map_cols, padded.shape[3]), jnp.float32)
    for tap_row in range(7):
        for tap_col in range(7):
            running = running + kernel[tap_row * 7 + tap_col] * padded[:, tap_row:tap_row + map_rows, tap_col:tap_col + map_cols, :]
    return running

def forward_parts(inputs, kernel, layernorm_gain_vector, w_in, w_out, layer_scale):
    map_rows, map_cols, channels = (inputs.shape[1], inputs.shape[2], inputs.shape[3])
    padded = jnp.pad(inputs.astype(jnp.float32), ((0, 0), (3, 3), (3, 3), (0, 0)))
    conv_out = depthwise(padded, kernel, map_rows, map_cols)
    flat_rows = conv_out.reshape(-1, channels)
    center = flat_rows - lax.optimization_barrier(jnp.mean(flat_rows, axis=1, keepdims=True))
    inverse_deviation = lax.rsqrt(lax.optimization_barrier(jnp.mean(center * center, axis=1, keepdims=True)) + EPS)
    normalized_map = center * inverse_deviation
    normed_low = (normalized_map * layernorm_gain_vector).astype(jnp.bfloat16)
    pre_gelu = jnp.dot(normed_low, w_in, preferred_element_type=jnp.float32)
    hidden = jax.nn.gelu(pre_gelu).astype(jnp.bfloat16)
    branch = jnp.dot(hidden, w_out, preferred_element_type=jnp.float32)
    residual = inputs.astype(jnp.float32).reshape(flat_rows.shape)
    result = (residual + layer_scale * branch).astype(jnp.bfloat16).reshape(inputs.shape)
    return (result, (padded, normalized_map, inverse_deviation, normed_low, pre_gelu, hidden, branch))

def backward_parts(grad_map, stored, kernel, layernorm_gain_vector, w_in, w_out, layer_scale):
    padded, normalized_map, inverse_deviation, normed_low, pre_gelu, hidden, branch = stored
    grid_shape = grad_map.shape
    map_rows, map_cols, channels = (grid_shape[1], grid_shape[2], grid_shape[3])
    grad_out = grad_map.astype(jnp.float32).reshape(-1, channels)
    grad_scale = lax.optimization_barrier(jnp.sum(grad_out * branch, axis=0))
    grad_branch = (grad_out * layer_scale).astype(jnp.bfloat16)
    grad_wout = jnp.dot(hidden.T, grad_branch, preferred_element_type=jnp.float32)
    grad_hidden = jnp.dot(grad_branch, w_out.T, preferred_element_type=jnp.float32)
    grad_pre = jax.vjp(jax.nn.gelu, pre_gelu)[1](grad_hidden)[0].astype(jnp.bfloat16)
    grad_win = jnp.dot(normed_low.T, grad_pre, preferred_element_type=jnp.float32)
    normalized_map_gradient = jnp.dot(grad_pre, w_in.T, preferred_element_type=jnp.float32)
    grad_gain = lax.optimization_barrier(jnp.sum(normalized_map_gradient * normalized_map, axis=0))
    standardized_input_gradient = normalized_map_gradient * layernorm_gain_vector
    depthwise_output_gradient = inverse_deviation * (standardized_input_gradient - lax.optimization_barrier(jnp.mean(standardized_input_gradient, axis=1, keepdims=True)) - normalized_map * lax.optimization_barrier(jnp.mean(standardized_input_gradient * normalized_map, axis=1, keepdims=True)))
    depthwise_output_gradient = depthwise_output_gradient.reshape(grid_shape)
    grad_padded = jnp.pad(depthwise_output_gradient, ((0, 0), (3, 3), (3, 3), (0, 0)))
    grad_input = grad_out.reshape(grid_shape)
    kernel_rows = []
    for tap_row in range(7):
        for tap_col in range(7):
            window = padded[:, tap_row:tap_row + map_rows, tap_col:tap_col + map_cols, :]
            kernel_rows.append(lax.optimization_barrier(jnp.sum(window * depthwise_output_gradient, axis=(0, 1, 2))))
            grad_input = grad_input + kernel[tap_row * 7 + tap_col] * grad_padded[:, 6 - tap_row:6 - tap_row + map_rows, 6 - tap_col:6 - tap_col + map_cols, :]
    grad_kernel = jnp.stack(kernel_rows)
    return (grad_input.astype(jnp.bfloat16), (grad_kernel, grad_gain, grad_win, grad_wout, grad_scale))

def stack_member(results, member):
    return jnp.stack([segment_grads[member] for segment_grads in results])

def reference(images, cotangent, kernels, norm_gains, w_in, w_out, scales):
    segment_inputs = [images]
    for relay_segment_index in range(N_SEGMENT - 1):
        block_params = (kernels[relay_segment_index], norm_gains[relay_segment_index], w_in[relay_segment_index], w_out[relay_segment_index], scales[relay_segment_index])

        def advance(single, block_params=block_params):
            return forward_parts(single[None], *block_params)[0][0]
        segment_inputs.append(lax.map(advance, segment_inputs[-1]))
    channels = images.shape[3]
    hidden_units = w_in.shape[2]
    flowing = cotangent
    results = []
    for relay_segment_index in range(N_SEGMENT - 1, -1, -1):
        block_params = (kernels[relay_segment_index], norm_gains[relay_segment_index], w_in[relay_segment_index], w_out[relay_segment_index], scales[relay_segment_index])

        def accumulate(running, step_pair, block_params=block_params):
            single, grad_single = step_pair
            stored = forward_parts(single[None], *block_params)[1]
            grad_input, grad_terms = backward_parts(grad_single[None], stored, *block_params)
            return (jax.tree.map(jnp.add, running, grad_terms), grad_input[0])
        zero_terms = (jnp.zeros((49, channels), jnp.float32), jnp.zeros((channels,), jnp.float32), jnp.zeros((channels, hidden_units), jnp.float32), jnp.zeros((hidden_units, channels), jnp.float32), jnp.zeros((channels,), jnp.float32))
        running, flowing = lax.scan(accumulate, zero_terms, (segment_inputs[relay_segment_index], flowing))
        results.insert(0, running)
    return (stack_member(results, 0), stack_member(results, 1), stack_member(results, 2), stack_member(results, 3), stack_member(results, 4))
```

```python
import functools
import jax
import jax.numpy as jnp
from jax import lax
from jax.sharding import PartitionSpec as P
from jax.experimental import pallas as pl
from jax.experimental.pallas import tpu as pltpu

EPS = 1e-06
GELU_C = 0.7978845608028654
GELU_A = 0.044715
LANES = 128
VMEM = pltpu.CompilerParams(vmem_limit_bytes=40 * 1024 * 1024)


def zero_borders(pad_ref, rows, cols):
    tiles = pad_ref.shape[0]
    for c in range(tiles):
        pad_ref[c, 0:3] = jnp.zeros((3, cols + 16, LANES), jnp.float32)
        pad_ref[c, rows + 3 : rows + 6] = jnp.zeros((3, cols + 16, LANES), jnp.float32)
        pad_ref[c, 3 : rows + 3, 0:8] = jnp.zeros((rows, 8, LANES), jnp.float32)
        pad_ref[c, 3 : rows + 3, cols + 8 : cols + 16] = jnp.zeros((rows, 8, LANES), jnp.float32)


def conv_norm_kernel(x_ref, k_ref, gain_ref, xhat_ref, normed_ref, inv_ref, pad_ref, conv_ref):
    rows, cols, channels = x_ref.shape
    tiles = channels // LANES
    zero_borders(pad_ref, rows, cols)
    for c in range(tiles):
        pad_ref[c, 3 : rows + 3, 8 : cols + 8] = x_ref[:, :, c * LANES : (c + 1) * LANES].astype(jnp.float32)

    for c in range(tiles):
        lanes = slice(c * LANES, (c + 1) * LANES)

        def strip(w, carry, c=c, lanes=lanes):
            base = pl.multiple_of(w * 8, 8)
            acc = jnp.zeros((rows, 8, LANES), jnp.float32)
            window = pad_ref.at[c, :, pl.ds(base, 24), :]
            for q in range(7):
                col = window[:, 5 + q : 13 + q, :]
                for r in range(7):
                    acc = acc + k_ref[r * 7 + q : r * 7 + q + 1, lanes][None] * col[r : r + rows]
            conv_ref[:, pl.ds(base, 8), lanes] = acc
            return carry

        lax.fori_loop(0, cols // 8, strip, 0)

    def norm(h, carry):
        value = conv_ref[pl.ds(h * 2, 2)].reshape(2 * cols, channels)
        mean = jnp.mean(value, axis=1, keepdims=True)
        center = value - mean
        inv = lax.rsqrt(jnp.mean(center * center, axis=1, keepdims=True) + EPS)
        xhat = center * inv
        at = pl.ds(pl.multiple_of(h * 2 * cols, 2 * cols), 2 * cols)
        xhat_ref[at, :] = xhat.astype(jnp.bfloat16)
        normed_ref[at, :] = (xhat * gain_ref[...]).astype(jnp.bfloat16)
        inv_ref[at, :] = jnp.broadcast_to(inv, (2 * cols, LANES))
        return carry

    lax.fori_loop(0, rows // 2, norm, 0, unroll=2)


def conv_norm(x, kernel, gain):
    rows, cols, channels = x.shape
    tiles = channels // LANES
    n = rows * cols
    return pl.pallas_call(
        conv_norm_kernel,
        out_shape=(
            jax.ShapeDtypeStruct((n, channels), jnp.bfloat16),
            jax.ShapeDtypeStruct((n, channels), jnp.bfloat16),
            jax.ShapeDtypeStruct((n, LANES), jnp.float32),
        ),
        scratch_shapes=[
            pltpu.VMEM((tiles, rows + 6, cols + 16, LANES), jnp.float32),
            pltpu.VMEM((rows, cols, channels), jnp.float32),
        ],
        compiler_params=VMEM,
        name="conv_norm",
    )(x, kernel, gain)


def tanh_arg(x):
    return jnp.tanh(x * (GELU_C + (GELU_C * GELU_A) * (x * x)))


def load_weights(sel_ref, w_ins, w_outs, w_in_ref, w_out_ref, sems):
    for m in range(len(w_ins)):

        @pl.when(sel_ref[0] == m)
        def _():
            pltpu.make_async_copy(w_ins[m], w_in_ref, sems.at[0]).start()
            pltpu.make_async_copy(w_outs[m], w_out_ref, sems.at[1]).start()

    return (
        pltpu.make_async_copy(w_ins[0], w_in_ref, sems.at[0]).wait,
        pltpu.make_async_copy(w_outs[0], w_out_ref, sems.at[1]).wait,
    )


def mlp_kernel(choices, sel_ref, normed_ref, x_ref, scale_ref, *rest):
    w_ins, w_outs = rest[:choices], rest[choices : 2 * choices]
    y_ref, pre_ref, branch_ref, hid_ref, acc_ref, w_in_ref, w_out_ref, sems = rest[2 * choices :]
    wait_in, wait_out = load_weights(sel_ref, w_ins, w_outs, w_in_ref, w_out_ref, sems)
    n, channels = normed_ref.shape
    hidden = w_in_ref.shape[1]
    wait_in()
    step = 256
    sub = 32
    for j in range(hidden // step):
        cut = slice(j * step, (j + 1) * step)
        pre = jnp.dot(normed_ref[...], w_in_ref[:, cut], preferred_element_type=jnp.float32)
        for i in range(n // sub):
            p = pre[i * sub : (i + 1) * sub]
            half = 0.5 * p
            hid_ref[i * sub : (i + 1) * sub, :] = (half + half * tanh_arg(p)).astype(jnp.bfloat16)
            pre_ref[i * sub : (i + 1) * sub, cut] = p.astype(jnp.bfloat16)
        if j == 0:
            wait_out()
        part = jnp.dot(hid_ref[...], w_out_ref[cut, :], preferred_element_type=jnp.float32)
        if j == 0:
            acc_ref[...] = part
        else:
            acc_ref[...] += part
    for i in range(n // sub):
        at = slice(i * sub, (i + 1) * sub)
        branch = acc_ref[at, :]
        branch_ref[at, :] = branch.astype(jnp.bfloat16)
        y_ref[at, :] = (x_ref[at, :].astype(jnp.float32) + scale_ref[...] * branch).astype(jnp.bfloat16)


def specs(sel, arrays, choices):
    return (
        [pl.BlockSpec(memory_space=pltpu.SMEM)]
        + [pl.BlockSpec(memory_space=pltpu.VMEM)] * arrays
        + [pl.BlockSpec(memory_space=pl.ANY)] * (2 * choices)
    )


def mlp(sel, normed, x, scale, w_ins, w_outs):
    n, channels = normed.shape
    hidden = w_ins[0].shape[1]
    return pl.pallas_call(
        functools.partial(mlp_kernel, len(w_ins)),
        in_specs=specs(sel, 3, len(w_ins)),
        out_shape=(
            jax.ShapeDtypeStruct((n, channels), jnp.bfloat16),
            jax.ShapeDtypeStruct((n, hidden), jnp.bfloat16),
            jax.ShapeDtypeStruct((n, channels), jnp.bfloat16),
        ),
        scratch_shapes=[
            pltpu.VMEM((n, 256), jnp.bfloat16),
            pltpu.VMEM((n, channels), jnp.float32),
            pltpu.VMEM((channels, hidden), jnp.bfloat16),
            pltpu.VMEM((hidden, channels), jnp.bfloat16),
            pltpu.SemaphoreType.DMA((2,)),
        ],
        compiler_params=VMEM,
        name="mlp",
    )(sel, normed, x, scale, *w_ins, *w_outs)


def mlp_back_kernel(choices, sel_ref, g_ref, branch_ref, pre_ref, xhat_ref, inv_ref, gain_ref, scale_ref, *rest):
    w_ins, w_outs = rest[:choices], rest[choices : 2 * choices]
    (keep_ref, send_ref, small_ref, gconv_ref,
     gb_ref, nm_ref, hid_ref, gp_ref, acc_ref, w_in_ref, w_out_ref, sems) = rest[2 * choices :]
    wait_in, wait_out = load_weights(sel_ref, w_ins, w_outs, w_in_ref, w_out_ref, sems)
    first = sel_ref[1] == 0
    n, channels = g_ref.shape
    hidden = w_in_ref.shape[1]
    step = 256
    sub = 32
    scale_sum = jnp.zeros((8, channels), jnp.float32)
    for i in range(n // sub):
        at = slice(i * sub, (i + 1) * sub)
        g = g_ref[at, :].astype(jnp.float32)
        scale_sum = scale_sum + jnp.sum((g * branch_ref[at, :].astype(jnp.float32)).reshape(sub // 8, 8, channels), axis=0)
        gb_ref[at, :] = (g * scale_ref[...]).astype(jnp.bfloat16)
        nm_ref[at, :] = (xhat_ref[at, :].astype(jnp.float32) * gain_ref[...]).astype(jnp.bfloat16)
    gb_t = gb_ref[...].T
    nm_t = nm_ref[...].T
    wait_in()
    wait_out()
    for j in range(hidden // step):
        cut = slice(j * step, (j + 1) * step)
        gh = lax.dot_general(gb_ref[...], w_out_ref[cut, :], (((1,), (1,)), ((), ())), preferred_element_type=jnp.float32)
        for i in range(n // sub):
            at = slice(i * sub, (i + 1) * sub)
            p = pre_ref[at, cut].astype(jnp.float32)
            sq = p * p
            t = jnp.tanh(p * (GELU_C + (GELU_C * GELU_A) * sq))
            cdf = 0.5 + 0.5 * t
            hid_ref[at, :] = (p * cdf).astype(jnp.bfloat16)
            slope = cdf + (0.5 * p) * (1.0 - t * t) * (GELU_C + (3.0 * GELU_C * GELU_A) * sq)
            gp_ref[at, :] = (gh[at, :] * slope).astype(jnp.bfloat16)
        t_out = jnp.dot(gb_t, hid_ref[...], preferred_element_type=jnp.float32)
        t_in = jnp.dot(nm_t, gp_ref[...], preferred_element_type=jnp.float32)
        keep_ref[:, cut] = jnp.where(first, t_in, t_out).astype(jnp.bfloat16)
        send_ref[:, cut] = jnp.where(first, t_out, t_in).astype(jnp.bfloat16)
        part = lax.dot_general(gp_ref[...], w_in_ref[:, cut], (((1,), (1,)), ((), ())), preferred_element_type=jnp.float32)
        if j == 0:
            acc_ref[...] = part
        else:
            acc_ref[...] += part
    gain_sum = jnp.zeros((8, channels), jnp.float32)
    for i in range(n // sub):
        at = slice(i * sub, (i + 1) * sub)
        gn = acc_ref[at, :]
        xhat = xhat_ref[at, :].astype(jnp.float32)
        gain_sum = gain_sum + jnp.sum((gn * xhat).reshape(sub // 8, 8, channels), axis=0)
        gx = gn * gain_ref[...]
        m1 = jnp.mean(gx, axis=1, keepdims=True)
        m2 = jnp.mean(gx * xhat, axis=1, keepdims=True)
        inv = inv_ref[at, 0:1]
        gconv_ref[at, :] = inv * (gx - m1 - xhat * m2)
    small_ref[0:1, :] = jnp.sum(gain_sum, axis=0, keepdims=True)
    small_ref[1:2, :] = jnp.sum(scale_sum, axis=0, keepdims=True)
    small_ref[2:8, :] = jnp.zeros((6, channels), jnp.float32)


def mlp_back(sel, g, branch, pre, xhat, inv, gain, scale, w_ins, w_outs):
    n, channels = g.shape
    hidden = w_ins[0].shape[1]
    return pl.pallas_call(
        functools.partial(mlp_back_kernel, len(w_ins)),
        in_specs=specs(sel, 7, len(w_ins)),
        out_shape=(
            jax.ShapeDtypeStruct((channels, hidden), jnp.bfloat16),
            jax.ShapeDtypeStruct((channels, hidden), jnp.bfloat16),
            jax.ShapeDtypeStruct((8, channels), jnp.float32),
            jax.ShapeDtypeStruct((n, channels), jnp.float32),
        ),
        scratch_shapes=[
            pltpu.VMEM((n, channels), jnp.bfloat16),
            pltpu.VMEM((n, channels), jnp.bfloat16),
            pltpu.VMEM((n, 256), jnp.bfloat16),
            pltpu.VMEM((n, 256), jnp.bfloat16),
            pltpu.VMEM((n, channels), jnp.float32),
            pltpu.VMEM((channels, hidden), jnp.bfloat16),
            pltpu.VMEM((hidden, channels), jnp.bfloat16),
            pltpu.SemaphoreType.DMA((2,)),
        ],
        compiler_params=VMEM,
        name="mlp_back",
    )(sel, g, branch, pre, xhat, inv, gain, scale, *w_ins, *w_outs)


def conv_back_kernel(need_map, gconv_ref, x_ref, g_ref, k_ref, *rest):
    if need_map:
        out_ref, tk_ref, pad_ref, sum_ref = rest
    else:
        tk_ref, pad_ref, sum_ref = rest
    rows, cols, channels = x_ref.shape
    tiles = channels // LANES
    zero_borders(pad_ref, rows, cols)
    for c in range(tiles):
        pad_ref[c, 3 : rows + 3, 8 : cols + 8] = gconv_ref[:, :, c * LANES : (c + 1) * LANES]
    for c in range(tiles):
        lanes = slice(c * LANES, (c + 1) * LANES)
        sum_ref[...] = jnp.zeros(sum_ref.shape, jnp.float32)

        def strip(w, carry, c=c, lanes=lanes):
            base = pl.multiple_of(w * 8, 8)
            window = pad_ref.at[c, :, pl.ds(base, 24), :]
            xs = x_ref[:, pl.ds(base, 8), lanes].astype(jnp.float32)
            if need_map:
                acc = g_ref[:, pl.ds(base, 8), lanes].astype(jnp.float32)
            for q in range(7):
                col = window[:, 11 - q : 19 - q, :]
                for r in range(7):
                    tap = r * 7 + q
                    shifted = col[6 - r : 6 - r + rows]
                    sum_ref[tap] += jnp.sum(xs * shifted, axis=0)
                    if need_map:
                        acc = acc + k_ref[tap : tap + 1, lanes][None] * shifted
            if need_map:
                out_ref[:, pl.ds(base, 8), lanes] = acc.astype(jnp.bfloat16)
            return carry

        lax.fori_loop(0, cols // 8, strip, 0)
        tk_ref[:, lanes] = jnp.sum(sum_ref[...], axis=1)


def conv_back(gconv, x, g, kernel, need_map=True):
    rows, cols, channels = x.shape
    tiles = channels // LANES
    taps = kernel.shape[0]
    out = (jax.ShapeDtypeStruct((taps, channels), jnp.float32),)
    if need_map:
        out = (jax.ShapeDtypeStruct((rows, cols, channels), jnp.bfloat16),) + out
    return pl.pallas_call(
        functools.partial(conv_back_kernel, need_map),
        out_shape=out,
        scratch_shapes=[
            pltpu.VMEM((tiles, rows + 6, cols + 16, LANES), jnp.float32),
            pltpu.VMEM((taps, 8, LANES), jnp.float32),
        ],
        compiler_params=VMEM,
        name="conv_back",
    )(gconv, x, g, kernel)


BF16 = jnp.bfloat16
F32 = jnp.float32


def block_forward(x, kernel, gain, scale, sel, w_ins, w_outs):
    rows, cols, channels = x.shape
    xhat, normed, inv = conv_norm(x, kernel, gain)
    y, pre, branch = mlp(sel, normed, x.reshape(rows * cols, channels), scale, w_ins, w_outs)
    return y.reshape(x.shape), (x, xhat, inv, pre, branch)


def block_backward(g, stored, kernel, gain, scale, sel, w_ins, w_outs, need_map):
    x, xhat, inv, pre, branch = stored
    rows, cols, channels = x.shape
    keep, send, small, gconv = mlp_back(
        sel, g.reshape(rows * cols, channels), branch, pre, xhat, inv, gain, scale, w_ins, w_outs
    )
    out = conv_back(gconv.reshape(x.shape), x, g, kernel, need_map)
    g_prev = out[0] if need_map else None
    return g_prev, keep, send, jnp.concatenate([out[-1], small[0:2]], axis=0)


def small_parameters(kernels, norm_gains, scales):
    taps = kernels.shape[1]
    fill = jnp.zeros((-(taps + 2) % 8, kernels.shape[2]), F32)
    return jnp.concatenate([kernels[0], norm_gains, scales, fill], axis=0)


def finish(t_kernel, t_gain, t_scale, t_in, t_out):
    return t_kernel[None], t_gain[None], t_in[None], t_out[None], t_scale[None]


def any_mesh(images, cotangent, kernels, norm_gains, w_in, w_out, scales):
    segments = lax.axis_size("segment")
    rank = lax.axis_index("segment")
    count = images.shape[0] // segments
    taps = kernels.shape[1]
    small = lax.all_gather(small_parameters(kernels, norm_gains, scales), "segment")
    all_in = lax.all_gather(w_in[0], "segment")
    all_out = lax.all_gather(w_out[0], "segment")
    zero = jnp.zeros((2,), jnp.int32)
    pieces = [[None] * 3 for _ in range(segments)]
    for i in range(count):
        x = lax.dynamic_index_in_dim(images, rank * count + i, 0, keepdims=False)
        g = lax.dynamic_index_in_dim(cotangent, rank * count + i, 0, keepdims=False)
        stash = []
        params = []
        for s in range(segments):
            params.append((small[s, :taps], small[s, taps : taps + 1], small[s, taps + 1 : taps + 2], zero, [all_in[s]], [all_out[s]]))
            x, kept = block_forward(x, *params[s])
            stash.append(kept)
        for s in reversed(range(segments)):
            g, t_in, t_out, t_small = block_backward(g, stash[s], *params[s], s > 0)
            terms = (t_in.astype(F32), t_out.astype(F32), t_small)
            pieces[s] = [b if a is None else a + b for a, b in zip(pieces[s], terms)]

    def summed(values, dim):
        mine = lax.psum_scatter(jnp.stack(values), "segment", scatter_dimension=0, tiled=False)
        return lax.psum_scatter(mine, "dp", scatter_dimension=dim, tiled=True)

    t_in = summed([p[0] for p in pieces], 0)
    t_out = summed([p[1] for p in pieces], 0).T
    t_small = summed([p[2] for p in pieces], 1)
    return finish(t_small[:taps], t_small[taps], t_small[taps + 1], t_in, t_out)


def partners(flip, extent=(4, 2, 2, 2)):
    pairs = []
    for index in range(32):
        z, y, x, c = index >> 3, (index >> 2) & 1, (index >> 1) & 1, index & 1
        other = ((z ^ flip[0]) << 3) | ((y ^ flip[1]) << 2) | ((x ^ flip[2]) << 1) | (c ^ flip[3])
        pairs.append((index, other))
    return pairs


def swap(value, z=0, y=0, x=0, c=0):
    return lax.ppermute(value, ("dp", "segment"), partners((z, y, x, c)))


def this_mesh(images, cotangent, kernels, norm_gains, w_in, w_out, scales):
    rank = lax.axis_index("segment")
    core = rank % 2
    chip = rank // 2
    depth = lax.axis_index("dp") // 2
    side = lax.axis_index("dp") % 2
    taps = kernels.shape[1]
    channels = kernels.shape[2]
    hidden = w_in.shape[2]
    share = channels // 8

    own = (small_parameters(kernels, norm_gains, scales), w_in[0], w_out[0])
    far = tuple(swap(v, x=1) for v in own)
    near = tuple(swap(v, c=1) for v in own)
    far_near = tuple(swap(v, c=1) for v in far)
    held = (own, near, far, far_near)
    small = jnp.stack([h[0] for h in held])
    w_ins = [h[1] for h in held]
    w_outs = [h[2] for h in held]

    x = lax.dynamic_index_in_dim(images, rank, 0, keepdims=False)
    g = lax.dynamic_index_in_dim(cotangent, rank, 0, keepdims=False)
    stash = []
    params = []
    for s in range(4):
        which = rank ^ s
        mine = lax.dynamic_index_in_dim(small, which, 0, keepdims=False)
        sel = jnp.stack([which, core]).astype(jnp.int32)
        params.append((mine[:taps], mine[taps : taps + 1], mine[taps + 1 : taps + 2], sel, w_ins, w_outs))
        x, kept = block_forward(x, *params[s])
        stash.append(kept)

    shares = [None] * 4
    smalls = [None] * 4
    for s in reversed(range(4)):
        g, keep, send, smalls[s] = block_backward(g, stash[s], *params[s], s > 0)
        keep = keep.reshape(4, 2, share, hidden)
        got = swap(send, c=1).reshape(4, 2, share, hidden)

        def half(value, which):
            return lax.dynamic_index_in_dim(value, which, 1, keepdims=False).astype(F32)

        across = (half(keep, 1 - side) + half(got, 1 - side)).astype(BF16)
        across = swap(across, y=1)
        line = (half(keep, side) + half(got, side) + across.astype(F32)).astype(BF16)

        def level(which):
            return lax.dynamic_index_in_dim(line, which, 0, keepdims=False)

        total = level(depth).astype(F32)
        for flip in (1, 2, 3):
            total = total + swap(level(depth ^ flip), z=flip).astype(F32)
        shares[s] = total

    rows = 56
    packed = jnp.stack([jnp.pad(v, ((0, rows - taps - 2), (0, 0))) for v in smalls])
    packed = packed.reshape(2, 2, rows, 8, share).transpose(1, 0, 3, 2, 4)
    mine = lax.dynamic_index_in_dim(packed, core, 0, keepdims=False)
    mine = mine + swap(lax.dynamic_index_in_dim(packed, 1 - core, 0, keepdims=False), c=1)
    mine = mine.reshape(2, 4, 2, rows, share)
    mine = lax.dynamic_index_in_dim(mine, side, 2, keepdims=False) + swap(
        lax.dynamic_index_in_dim(mine, 1 - side, 2, keepdims=False), y=1
    )
    line = mine
    mine = lax.dynamic_index_in_dim(line, depth, 1, keepdims=False)
    for flip in (1, 2, 3):
        mine = mine + swap(lax.dynamic_index_in_dim(line, depth ^ flip, 1, keepdims=False), z=flip)
    t_small = lax.dynamic_index_in_dim(mine, chip, 0, keepdims=False) + swap(
        lax.dynamic_index_in_dim(mine, 1 - chip, 0, keepdims=False), x=1
    )

    all_shares = jnp.stack(shares).reshape(2, 2, share, hidden)
    mine = lax.dynamic_index_in_dim(all_shares, chip, 0, keepdims=False) + swap(
        lax.dynamic_index_in_dim(all_shares, 1 - chip, 0, keepdims=False).astype(BF16), x=1
    ).astype(F32)
    kept = lax.dynamic_index_in_dim(mine, core, 0, keepdims=False)
    got = swap(lax.dynamic_index_in_dim(mine, 1 - core, 0, keepdims=False), c=1)
    t_in = jnp.where(core == 0, kept, got)
    t_out = jnp.where(core == 0, got, kept).T
    return finish(t_small[:taps], t_small[taps], t_small[taps + 1], t_in, t_out)


def solution(mesh):
    in_specs = (
        P("dp", None, None, None),
        P("dp", None, None, None),
        P("segment", None, None),
        P("segment", None),
        P("segment", None, None),
        P("segment", None, None),
        P("segment", None),
    )
    out_specs = (
        P("segment", None, "dp"),
        P("segment", "dp"),
        P("segment", "dp", None),
        P("segment", None, "dp"),
        P("segment", "dp"),
    )
    fits = dict(mesh.shape) == {"dp": 8, "segment": 4}

    def whole(images, *rest):
        local = this_mesh if fits and images.shape[0] == 32 else any_mesh
        return jax.shard_map(local, mesh=mesh, in_specs=in_specs, out_specs=out_specs, check_vma=False)(images, *rest)

    return whole
```

```python
import functools
import types
import jax
import jax.numpy as jnp
from jax import lax
from jax.sharding import PartitionSpec as P
from jax.experimental import pallas as pl
from jax.experimental.pallas import tpu as pltpu

EPS = 1e-06
GELU_C = 0.7978845608028654
GELU_A = 0.044715
LANES = 128
def estimate(microseconds):
    return pl.CostEstimate(flops=int(microseconds * 1.1e9), bytes_accessed=int(microseconds * 3.6e6), transcendentals=0)


LIMIT = 40


def vmem(mebibytes):
    return pltpu.CompilerParams(vmem_limit_bytes=mebibytes * 1024 * 1024)


def zero_borders(pad_ref):
    tiles, rows, width, _ = pad_ref.shape
    for c in range(tiles):
        pad_ref[c, :, 0:8] = jnp.zeros((rows, 8, LANES), jnp.float32)
        pad_ref[c, :, width - 8 :] = jnp.zeros((rows, 8, LANES), jnp.float32)


def conv_norm_body(x_ref, small_ref, xhat_ref, normed_ref, inv_ref, pad_ref, conv_ref):
    rows, cols, channels = x_ref.shape
    tiles = channels // LANES
    for c in range(tiles):
        pad_ref[c, :, 8 : cols + 8] = x_ref[:, :, c * LANES : (c + 1) * LANES].astype(jnp.float32)

    def tile(c, carry):
        lanes = pl.ds(pl.multiple_of(c * LANES, LANES), LANES)

        def strip(w, carry):
            base = pl.multiple_of(w * 8, 8)
            window = pad_ref.at[c, :, pl.ds(base, 24), :]
            acc = [None] * rows
            for q in range(7):
                col = [window[h, 5 + q : 13 + q, :] for h in range(rows)]
                for r in range(7):
                    weight = small_ref[r * 7 + q : r * 7 + q + 1, lanes]
                    for h in range(max(0, 3 - r), min(rows, rows + 3 - r)):
                        term = weight * col[h + r - 3]
                        acc[h] = term if acc[h] is None else acc[h] + term
            for h in range(rows):
                conv_ref[h, pl.ds(base, 8), lanes] = acc[h]
            return carry

        return lax.fori_loop(0, cols // 8, strip, carry)

    lax.fori_loop(0, tiles, tile, 0)

    def norm(h, carry):
        value = conv_ref[pl.ds(h * 2, 2)].reshape(2 * cols, channels)
        mean = jnp.mean(value, axis=1, keepdims=True)
        center = value - mean
        inv = lax.rsqrt(jnp.mean(center * center, axis=1, keepdims=True) + EPS)
        xhat = center * inv
        at = pl.ds(pl.multiple_of(h * 2 * cols, 2 * cols), 2 * cols)
        xhat_ref[at, :] = xhat.astype(jnp.bfloat16)
        normed_ref[at, :] = (xhat * small_ref[TAPS : TAPS + 1, :]).astype(jnp.bfloat16)
        inv_ref[at, :] = jnp.broadcast_to(inv, (2 * cols, LANES))
        return carry

    lax.fori_loop(0, rows // 2, norm, 0, unroll=2)


def pad_shape(rows, cols, channels):
    return pltpu.VMEM((channels // LANES, rows, cols + 16, LANES), jnp.float32)


def conv_norm_kernel(x_ref, small_ref, *rest):
    xhat_ref, normed_ref, inv_ref, pad_ref, conv_ref = rest[-5:]
    zero_borders(pad_ref)
    conv_norm_body(x_ref, small_ref, xhat_ref, normed_ref, inv_ref, pad_ref, conv_ref)


def conv_norm(x, small, after=()):
    rows, cols, channels = x.shape
    n = rows * cols
    return pl.pallas_call(
        conv_norm_kernel,
        in_specs=[pl.BlockSpec(memory_space=pltpu.VMEM)] * 2 + [pl.BlockSpec(memory_space=pl.ANY)] * len(after),
        out_shape=(
            jax.ShapeDtypeStruct((n, channels), jnp.bfloat16),
            jax.ShapeDtypeStruct((n, channels), jnp.bfloat16),
            jax.ShapeDtypeStruct((n, LANES), jnp.float32),
        ),
        scratch_shapes=[pad_shape(rows, cols, channels), pltpu.VMEM((rows, cols, channels), jnp.float32)],
        compiler_params=vmem(LIMIT),
        name="conv_norm",
        cost_estimate=estimate(2.6),
    )(x, small, *after)


def in_hbm(arrays):
    return [pltpu.with_memory_space_constraint(a, pltpu.HBM) for a in arrays]


def copy_chosen(which, sources, target, sem):
    for m, source in enumerate(sources):

        @pl.when(which == m)
        def _():
            pltpu.make_async_copy(source, target, sem).start()

    return lambda: pltpu.make_async_copy(sources[0], target, sem).wait()


def forward_kernel(choices, blocks, sel_ref, x_ref, normed0_ref, small_ref, *rest):
    w_ins, w_outs, rest = rest[:choices], rest[choices : 2 * choices], rest[2 * choices :]
    xs = [x_ref] + list(rest[: blocks - 1])
    xhats, invs, rest = rest[blocks - 1 : 2 * blocks - 2], rest[2 * blocks - 2 : 3 * blocks - 3], rest[3 * blocks - 3 :]
    pres, branches, rest = rest[:blocks], rest[blocks : 2 * blocks], rest[2 * blocks :]
    normed_ref, hid_ref, acc_ref, pad_ref, conv_ref, w_in_ref, w_out_ref, sems = rest
    rows, cols, channels = x_ref.shape
    n = rows * cols
    hidden = w_in_ref.shape[2]
    waits = []
    for s in range(blocks):
        waits.append((
            copy_chosen(sel_ref[s], w_ins, w_in_ref.at[s], sems.at[0, s]),
            copy_chosen(sel_ref[s], w_outs, w_out_ref.at[s], sems.at[1, s]),
        ))
    zero_borders(pad_ref)
    step, sub = 256, 2 * cols
    for s in range(blocks):
        normed = normed0_ref if s == 0 else normed_ref
        waits[s][0]()
        for j in range(hidden // step):
            cut = slice(j * step, (j + 1) * step)
            pre = jnp.dot(normed[...], w_in_ref[s, :, cut], preferred_element_type=jnp.float32)
            for i in range(n // sub):
                p = pre[i * sub : (i + 1) * sub]
                half = 0.5 * p
                hid_ref[i * sub : (i + 1) * sub, :] = (half + half * tanh_arg(p)).astype(jnp.bfloat16)
                pres[s][i * sub : (i + 1) * sub, cut] = p.astype(jnp.bfloat16)
            if j == 0:
                waits[s][1]()
            part = jnp.dot(hid_ref[...], w_out_ref[s, cut, :], preferred_element_type=jnp.float32)
            if j == 0:
                acc_ref[...] = part
            else:
                acc_ref[...] += part
        scale = small_ref[s, TAPS + 1 : TAPS + 2, :]
        for i in range(n // sub):
            branch = acc_ref[i * sub : (i + 1) * sub, :]
            branches[s][i * sub : (i + 1) * sub, :] = branch.astype(jnp.bfloat16)
            if s < blocks - 1:
                x_old = xs[s][2 * i : 2 * i + 2].astype(jnp.float32).reshape(sub, channels)
                xs[s + 1][2 * i : 2 * i + 2] = (x_old + scale * branch).astype(jnp.bfloat16).reshape(2, cols, channels)
        if s < blocks - 1:
            conv_norm_body(xs[s + 1], small_ref.at[s + 1], xhats[s], normed_ref, invs[s], pad_ref, conv_ref)


def forward(sel, x, normed0, small, w_ins, w_outs):
    blocks = small.shape[0]
    rows, cols, channels = x.shape
    n = rows * cols
    hidden = w_ins[0].shape[1]
    out = pl.pallas_call(
        functools.partial(forward_kernel, len(w_ins), blocks),
        in_specs=[pl.BlockSpec(memory_space=pltpu.SMEM)]
        + [pl.BlockSpec(memory_space=pltpu.VMEM)] * 3
        + [pl.BlockSpec(memory_space=pl.ANY)] * (2 * len(w_ins)),
        out_shape=(jax.ShapeDtypeStruct((rows, cols, channels), jnp.bfloat16),) * (blocks - 1)
        + (jax.ShapeDtypeStruct((n, channels), jnp.bfloat16),) * (blocks - 1)
        + (jax.ShapeDtypeStruct((n, LANES), jnp.float32),) * (blocks - 1)
        + (jax.ShapeDtypeStruct((n, hidden), jnp.bfloat16),) * blocks
        + (jax.ShapeDtypeStruct((n, channels), jnp.bfloat16),) * blocks,
        scratch_shapes=[
            pltpu.VMEM((n, channels), jnp.bfloat16),
            pltpu.VMEM((n, 256), jnp.bfloat16),
            pltpu.VMEM((n, channels), jnp.float32),
            pad_shape(rows, cols, channels),
            pltpu.VMEM((rows, cols, channels), jnp.float32),
            pltpu.VMEM((blocks, channels, hidden), jnp.bfloat16),
            pltpu.VMEM((blocks, hidden, channels), jnp.bfloat16),
            pltpu.SemaphoreType.DMA((2, blocks)),
        ],
        compiler_params=vmem(LIMIT),
        name="forward",
        cost_estimate=estimate(15),
    )(sel, x, normed0, small, *in_hbm(w_ins), *in_hbm(w_outs))
    k = blocks - 1
    return out[:k], out[k : 2 * k], out[2 * k : 3 * k], out[3 * k : 3 * k + blocks], out[3 * k + blocks :]


def tanh_arg(x):
    return jnp.tanh(x * (GELU_C + (GELU_C * GELU_A) * (x * x)))


def load_weights(sel_ref, w_ins, w_outs, w_in_ref, w_out_ref, sems):
    for m in range(len(w_ins)):

        @pl.when(sel_ref[0] == m)
        def _():
            pltpu.make_async_copy(w_ins[m], w_in_ref, sems.at[0]).start()
            pltpu.make_async_copy(w_outs[m], w_out_ref, sems.at[1]).start()

    return (
        pltpu.make_async_copy(w_ins[0], w_in_ref, sems.at[0]).wait,
        pltpu.make_async_copy(w_outs[0], w_out_ref, sems.at[1]).wait,
    )


def specs(sel, arrays, choices, after=0):
    return (
        [pl.BlockSpec(memory_space=pltpu.SMEM)]
        + [pl.BlockSpec(memory_space=pltpu.VMEM)] * arrays
        + [pl.BlockSpec(memory_space=pl.ANY)] * (2 * choices + after)
    )


def mlp_back_kernel(choices, after, sel_ref, g_ref, branch_ref, pre_ref, xhat_ref, inv_ref, gain_ref, scale_ref, *rest):
    w_ins, w_outs = rest[:choices], rest[choices : 2 * choices]
    (keep_ref, send_ref, small_ref, gconv_ref,
     gb_ref, nm_ref, hid_ref, gp_ref, acc_ref, w_in_ref, w_out_ref, sems) = rest[2 * choices + after :]
    wait_in, wait_out = load_weights(sel_ref, w_ins, w_outs, w_in_ref, w_out_ref, sems)
    first = sel_ref[1] == 0
    n, channels = g_ref.shape
    hidden = w_in_ref.shape[1]
    step = 256
    sub = 32
    scale_sum = jnp.zeros((8, channels), jnp.float32)
    for i in range(n // sub):
        at = slice(i * sub, (i + 1) * sub)
        g = g_ref[at, :].astype(jnp.float32)
        scale_sum = scale_sum + jnp.sum((g * branch_ref[at, :].astype(jnp.float32)).reshape(sub // 8, 8, channels), axis=0)
        gb_ref[at, :] = (g * scale_ref[...]).astype(jnp.bfloat16)
        nm_ref[at, :] = (xhat_ref[at, :].astype(jnp.float32) * gain_ref[...]).astype(jnp.bfloat16)
    gb_t = gb_ref[...].T
    nm_t = nm_ref[...].T
    wait_in()
    wait_out()
    for j in range(hidden // step):
        cut = slice(j * step, (j + 1) * step)
        gh = lax.dot_general(gb_ref[...], w_out_ref[cut, :], (((1,), (1,)), ((), ())), preferred_element_type=jnp.float32)
        for i in range(n // sub):
            at = slice(i * sub, (i + 1) * sub)
            p = pre_ref[at, cut].astype(jnp.float32)
            sq = p * p
            t = jnp.tanh(p * (GELU_C + (GELU_C * GELU_A) * sq))
            cdf = 0.5 + 0.5 * t
            hid_ref[at, :] = (p * cdf).astype(jnp.bfloat16)
            slope = cdf + (0.5 * p) * (1.0 - t * t) * (GELU_C + (3.0 * GELU_C * GELU_A) * sq)
            gp_ref[at, :] = (gh[at, :] * slope).astype(jnp.bfloat16)
        t_out = jnp.dot(gb_t, hid_ref[...], preferred_element_type=jnp.float32)
        t_in = jnp.dot(nm_t, gp_ref[...], preferred_element_type=jnp.float32)
        keep_ref[:, cut] = jnp.where(first, t_in, t_out).astype(jnp.bfloat16)
        send_ref[:, cut] = jnp.where(first, t_out, t_in).astype(jnp.bfloat16)
        part = lax.dot_general(gp_ref[...], w_in_ref[:, cut], (((1,), (1,)), ((), ())), preferred_element_type=jnp.float32)
        if j == 0:
            acc_ref[...] = part
        else:
            acc_ref[...] += part
    gain_sum = jnp.zeros((8, channels), jnp.float32)
    for i in range(n // sub):
        at = slice(i * sub, (i + 1) * sub)
        gn = acc_ref[at, :]
        xhat = xhat_ref[at, :].astype(jnp.float32)
        gain_sum = gain_sum + jnp.sum((gn * xhat).reshape(sub // 8, 8, channels), axis=0)
        gx = gn * gain_ref[...]
        m1 = jnp.mean(gx, axis=1, keepdims=True)
        m2 = jnp.mean(gx * xhat, axis=1, keepdims=True)
        inv = inv_ref[at, 0:1]
        gconv_ref[at, :] = inv * (gx - m1 - xhat * m2)
    small_ref[0:1, :] = jnp.sum(gain_sum, axis=0, keepdims=True)
    small_ref[1:2, :] = jnp.sum(scale_sum, axis=0, keepdims=True)
    small_ref[2:8, :] = jnp.zeros((6, channels), jnp.float32)


def mlp_back(sel, g, branch, pre, xhat, inv, gain, scale, w_ins, w_outs, after=()):
    n, channels = g.shape
    hidden = w_ins[0].shape[1]
    return pl.pallas_call(
        functools.partial(mlp_back_kernel, len(w_ins), len(after)),
        in_specs=specs(sel, 7, len(w_ins), len(after)),
        out_shape=(
            jax.ShapeDtypeStruct((channels, hidden), jnp.bfloat16),
            jax.ShapeDtypeStruct((channels, hidden), jnp.bfloat16),
            jax.ShapeDtypeStruct((8, channels), jnp.float32),
            jax.ShapeDtypeStruct((n, channels), jnp.float32),
        ),
        scratch_shapes=[
            pltpu.VMEM((n, channels), jnp.bfloat16),
            pltpu.VMEM((n, channels), jnp.bfloat16),
            pltpu.VMEM((n, 256), jnp.bfloat16),
            pltpu.VMEM((n, 256), jnp.bfloat16),
            pltpu.VMEM((n, channels), jnp.float32),
            pltpu.VMEM((channels, hidden), jnp.bfloat16),
            pltpu.VMEM((hidden, channels), jnp.bfloat16),
            pltpu.SemaphoreType.DMA((2,)),
        ],
        compiler_params=vmem(LIMIT),
        name="mlp_back",
        cost_estimate=estimate(2.5),
    )(sel, g, branch, pre, xhat, inv, gain, scale, *in_hbm(w_ins), *in_hbm(w_outs), *after)


SMALL_ROWS = 64
TAPS = 49


def conv_back_kernel(need_map, after, gconv_ref, x_ref, g_ref, k_ref, small_ref, *rest):
    *out_ref, tk_ref, pad_ref, sum_ref, wide_ref, map_ref = rest[after:]
    conv_back_body(gconv_ref, x_ref, g_ref, k_ref, small_ref, out_ref[0] if need_map else None, tk_ref,
                   pad_ref, sum_ref, wide_ref, map_ref)


def conv_back(gconv, x, g, kernel, small, need_map=True, after=()):
    rows, cols, channels = x.shape
    out = (jax.ShapeDtypeStruct((SMALL_ROWS, channels), jnp.float32),)
    if need_map:
        out = (jax.ShapeDtypeStruct((rows, cols, channels), jnp.bfloat16),) + out
    return pl.pallas_call(
        functools.partial(conv_back_kernel, need_map, len(after)),
        in_specs=[pl.BlockSpec(memory_space=pltpu.VMEM)] * 5 + [pl.BlockSpec(memory_space=pl.ANY)] * len(after),
        out_shape=out,
        scratch_shapes=[
            pad_shape(rows, cols, channels),
            pltpu.VMEM((cols // 8, TAPS, 8, LANES), jnp.float32),
            pltpu.VMEM((rows, cols, channels), jnp.float32),
            pltpu.VMEM((rows, cols, channels), jnp.float32),
        ],
        compiler_params=vmem(LIMIT),
        name="conv_back",
        cost_estimate=estimate(3.4 if need_map else 1.6),
    )(gconv, x, g, kernel, small, *after)


def small_call(kernel, name, outs, *args, scratch=(), after=()):
    used = len(args)

    def body(*refs):
        kernel(*refs[:used], *refs[used + len(after) :])

    return pl.pallas_call(
        body,
        in_specs=[pl.BlockSpec(memory_space=pltpu.SMEM)]
        + [pl.BlockSpec(memory_space=pltpu.VMEM)] * (used - 1)
        + [pl.BlockSpec(memory_space=pl.ANY)] * len(after),
        out_shape=tuple(jax.ShapeDtypeStruct(*o) for o in outs),
        scratch_shapes=list(scratch),
        compiler_params=vmem(LIMIT),
        name=name,
        cost_estimate=estimate(0.7),
    )(*args, *after)


def conv_back_body(gconv_ref, x_ref, g_ref, small_ref, sums8_ref, out_ref, tk_ref, pad_ref, sum_ref, wide_ref, map_ref):
    rows, cols, channels = x_ref.shape
    tiles = channels // LANES
    zero_borders(pad_ref)
    for c in range(tiles):
        pad_ref[c, :, 8 : cols + 8] = gconv_ref[:, c * LANES : (c + 1) * LANES].reshape(rows, cols, LANES)

    for h in range(rows):
        wide_ref[h] = x_ref[h].astype(jnp.float32)

    def tile(c, carry):
        lanes = pl.ds(pl.multiple_of(c * LANES, LANES), LANES)

        def strip(w, carry):
            base = pl.multiple_of(w * 8, 8)
            window = pad_ref.at[c, :, pl.ds(base, 24), :]
            xs = [wide_ref[h, pl.ds(base, 8), lanes] for h in range(rows)]
            acc = [None] * rows
            for q in range(7):
                col = [window[h, 11 - q : 19 - q, :] for h in range(rows)]
                for r in range(7):
                    tap = r * 7 + q
                    if out_ref is not None:
                        weight = small_ref[tap : tap + 1, lanes]
                    total = None
                    for h in range(max(0, r - 3), min(rows, rows + r - 3)):
                        shifted = col[h + 3 - r]
                        term = xs[h] * shifted
                        total = term if total is None else total + term
                        if out_ref is not None:
                            moved = weight * shifted
                            acc[h] = moved if acc[h] is None else acc[h] + moved
                    sum_ref[w, tap] = total
            if out_ref is not None:
                for h in range(rows):
                    map_ref[h, pl.ds(base, 8), lanes] = acc[h]
            return carry

        lax.fori_loop(0, cols // 8, strip, 0)
        tk_ref[0:TAPS, lanes] = jnp.sum(sum_ref[0] + sum_ref[1], axis=1)
        return carry

    lax.fori_loop(0, tiles, tile, 0)
    if out_ref is not None:
        for h in range(rows):
            out_ref[h] = (g_ref[h].astype(jnp.float32) + map_ref[h]).astype(jnp.bfloat16)
    tk_ref[TAPS : TAPS + 2, :] = sums8_ref[0:2, :]
    tk_ref[TAPS + 2 :, :] = jnp.zeros((SMALL_ROWS - TAPS - 2, channels), jnp.float32)


def mlp_back_body(first, g_ref, branch_ref, pre_ref, xhat_ref, inv_ref, small_ref, wait_in, wait_out, w_in_ref, w_out_ref,
                  keep_ref, send_ref, sums8_ref, gconv_ref, gb_ref, nm_ref, hid_ref, gp_ref, acc_ref, before=None):
    rows, cols, channels = g_ref.shape
    n = rows * cols
    hidden = w_in_ref.shape[1]
    step = 256
    sub = 2 * cols
    gain = small_ref[TAPS : TAPS + 1, :]
    scale = small_ref[TAPS + 1 : TAPS + 2, :]
    scale_sum = jnp.zeros((8, channels), jnp.float32)
    for i in range(n // sub):
        at = slice(i * sub, (i + 1) * sub)
        g = g_ref[2 * i : 2 * i + 2].astype(jnp.float32).reshape(sub, channels)
        scale_sum = scale_sum + jnp.sum((g * branch_ref[at, :].astype(jnp.float32)).reshape(sub // 8, 8, channels), axis=0)
        gb_ref[at, :] = (g * scale).astype(jnp.bfloat16)
        nm_ref[at, :] = (xhat_ref[at, :].astype(jnp.float32) * gain).astype(jnp.bfloat16)
    gb_t = gb_ref[...].T
    nm_t = nm_ref[...].T
    wait_in()
    wait_out()
    for j in range(hidden // step):
        cut = slice(j * step, (j + 1) * step)
        gh = lax.dot_general(gb_ref[...], w_out_ref[cut, :], (((1,), (1,)), ((), ())), preferred_element_type=jnp.float32)
        for i in range(n // sub):
            at = slice(i * sub, (i + 1) * sub)
            p = pre_ref[at, cut].astype(jnp.float32)
            sq = p * p
            t = jnp.tanh(p * (GELU_C + (GELU_C * GELU_A) * sq))
            cdf = 0.5 + 0.5 * t
            hid_ref[at, :] = (p * cdf).astype(jnp.bfloat16)
            slope = cdf + (0.5 * p) * (1.0 - t * t) * (GELU_C + (3.0 * GELU_C * GELU_A) * sq)
            gp_ref[at, :] = (gh[at, :] * slope).astype(jnp.bfloat16)
        t_out = jnp.dot(gb_t, hid_ref[...], preferred_element_type=jnp.float32)
        t_in = jnp.dot(nm_t, gp_ref[...], preferred_element_type=jnp.float32)
        t_keep = jnp.where(first, t_in, t_out)
        t_send = jnp.where(first, t_out, t_in)
        if before is not None:
            t_keep = t_keep + before[0][:, cut].astype(jnp.float32)
            t_send = t_send + before[1][:, cut].astype(jnp.float32)
        keep_ref[:, cut] = t_keep.astype(jnp.bfloat16)
        send_ref[:, cut] = t_send.astype(jnp.bfloat16)
        part = lax.dot_general(gp_ref[...], w_in_ref[:, cut], (((1,), (1,)), ((), ())), preferred_element_type=jnp.float32)
        if j == 0:
            acc_ref[...] = part
        else:
            acc_ref[...] += part
    gain_sum = jnp.zeros((8, channels), jnp.float32)
    for i in range(n // sub):
        at = slice(i * sub, (i + 1) * sub)
        gn = acc_ref[at, :]
        xhat = xhat_ref[at, :].astype(jnp.float32)
        gain_sum = gain_sum + jnp.sum((gn * xhat).reshape(sub // 8, 8, channels), axis=0)
        gx = gn * gain
        m1 = jnp.mean(gx, axis=1, keepdims=True)
        m2 = jnp.mean(gx * xhat, axis=1, keepdims=True)
        gconv_ref[at, :] = inv_ref[at, 0:1] * (gx - m1 - xhat * m2)
    sums8_ref[0:1, :] = jnp.sum(gain_sum, axis=0, keepdims=True)
    sums8_ref[1:2, :] = jnp.sum(scale_sum, axis=0, keepdims=True)
    sums8_ref[2:8, :] = jnp.zeros((6, channels), jnp.float32)


def named_call(name, body, ins, outs, scratch, cost):
    names = list(ins) + list(outs) + list(scratch)
    spaces = {"v": pltpu.VMEM, "s": pltpu.SMEM, "a": pl.ANY, "h": pl.ANY}

    def kernel(*refs):
        body(types.SimpleNamespace(**dict(zip(names, refs))))

    args = [pltpu.with_memory_space_constraint(a, pltpu.HBM) if kind == "h" else a for a, kind in ins.values()]
    result = pl.pallas_call(
        kernel,
        in_specs=[pl.BlockSpec(memory_space=spaces[kind]) for _, kind in ins.values()],
        out_shape=tuple(jax.ShapeDtypeStruct(*o) for o in outs.values()),
        scratch_shapes=list(scratch.values()),
        compiler_params=vmem(LIMIT),
        name=name,
        cost_estimate=estimate(cost),
    )(*args)
    return types.SimpleNamespace(**dict(zip(outs, result)))


def mlp_body(normed_ref, wait_in, wait_out, w_in_ref, w_out_ref, pre_ref, hid_ref, acc_ref):
    n = normed_ref.shape[0]
    hidden = w_in_ref.shape[1]
    step, sub = 256, 32
    wait_in()
    for j in range(hidden // step):
        cut = slice(j * step, (j + 1) * step)
        pre = jnp.dot(normed_ref[...], w_in_ref[:, cut], preferred_element_type=jnp.float32)
        for i in range(n // sub):
            p = pre[i * sub : (i + 1) * sub]
            half = 0.5 * p
            hid_ref[i * sub : (i + 1) * sub, :] = (half + half * tanh_arg(p)).astype(jnp.bfloat16)
            pre_ref[i * sub : (i + 1) * sub, cut] = p.astype(jnp.bfloat16)
        if j == 0:
            wait_out()
        part = jnp.dot(hid_ref[...], w_out_ref[cut, :], preferred_element_type=jnp.float32)
        if j == 0:
            acc_ref[...] = part
        else:
            acc_ref[...] += part


def residual_body(x_ref, small_ref, acc_ref, branch_ref, y_ref):
    rows, cols, channels = x_ref.shape
    scale = small_ref[TAPS + 1 : TAPS + 2, :]
    sub = 2 * cols
    for i in range(rows // 2):
        branch = acc_ref[i * sub : (i + 1) * sub, :]
        branch_ref[i * sub : (i + 1) * sub, :] = branch.astype(jnp.bfloat16)
        if y_ref is not None:
            old = x_ref[2 * i : 2 * i + 2].astype(jnp.float32).reshape(sub, channels)
            y_ref[2 * i : 2 * i + 2] = (old + scale * branch).astype(jnp.bfloat16).reshape(2, cols, channels)


def weight_ins(pair):
    return {k: (v, "h") for k, v in zip(("own_in", "near_in", "own_out", "near_out"), pair)}


def weight_scratch(blocks, channels, hidden):
    return {
        "w_in": pltpu.VMEM((blocks, channels, hidden), jnp.bfloat16),
        "w_out": pltpu.VMEM((blocks, hidden, channels), jnp.bfloat16),
        "w_sem": pltpu.SemaphoreType.DMA((2, blocks)),
    }


def start_weights(r, slot, block):
    return (
        copy_chosen(r.sel[block], (r.own_in, r.near_in), r.w_in.at[slot], r.w_sem.at[0, slot]),
        copy_chosen(r.sel[block], (r.own_out, r.near_out), r.w_out.at[slot], r.w_sem.at[1, slot]),
    )


def pair_forward(sel, x, first, small, weights):
    rows, cols, channels = x.shape
    n, hidden = rows * cols, weights[0].shape[1]
    bf16, f32 = jnp.bfloat16, jnp.float32

    def body(r):
        low, high = start_weights(r, 0, 0), start_weights(r, 1, 1)
        zero_borders(r.pad)
        mlp_body(r.normed0, *low, r.w_in.at[0], r.w_out.at[0], r.pre0, r.hid, r.acc)
        residual_body(r.x, r.small.at[0], r.acc, r.branch0, r.x1)
        conv_norm_body(r.x1, r.small.at[1], r.xhat1, r.normed, r.inv1, r.pad, r.conv)
        mlp_body(r.normed, *high, r.w_in.at[1], r.w_out.at[1], r.pre1, r.hid, r.acc)
        residual_body(r.x1, r.small.at[1], r.acc, r.branch1, r.y)

    return named_call(
        "pair_forward", body,
        {"sel": (sel, "s"), "x": (x, "v"), "normed0": (first[1], "v"), "small": (small, "v"), **weight_ins(weights)},
        {"y": (x.shape, bf16), "x1": (x.shape, bf16), "xhat1": ((n, channels), bf16), "inv1": ((n, LANES), f32),
         "pre0": ((n, hidden), bf16), "pre1": ((n, hidden), bf16),
         "branch0": ((n, channels), bf16), "branch1": ((n, channels), bf16)},
        {"normed": pltpu.VMEM((n, channels), bf16), "hid": pltpu.VMEM((n, 256), bf16), "acc": pltpu.VMEM((n, channels), f32),
         "pad": pad_shape(rows, cols, channels), "conv": pltpu.VMEM((rows, cols, channels), f32),
         **weight_scratch(2, channels, hidden)},
        7.5,
    )


def back_scratch(n, channels):
    bf16, f32 = jnp.bfloat16, jnp.float32
    return {"gb": pltpu.VMEM((n, channels), bf16), "nm": pltpu.VMEM((n, channels), bf16),
            "hid": pltpu.VMEM((n, 256), bf16), "gp": pltpu.VMEM((n, 256), bf16), "acc": pltpu.VMEM((n, channels), f32)}


def back_temps(r):
    return r.gb, r.nm, r.hid, r.gp, r.acc


GRADS = ("keep0", "send0", "keep1", "send1")


def pair_both(sel, x, g, small, weights, before=None):
    rows, cols, channels = x.shape
    n, hidden = rows * cols, weights[0].shape[1]
    bf16, f32 = jnp.bfloat16, jnp.float32

    def body(r):
        @pl.when(r.sel[2] == 1)
        def _():
            core = r.sel[3] == 0
            low, high = start_weights(r, 0, 0), start_weights(r, 1, 1)
            waits = []
            if before is not None:
                for k, name in enumerate(GRADS):
                    copy = pltpu.make_async_copy(getattr(r, "old_" + name), r.olds.at[k], r.o_sem.at[k])
                    copy.start()
                    waits.append(copy.wait)
            zero_borders(r.pad)
            s0, s1 = r.small.at[0], r.small.at[1]
            conv_norm_body(r.x, s0, r.xhat0, r.normed, r.inv0, r.pad, r.conv)
            mlp_body(r.normed, *low, r.w_in.at[0], r.w_out.at[0], r.pre0, r.hid, r.acc)
            residual_body(r.x, s0, r.acc, r.branch0, r.x1)
            conv_norm_body(r.x1, s1, r.xhat1, r.normed, r.inv1, r.pad, r.conv)
            mlp_body(r.normed, *high, r.w_in.at[1], r.w_out.at[1], r.pre1, r.hid, r.acc)
            residual_body(r.x1, s1, r.acc, r.branch1, None)
            for wait in waits:
                wait()
            done = (lambda: None,) * 2
            mlp_back_body(core, r.g, r.branch1, r.pre1, r.xhat1, r.inv1, s1, *done, r.w_in.at[1], r.w_out.at[1],
                          r.keep1, r.send1, r.sums8, r.gconv, *back_temps(r),
                          before=None if before is None else (r.olds.at[2], r.olds.at[3]))
            conv_back_body(r.gconv, r.x1, r.g, s1, r.sums8, r.g1, r.small1, r.pad, r.sum, r.wide, r.map)
            mlp_back_body(core, r.g1, r.branch0, r.pre0, r.xhat0, r.inv0, s0, *done, r.w_in.at[0], r.w_out.at[0],
                          r.keep0, r.send0, r.sums8, r.gconv, *back_temps(r),
                          before=None if before is None else (r.olds.at[0], r.olds.at[1]))
            conv_back_body(r.gconv, r.x, r.g1, s0, r.sums8, r.g0, r.small0, r.pad, r.sum, r.wide, r.map)
            if before is not None:
                r.small0[...] += r.old_small0[...]
                r.small1[...] += r.old_small1[...]

    ins = {"sel": (sel, "s"), "x": (x, "v"), "g": (g, "v"), "small": (small, "v"), **weight_ins(weights)}
    scratch = {}
    if before is not None:
        ins.update({"old_" + name: (getattr(before, name), "a") for name in GRADS})
        ins.update({"old_" + name: (getattr(before, name), "v") for name in ("small0", "small1")})
        scratch = {"olds": pltpu.VMEM((4, channels, hidden), bf16), "o_sem": pltpu.SemaphoreType.DMA((4,))}
    grad = ((channels, hidden), bf16)
    small_out = ((SMALL_ROWS, channels), f32)
    return named_call(
        "pair_both", body, ins,
        {"g0": (x.shape, bf16), "keep0": grad, "send0": grad, "keep1": grad, "send1": grad,
         "small0": small_out, "small1": small_out},
        {"x1": pltpu.VMEM(x.shape, bf16), "g1": pltpu.VMEM(x.shape, bf16),
         "xhat0": pltpu.VMEM((n, channels), bf16), "xhat1": pltpu.VMEM((n, channels), bf16),
         "inv0": pltpu.VMEM((n, LANES), f32), "inv1": pltpu.VMEM((n, LANES), f32),
         "pre0": pltpu.VMEM((n, hidden), bf16), "pre1": pltpu.VMEM((n, hidden), bf16),
         "branch0": pltpu.VMEM((n, channels), bf16), "branch1": pltpu.VMEM((n, channels), bf16),
         "normed": pltpu.VMEM((n, channels), bf16), "gconv": pltpu.VMEM((n, channels), f32),
         "sums8": pltpu.VMEM((8, channels), f32),
         "pad": pad_shape(rows, cols, channels), "conv": pltpu.VMEM((rows, cols, channels), f32),
         "sum": pltpu.VMEM((cols // 8, TAPS, 8, LANES), f32),
         "wide": pltpu.VMEM(x.shape, f32), "map": pltpu.VMEM(x.shape, f32),
         **back_scratch(n, channels), **weight_scratch(2, channels, hidden), **scratch},
        17,
    )


def start_olds(r):
    return [copy_chosen(r.sel[2], (getattr(r, "a_" + name), getattr(r, "p_" + name)), r.olds.at[k], r.o_sem.at[k])
            for k, name in enumerate(("keep", "send"))]


def old_ins(before, block):
    ins = {}
    for prefix, part in zip("ap", before):
        for name in ("keep", "send"):
            ins[prefix + "_" + name] = (getattr(part, name + str(block)), "a")
    return ins


def pair_back_high(sel, g, kept, small, weights, before=None, after=()):
    rows, cols, channels = g.shape
    n, hidden = rows * cols, weights[0].shape[1]
    bf16, f32 = jnp.bfloat16, jnp.float32

    def body(r):
        waits = [] if before is None else start_olds(r)

        @pl.when(r.sel[2] == 0)
        def _():
            high = start_weights(r, 0, 1)
            for wait in waits:
                wait()
            mlp_back_body(r.sel[3] == 0, r.g, r.branch1, r.pre1, r.xhat1, r.inv1, r.small.at[1], *high,
                          r.w_in.at[0], r.w_out.at[0], r.keep, r.send, r.sums8, r.gconv, *back_temps(r),
                          before=None if before is None else (r.olds.at[0], r.olds.at[1]))

        if before is not None:

            @pl.when(r.sel[2] == 1)
            def _():
                for wait in waits:
                    wait()
                r.keep[...] = r.olds[0]
                r.send[...] = r.olds[1]

    ins = {"sel": (sel, "s"), "g": (g, "v"), "branch1": (kept.branch1, "v"), "pre1": (kept.pre1, "v"),
           "xhat1": (kept.xhat1, "v"), "inv1": (kept.inv1, "v"), "small": (small, "v"), **weight_ins(weights)}
    scratch = {}
    if before is not None:
        ins.update(old_ins(before, 1))
        ins.update({"after%d" % k: (v, "a") for k, v in enumerate(after)})
        scratch = {"olds": pltpu.VMEM((2, channels, hidden), bf16), "o_sem": pltpu.SemaphoreType.DMA((2,))}
    return named_call(
        "pair_back_high", body, ins,
        {"keep": ((channels, hidden), bf16), "send": ((channels, hidden), bf16), "sums8": ((8, channels), f32),
         "gconv": ((n, channels), f32)},
        {**back_scratch(n, channels), **weight_scratch(1, channels, hidden), **scratch},
        2.5,
    )


def pair_back_low(sel, g, high, x, x1, first, kept, small, weights, before=None, after=()):
    rows, cols, channels = g.shape
    n, hidden = rows * cols, weights[0].shape[1]
    bf16, f32 = jnp.bfloat16, jnp.float32

    def body(r):
        waits = [] if before is None else start_olds(r)

        @pl.when(r.sel[2] == 0)
        def _():
            low = start_weights(r, 0, 0)
            conv_back_body(r.gconv1, r.x1, r.g, r.small.at[1], r.sums1, r.g1, r.small1, r.pad, r.sum, r.wide, r.map)
            if before is not None:
                r.small1[...] += r.a_small1[...]
            for wait in waits:
                wait()
            mlp_back_body(r.sel[3] == 0, r.g1, r.branch0, r.pre0, r.xhat0, r.inv0, r.small.at[0], *low,
                          r.w_in.at[0], r.w_out.at[0], r.keep, r.send, r.sums8, r.gconv, *back_temps(r),
                          before=None if before is None else (r.olds.at[0], r.olds.at[1]))

        if before is not None:

            @pl.when(r.sel[2] == 1)
            def _():
                for wait in waits:
                    wait()
                r.keep[...] = r.olds[0]
                r.send[...] = r.olds[1]
                r.small1[...] = r.p_small1[...]

    ins = {"sel": (sel, "s"), "g": (g, "v"), "gconv1": (high.gconv, "v"), "sums1": (high.sums8, "v"), "x1": (x1, "v"),
           "branch0": (kept.branch0, "v"), "pre0": (kept.pre0, "v"), "xhat0": (first[0], "v"), "inv0": (first[2], "v"),
           "small": (small, "v"), **weight_ins(weights)}
    scratch = {}
    if before is not None:
        ins.update(old_ins(before, 0))
        ins.update({"a_small1": (before[0].small1, "v"), "p_small1": (before[1].small1, "v")})
        scratch = {"olds": pltpu.VMEM((2, channels, hidden), bf16), "o_sem": pltpu.SemaphoreType.DMA((2,))}
    ins.update({"after%d" % k: (v, "a") for k, v in enumerate(after)})
    return named_call(
        "pair_back_low", body, ins,
        {"small1": ((SMALL_ROWS, channels), f32), "keep": ((channels, hidden), bf16), "send": ((channels, hidden), bf16),
         "sums8": ((8, channels), f32), "gconv": ((n, channels), f32)},
        {"g1": pltpu.VMEM(g.shape, bf16), "pad": pad_shape(rows, cols, channels), "sum": pltpu.VMEM((cols // 8, TAPS, 8, LANES), f32),
         "wide": pltpu.VMEM(x.shape, f32), "map": pltpu.VMEM(x.shape, f32),
         **back_scratch(n, channels), **weight_scratch(1, channels, hidden), **scratch},
        5.5,
    )


def pair_back_conv(sel, low, x, before=None, after=()):
    rows, cols, channels = x.shape

    def body(r):
        @pl.when(r.sel[2] == 0)
        def _():
            conv_back_body(r.gconv, r.x, None, None, r.sums8, None, r.small0, r.pad, r.sum, r.wide, r.map)
            if before is not None:
                r.small0[...] += r.a_small0[...]

        if before is not None:

            @pl.when(r.sel[2] == 1)
            def _():
                r.small0[...] = r.p_small0[...]

    ins = {"sel": (sel, "s"), "gconv": (low.gconv, "v"), "sums8": (low.sums8, "v"), "x": (x, "v")}
    if before is not None:
        ins.update({"a_small0": (before[0].small0, "v"), "p_small0": (before[1].small0, "v")})
    ins.update({"after%d" % k: (v, "a") for k, v in enumerate(after)})
    return named_call(
        "pair_back_conv", body, ins, {"small0": ((SMALL_ROWS, channels), jnp.float32)},
        {"pad": pad_shape(rows, cols, channels), "sum": pltpu.VMEM((cols // 8, TAPS, 8, LANES), jnp.float32),
         "wide": pltpu.VMEM(x.shape, jnp.float32), "map": pltpu.VMEM(x.shape, jnp.float32)},
        1.6,
    ).small0


def pack_kernel(sel_ref, s0_ref, s1_ref, out_ref):
    out_ref[...] = jnp.concatenate([s0_ref[...], s1_ref[...]], axis=0).T.astype(jnp.bfloat16)


def pack(core, smalls):
    return small_call(pack_kernel, "pack", (((smalls[0].shape[1], 2 * SMALL_ROWS), jnp.bfloat16),), core, *smalls)[0]


def add(a, b):
    return a.astype(jnp.float32) + b.astype(jnp.float32)


def side_kernel(sel_ref, keep_ref, got_ref, *refs):
    *small_ref, across_ref, mine_ref = refs
    side = sel_ref[0]
    levels, _, _, hidden = keep_ref.shape
    for level in range(levels):
        for out_ref, which in ((across_ref, 1 - side), (mine_ref, side)):
            out_ref[level, :, :hidden] = add(keep_ref[level, which], got_ref[level, which]).astype(jnp.bfloat16)
            if small_ref:
                out_ref[level, :, hidden:] = small_ref[0][level, which]


def to_side(side, *arrays):
    arrays = [v.reshape(4, 2, v.shape[0] // 8, v.shape[1]) for v in arrays]
    width = sum(v.shape[3] for v in arrays[1:])
    out = ((4, arrays[0].shape[2], width), jnp.bfloat16)
    return small_call(side_kernel, "to_side", (out, out), side, *arrays)


def depth_kernel(sel_ref, mine_ref, got_ref, *out_refs):
    for k, out_ref in enumerate(out_refs):
        out_ref[...] = add(mine_ref[sel_ref[k]], got_ref[sel_ref[k]]).astype(jnp.bfloat16)


def to_depths(levels, mine, got, after=()):
    return small_call(depth_kernel, "to_depths", ((mine.shape[1:], jnp.bfloat16),) * 4, levels, mine, got, after=after)


def core_kernel(sel_ref, *refs):
    *parts, own_ref, send_ref = refs
    hidden = parts[-1].shape[1]
    low, high = (add(a[...], b[...]) + add(c[...], d[...]) for a, b, c, d in (parts[:4], parts[4:]))
    first = sel_ref[0] == 0
    small = low[:, hidden:]
    turned = pltpu.roll(small, SMALL_ROWS, 1)
    low = low[:, :hidden]
    own_ref[:, :hidden] = jnp.where(first, low, high)
    own_ref[:, hidden:] = jnp.where(first, small, turned)
    send_ref[:, :hidden] = jnp.where(first, high, low).astype(jnp.bfloat16)
    send_ref[:, hidden:] = jnp.where(first, turned, small).astype(jnp.bfloat16)


def to_core(core, parts):
    shape = (parts[-1].shape[0], parts[-1].shape[1] + 2 * SMALL_ROWS)
    return small_call(core_kernel, "to_core", ((shape, jnp.float32), (shape, jnp.bfloat16)), core, *parts)


def final_kernel(sel_ref, own_ref, got_ref, k_ref, gain_ref, in_ref, out_ref, scale_ref, pad_ref):
    share, hidden = own_ref.shape[0], in_ref.shape[2]
    taps = k_ref.shape[2]
    first = sel_ref[0] == 0
    own, got = own_ref[:, :hidden], got_ref[:, :hidden].astype(jnp.float32)
    in_ref[0] = jnp.where(first, own, got)
    out_ref[0] = jnp.where(first, got, own)
    small = add(own_ref[:, hidden:], got_ref[:, hidden:])
    k_ref[0] = small[:, :taps]
    pad_ref[0:share, :] = small
    turned = pad_ref[...].T
    gain_ref[...] = turned[taps : taps + 1, :share]
    scale_ref[...] = turned[taps + 1 : taps + 2, :share]


def final(core, own, got, taps):
    share, hidden = own.shape[0], own.shape[1] - 2 * SMALL_ROWS
    outs = (
        ((1, share, taps), jnp.float32),
        ((1, share), jnp.float32),
        ((1, share, hidden), jnp.float32),
        ((1, share, hidden), jnp.float32),
        ((1, share), jnp.float32),
    )
    t_kernel, t_gain, t_in, t_out, t_scale = small_call(
        final_kernel, "final", outs, core, own, got, scratch=[pltpu.VMEM((LANES, 2 * SMALL_ROWS), jnp.float32)]
    )
    return t_kernel.transpose(0, 2, 1), t_gain, t_in, t_out.transpose(0, 2, 1), t_scale


BF16 = jnp.bfloat16
F32 = jnp.float32


def one_image(x, g, small, sels, w_ins, w_outs, first, passing):
    blocks = small.shape[0]
    rows, cols, channels = x.shape
    which = jnp.stack([sel[0] for sel in sels])
    xs, xhats, invs, pres, branches = forward(which, x, first[1], small, w_ins, w_outs)
    xs, xhats, invs = (x,) + tuple(xs), first[:1] + tuple(xhats), first[2:] + tuple(invs)
    smalls = [None] * blocks
    for s in reversed(range(blocks)):
        keep, send, sums8, gconv = mlp_back(
            sels[s], g.reshape(rows * cols, channels), branches[s], pres[s], xhats[s], invs[s],
            small[s, TAPS : TAPS + 1], small[s, TAPS + 1 : TAPS + 2], w_ins, w_outs, passing.before("mlp", s),
        )
        passing.done(s, keep, send)
        *g_next, smalls[s] = conv_back(
            gconv, xs[s], g, small[s, :TAPS], sums8, s > 0, passing.before("conv", s)
        )
        g = g_next[0] if g_next else None
    return smalls


def small_parameters(kernels, norm_gains, scales):
    taps = kernels.shape[1]
    fill = jnp.zeros((56 - taps - 2, kernels.shape[2]), F32)
    return jnp.concatenate([kernels[0], norm_gains, scales, fill], axis=0)


def finish(t_kernel, t_gain, t_scale, t_in, t_out):
    return t_kernel[None], t_gain[None], t_in[None], t_out[None], t_scale[None]


def any_mesh(images, cotangent, kernels, norm_gains, w_in, w_out, scales):
    segments = lax.axis_size("segment")
    rank = lax.axis_index("segment")
    count = images.shape[0] // segments
    taps = kernels.shape[1]
    small = lax.all_gather(small_parameters(kernels, norm_gains, scales), "segment")
    all_in = lax.all_gather(w_in[0], "segment")
    all_out = lax.all_gather(w_out[0], "segment")
    sels = [jnp.array([s, 0], jnp.int32) for s in range(segments)]
    pieces = [[None] * 3 for _ in range(segments)]

    class Sums:
        def before(self, part, s):
            return ()

        def done(self, s, keep, send):
            self.add(s, 0, keep.astype(F32))
            self.add(s, 1, send.astype(F32))

        def add(self, s, k, value):
            pieces[s][k] = value if pieces[s][k] is None else pieces[s][k] + value

    sums = Sums()
    w_ins = [all_in[s] for s in range(segments)]
    w_outs = [all_out[s] for s in range(segments)]
    for i in range(count):
        x = lax.dynamic_index_in_dim(images, rank * count + i, 0, keepdims=False)
        g = lax.dynamic_index_in_dim(cotangent, rank * count + i, 0, keepdims=False)
        smalls = one_image(x, g, small, sels, w_ins, w_outs, conv_norm(x, small[0]), sums)
        for s in range(segments):
            sums.add(s, 2, smalls[s])

    def summed(values, dim):
        mine = lax.psum_scatter(jnp.stack(values), "segment", scatter_dimension=0, tiled=False)
        return lax.psum_scatter(mine, "dp", scatter_dimension=dim, tiled=True)

    t_in = summed([p[0] for p in pieces], 0)
    t_out = summed([p[1] for p in pieces], 0).T
    t_small = summed([p[2] for p in pieces], 1)
    return finish(t_small[:taps], t_small[taps], t_small[taps + 1], t_in, t_out)


def partners(flip, extent=(4, 2, 2, 2)):
    pairs = []
    for index in range(32):
        z, y, x, c = index >> 3, (index >> 2) & 1, (index >> 1) & 1, index & 1
        other = ((z ^ flip[0]) << 3) | ((y ^ flip[1]) << 2) | ((x ^ flip[2]) << 1) | (c ^ flip[3])
        pairs.append((index, other))
    return pairs


def swap(value, z=0, y=0, x=0, c=0):
    return lax.ppermute(value, ("dp", "segment"), partners((z, y, x, c)))


def along_x(value, to_last):
    pairs = [(i, j) for i, j in partners((0, 0, 1, 0)) if (i >> 1) & 1 == (0 if to_last else 1)]
    return lax.ppermute(value, ("dp", "segment"), pairs)


def this_mesh(images, cotangent, kernels, norm_gains, w_in, w_out, scales):
    rank = lax.axis_index("segment")
    core = rank % 2
    chip = rank // 2
    depth = lax.axis_index("dp") // 2
    side = lax.axis_index("dp") % 2
    own_small = small_parameters(kernels, norm_gains, scales)
    near_small = swap(own_small, c=1)
    near_in, near_out = swap(w_in[0], c=1), swap(w_out[0], c=1)
    small = jnp.where(core == 0, jnp.stack([own_small, near_small]), jnp.stack([near_small, own_small]))
    weights = (w_in[0], near_in, w_out[0], near_out)
    sel = jnp.stack([core, 1 - core, chip, core]).astype(jnp.int32)
    cores = core[None].astype(jnp.int32)
    sides = side[None].astype(jnp.int32)
    levels = jnp.stack([depth, depth ^ 1, depth ^ 2, depth ^ 3]).astype(jnp.int32)

    maps = [lax.dynamic_index_in_dim(images, 2 * core + i, 0, keepdims=False) for i in range(2)]
    ends = [lax.dynamic_index_in_dim(cotangent, 2 * core + i, 0, keepdims=False) for i in range(2)]
    firsts, kept = [], []
    for x in maps:
        firsts.append(conv_norm(x, small[0], tuple(k.inv1 for k in kept)))
        kept.append(pair_forward(sel, x, firsts[-1], small, weights))
    passed = [along_x(k.y, True) for k in kept]
    both = pair_both(sel, passed[0], ends[0], small, weights)
    g_first = along_x(both.g0, False)
    both = pair_both(sel, passed[1], ends[1], small, weights, both)
    g_second = along_x(both.g0, False)

    def back(i, g, before):
        high = pair_back_high(sel, g, kept[i], small, weights, before, (before[0].small0,) if before else ())
        high_core = swap(high.send, c=1) if before else None
        low = pair_back_low(sel, g, high, maps[i], kept[i].x1, firsts[i], kept[i], small, weights, before)
        low_core = swap(low.send, c=1) if before else None
        small0 = pair_back_conv(sel, low, maps[i], before)
        return types.SimpleNamespace(keep0=low.keep, send0=low.send, keep1=high.keep, send1=high.send,
                                     small0=small0, small1=low.small1, core0=low_core, core1=high_core)

    grads = back(0, g_first, None)
    grads = back(1, g_second, (grads, both))

    def along_y(*pairs):
        across, mine = to_side(sides, *pairs)
        return mine, swap(across, y=1)

    def along_z(mine, got):
        own, *others = to_depths(levels, mine, got)
        return [own] + [swap(v, z=flip) for v, flip in zip(others, (1, 2, 3))]

    high = along_y(grads.keep1, grads.core1)
    low = along_y(grads.keep0, grads.core0, pack(cores, (grads.small0, grads.small1)))
    high = along_z(*high)
    low = along_z(*low)
    own, send = to_core(cores, low + high)
    return final(cores, own, swap(send, c=1), kernels.shape[1])


def solution(mesh):
    in_specs = (
        P("dp", None, None, None),
        P("dp", None, None, None),
        P("segment", None, None),
        P("segment", None),
        P("segment", None, None),
        P("segment", None, None),
        P("segment", None),
    )
    out_specs = (
        P("segment", None, "dp"),
        P("segment", "dp"),
        P("segment", "dp", None),
        P("segment", None, "dp"),
        P("segment", "dp"),
    )
    fits = dict(mesh.shape) == {"dp": 8, "segment": 4}

    def whole(images, *rest):
        local = this_mesh if fits and images.shape[0] == 32 else any_mesh
        return jax.shard_map(local, mesh=mesh, in_specs=in_specs, out_specs=out_specs, check_vma=False)(images, *rest)

    return whole
```

```python
import functools
import types
import jax
import jax.numpy as jnp
from jax import lax
from jax.sharding import PartitionSpec as P
from jax.experimental import pallas as pl
from jax.experimental.pallas import tpu as pltpu

EPS = 1e-06
GELU_C = 0.7978845608028654
GELU_A = 0.044715
LANES = 128
def estimate(microseconds):
    return pl.CostEstimate(flops=int(microseconds * 1.1e9), bytes_accessed=int(microseconds * 3.6e6), transcendentals=0)


LIMIT = 40


def vmem(mebibytes):
    return pltpu.CompilerParams(vmem_limit_bytes=mebibytes * 1024 * 1024)


def zero_borders(pad_ref):
    tiles, rows, width, _ = pad_ref.shape
    for c in range(tiles):
        pad_ref[c, :, 0:8] = jnp.zeros((rows, 8, LANES), jnp.float32)
        pad_ref[c, :, width - 8 :] = jnp.zeros((rows, 8, LANES), jnp.float32)


def conv_norm_body(x_ref, small_ref, xhat_ref, normed_ref, inv_ref, pad_ref, conv_ref):
    rows, cols, channels = x_ref.shape
    tiles = channels // LANES
    for c in range(tiles):
        pad_ref[c, :, 8 : cols + 8] = x_ref[:, :, c * LANES : (c + 1) * LANES].astype(jnp.float32)

    def tile(c, carry):
        lanes = pl.ds(pl.multiple_of(c * LANES, LANES), LANES)

        def strip(w, carry):
            base = pl.multiple_of(w * 8, 8)
            window = pad_ref.at[c, :, pl.ds(base, 24), :]
            acc = [None] * rows
            for q in range(7):
                col = [window[h, 5 + q : 13 + q, :] for h in range(rows)]
                for r in range(7):
                    weight = small_ref[r * 7 + q : r * 7 + q + 1, lanes]
                    for h in range(max(0, 3 - r), min(rows, rows + 3 - r)):
                        term = weight * col[h + r - 3]
                        acc[h] = term if acc[h] is None else acc[h] + term
            for h in range(rows):
                conv_ref[h, pl.ds(base, 8), lanes] = acc[h]
            return carry

        return lax.fori_loop(0, cols // 8, strip, carry)

    lax.fori_loop(0, tiles, tile, 0)

    def norm(h, carry):
        value = conv_ref[pl.ds(h * 2, 2)].reshape(2 * cols, channels)
        mean = jnp.mean(value, axis=1, keepdims=True)
        center = value - mean
        inv = lax.rsqrt(jnp.mean(center * center, axis=1, keepdims=True) + EPS)
        xhat = center * inv
        at = pl.ds(pl.multiple_of(h * 2 * cols, 2 * cols), 2 * cols)
        xhat_ref[at, :] = xhat.astype(jnp.bfloat16)
        normed_ref[at, :] = (xhat * small_ref[TAPS : TAPS + 1, :]).astype(jnp.bfloat16)
        inv_ref[at, :] = jnp.broadcast_to(inv, (2 * cols, LANES))
        return carry

    lax.fori_loop(0, rows // 2, norm, 0, unroll=True)


def pad_shape(rows, cols, channels):
    return pltpu.VMEM((channels // LANES, rows, cols + 16, LANES), jnp.float32)


def in_hbm(arrays):
    return [pltpu.with_memory_space_constraint(a, pltpu.HBM) for a in arrays]


def parameters_kernel(k_ref, gain_ref, scale_ref, out_ref, taps_ref, rows_ref, sems):
    copies = [
        pltpu.make_async_copy(source, target, sems.at[i])
        for i, (source, target) in enumerate(((k_ref, taps_ref), (gain_ref, rows_ref.at[0]), (scale_ref, rows_ref.at[1])))
    ]
    for copy in copies:
        copy.start()
    taps = taps_ref.shape[0]
    out_ref[taps + 2 :, :] = jnp.zeros((out_ref.shape[0] - taps - 2, out_ref.shape[1]), jnp.float32)
    for copy in copies:
        copy.wait()
    for t in range(taps):
        out_ref[t : t + 1, :] = taps_ref[t]
    out_ref[taps : taps + 1, :] = rows_ref[0]
    out_ref[taps + 1 : taps + 2, :] = rows_ref[1]


def parameters(kernels, norm_gains, scales):
    taps, channels = kernels.shape[1:]
    return pl.pallas_call(
        parameters_kernel,
        in_specs=[pl.BlockSpec(memory_space=pl.ANY)] * 3,
        out_shape=jax.ShapeDtypeStruct((56, channels), jnp.float32),
        scratch_shapes=[
            pltpu.VMEM((taps, 1, channels), jnp.float32),
            pltpu.VMEM((2, 1, channels), jnp.float32),
            pltpu.SemaphoreType.DMA((3,)),
        ],
        compiler_params=vmem(LIMIT),
        name="parameters",
        cost_estimate=estimate(0.5),
    )(*in_hbm([kernels.transpose(1, 0, 2), norm_gains, scales]))


def choose_small(r):
    first = r.sel[0] == 0
    own, near = r.own_small[...], r.near_small[...]
    r.small[0] = jnp.where(first, own, near)
    r.small[1] = jnp.where(first, near, own)


def conv_norm_kernel(choices, sel_ref, x_ref, *rest):
    smalls, rest = rest[:choices], rest[choices:]
    xhat_ref, normed_ref, inv_ref, pad_ref, conv_ref, small_ref = rest[-6:]
    active = sel_ref[1] == 0

    @pl.when(active)
    def _():
        zero_borders(pad_ref)
        small_ref[...] = smalls[0][...]
        for k in range(1, choices):

            @pl.when(sel_ref[0] == k)
            def _():
                small_ref[...] = smalls[k][...]

        conv_norm_body(x_ref, small_ref, xhat_ref, normed_ref, inv_ref, pad_ref, conv_ref)


def conv_norm(sel, x, smalls, after=()):
    rows, cols, channels = x.shape
    n = rows * cols
    return pl.pallas_call(
        functools.partial(conv_norm_kernel, len(smalls)),
        in_specs=[pl.BlockSpec(memory_space=pltpu.SMEM)]
        + [pl.BlockSpec(memory_space=pltpu.VMEM)] * (1 + len(smalls))
        + [pl.BlockSpec(memory_space=pl.ANY)] * len(after),
        out_shape=(
            jax.ShapeDtypeStruct((n, channels), jnp.bfloat16),
            jax.ShapeDtypeStruct((n, channels), jnp.bfloat16),
            jax.ShapeDtypeStruct((n, LANES), jnp.float32),
        ),
        scratch_shapes=[
            pad_shape(rows, cols, channels),
            pltpu.VMEM((rows, cols, channels), jnp.float32),
            pltpu.VMEM(smalls[0].shape, jnp.float32),
        ],
        compiler_params=vmem(LIMIT),
        name="conv_norm",
        cost_estimate=estimate(2.0),
    )(sel, x, *smalls, *after)


def copy_chosen(which, sources, target, sem):
    for m, source in enumerate(sources):

        @pl.when(which == m)
        def _():
            pltpu.make_async_copy(source, target, sem).start()

    return lambda: pltpu.make_async_copy(sources[0], target, sem).wait()


def forward_kernel(choices, blocks, sel_ref, x_ref, normed0_ref, small_ref, *rest):
    w_ins, w_outs, rest = rest[:choices], rest[choices : 2 * choices], rest[2 * choices :]
    xs = [x_ref] + list(rest[: blocks - 1])
    xhats, invs, rest = rest[blocks - 1 : 2 * blocks - 2], rest[2 * blocks - 2 : 3 * blocks - 3], rest[3 * blocks - 3 :]
    pres, branches, rest = rest[:blocks], rest[blocks : 2 * blocks], rest[2 * blocks :]
    normed_ref, hid_ref, acc_ref, pad_ref, conv_ref, w_in_ref, w_out_ref, sems = rest
    rows, cols, channels = x_ref.shape
    n = rows * cols
    hidden = w_in_ref.shape[2]
    waits = []
    for s in range(blocks):
        waits.append((
            copy_chosen(sel_ref[s], w_ins, w_in_ref.at[s], sems.at[0, s]),
            copy_chosen(sel_ref[s], w_outs, w_out_ref.at[s], sems.at[1, s]),
        ))
    zero_borders(pad_ref)
    step, sub = 256, 2 * cols
    for s in range(blocks):
        normed = normed0_ref if s == 0 else normed_ref
        waits[s][0]()
        for j in range(hidden // step):
            cut = slice(j * step, (j + 1) * step)
            pre = jnp.dot(normed[...], w_in_ref[s, :, cut], preferred_element_type=jnp.float32)
            for i in range(n // sub):
                p = pre[i * sub : (i + 1) * sub]
                half = 0.5 * p
                hid_ref[i * sub : (i + 1) * sub, :] = (half + half * tanh_arg(p)).astype(jnp.bfloat16)
                pres[s][i * sub : (i + 1) * sub, cut] = p.astype(jnp.bfloat16)
            if j == 0:
                waits[s][1]()
            part = jnp.dot(hid_ref[...], w_out_ref[s, cut, :], preferred_element_type=jnp.float32)
            if j == 0:
                acc_ref[...] = part
            else:
                acc_ref[...] += part
        scale = small_ref[s, TAPS + 1 : TAPS + 2, :]
        for i in range(n // sub):
            branch = acc_ref[i * sub : (i + 1) * sub, :]
            branches[s][i * sub : (i + 1) * sub, :] = branch.astype(jnp.bfloat16)
            if s < blocks - 1:
                x_old = xs[s][2 * i : 2 * i + 2].astype(jnp.float32).reshape(sub, channels)
                xs[s + 1][2 * i : 2 * i + 2] = (x_old + scale * branch).astype(jnp.bfloat16).reshape(2, cols, channels)
        if s < blocks - 1:
            conv_norm_body(xs[s + 1], small_ref.at[s + 1], xhats[s], normed_ref, invs[s], pad_ref, conv_ref)


def forward(sel, x, normed0, small, w_ins, w_outs):
    blocks = small.shape[0]
    rows, cols, channels = x.shape
    n = rows * cols
    hidden = w_ins[0].shape[1]
    out = pl.pallas_call(
        functools.partial(forward_kernel, len(w_ins), blocks),
        in_specs=[pl.BlockSpec(memory_space=pltpu.SMEM)]
        + [pl.BlockSpec(memory_space=pltpu.VMEM)] * 3
        + [pl.BlockSpec(memory_space=pl.ANY)] * (2 * len(w_ins)),
        out_shape=(jax.ShapeDtypeStruct((rows, cols, channels), jnp.bfloat16),) * (blocks - 1)
        + (jax.ShapeDtypeStruct((n, channels), jnp.bfloat16),) * (blocks - 1)
        + (jax.ShapeDtypeStruct((n, LANES), jnp.float32),) * (blocks - 1)
        + (jax.ShapeDtypeStruct((n, hidden), jnp.bfloat16),) * blocks
        + (jax.ShapeDtypeStruct((n, channels), jnp.bfloat16),) * blocks,
        scratch_shapes=[
            pltpu.VMEM((n, channels), jnp.bfloat16),
            pltpu.VMEM((n, 256), jnp.bfloat16),
            pltpu.VMEM((n, channels), jnp.float32),
            pad_shape(rows, cols, channels),
            pltpu.VMEM((rows, cols, channels), jnp.float32),
            pltpu.VMEM((blocks, channels, hidden), jnp.bfloat16),
            pltpu.VMEM((blocks, hidden, channels), jnp.bfloat16),
            pltpu.SemaphoreType.DMA((2, blocks)),
        ],
        compiler_params=vmem(LIMIT),
        name="forward",
        cost_estimate=estimate(15),
    )(sel, x, normed0, small, *in_hbm(w_ins), *in_hbm(w_outs))
    k = blocks - 1
    return out[:k], out[k : 2 * k], out[2 * k : 3 * k], out[3 * k : 3 * k + blocks], out[3 * k + blocks :]


def tanh_arg(x):
    return jnp.tanh(x * (GELU_C + (GELU_C * GELU_A) * (x * x)))


def load_weights(sel_ref, w_ins, w_outs, w_in_ref, w_out_ref, sems):
    for m in range(len(w_ins)):

        @pl.when(sel_ref[0] == m)
        def _():
            pltpu.make_async_copy(w_ins[m], w_in_ref, sems.at[0]).start()
            pltpu.make_async_copy(w_outs[m], w_out_ref, sems.at[1]).start()

    return (
        pltpu.make_async_copy(w_ins[0], w_in_ref, sems.at[0]).wait,
        pltpu.make_async_copy(w_outs[0], w_out_ref, sems.at[1]).wait,
    )


def specs(sel, arrays, choices, after=0):
    return (
        [pl.BlockSpec(memory_space=pltpu.SMEM)]
        + [pl.BlockSpec(memory_space=pltpu.VMEM)] * arrays
        + [pl.BlockSpec(memory_space=pl.ANY)] * (2 * choices + after)
    )


def mlp_back_kernel(choices, after, sel_ref, g_ref, branch_ref, pre_ref, xhat_ref, inv_ref, gain_ref, scale_ref, *rest):
    w_ins, w_outs = rest[:choices], rest[choices : 2 * choices]
    (keep_ref, send_ref, small_ref, gconv_ref,
     gb_ref, nm_ref, hid_ref, gp_ref, acc_ref, w_in_ref, w_out_ref, sems) = rest[2 * choices + after :]
    wait_in, wait_out = load_weights(sel_ref, w_ins, w_outs, w_in_ref, w_out_ref, sems)
    first = sel_ref[1] == 0
    n, channels = g_ref.shape
    hidden = w_in_ref.shape[1]
    step = 256
    sub = 32
    scale_sum = jnp.zeros((8, channels), jnp.float32)
    for i in range(n // sub):
        at = slice(i * sub, (i + 1) * sub)
        g = g_ref[at, :].astype(jnp.float32)
        scale_sum = scale_sum + jnp.sum((g * branch_ref[at, :].astype(jnp.float32)).reshape(sub // 8, 8, channels), axis=0)
        gb_ref[at, :] = (g * scale_ref[...]).astype(jnp.bfloat16)
        nm_ref[at, :] = (xhat_ref[at, :].astype(jnp.float32) * gain_ref[...]).astype(jnp.bfloat16)
    gb_t = gb_ref[...].T
    nm_t = nm_ref[...].T
    wait_in()
    wait_out()
    for j in range(hidden // step):
        cut = slice(j * step, (j + 1) * step)
        gh = lax.dot_general(gb_ref[...], w_out_ref[cut, :], (((1,), (1,)), ((), ())), preferred_element_type=jnp.float32)
        for i in range(n // sub):
            at = slice(i * sub, (i + 1) * sub)
            p = pre_ref[at, cut].astype(jnp.float32)
            sq = p * p
            t = jnp.tanh(p * (GELU_C + (GELU_C * GELU_A) * sq))
            cdf = 0.5 + 0.5 * t
            hid_ref[at, :] = (p * cdf).astype(jnp.bfloat16)
            slope = cdf + (0.5 * p) * (1.0 - t * t) * (GELU_C + (3.0 * GELU_C * GELU_A) * sq)
            gp_ref[at, :] = (gh[at, :] * slope).astype(jnp.bfloat16)
        t_out = jnp.dot(gb_t, hid_ref[...], preferred_element_type=jnp.float32)
        t_in = jnp.dot(nm_t, gp_ref[...], preferred_element_type=jnp.float32)
        keep_ref[:, cut] = jnp.where(first, t_in, t_out).astype(jnp.bfloat16)
        send_ref[:, cut] = jnp.where(first, t_out, t_in).astype(jnp.bfloat16)
        part = lax.dot_general(gp_ref[...], w_in_ref[:, cut], (((1,), (1,)), ((), ())), preferred_element_type=jnp.float32)
        if j == 0:
            acc_ref[...] = part
        else:
            acc_ref[...] += part
    gain_sum = jnp.zeros((8, channels), jnp.float32)
    for i in range(n // sub):
        at = slice(i * sub, (i + 1) * sub)
        gn = acc_ref[at, :]
        xhat = xhat_ref[at, :].astype(jnp.float32)
        gain_sum = gain_sum + jnp.sum((gn * xhat).reshape(sub // 8, 8, channels), axis=0)
        gx = gn * gain_ref[...]
        m1 = jnp.mean(gx, axis=1, keepdims=True)
        m2 = jnp.mean(gx * xhat, axis=1, keepdims=True)
        inv = inv_ref[at, 0:1]
        gconv_ref[at, :] = inv * (gx - m1 - xhat * m2)
    small_ref[0:1, :] = jnp.sum(gain_sum, axis=0, keepdims=True)
    small_ref[1:2, :] = jnp.sum(scale_sum, axis=0, keepdims=True)
    small_ref[2:8, :] = jnp.zeros((6, channels), jnp.float32)


def mlp_back(sel, g, branch, pre, xhat, inv, gain, scale, w_ins, w_outs, after=()):
    n, channels = g.shape
    hidden = w_ins[0].shape[1]
    return pl.pallas_call(
        functools.partial(mlp_back_kernel, len(w_ins), len(after)),
        in_specs=specs(sel, 7, len(w_ins), len(after)),
        out_shape=(
            jax.ShapeDtypeStruct((channels, hidden), jnp.bfloat16),
            jax.ShapeDtypeStruct((channels, hidden), jnp.bfloat16),
            jax.ShapeDtypeStruct((8, channels), jnp.float32),
            jax.ShapeDtypeStruct((n, channels), jnp.float32),
        ),
        scratch_shapes=[
            pltpu.VMEM((n, channels), jnp.bfloat16),
            pltpu.VMEM((n, channels), jnp.bfloat16),
            pltpu.VMEM((n, 256), jnp.bfloat16),
            pltpu.VMEM((n, 256), jnp.bfloat16),
            pltpu.VMEM((n, channels), jnp.float32),
            pltpu.VMEM((channels, hidden), jnp.bfloat16),
            pltpu.VMEM((hidden, channels), jnp.bfloat16),
            pltpu.SemaphoreType.DMA((2,)),
        ],
        compiler_params=vmem(LIMIT),
        name="mlp_back",
        cost_estimate=estimate(2.5),
    )(sel, g, branch, pre, xhat, inv, gain, scale, *in_hbm(w_ins), *in_hbm(w_outs), *after)


SMALL_ROWS = 64
TAPS = 49


def conv_back_kernel(need_map, after, gconv_ref, x_ref, g_ref, k_ref, small_ref, *rest):
    *out_ref, tk_ref, pad_ref, sum_ref, wide_ref, map_ref = rest[after:]
    conv_back_body(gconv_ref, x_ref, g_ref, k_ref, small_ref, out_ref[0] if need_map else None, tk_ref,
                   pad_ref, sum_ref, wide_ref, map_ref)


def conv_back(gconv, x, g, kernel, small, need_map=True, after=()):
    rows, cols, channels = x.shape
    out = (jax.ShapeDtypeStruct((SMALL_ROWS, channels), jnp.float32),)
    if need_map:
        out = (jax.ShapeDtypeStruct((rows, cols, channels), jnp.bfloat16),) + out
    return pl.pallas_call(
        functools.partial(conv_back_kernel, need_map, len(after)),
        in_specs=[pl.BlockSpec(memory_space=pltpu.VMEM)] * 5 + [pl.BlockSpec(memory_space=pl.ANY)] * len(after),
        out_shape=out,
        scratch_shapes=[
            pad_shape(rows, cols, channels),
            pltpu.VMEM((cols // 8, TAPS, 8, LANES), jnp.float32),
            pltpu.VMEM((rows, cols, channels), jnp.float32),
            pltpu.VMEM((rows, cols, channels), jnp.float32),
        ],
        compiler_params=vmem(LIMIT),
        name="conv_back",
        cost_estimate=estimate(3.4 if need_map else 1.6),
    )(gconv, x, g, kernel, small, *after)


def small_call(kernel, name, outs, *args, scratch=(), after=()):
    used = len(args)

    def body(*refs):
        kernel(*refs[:used], *refs[used + len(after) :])

    return pl.pallas_call(
        body,
        in_specs=[pl.BlockSpec(memory_space=pltpu.SMEM)]
        + [pl.BlockSpec(memory_space=pltpu.VMEM)] * (used - 1)
        + [pl.BlockSpec(memory_space=pl.ANY)] * len(after),
        out_shape=tuple(out_struct(*o) for o in outs),
        scratch_shapes=list(scratch),
        compiler_params=vmem(LIMIT),
        name=name,
        cost_estimate=estimate(0.7),
    )(*args, *after)


def conv_back_body(gconv_ref, x_ref, g_ref, small_ref, sums8_ref, out_ref, tk_ref, pad_ref, sum_ref, wide_ref, map_ref):
    rows, cols, channels = x_ref.shape
    tiles = channels // LANES
    zero_borders(pad_ref)
    for c in range(tiles):
        pad_ref[c, :, 8 : cols + 8] = gconv_ref[:, c * LANES : (c + 1) * LANES].reshape(rows, cols, LANES)

    for h in range(rows):
        wide_ref[h] = x_ref[h].astype(jnp.float32)

    def tile(c, carry):
        lanes = pl.ds(pl.multiple_of(c * LANES, LANES), LANES)

        def strip(w, carry):
            base = pl.multiple_of(w * 8, 8)
            window = pad_ref.at[c, :, pl.ds(base, 24), :]
            xs = [wide_ref[h, pl.ds(base, 8), lanes] for h in range(rows)]
            acc = [None] * rows
            for q in range(7):
                col = [window[h, 11 - q : 19 - q, :] for h in range(rows)]
                for r in range(7):
                    tap = r * 7 + q
                    if out_ref is not None:
                        weight = small_ref[tap : tap + 1, lanes]
                    total = None
                    for h in range(max(0, r - 3), min(rows, rows + r - 3)):
                        shifted = col[h + 3 - r]
                        term = xs[h] * shifted
                        total = term if total is None else total + term
                        if out_ref is not None:
                            moved = weight * shifted
                            acc[h] = moved if acc[h] is None else acc[h] + moved
                    sum_ref[w, tap] = total
            if out_ref is not None:
                for h in range(rows):
                    map_ref[h, pl.ds(base, 8), lanes] = acc[h]
            return carry

        lax.fori_loop(0, cols // 8, strip, 0)
        tk_ref[0:TAPS, lanes] = jnp.sum(sum_ref[0] + sum_ref[1], axis=1)
        return carry

    lax.fori_loop(0, tiles, tile, 0)
    if out_ref is not None:
        for h in range(rows):
            out_ref[h] = (g_ref[h].astype(jnp.float32) + map_ref[h]).astype(jnp.bfloat16)
    tk_ref[TAPS : TAPS + 2, :] = sums8_ref[0:2, :]
    tk_ref[TAPS + 2 :, :] = jnp.zeros((SMALL_ROWS - TAPS - 2, channels), jnp.float32)


def conv_map_body(gconv_ref, g_ref, small_ref, out_ref, pad_ref, map_ref):
    rows, cols, channels = g_ref.shape
    tiles = channels // LANES
    zero_borders(pad_ref)
    for c in range(tiles):
        pad_ref[c, :, 8 : cols + 8] = gconv_ref[:, c * LANES : (c + 1) * LANES].reshape(rows, cols, LANES)

    def tile(c, carry):
        lanes = pl.ds(pl.multiple_of(c * LANES, LANES), LANES)

        def strip(w, carry):
            base = pl.multiple_of(w * 8, 8)
            window = pad_ref.at[c, :, pl.ds(base, 24), :]
            acc = [None] * rows
            for q in range(7):
                col = [window[h, 11 - q : 19 - q, :] for h in range(rows)]
                for r in range(7):
                    weight = small_ref[r * 7 + q : r * 7 + q + 1, lanes]
                    for h in range(max(0, r - 3), min(rows, rows + r - 3)):
                        term = weight * col[h + 3 - r]
                        acc[h] = term if acc[h] is None else acc[h] + term
            for h in range(rows):
                map_ref[h, pl.ds(base, 8), lanes] = acc[h]
            return carry

        return lax.fori_loop(0, cols // 8, strip, carry)

    lax.fori_loop(0, tiles, tile, 0)
    for h in range(rows):
        out_ref[h] = (g_ref[h].astype(jnp.float32) + map_ref[h]).astype(jnp.bfloat16)


def mlp_back_map_body(g_ref, branch_ref, pre_ref, xhat_ref, inv_ref, small_ref, w_in_ref, w_out_ref,
                      sums8_ref, gconv_ref, gb_ref, nm_ref, hid_ref, gp_ref, acc_ref, ready):
    rows, cols, channels = g_ref.shape
    n = rows * cols
    hidden = w_in_ref.shape[1]
    step = 256
    sub = 2 * cols
    gain = small_ref[TAPS : TAPS + 1, :]
    scale = small_ref[TAPS + 1 : TAPS + 2, :]
    scale_sum = jnp.zeros((8, channels), jnp.float32)
    for i in range(n // sub):
        at = slice(i * sub, (i + 1) * sub)
        g = g_ref[2 * i : 2 * i + 2].astype(jnp.float32).reshape(sub, channels)
        scale_sum = scale_sum + jnp.sum((g * branch_ref[at, :].astype(jnp.float32)).reshape(sub // 8, 8, channels), axis=0)
        gb_ref[at, :] = (g * scale).astype(jnp.bfloat16)
        nm_ref[at, :] = (xhat_ref[at, :].astype(jnp.float32) * gain).astype(jnp.bfloat16)
    ready("gb", "nm")
    for j in range(hidden // step):
        cut = slice(j * step, (j + 1) * step)
        gh = lax.dot_general(gb_ref[...], w_out_ref[cut, :], (((1,), (1,)), ((), ())), preferred_element_type=jnp.float32)
        for i in range(n // sub):
            at = slice(i * sub, (i + 1) * sub)
            p = pre_ref[at, cut].astype(jnp.float32)
            sq = p * p
            t = jnp.tanh(p * (GELU_C + (GELU_C * GELU_A) * sq))
            cdf = 0.5 + 0.5 * t
            hid_ref[at, cut] = (p * cdf).astype(jnp.bfloat16)
            slope = cdf + (0.5 * p) * (1.0 - t * t) * (GELU_C + (3.0 * GELU_C * GELU_A) * sq)
            gp_ref[at, cut] = (gh[at, :] * slope).astype(jnp.bfloat16)
        part = lax.dot_general(gp_ref[:, cut], w_in_ref[:, cut], (((1,), (1,)), ((), ())), preferred_element_type=jnp.float32)
        if j == 0:
            acc_ref[...] = part
        else:
            acc_ref[...] += part
    ready("hid", "gp")
    gain_sum = jnp.zeros((8, channels), jnp.float32)
    for i in range(n // sub):
        at = slice(i * sub, (i + 1) * sub)
        gn = acc_ref[at, :]
        xhat = xhat_ref[at, :].astype(jnp.float32)
        gain_sum = gain_sum + jnp.sum((gn * xhat).reshape(sub // 8, 8, channels), axis=0)
        gx = gn * gain
        m1 = jnp.mean(gx, axis=1, keepdims=True)
        m2 = jnp.mean(gx * xhat, axis=1, keepdims=True)
        gconv_ref[at, :] = inv_ref[at, 0:1] * (gx - m1 - xhat * m2)
    sums8_ref[0:1, :] = jnp.sum(gain_sum, axis=0, keepdims=True)
    sums8_ref[1:2, :] = jnp.sum(scale_sum, axis=0, keepdims=True)
    sums8_ref[2:8, :] = jnp.zeros((6, channels), jnp.float32)
    ready("gconv", "sums")


def mlp_back_body(first, g_ref, branch_ref, pre_ref, xhat_ref, inv_ref, small_ref, wait_in, wait_out, w_in_ref, w_out_ref,
                  keep_ref, send_ref, sums8_ref, gconv_ref, gb_ref, nm_ref, hid_ref, gp_ref, acc_ref, before=None):
    rows, cols, channels = g_ref.shape
    n = rows * cols
    hidden = w_in_ref.shape[1]
    step = 256
    sub = 2 * cols
    gain = small_ref[TAPS : TAPS + 1, :]
    scale = small_ref[TAPS + 1 : TAPS + 2, :]
    scale_sum = jnp.zeros((8, channels), jnp.float32)
    for i in range(n // sub):
        at = slice(i * sub, (i + 1) * sub)
        g = g_ref[2 * i : 2 * i + 2].astype(jnp.float32).reshape(sub, channels)
        scale_sum = scale_sum + jnp.sum((g * branch_ref[at, :].astype(jnp.float32)).reshape(sub // 8, 8, channels), axis=0)
        gb_ref[at, :] = (g * scale).astype(jnp.bfloat16)
        nm_ref[at, :] = (xhat_ref[at, :].astype(jnp.float32) * gain).astype(jnp.bfloat16)
    gb_t = gb_ref[...].T
    nm_t = nm_ref[...].T
    wait_in()
    wait_out()
    for j in range(hidden // step):
        cut = slice(j * step, (j + 1) * step)
        gh = lax.dot_general(gb_ref[...], w_out_ref[cut, :], (((1,), (1,)), ((), ())), preferred_element_type=jnp.float32)
        for i in range(n // sub):
            at = slice(i * sub, (i + 1) * sub)
            p = pre_ref[at, cut].astype(jnp.float32)
            sq = p * p
            t = jnp.tanh(p * (GELU_C + (GELU_C * GELU_A) * sq))
            cdf = 0.5 + 0.5 * t
            hid_ref[at, :] = (p * cdf).astype(jnp.bfloat16)
            slope = cdf + (0.5 * p) * (1.0 - t * t) * (GELU_C + (3.0 * GELU_C * GELU_A) * sq)
            gp_ref[at, :] = (gh[at, :] * slope).astype(jnp.bfloat16)
        t_out = jnp.dot(gb_t, hid_ref[...], preferred_element_type=jnp.float32)
        t_in = jnp.dot(nm_t, gp_ref[...], preferred_element_type=jnp.float32)
        t_keep = jnp.where(first, t_in, t_out)
        t_send = jnp.where(first, t_out, t_in)
        if before is not None:
            if j == 0:
                old_keep, old_send = before()
            t_keep = t_keep + old_keep[:, cut].astype(jnp.float32)
            t_send = t_send + old_send[:, cut].astype(jnp.float32)
        keep_ref[:, cut] = t_keep.astype(jnp.bfloat16)
        send_ref[:, cut] = t_send.astype(jnp.bfloat16)
        part = lax.dot_general(gp_ref[...], w_in_ref[:, cut], (((1,), (1,)), ((), ())), preferred_element_type=jnp.float32)
        if j == 0:
            acc_ref[...] = part
        else:
            acc_ref[...] += part
    gain_sum = jnp.zeros((8, channels), jnp.float32)
    for i in range(n // sub):
        at = slice(i * sub, (i + 1) * sub)
        gn = acc_ref[at, :]
        xhat = xhat_ref[at, :].astype(jnp.float32)
        gain_sum = gain_sum + jnp.sum((gn * xhat).reshape(sub // 8, 8, channels), axis=0)
        gx = gn * gain
        m1 = jnp.mean(gx, axis=1, keepdims=True)
        m2 = jnp.mean(gx * xhat, axis=1, keepdims=True)
        gconv_ref[at, :] = inv_ref[at, 0:1] * (gx - m1 - xhat * m2)
    sums8_ref[0:1, :] = jnp.sum(gain_sum, axis=0, keepdims=True)
    sums8_ref[1:2, :] = jnp.sum(scale_sum, axis=0, keepdims=True)
    sums8_ref[2:8, :] = jnp.zeros((6, channels), jnp.float32)


def out_struct(shape, dtype, by_hand=False):
    return pltpu.HBM(shape, dtype) if by_hand else jax.ShapeDtypeStruct(shape, dtype)


def named_call(name, body, ins, outs, scratch, cost):
    names = list(ins) + list(outs) + list(scratch)
    spaces = {"v": pltpu.VMEM, "s": pltpu.SMEM, "a": pl.ANY, "h": pl.ANY}

    def kernel(*refs):
        body(types.SimpleNamespace(**dict(zip(names, refs))))

    args = [pltpu.with_memory_space_constraint(a, pltpu.HBM) if kind == "h" else a for a, kind in ins.values()]
    result = pl.pallas_call(
        kernel,
        in_specs=[pl.BlockSpec(memory_space=spaces[kind]) for _, kind in ins.values()],
        out_specs=tuple(pl.BlockSpec(memory_space=pl.ANY if len(o) > 2 else pltpu.VMEM) for o in outs.values()),
        out_shape=tuple(out_struct(*o) for o in outs.values()),
        scratch_shapes=list(scratch.values()),
        compiler_params=vmem(LIMIT),
        name=name,
        cost_estimate=estimate(cost),
    )(*args)
    return types.SimpleNamespace(**dict(zip(outs, result)))


def mlp_body(normed_ref, wait_in, wait_out, w_in_ref, w_out_ref, pre_ref, hid_ref, acc_ref):
    n = normed_ref.shape[0]
    hidden = w_in_ref.shape[1]
    step, sub = 256, 32
    wait_in()
    for j in range(hidden // step):
        cut = slice(j * step, (j + 1) * step)
        pre = jnp.dot(normed_ref[...], w_in_ref[:, cut], preferred_element_type=jnp.float32)
        for i in range(n // sub):
            p = pre[i * sub : (i + 1) * sub]
            half = 0.5 * p
            hid_ref[i * sub : (i + 1) * sub, :] = (half + half * tanh_arg(p)).astype(jnp.bfloat16)
            pre_ref[i * sub : (i + 1) * sub, cut] = p.astype(jnp.bfloat16)
        if j == 0:
            wait_out()
        part = jnp.dot(hid_ref[...], w_out_ref[cut, :], preferred_element_type=jnp.float32)
        if j == 0:
            acc_ref[...] = part
        else:
            acc_ref[...] += part


def residual_body(x_ref, small_ref, acc_ref, branch_ref, y_ref):
    rows, cols, channels = x_ref.shape
    scale = small_ref[TAPS + 1 : TAPS + 2, :]
    sub = 2 * cols
    for i in range(rows // 2):
        branch = acc_ref[i * sub : (i + 1) * sub, :]
        branch_ref[i * sub : (i + 1) * sub, :] = branch.astype(jnp.bfloat16)
        if y_ref is not None:
            old = x_ref[2 * i : 2 * i + 2].astype(jnp.float32).reshape(sub, channels)
            y_ref[2 * i : 2 * i + 2] = (old + scale * branch).astype(jnp.bfloat16).reshape(2, cols, channels)


def small_ins(pair):
    return {"own_small": (pair[0], "v"), "near_small": (pair[1], "v")}


def small_scratch(pair):
    return {"small": pltpu.VMEM((2,) + pair[0].shape, jnp.float32)}


def weight_ins(pair):
    return {k: (v, "h") for k, v in zip(("own_in", "near_in", "own_out", "near_out"), pair)}


def weight_scratch(blocks, channels, hidden):
    return {
        "w_in": pltpu.VMEM((blocks, channels, hidden), jnp.bfloat16),
        "w_out": pltpu.VMEM((blocks, hidden, channels), jnp.bfloat16),
        "w_sem": pltpu.SemaphoreType.DMA((2, blocks)),
    }


def start_weights(r, slot, block):
    return (
        copy_chosen(r.sel[block], (r.own_in, r.near_in), r.w_in.at[slot], r.w_sem.at[0, slot]),
        copy_chosen(r.sel[block], (r.own_out, r.near_out), r.w_out.at[slot], r.w_sem.at[1, slot]),
    )


def pair_forward(sel, x, first, small, weights):
    rows, cols, channels = x.shape
    n, hidden = rows * cols, weights[0].shape[1]
    bf16, f32 = jnp.bfloat16, jnp.float32

    def body(r):
        @pl.when(r.sel[4] == 0)
        def _():
            low, high = start_weights(r, 0, 0), start_weights(r, 1, 1)
            choose_small(r)
            zero_borders(r.pad)
            mlp_body(r.normed0, *low, r.w_in.at[0], r.w_out.at[0], r.pre0, r.hid, r.acc)
            residual_body(r.x, r.small.at[0], r.acc, r.branch0, r.x1)
            conv_norm_body(r.x1, r.small.at[1], r.xhat1, r.normed, r.inv1, r.pad, r.conv)
            mlp_body(r.normed, *high, r.w_in.at[1], r.w_out.at[1], r.pre1, r.hid, r.acc)
            residual_body(r.x1, r.small.at[1], r.acc, r.branch1, r.y)

    return named_call(
        "pair_forward", body,
        {"sel": (sel, "s"), "x": (x, "v"), "normed0": (first[1], "v"), **small_ins(small), **weight_ins(weights)},
        {"y": (x.shape, bf16), "x1": (x.shape, bf16), "xhat1": ((n, channels), bf16), "inv1": ((n, LANES), f32),
         "pre0": ((n, hidden), bf16), "pre1": ((n, hidden), bf16),
         "branch0": ((n, channels), bf16), "branch1": ((n, channels), bf16)},
        {"normed": pltpu.VMEM((n, channels), bf16), "hid": pltpu.VMEM((n, 256), bf16), "acc": pltpu.VMEM((n, channels), f32),
         "pad": pad_shape(rows, cols, channels), "conv": pltpu.VMEM((rows, cols, channels), f32),
         **weight_scratch(2, channels, hidden), **small_scratch(small)},
        7.5,
    )


def back_scratch(n, channels):
    bf16, f32 = jnp.bfloat16, jnp.float32
    return {"gb": pltpu.VMEM((n, channels), bf16), "nm": pltpu.VMEM((n, channels), bf16),
            "hid": pltpu.VMEM((n, 256), bf16), "gp": pltpu.VMEM((n, 256), bf16), "acc": pltpu.VMEM((n, channels), f32)}


def back_temps(r):
    return r.gb, r.nm, r.hid, r.gp, r.acc


GRADS = ("keep0", "send0", "keep1", "send1")
FACTORS = ("gb", "nm", "hid", "gp", "gconv", "sums")


def factor_shapes(n, channels, hidden):
    bf16, f32 = jnp.bfloat16, jnp.float32
    one = {"gb": ((n, channels), bf16), "nm": ((n, channels), bf16), "hid": ((n, hidden), bf16), "gp": ((n, hidden), bf16),
           "gconv": ((n, channels), f32), "sums": ((8, channels), f32)}
    return {name + str(k): one[name] for k in (0, 1) for name in FACTORS}


def pair_map(sel, x, g, small, weights):
    rows, cols, channels = x.shape
    n, hidden = rows * cols, weights[0].shape[1]
    bf16, f32 = jnp.bfloat16, jnp.float32
    shapes = factor_shapes(n, channels, hidden)
    saved = {**shapes, "x1": (x.shape, bf16)}
    order = list(saved)

    def body(r):
        @pl.when(r.sel[2] == 1)
        def _():
            def copy_out(name):
                return pltpu.make_async_copy(getattr(r, "v_" + name), getattr(r, name), r.s_sem.at[order.index(name)])

            low, high = start_weights(r, 0, 0), start_weights(r, 1, 1)
            choose_small(r)
            zero_borders(r.pad)
            s0, s1 = r.small.at[0], r.small.at[1]
            conv_norm_body(r.x, s0, r.xhat0, r.normed, r.inv0, r.pad, r.conv)
            mlp_body(r.normed, *low, r.w_in.at[0], r.w_out.at[0], r.pre0, r.hid, r.acc)
            residual_body(r.x, s0, r.acc, r.branch0, r.v_x1)
            copy_out("x1").start()
            conv_norm_body(r.v_x1, s1, r.xhat1, r.normed, r.inv1, r.pad, r.conv)
            mlp_body(r.normed, *high, r.w_in.at[1], r.w_out.at[1], r.pre1, r.hid, r.acc)
            residual_body(r.v_x1, s1, r.acc, r.branch1, None)

            def ready(k):
                def start(*names):
                    for name in names:
                        copy_out(name + str(k)).start()

                return start

            mlp_back_map_body(r.g, r.branch1, r.pre1, r.xhat1, r.inv1, s1, r.w_in.at[1], r.w_out.at[1],
                              r.v_sums1, r.v_gconv1, r.v_gb1, r.v_nm1, r.v_hid1, r.v_gp1, r.acc, ready(1))
            conv_map_body(r.v_gconv1, r.g, s1, r.g1, r.pad, r.conv)
            mlp_back_map_body(r.g1, r.branch0, r.pre0, r.xhat0, r.inv0, s0, r.w_in.at[0], r.w_out.at[0],
                              r.v_sums0, r.v_gconv0, r.v_gb0, r.v_nm0, r.v_hid0, r.v_gp0, r.acc, ready(0))
            conv_map_body(r.v_gconv0, r.g1, s0, r.g0, r.pad, r.conv)
            for name in order:
                copy_out(name).wait()

    return named_call(
        "pair_map", body,
        {"sel": (sel, "s"), "x": (x, "v"), "g": (g, "v"), **small_ins(small), **weight_ins(weights)},
        {"g0": (x.shape, bf16), **{name: shape + (True,) for name, shape in saved.items()}},
        {**{"v_" + name: pltpu.VMEM(*shape) for name, shape in saved.items()},
         "s_sem": pltpu.SemaphoreType.DMA((len(order),)),
         "g1": pltpu.VMEM(x.shape, bf16),
         "xhat0": pltpu.VMEM((n, channels), bf16), "xhat1": pltpu.VMEM((n, channels), bf16),
         "inv0": pltpu.VMEM((n, LANES), f32), "inv1": pltpu.VMEM((n, LANES), f32),
         "pre0": pltpu.VMEM((n, hidden), bf16), "pre1": pltpu.VMEM((n, hidden), bf16),
         "branch0": pltpu.VMEM((n, channels), bf16), "branch1": pltpu.VMEM((n, channels), bf16),
         "normed": pltpu.VMEM((n, channels), bf16), "hid": pltpu.VMEM((n, 256), bf16), "acc": pltpu.VMEM((n, channels), f32),
         "pad": pad_shape(rows, cols, channels), "conv": pltpu.VMEM((rows, cols, channels), f32),
         **weight_scratch(2, channels, hidden), **small_scratch(small)},
        12,
    )


def pair_grads(sel, xs, parts):
    rows, cols, channels = xs[0].shape
    n, hidden = rows * cols, parts[0].hid0.shape[1]
    bf16, f32 = jnp.bfloat16, jnp.float32
    shapes = factor_shapes(n, channels, hidden)
    order = list(shapes) + ["x1"]

    def body(r):
        @pl.when(r.sel[2] == 1)
        def _():
            def copy_out(k):
                return pltpu.make_async_copy(r.grads.at[k], getattr(r, GRADS[k]), r.o_sem.at[k])

            copies = {}
            for k in (1, 0):
                for name in FACTORS + (("x1",) if k else ()):
                    full = name + str(k) if name != "x1" else name
                    for i in range(2):
                        copies[full, i] = pltpu.make_async_copy(
                            getattr(r, "i%d_%s" % (i, full)), getattr(r, "v_" + full).at[i], r.s_sem.at[i, order.index(full)]
                        )
                        copies[full, i].start()
            first = r.sel[3] == 0
            for k in (1, 0):
                gb, nm, hid, gp = (getattr(r, "v_%s%d" % (name, k)) for name in FACTORS[:4])
                keep, send = r.grads.at[2 * k], r.grads.at[2 * k + 1]
                for name in FACTORS + (("x1",) if k else ()):
                    for i in range(2):
                        copies[name + str(k) if name != "x1" else name, i].wait()
                gb_t = gb[...].reshape(2 * n, channels).T
                nm_t = nm[...].reshape(2 * n, channels).T
                for j in range(hidden // 256):
                    cut = slice(j * 256, (j + 1) * 256)
                    t_out = jnp.dot(gb_t, hid[:, :, cut].reshape(2 * n, 256), preferred_element_type=f32)
                    t_in = jnp.dot(nm_t, gp[:, :, cut].reshape(2 * n, 256), preferred_element_type=f32)
                    keep[:, cut] = jnp.where(first, t_in, t_out).astype(bf16)
                    send[:, cut] = jnp.where(first, t_out, t_in).astype(bf16)
                copy_out(2 * k).start()
                copy_out(2 * k + 1).start()
                out = getattr(r, "small%d" % k)
                for i in range(2):
                    x = r.v_x1.at[i] if k else getattr(r, "x_%d" % i)
                    gconv, sums = getattr(r, "v_gconv%d" % k).at[i], getattr(r, "v_sums%d" % k).at[i]
                    target = out if i == 0 else r.tk
                    conv_back_body(gconv, x, None, None, sums, None, target, r.pad, r.sum, r.wide, None)
                out[...] += r.tk[...]
            for k in range(4):
                copy_out(k).wait()

    ins = {"sel": (sel, "s")}
    for i in range(2):
        ins["x_%d" % i] = (xs[i], "v")
        ins.update({"i%d_%s" % (i, name): (getattr(parts[i], name), "h") for name in order})
    grad = ((channels, hidden), bf16)
    small_out = ((SMALL_ROWS, channels), f32)
    scratch = {"v_" + name: pltpu.VMEM((2,) + shape, dtype) for name, (shape, dtype) in shapes.items()}
    return named_call(
        "pair_grads", body, ins,
        {**{name: grad + (True,) for name in GRADS}, "small0": small_out, "small1": small_out},
        {**scratch, "grads": pltpu.VMEM((4, channels, hidden), bf16), "o_sem": pltpu.SemaphoreType.DMA((4,)), "v_x1": pltpu.VMEM((2,) + xs[0].shape, bf16), "s_sem": pltpu.SemaphoreType.DMA((2, len(order))),
         "pad": pad_shape(rows, cols, channels), "sum": pltpu.VMEM((cols // 8, TAPS, 8, LANES), f32),
         "wide": pltpu.VMEM(xs[0].shape, f32), "tk": pltpu.VMEM((SMALL_ROWS, channels), f32)},
        10,
    )


def pair_back(sel, g, x, first, kept, small, weights, before=None, after=()):
    rows, cols, channels = g.shape
    n, hidden = rows * cols, weights[0].shape[1]
    bf16, f32 = jnp.bfloat16, jnp.float32

    def body(r):
        def copy_old(k):
            return copy_chosen(r.sel[2], (getattr(r, "a_" + GRADS[k]), getattr(r, "p_" + GRADS[k])), r.olds.at[k], r.o_sem.at[k])

        def copy_out(k, source):
            return pltpu.make_async_copy(source, getattr(r, GRADS[k]), r.s_sem.at[k])

        @pl.when(r.sel[2] == 0)
        def _():
            core = r.sel[3] == 0
            high, low = start_weights(r, 1, 1), start_weights(r, 0, 0)
            waits = {}
            if before is not None:
                waits = {k: copy_old(k) for k in (2, 3, 0, 1)}
            choose_small(r)
            s0, s1 = r.small.at[0], r.small.at[1]

            def old(k):
                def both():
                    waits[2 * k]()
                    waits[2 * k + 1]()
                    return r.olds.at[2 * k], r.olds.at[2 * k + 1]

                return both if waits else None

            mlp_back_body(core, r.g, r.branch1, r.pre1, r.xhat1, r.inv1, s1, *high, r.w_in.at[1], r.w_out.at[1],
                          r.grads.at[2], r.grads.at[3], r.sums8, r.gconv, *back_temps(r), before=old(1))
            copy_out(2, r.grads.at[2]).start()
            copy_out(3, r.grads.at[3]).start()
            conv_back_body(r.gconv, r.x1, r.g, s1, r.sums8, r.g1, r.small1, r.pad, r.sum, r.wide, r.map)
            mlp_back_body(core, r.g1, r.branch0, r.pre0, r.xhat0, r.inv0, s0, *low, r.w_in.at[0], r.w_out.at[0],
                          r.grads.at[0], r.grads.at[1], r.sums8, r.gconv, *back_temps(r), before=old(0))
            copy_out(0, r.grads.at[0]).start()
            copy_out(1, r.grads.at[1]).start()
            conv_back_body(r.gconv, r.x, None, None, r.sums8, None, r.small0, r.pad, r.sum, r.wide, None)
            if before is not None:
                r.small0[...] += r.a_small0[...]
                r.small1[...] += r.a_small1[...]
                r.packed[...] = jnp.concatenate([r.small0[...], r.small1[...]], axis=0).T.astype(bf16)
            for k in range(4):
                copy_out(k, r.grads.at[k]).wait()

        if before is not None:

            @pl.when(r.sel[2] == 1)
            def _():
                waits = [copy_old(k) for k in range(4)]
                r.packed[...] = jnp.concatenate([r.p_small0[...], r.p_small1[...]], axis=0).T.astype(bf16)
                for k, wait in enumerate(waits):
                    wait()
                    copy_out(k, r.olds.at[k]).start()
                for k in range(4):
                    copy_out(k, r.olds.at[k]).wait()

    ins = {"sel": (sel, "s"), "g": (g, "v"), "x": (x, "v"), "x1": (kept.x1, "v"),
           "branch1": (kept.branch1, "v"), "pre1": (kept.pre1, "v"), "xhat1": (kept.xhat1, "v"), "inv1": (kept.inv1, "v"),
           "branch0": (kept.branch0, "v"), "pre0": (kept.pre0, "v"), "xhat0": (first[0], "v"), "inv0": (first[2], "v"),
           **small_ins(small), **weight_ins(weights)}
    grad = ((channels, hidden), bf16)
    small_out = ((SMALL_ROWS, channels), f32)
    outs = {name: grad + (True,) for name in GRADS}
    scratch = {"grads": pltpu.VMEM((4, channels, hidden), bf16), "s_sem": pltpu.SemaphoreType.DMA((4,)), "g1": pltpu.VMEM(g.shape, bf16), "sums8": pltpu.VMEM((8, channels), f32), "gconv": pltpu.VMEM((n, channels), f32),
               "pad": pad_shape(rows, cols, channels), "sum": pltpu.VMEM((cols // 8, TAPS, 8, LANES), f32),
               "wide": pltpu.VMEM(x.shape, f32), "map": pltpu.VMEM(x.shape, f32),
               **back_scratch(n, channels), **weight_scratch(2, channels, hidden), **small_scratch(small)}
    if before is None:
        outs.update({"small0": small_out, "small1": small_out})
    else:
        for prefix, part in zip("ap", before):
            ins.update({prefix + "_" + name: (getattr(part, name), "h") for name in GRADS})
            ins.update({prefix + "_" + name: (getattr(part, name), "v") for name in ("small0", "small1")})
        outs["packed"] = ((channels, 2 * SMALL_ROWS), bf16)
        scratch.update({"small0": pltpu.VMEM(*small_out), "small1": pltpu.VMEM(*small_out),
                        "olds": pltpu.VMEM((4, channels, hidden), bf16), "o_sem": pltpu.SemaphoreType.DMA((4,))})
    ins.update({"after%d" % k: (v, "a") for k, v in enumerate(after)})
    return named_call("pair_back", body, ins, outs, scratch, 9)


def add(a, b):
    return a.astype(jnp.float32) + b.astype(jnp.float32)


def side_kernel(sel_ref, keep_ref, got_ref, *refs):
    *small_ref, across_ref, mine_ref = refs
    side = sel_ref[0]
    levels, _, _, hidden = keep_ref.shape
    for level in range(levels):
        for out_ref, which in ((across_ref, 1 - side), (mine_ref, side)):
            out_ref[level, :, :hidden] = add(keep_ref[level, which], got_ref[level, which]).astype(jnp.bfloat16)
            if small_ref:
                out_ref[level, :, hidden:] = small_ref[0][level, which]


def to_side(side, *arrays):
    arrays = [v.reshape(4, 2, v.shape[0] // 8, v.shape[1]) for v in arrays]
    width = sum(v.shape[3] for v in arrays[1:])
    out = ((4, arrays[0].shape[2], width), jnp.bfloat16)
    return small_call(side_kernel, "to_side", (out, out), side, *arrays)


def depth_kernel(sel_ref, mine_ref, got_ref, *out_refs):
    for k, out_ref in enumerate(out_refs):
        out_ref[...] = add(mine_ref[sel_ref[k]], got_ref[sel_ref[k]]).astype(jnp.bfloat16)


def to_depths(levels, mine, got, after=()):
    return small_call(depth_kernel, "to_depths", ((mine.shape[1:], jnp.bfloat16),) * 4, levels, mine, got, after=after)


def core_kernel(sel_ref, *refs):
    *parts, own_ref, send_ref = refs
    hidden = parts[-1].shape[1]
    low, high = (add(a[...], b[...]) + add(c[...], d[...]) for a, b, c, d in (parts[:4], parts[4:]))
    first = sel_ref[0] == 0
    small = low[:, hidden:]
    turned = pltpu.roll(small, SMALL_ROWS, 1)
    low = low[:, :hidden]
    own_ref[:, :hidden] = jnp.where(first, low, high)
    own_ref[:, hidden:] = jnp.where(first, small, turned)
    send_ref[:, :hidden] = jnp.where(first, high, low).astype(jnp.bfloat16)
    send_ref[:, hidden:] = jnp.where(first, turned, small).astype(jnp.bfloat16)


def to_core(core, parts):
    shape = (parts[-1].shape[0], parts[-1].shape[1] + 2 * SMALL_ROWS)
    return small_call(core_kernel, "to_core", ((shape, jnp.float32), (shape, jnp.bfloat16)), core, *parts)


def final_kernel(sel_ref, own_ref, got_ref, k_ref, gain_ref, in_ref, out_ref, scale_ref, pad_ref):
    share, hidden = own_ref.shape[0], in_ref.shape[2]
    taps = k_ref.shape[2]
    first = sel_ref[0] == 0
    own, got = own_ref[:, :hidden], got_ref[:, :hidden].astype(jnp.float32)
    in_ref[0] = jnp.where(first, own, got)
    out_ref[0] = jnp.where(first, got, own)
    small = add(own_ref[:, hidden:], got_ref[:, hidden:])
    k_ref[0] = small[:, :taps]
    pad_ref[0:share, :] = small
    turned = pad_ref[...].T
    gain_ref[...] = turned[taps : taps + 1, :share]
    scale_ref[...] = turned[taps + 1 : taps + 2, :share]


def final(core, own, got, taps):
    share, hidden = own.shape[0], own.shape[1] - 2 * SMALL_ROWS
    outs = (
        ((1, share, taps), jnp.float32),
        ((1, share), jnp.float32),
        ((1, share, hidden), jnp.float32),
        ((1, share, hidden), jnp.float32),
        ((1, share), jnp.float32),
    )
    t_kernel, t_gain, t_in, t_out, t_scale = small_call(
        final_kernel, "final", outs, core, own, got, scratch=[pltpu.VMEM((LANES, 2 * SMALL_ROWS), jnp.float32)]
    )
    return t_kernel.transpose(0, 2, 1), t_gain, t_in, t_out.transpose(0, 2, 1), t_scale


BF16 = jnp.bfloat16
F32 = jnp.float32


def one_image(x, g, small, sels, w_ins, w_outs, first, passing):
    blocks = small.shape[0]
    rows, cols, channels = x.shape
    which = jnp.stack([sel[0] for sel in sels])
    xs, xhats, invs, pres, branches = forward(which, x, first[1], small, w_ins, w_outs)
    xs, xhats, invs = (x,) + tuple(xs), first[:1] + tuple(xhats), first[2:] + tuple(invs)
    smalls = [None] * blocks
    for s in reversed(range(blocks)):
        keep, send, sums8, gconv = mlp_back(
            sels[s], g.reshape(rows * cols, channels), branches[s], pres[s], xhats[s], invs[s],
            small[s, TAPS : TAPS + 1], small[s, TAPS + 1 : TAPS + 2], w_ins, w_outs, passing.before("mlp", s),
        )
        passing.done(s, keep, send)
        *g_next, smalls[s] = conv_back(
            gconv, xs[s], g, small[s, :TAPS], sums8, s > 0, passing.before("conv", s)
        )
        g = g_next[0] if g_next else None
    return smalls


def finish(t_kernel, t_gain, t_scale, t_in, t_out):
    return t_kernel[None], t_gain[None], t_in[None], t_out[None], t_scale[None]


def any_mesh(images, cotangent, kernels, norm_gains, w_in, w_out, scales):
    segments = lax.axis_size("segment")
    rank = lax.axis_index("segment")
    count = images.shape[0] // segments
    taps = kernels.shape[1]
    small = lax.all_gather(parameters(kernels, norm_gains, scales), "segment")
    all_in = lax.all_gather(w_in[0], "segment")
    all_out = lax.all_gather(w_out[0], "segment")
    sels = [jnp.array([s, 0], jnp.int32) for s in range(segments)]
    pieces = [[None] * 3 for _ in range(segments)]

    class Sums:
        def before(self, part, s):
            return ()

        def done(self, s, keep, send):
            self.add(s, 0, keep.astype(F32))
            self.add(s, 1, send.astype(F32))

        def add(self, s, k, value):
            pieces[s][k] = value if pieces[s][k] is None else pieces[s][k] + value

    sums = Sums()
    w_ins = [all_in[s] for s in range(segments)]
    w_outs = [all_out[s] for s in range(segments)]
    for i in range(count):
        x = lax.dynamic_index_in_dim(images, rank * count + i, 0, keepdims=False)
        g = lax.dynamic_index_in_dim(cotangent, rank * count + i, 0, keepdims=False)
        smalls = one_image(x, g, small, sels, w_ins, w_outs, conv_norm(sels[0] * 0, x, [small[0]]), sums)
        for s in range(segments):
            sums.add(s, 2, smalls[s])

    def summed(values, dim):
        mine = lax.psum_scatter(jnp.stack(values), "segment", scatter_dimension=0, tiled=False)
        return lax.psum_scatter(mine, "dp", scatter_dimension=dim, tiled=True)

    t_in = summed([p[0] for p in pieces], 0)
    t_out = summed([p[1] for p in pieces], 0).T
    t_small = summed([p[2] for p in pieces], 1)
    return finish(t_small[:taps], t_small[taps], t_small[taps + 1], t_in, t_out)


def partners(flip, extent=(4, 2, 2, 2)):
    pairs = []
    for index in range(32):
        z, y, x, c = index >> 3, (index >> 2) & 1, (index >> 1) & 1, index & 1
        other = ((z ^ flip[0]) << 3) | ((y ^ flip[1]) << 2) | ((x ^ flip[2]) << 1) | (c ^ flip[3])
        pairs.append((index, other))
    return pairs


def swap(value, z=0, y=0, x=0, c=0):
    return lax.ppermute(value, ("dp", "segment"), partners((z, y, x, c)))


def along_x(value, to_last):
    pairs = [(i, j) for i, j in partners((0, 0, 1, 0)) if (i >> 1) & 1 == (0 if to_last else 1)]
    return lax.ppermute(value, ("dp", "segment"), pairs)


def this_mesh(images, cotangent, kernels, norm_gains, w_in, w_out, scales):
    rank = lax.axis_index("segment")
    core = rank % 2
    chip = rank // 2
    depth = lax.axis_index("dp") // 2
    side = lax.axis_index("dp") % 2
    own_small = parameters(kernels, norm_gains, scales)
    near_small = swap(own_small, c=1)
    near_in, near_out = swap(w_in[0], c=1), swap(w_out[0], c=1)
    small = (own_small, near_small)
    weights = (w_in[0], near_in, w_out[0], near_out)
    zero = jnp.zeros_like(chip)
    sel = jnp.stack([core, 1 - core, chip, core, zero]).astype(jnp.int32)
    sel_first = jnp.stack([core, 1 - core, chip, core, chip]).astype(jnp.int32)
    sel_conv = (jnp.stack([core, zero]).astype(jnp.int32), jnp.stack([core, chip]).astype(jnp.int32))
    cores = core[None].astype(jnp.int32)
    sides = side[None].astype(jnp.int32)
    levels = jnp.stack([depth, depth ^ 1, depth ^ 2, depth ^ 3]).astype(jnp.int32)

    maps = [lax.dynamic_index_in_dim(images, 2 * core + i, 0, keepdims=False) for i in range(2)]
    ends = [lax.dynamic_index_in_dim(cotangent, 2 * core + i, 0, keepdims=False) for i in range(2)]
    firsts, kept = [], []
    for x, chosen in zip(maps, sel_conv):
        firsts.append(conv_norm(chosen, x, small, tuple(k.inv1 for k in kept)))
        kept.append(pair_forward(sel_first if kept else sel, x, firsts[-1], small, weights))
    passed = [along_x(k.y, True) for k in kept]
    parts, starts = [], []
    for x, g in zip(passed, ends):
        parts.append(pair_map(sel, x, g, small, weights))
        starts.append(along_x(parts[-1].g0, False))
    totals = pair_grads(sel, passed, parts)
    grads = pair_back(sel, starts[0], maps[0], firsts[0], kept[0], small, weights)
    grads = pair_back(sel, starts[1], maps[1], firsts[1], kept[1], small, weights, (grads, totals))
    core1, core0 = swap(grads.send1, c=1), swap(grads.send0, c=1)

    def along_y(*pairs):
        across, mine = to_side(sides, *pairs)
        return mine, swap(across, y=1)

    def along_z(mine, got):
        own, *others = to_depths(levels, mine, got)
        return [own] + [swap(v, z=flip) for v, flip in zip(others, (1, 2, 3))]

    high = along_y(grads.keep1, core1)
    low = along_y(grads.keep0, core0, grads.packed)
    high = along_z(*high)
    low = along_z(*low)
    own, send = to_core(cores, low + high)
    return final(cores, own, swap(send, c=1), kernels.shape[1])


def solution(mesh):
    in_specs = (
        P("dp", None, None, None),
        P("dp", None, None, None),
        P("segment", None, None),
        P("segment", None),
        P("segment", None, None),
        P("segment", None, None),
        P("segment", None),
    )
    out_specs = (
        P("segment", None, "dp"),
        P("segment", "dp"),
        P("segment", "dp", None),
        P("segment", None, "dp"),
        P("segment", "dp"),
    )
    fits = dict(mesh.shape) == {"dp": 8, "segment": 4}

    def whole(images, *rest):
        local = this_mesh if fits and images.shape[0] == 32 else any_mesh
        return jax.shard_map(local, mesh=mesh, in_specs=in_specs, out_specs=out_specs, check_vma=False)(images, *rest)

    return whole
```

```python
import functools
import types
import jax
import jax.numpy as jnp
from jax import lax
from jax.sharding import PartitionSpec as P
from jax.experimental import pallas as pl
from jax.experimental.pallas import tpu as pltpu

EPS = 1e-06
GELU_C = 0.7978845608028654
GELU_A = 0.044715
LANES = 128
def estimate(microseconds):
    return pl.CostEstimate(flops=int(microseconds * 1.1e9), bytes_accessed=int(microseconds * 3.6e6), transcendentals=0)


LIMIT = 40


def vmem(mebibytes):
    return pltpu.CompilerParams(vmem_limit_bytes=mebibytes * 1024 * 1024)


def zero_borders(pad_ref):
    tiles, rows, width, _ = pad_ref.shape
    for c in range(tiles):
        pad_ref[c, :, 0:8] = jnp.zeros((rows, 8, LANES), jnp.float32)
        pad_ref[c, :, width - 8 :] = jnp.zeros((rows, 8, LANES), jnp.float32)


def conv_norm_body(x_ref, small_ref, xhat_ref, normed_ref, inv_ref, pad_ref, conv_ref):
    rows, cols, channels = x_ref.shape
    tiles = channels // LANES
    for c in range(tiles):
        pad_ref[c, :, 8 : cols + 8] = x_ref[:, :, c * LANES : (c + 1) * LANES].astype(jnp.float32)

    def tile(c, carry):
        lanes = pl.ds(pl.multiple_of(c * LANES, LANES), LANES)

        def strip(w, carry):
            base = pl.multiple_of(w * 8, 8)
            window = pad_ref.at[c, :, pl.ds(base, 24), :]
            acc = [None] * rows
            for q in range(7):
                col = [window[h, 5 + q : 13 + q, :] for h in range(rows)]
                for r in range(7):
                    weight = small_ref[r * 7 + q : r * 7 + q + 1, lanes]
                    for h in range(max(0, 3 - r), min(rows, rows + 3 - r)):
                        term = weight * col[h + r - 3]
                        acc[h] = term if acc[h] is None else acc[h] + term
            for h in range(rows):
                conv_ref[h, pl.ds(base, 8), lanes] = acc[h]
            return carry

        return lax.fori_loop(0, cols // 8, strip, carry)

    lax.fori_loop(0, tiles, tile, 0)

    def norm(h, carry):
        value = conv_ref[pl.ds(h * 2, 2)].reshape(2 * cols, channels)
        mean = jnp.mean(value, axis=1, keepdims=True)
        center = value - mean
        inv = lax.rsqrt(jnp.mean(center * center, axis=1, keepdims=True) + EPS)
        xhat = center * inv
        at = pl.ds(pl.multiple_of(h * 2 * cols, 2 * cols), 2 * cols)
        xhat_ref[at, :] = xhat.astype(jnp.bfloat16)
        normed_ref[at, :] = (xhat * small_ref[TAPS : TAPS + 1, :]).astype(jnp.bfloat16)
        inv_ref[at, :] = jnp.broadcast_to(inv, (2 * cols, LANES))
        return carry

    lax.fori_loop(0, rows // 2, norm, 0, unroll=True)


def pad_shape(rows, cols, channels):
    return pltpu.VMEM((channels // LANES, rows, cols + 16, LANES), jnp.float32)


def in_hbm(arrays):
    return [pltpu.with_memory_space_constraint(a, pltpu.HBM) for a in arrays]


def parameters_kernel(k_ref, gain_ref, scale_ref, out_ref, taps_ref, rows_ref, sems):
    copies = [
        pltpu.make_async_copy(source, target, sems.at[i])
        for i, (source, target) in enumerate(((k_ref, taps_ref), (gain_ref, rows_ref.at[0]), (scale_ref, rows_ref.at[1])))
    ]
    for copy in copies:
        copy.start()
    taps = taps_ref.shape[0]
    out_ref[taps + 2 :, :] = jnp.zeros((out_ref.shape[0] - taps - 2, out_ref.shape[1]), jnp.float32)
    for copy in copies:
        copy.wait()
    for t in range(taps):
        out_ref[t : t + 1, :] = taps_ref[t]
    out_ref[taps : taps + 1, :] = rows_ref[0]
    out_ref[taps + 1 : taps + 2, :] = rows_ref[1]


def parameters(kernels, norm_gains, scales):
    taps, channels = kernels.shape[1:]
    return pl.pallas_call(
        parameters_kernel,
        in_specs=[pl.BlockSpec(memory_space=pl.ANY)] * 3,
        out_shape=jax.ShapeDtypeStruct((56, channels), jnp.float32),
        scratch_shapes=[
            pltpu.VMEM((taps, 1, channels), jnp.float32),
            pltpu.VMEM((2, 1, channels), jnp.float32),
            pltpu.SemaphoreType.DMA((3,)),
        ],
        compiler_params=vmem(LIMIT),
        name="parameters",
        cost_estimate=estimate(0.5),
    )(*in_hbm([kernels.transpose(1, 0, 2), norm_gains, scales]))


def choose_small(r):
    first = r.sel[0] == 0
    own, near = r.own_small[...], r.near_small[...]
    r.small[0] = jnp.where(first, own, near)
    r.small[1] = jnp.where(first, near, own)


def conv_norm_kernel(choices, sel_ref, x_ref, *rest):
    smalls, rest = rest[:choices], rest[choices:]
    xhat_ref, normed_ref, inv_ref, pad_ref, conv_ref, small_ref = rest[-6:]
    active = sel_ref[1] == 0

    @pl.when(active)
    def _():
        zero_borders(pad_ref)
        small_ref[...] = smalls[0][...]
        for k in range(1, choices):

            @pl.when(sel_ref[0] == k)
            def _():
                small_ref[...] = smalls[k][...]

        conv_norm_body(x_ref, small_ref, xhat_ref, normed_ref, inv_ref, pad_ref, conv_ref)


def conv_norm(sel, x, smalls, after=()):
    rows, cols, channels = x.shape
    n = rows * cols
    return pl.pallas_call(
        functools.partial(conv_norm_kernel, len(smalls)),
        in_specs=[pl.BlockSpec(memory_space=pltpu.SMEM)]
        + [pl.BlockSpec(memory_space=pltpu.VMEM)] * (1 + len(smalls))
        + [pl.BlockSpec(memory_space=pl.ANY)] * len(after),
        out_shape=(
            jax.ShapeDtypeStruct((n, channels), jnp.bfloat16),
            jax.ShapeDtypeStruct((n, channels), jnp.bfloat16),
            jax.ShapeDtypeStruct((n, LANES), jnp.float32),
        ),
        scratch_shapes=[
            pad_shape(rows, cols, channels),
            pltpu.VMEM((rows, cols, channels), jnp.float32),
            pltpu.VMEM(smalls[0].shape, jnp.float32),
        ],
        compiler_params=vmem(LIMIT),
        name="conv_norm",
        cost_estimate=estimate(2.0),
    )(sel, x, *smalls, *after)


def copy_chosen(which, sources, target, sem):
    for m, source in enumerate(sources):

        @pl.when(which == m)
        def _():
            pltpu.make_async_copy(source, target, sem).start()

    return lambda: pltpu.make_async_copy(sources[0], target, sem).wait()


def forward_kernel(choices, blocks, sel_ref, x_ref, normed0_ref, small_ref, *rest):
    w_ins, w_outs, rest = rest[:choices], rest[choices : 2 * choices], rest[2 * choices :]
    xs = [x_ref] + list(rest[: blocks - 1])
    xhats, invs, rest = rest[blocks - 1 : 2 * blocks - 2], rest[2 * blocks - 2 : 3 * blocks - 3], rest[3 * blocks - 3 :]
    pres, branches, rest = rest[:blocks], rest[blocks : 2 * blocks], rest[2 * blocks :]
    normed_ref, hid_ref, acc_ref, pad_ref, conv_ref, w_in_ref, w_out_ref, sems = rest
    rows, cols, channels = x_ref.shape
    n = rows * cols
    hidden = w_in_ref.shape[2]
    waits = []
    for s in range(blocks):
        waits.append((
            copy_chosen(sel_ref[s], w_ins, w_in_ref.at[s], sems.at[0, s]),
            copy_chosen(sel_ref[s], w_outs, w_out_ref.at[s], sems.at[1, s]),
        ))
    zero_borders(pad_ref)
    step, sub = 256, 2 * cols
    for s in range(blocks):
        normed = normed0_ref if s == 0 else normed_ref
        waits[s][0]()
        for j in range(hidden // step):
            cut = slice(j * step, (j + 1) * step)
            pre = jnp.dot(normed[...], w_in_ref[s, :, cut], preferred_element_type=jnp.float32)
            for i in range(n // sub):
                p = pre[i * sub : (i + 1) * sub]
                half = 0.5 * p
                hid_ref[i * sub : (i + 1) * sub, :] = (half + half * tanh_arg(p)).astype(jnp.bfloat16)
                pres[s][i * sub : (i + 1) * sub, cut] = p.astype(jnp.bfloat16)
            if j == 0:
                waits[s][1]()
            part = jnp.dot(hid_ref[...], w_out_ref[s, cut, :], preferred_element_type=jnp.float32)
            if j == 0:
                acc_ref[...] = part
            else:
                acc_ref[...] += part
        scale = small_ref[s, TAPS + 1 : TAPS + 2, :]
        for i in range(n // sub):
            branch = acc_ref[i * sub : (i + 1) * sub, :]
            branches[s][i * sub : (i + 1) * sub, :] = branch.astype(jnp.bfloat16)
            if s < blocks - 1:
                x_old = xs[s][2 * i : 2 * i + 2].astype(jnp.float32).reshape(sub, channels)
                xs[s + 1][2 * i : 2 * i + 2] = (x_old + scale * branch).astype(jnp.bfloat16).reshape(2, cols, channels)
        if s < blocks - 1:
            conv_norm_body(xs[s + 1], small_ref.at[s + 1], xhats[s], normed_ref, invs[s], pad_ref, conv_ref)


def forward(sel, x, normed0, small, w_ins, w_outs):
    blocks = small.shape[0]
    rows, cols, channels = x.shape
    n = rows * cols
    hidden = w_ins[0].shape[1]
    out = pl.pallas_call(
        functools.partial(forward_kernel, len(w_ins), blocks),
        in_specs=[pl.BlockSpec(memory_space=pltpu.SMEM)]
        + [pl.BlockSpec(memory_space=pltpu.VMEM)] * 3
        + [pl.BlockSpec(memory_space=pl.ANY)] * (2 * len(w_ins)),
        out_shape=(jax.ShapeDtypeStruct((rows, cols, channels), jnp.bfloat16),) * (blocks - 1)
        + (jax.ShapeDtypeStruct((n, channels), jnp.bfloat16),) * (blocks - 1)
        + (jax.ShapeDtypeStruct((n, LANES), jnp.float32),) * (blocks - 1)
        + (jax.ShapeDtypeStruct((n, hidden), jnp.bfloat16),) * blocks
        + (jax.ShapeDtypeStruct((n, channels), jnp.bfloat16),) * blocks,
        scratch_shapes=[
            pltpu.VMEM((n, channels), jnp.bfloat16),
            pltpu.VMEM((n, 256), jnp.bfloat16),
            pltpu.VMEM((n, channels), jnp.float32),
            pad_shape(rows, cols, channels),
            pltpu.VMEM((rows, cols, channels), jnp.float32),
            pltpu.VMEM((blocks, channels, hidden), jnp.bfloat16),
            pltpu.VMEM((blocks, hidden, channels), jnp.bfloat16),
            pltpu.SemaphoreType.DMA((2, blocks)),
        ],
        compiler_params=vmem(LIMIT),
        name="forward",
        cost_estimate=estimate(15),
    )(sel, x, normed0, small, *in_hbm(w_ins), *in_hbm(w_outs))
    k = blocks - 1
    return out[:k], out[k : 2 * k], out[2 * k : 3 * k], out[3 * k : 3 * k + blocks], out[3 * k + blocks :]


def tanh_arg(x):
    return jnp.tanh(x * (GELU_C + (GELU_C * GELU_A) * (x * x)))


def load_weights(sel_ref, w_ins, w_outs, w_in_ref, w_out_ref, sems):
    for m in range(len(w_ins)):

        @pl.when(sel_ref[0] == m)
        def _():
            pltpu.make_async_copy(w_ins[m], w_in_ref, sems.at[0]).start()
            pltpu.make_async_copy(w_outs[m], w_out_ref, sems.at[1]).start()

    return (
        pltpu.make_async_copy(w_ins[0], w_in_ref, sems.at[0]).wait,
        pltpu.make_async_copy(w_outs[0], w_out_ref, sems.at[1]).wait,
    )


def specs(sel, arrays, choices, after=0):
    return (
        [pl.BlockSpec(memory_space=pltpu.SMEM)]
        + [pl.BlockSpec(memory_space=pltpu.VMEM)] * arrays
        + [pl.BlockSpec(memory_space=pl.ANY)] * (2 * choices + after)
    )


def mlp_back_kernel(choices, after, sel_ref, g_ref, branch_ref, pre_ref, xhat_ref, inv_ref, gain_ref, scale_ref, *rest):
    w_ins, w_outs = rest[:choices], rest[choices : 2 * choices]
    (keep_ref, send_ref, small_ref, gconv_ref,
     gb_ref, nm_ref, hid_ref, gp_ref, acc_ref, w_in_ref, w_out_ref, sems) = rest[2 * choices + after :]
    wait_in, wait_out = load_weights(sel_ref, w_ins, w_outs, w_in_ref, w_out_ref, sems)
    first = sel_ref[1] == 0
    n, channels = g_ref.shape
    hidden = w_in_ref.shape[1]
    step = 256
    sub = 32
    scale_sum = jnp.zeros((8, channels), jnp.float32)
    for i in range(n // sub):
        at = slice(i * sub, (i + 1) * sub)
        g = g_ref[at, :].astype(jnp.float32)
        scale_sum = scale_sum + jnp.sum((g * branch_ref[at, :].astype(jnp.float32)).reshape(sub // 8, 8, channels), axis=0)
        gb_ref[at, :] = (g * scale_ref[...]).astype(jnp.bfloat16)
        nm_ref[at, :] = (xhat_ref[at, :].astype(jnp.float32) * gain_ref[...]).astype(jnp.bfloat16)
    gb_t = gb_ref[...].T
    nm_t = nm_ref[...].T
    wait_in()
    wait_out()
    for j in range(hidden // step):
        cut = slice(j * step, (j + 1) * step)
        gh = lax.dot_general(gb_ref[...], w_out_ref[cut, :], (((1,), (1,)), ((), ())), preferred_element_type=jnp.float32)
        for i in range(n // sub):
            at = slice(i * sub, (i + 1) * sub)
            p = pre_ref[at, cut].astype(jnp.float32)
            sq = p * p
            t = jnp.tanh(p * (GELU_C + (GELU_C * GELU_A) * sq))
            cdf = 0.5 + 0.5 * t
            hid_ref[at, :] = (p * cdf).astype(jnp.bfloat16)
            slope = cdf + (0.5 * p) * (1.0 - t * t) * (GELU_C + (3.0 * GELU_C * GELU_A) * sq)
            gp_ref[at, :] = (gh[at, :] * slope).astype(jnp.bfloat16)
        t_out = jnp.dot(gb_t, hid_ref[...], preferred_element_type=jnp.float32)
        t_in = jnp.dot(nm_t, gp_ref[...], preferred_element_type=jnp.float32)
        keep_ref[:, cut] = jnp.where(first, t_in, t_out).astype(jnp.bfloat16)
        send_ref[:, cut] = jnp.where(first, t_out, t_in).astype(jnp.bfloat16)
        part = lax.dot_general(gp_ref[...], w_in_ref[:, cut], (((1,), (1,)), ((), ())), preferred_element_type=jnp.float32)
        if j == 0:
            acc_ref[...] = part
        else:
            acc_ref[...] += part
    gain_sum = jnp.zeros((8, channels), jnp.float32)
    for i in range(n // sub):
        at = slice(i * sub, (i + 1) * sub)
        gn = acc_ref[at, :]
        xhat = xhat_ref[at, :].astype(jnp.float32)
        gain_sum = gain_sum + jnp.sum((gn * xhat).reshape(sub // 8, 8, channels), axis=0)
        gx = gn * gain_ref[...]
        m1 = jnp.mean(gx, axis=1, keepdims=True)
        m2 = jnp.mean(gx * xhat, axis=1, keepdims=True)
        inv = inv_ref[at, 0:1]
        gconv_ref[at, :] = inv * (gx - m1 - xhat * m2)
    small_ref[0:1, :] = jnp.sum(gain_sum, axis=0, keepdims=True)
    small_ref[1:2, :] = jnp.sum(scale_sum, axis=0, keepdims=True)
    small_ref[2:8, :] = jnp.zeros((6, channels), jnp.float32)


def mlp_back(sel, g, branch, pre, xhat, inv, gain, scale, w_ins, w_outs, after=()):
    n, channels = g.shape
    hidden = w_ins[0].shape[1]
    return pl.pallas_call(
        functools.partial(mlp_back_kernel, len(w_ins), len(after)),
        in_specs=specs(sel, 7, len(w_ins), len(after)),
        out_shape=(
            jax.ShapeDtypeStruct((channels, hidden), jnp.bfloat16),
            jax.ShapeDtypeStruct((channels, hidden), jnp.bfloat16),
            jax.ShapeDtypeStruct((8, channels), jnp.float32),
            jax.ShapeDtypeStruct((n, channels), jnp.float32),
        ),
        scratch_shapes=[
            pltpu.VMEM((n, channels), jnp.bfloat16),
            pltpu.VMEM((n, channels), jnp.bfloat16),
            pltpu.VMEM((n, 256), jnp.bfloat16),
            pltpu.VMEM((n, 256), jnp.bfloat16),
            pltpu.VMEM((n, channels), jnp.float32),
            pltpu.VMEM((channels, hidden), jnp.bfloat16),
            pltpu.VMEM((hidden, channels), jnp.bfloat16),
            pltpu.SemaphoreType.DMA((2,)),
        ],
        compiler_params=vmem(LIMIT),
        name="mlp_back",
        cost_estimate=estimate(2.5),
    )(sel, g, branch, pre, xhat, inv, gain, scale, *in_hbm(w_ins), *in_hbm(w_outs), *after)


SMALL_ROWS = 64
TAPS = 49


def conv_back_kernel(need_map, after, gconv_ref, x_ref, g_ref, k_ref, small_ref, *rest):
    *out_ref, tk_ref, pad_ref, sum_ref, wide_ref, map_ref = rest[after:]
    conv_back_body(gconv_ref, x_ref, g_ref, k_ref, small_ref, out_ref[0] if need_map else None, tk_ref,
                   pad_ref, sum_ref, wide_ref, map_ref)


def conv_back(gconv, x, g, kernel, small, need_map=True, after=()):
    rows, cols, channels = x.shape
    out = (jax.ShapeDtypeStruct((SMALL_ROWS, channels), jnp.float32),)
    if need_map:
        out = (jax.ShapeDtypeStruct((rows, cols, channels), jnp.bfloat16),) + out
    return pl.pallas_call(
        functools.partial(conv_back_kernel, need_map, len(after)),
        in_specs=[pl.BlockSpec(memory_space=pltpu.VMEM)] * 5 + [pl.BlockSpec(memory_space=pl.ANY)] * len(after),
        out_shape=out,
        scratch_shapes=[
            pad_shape(rows, cols, channels),
            pltpu.VMEM((cols // 8, TAPS, 8, LANES), jnp.float32),
            pltpu.VMEM((rows, cols, channels), jnp.float32),
            pltpu.VMEM((rows, cols, channels), jnp.float32),
        ],
        compiler_params=vmem(LIMIT),
        name="conv_back",
        cost_estimate=estimate(3.4 if need_map else 1.6),
    )(gconv, x, g, kernel, small, *after)


def small_call(kernel, name, outs, *args, scratch=(), after=()):
    used = len(args)

    def body(*refs):
        kernel(*refs[:used], *refs[used + len(after) :])

    return pl.pallas_call(
        body,
        in_specs=[pl.BlockSpec(memory_space=pltpu.SMEM)]
        + [pl.BlockSpec(memory_space=pltpu.VMEM)] * (used - 1)
        + [pl.BlockSpec(memory_space=pl.ANY)] * len(after),
        out_shape=tuple(out_struct(*o) for o in outs),
        scratch_shapes=list(scratch),
        compiler_params=vmem(LIMIT),
        name=name,
        cost_estimate=estimate(0.7),
    )(*args, *after)


def conv_back_body(gconv_ref, x_ref, g_ref, small_ref, sums8_ref, out_ref, tk_ref, pad_ref, sum_ref, wide_ref, map_ref):
    rows, cols, channels = x_ref.shape
    tiles = channels // LANES
    zero_borders(pad_ref)
    for c in range(tiles):
        pad_ref[c, :, 8 : cols + 8] = gconv_ref[:, c * LANES : (c + 1) * LANES].reshape(rows, cols, LANES)

    for h in range(rows):
        wide_ref[h] = x_ref[h].astype(jnp.float32)

    def tile(c, carry):
        lanes = pl.ds(pl.multiple_of(c * LANES, LANES), LANES)

        def strip(w, carry):
            base = pl.multiple_of(w * 8, 8)
            window = pad_ref.at[c, :, pl.ds(base, 24), :]
            xs = [wide_ref[h, pl.ds(base, 8), lanes] for h in range(rows)]
            acc = [None] * rows
            for q in range(7):
                col = [window[h, 11 - q : 19 - q, :] for h in range(rows)]
                for r in range(7):
                    tap = r * 7 + q
                    if out_ref is not None:
                        weight = small_ref[tap : tap + 1, lanes]
                    total = None
                    for h in range(max(0, r - 3), min(rows, rows + r - 3)):
                        shifted = col[h + 3 - r]
                        term = xs[h] * shifted
                        total = term if total is None else total + term
                        if out_ref is not None:
                            moved = weight * shifted
                            acc[h] = moved if acc[h] is None else acc[h] + moved
                    sum_ref[w, tap] = total
            if out_ref is not None:
                for h in range(rows):
                    map_ref[h, pl.ds(base, 8), lanes] = acc[h]
            return carry

        lax.fori_loop(0, cols // 8, strip, 0)
        tk_ref[0:TAPS, lanes] = jnp.sum(sum_ref[0] + sum_ref[1], axis=1)
        return carry

    lax.fori_loop(0, tiles, tile, 0)
    if out_ref is not None:
        for h in range(rows):
            out_ref[h] = (g_ref[h].astype(jnp.float32) + map_ref[h]).astype(jnp.bfloat16)
    tk_ref[TAPS : TAPS + 2, :] = sums8_ref[0:2, :]
    tk_ref[TAPS + 2 :, :] = jnp.zeros((SMALL_ROWS - TAPS - 2, channels), jnp.float32)


def conv_map_body(gconv_ref, g_ref, small_ref, out_ref, pad_ref, map_ref):
    rows, cols, channels = g_ref.shape
    tiles = channels // LANES
    zero_borders(pad_ref)
    for c in range(tiles):
        pad_ref[c, :, 8 : cols + 8] = gconv_ref[:, c * LANES : (c + 1) * LANES].reshape(rows, cols, LANES)

    def tile(c, carry):
        lanes = pl.ds(pl.multiple_of(c * LANES, LANES), LANES)

        def strip(w, carry):
            base = pl.multiple_of(w * 8, 8)
            window = pad_ref.at[c, :, pl.ds(base, 24), :]
            acc = [None] * rows
            for q in range(7):
                col = [window[h, 11 - q : 19 - q, :] for h in range(rows)]
                for r in range(7):
                    weight = small_ref[r * 7 + q : r * 7 + q + 1, lanes]
                    for h in range(max(0, r - 3), min(rows, rows + r - 3)):
                        term = weight * col[h + 3 - r]
                        acc[h] = term if acc[h] is None else acc[h] + term
            for h in range(rows):
                map_ref[h, pl.ds(base, 8), lanes] = acc[h]
            return carry

        return lax.fori_loop(0, cols // 8, strip, carry)

    lax.fori_loop(0, tiles, tile, 0)
    for h in range(rows):
        out_ref[h] = (g_ref[h].astype(jnp.float32) + map_ref[h]).astype(jnp.bfloat16)


def mlp_back_map_body(g_ref, branch_ref, pre_ref, xhat_ref, inv_ref, small_ref, w_in_ref, w_out_ref,
                      sums8_ref, gconv_ref, gb_ref, nm_ref, hid_ref, gp_ref, acc_ref, ready):
    rows, cols, channels = g_ref.shape
    n = rows * cols
    hidden = w_in_ref.shape[1]
    step = 256
    sub = 2 * cols
    gain = small_ref[TAPS : TAPS + 1, :]
    scale = small_ref[TAPS + 1 : TAPS + 2, :]
    scale_sum = jnp.zeros((8, channels), jnp.float32)
    for i in range(n // sub):
        at = slice(i * sub, (i + 1) * sub)
        g = g_ref[2 * i : 2 * i + 2].astype(jnp.float32).reshape(sub, channels)
        scale_sum = scale_sum + jnp.sum((g * branch_ref[at, :].astype(jnp.float32)).reshape(sub // 8, 8, channels), axis=0)
        gb_ref[at, :] = (g * scale).astype(jnp.bfloat16)
        nm_ref[at, :] = (xhat_ref[at, :].astype(jnp.float32) * gain).astype(jnp.bfloat16)
    ready("gb", "nm")
    for j in range(hidden // step):
        cut = slice(j * step, (j + 1) * step)
        gh = lax.dot_general(gb_ref[...], w_out_ref[cut, :], (((1,), (1,)), ((), ())), preferred_element_type=jnp.float32)
        for i in range(n // sub):
            at = slice(i * sub, (i + 1) * sub)
            p = pre_ref[at, cut].astype(jnp.float32)
            sq = p * p
            t = jnp.tanh(p * (GELU_C + (GELU_C * GELU_A) * sq))
            cdf = 0.5 + 0.5 * t
            hid_ref[at, cut] = (p * cdf).astype(jnp.bfloat16)
            slope = cdf + (0.5 * p) * (1.0 - t * t) * (GELU_C + (3.0 * GELU_C * GELU_A) * sq)
            gp_ref[at, cut] = (gh[at, :] * slope).astype(jnp.bfloat16)
        part = lax.dot_general(gp_ref[:, cut], w_in_ref[:, cut], (((1,), (1,)), ((), ())), preferred_element_type=jnp.float32)
        if j == 0:
            acc_ref[...] = part
        else:
            acc_ref[...] += part
    ready("hid", "gp")
    gain_sum = jnp.zeros((8, channels), jnp.float32)
    for i in range(n // sub):
        at = slice(i * sub, (i + 1) * sub)
        gn = acc_ref[at, :]
        xhat = xhat_ref[at, :].astype(jnp.float32)
        gain_sum = gain_sum + jnp.sum((gn * xhat).reshape(sub // 8, 8, channels), axis=0)
        gx = gn * gain
        m1 = jnp.mean(gx, axis=1, keepdims=True)
        m2 = jnp.mean(gx * xhat, axis=1, keepdims=True)
        gconv_ref[at, :] = inv_ref[at, 0:1] * (gx - m1 - xhat * m2)
    sums8_ref[0:1, :] = jnp.sum(gain_sum, axis=0, keepdims=True)
    sums8_ref[1:2, :] = jnp.sum(scale_sum, axis=0, keepdims=True)
    sums8_ref[2:8, :] = jnp.zeros((6, channels), jnp.float32)
    ready("gconv", "sums")


def mlp_back_body(first, g_ref, branch_ref, pre_ref, xhat_ref, inv_ref, small_ref, wait_in, wait_out, w_in_ref, w_out_ref,
                  keep_ref, send_ref, sums8_ref, gconv_ref, gb_ref, nm_ref, hid_ref, gp_ref, acc_ref, before=None):
    rows, cols, channels = g_ref.shape
    n = rows * cols
    hidden = w_in_ref.shape[1]
    step = 256
    sub = 2 * cols
    gain = small_ref[TAPS : TAPS + 1, :]
    scale = small_ref[TAPS + 1 : TAPS + 2, :]
    scale_sum = jnp.zeros((8, channels), jnp.float32)
    for i in range(n // sub):
        at = slice(i * sub, (i + 1) * sub)
        g = g_ref[2 * i : 2 * i + 2].astype(jnp.float32).reshape(sub, channels)
        scale_sum = scale_sum + jnp.sum((g * branch_ref[at, :].astype(jnp.float32)).reshape(sub // 8, 8, channels), axis=0)
        gb_ref[at, :] = (g * scale).astype(jnp.bfloat16)
        nm_ref[at, :] = (xhat_ref[at, :].astype(jnp.float32) * gain).astype(jnp.bfloat16)
    gb_t = gb_ref[...].T
    nm_t = nm_ref[...].T
    wait_out()
    for j in range(hidden // step):
        cut = slice(j * step, (j + 1) * step)
        gh = lax.dot_general(gb_ref[...], w_out_ref[cut, :], (((1,), (1,)), ((), ())), preferred_element_type=jnp.float32)
        for i in range(n // sub):
            at = slice(i * sub, (i + 1) * sub)
            p = pre_ref[at, cut].astype(jnp.float32)
            sq = p * p
            t = jnp.tanh(p * (GELU_C + (GELU_C * GELU_A) * sq))
            cdf = 0.5 + 0.5 * t
            hid_ref[at, :] = (p * cdf).astype(jnp.bfloat16)
            slope = cdf + (0.5 * p) * (1.0 - t * t) * (GELU_C + (3.0 * GELU_C * GELU_A) * sq)
            gp_ref[at, :] = (gh[at, :] * slope).astype(jnp.bfloat16)
        t_out = jnp.dot(gb_t, hid_ref[...], preferred_element_type=jnp.float32)
        t_in = jnp.dot(nm_t, gp_ref[...], preferred_element_type=jnp.float32)
        t_keep = jnp.where(first, t_in, t_out)
        t_send = jnp.where(first, t_out, t_in)
        if before is not None:
            if j == 0:
                old_keep, old_send = before()
            t_keep = t_keep + old_keep[:, cut].astype(jnp.float32)
            t_send = t_send + old_send[:, cut].astype(jnp.float32)
        keep_ref[:, cut] = t_keep.astype(jnp.bfloat16)
        send_ref[:, cut] = t_send.astype(jnp.bfloat16)
        if j == 0:
            wait_in()
        part = lax.dot_general(gp_ref[...], w_in_ref[:, cut], (((1,), (1,)), ((), ())), preferred_element_type=jnp.float32)
        if j == 0:
            acc_ref[...] = part
        else:
            acc_ref[...] += part
    gain_sum = jnp.zeros((8, channels), jnp.float32)
    for i in range(n // sub):
        at = slice(i * sub, (i + 1) * sub)
        gn = acc_ref[at, :]
        xhat = xhat_ref[at, :].astype(jnp.float32)
        gain_sum = gain_sum + jnp.sum((gn * xhat).reshape(sub // 8, 8, channels), axis=0)
        gx = gn * gain
        m1 = jnp.mean(gx, axis=1, keepdims=True)
        m2 = jnp.mean(gx * xhat, axis=1, keepdims=True)
        gconv_ref[at, :] = inv_ref[at, 0:1] * (gx - m1 - xhat * m2)
    sums8_ref[0:1, :] = jnp.sum(gain_sum, axis=0, keepdims=True)
    sums8_ref[1:2, :] = jnp.sum(scale_sum, axis=0, keepdims=True)
    sums8_ref[2:8, :] = jnp.zeros((6, channels), jnp.float32)


def out_struct(shape, dtype, by_hand=False):
    return pltpu.HBM(shape, dtype) if by_hand else jax.ShapeDtypeStruct(shape, dtype)


def named_call(name, body, ins, outs, scratch, cost):
    names = list(ins) + list(outs) + list(scratch)
    spaces = {"v": pltpu.VMEM, "s": pltpu.SMEM, "a": pl.ANY, "h": pl.ANY}

    def kernel(*refs):
        body(types.SimpleNamespace(**dict(zip(names, refs))))

    args = [pltpu.with_memory_space_constraint(a, pltpu.HBM) if kind == "h" else a for a, kind in ins.values()]
    result = pl.pallas_call(
        kernel,
        in_specs=[pl.BlockSpec(memory_space=spaces[kind]) for _, kind in ins.values()],
        out_specs=tuple(pl.BlockSpec(memory_space=pl.ANY if len(o) > 2 else pltpu.VMEM) for o in outs.values()),
        out_shape=tuple(out_struct(*o) for o in outs.values()),
        scratch_shapes=list(scratch.values()),
        compiler_params=vmem(LIMIT),
        name=name,
        cost_estimate=estimate(cost),
    )(*args)
    return types.SimpleNamespace(**dict(zip(outs, result)))


def mlp_body(normed_ref, wait_in, wait_out, w_in_ref, w_out_ref, pre_ref, hid_ref, acc_ref):
    n = normed_ref.shape[0]
    hidden = w_in_ref.shape[1]
    step, sub = 256, 32
    wait_in()
    for j in range(hidden // step):
        cut = slice(j * step, (j + 1) * step)
        pre = jnp.dot(normed_ref[...], w_in_ref[:, cut], preferred_element_type=jnp.float32)
        for i in range(n // sub):
            p = pre[i * sub : (i + 1) * sub]
            half = 0.5 * p
            hid_ref[i * sub : (i + 1) * sub, :] = (half + half * tanh_arg(p)).astype(jnp.bfloat16)
            pre_ref[i * sub : (i + 1) * sub, cut] = p.astype(jnp.bfloat16)
        if j == 0:
            wait_out()
        part = jnp.dot(hid_ref[...], w_out_ref[cut, :], preferred_element_type=jnp.float32)
        if j == 0:
            acc_ref[...] = part
        else:
            acc_ref[...] += part


def residual_body(x_ref, small_ref, acc_ref, branch_ref, y_ref):
    rows, cols, channels = x_ref.shape
    scale = small_ref[TAPS + 1 : TAPS + 2, :]
    sub = 2 * cols
    for i in range(rows // 2):
        branch = acc_ref[i * sub : (i + 1) * sub, :]
        branch_ref[i * sub : (i + 1) * sub, :] = branch.astype(jnp.bfloat16)
        if y_ref is not None:
            old = x_ref[2 * i : 2 * i + 2].astype(jnp.float32).reshape(sub, channels)
            y_ref[2 * i : 2 * i + 2] = (old + scale * branch).astype(jnp.bfloat16).reshape(2, cols, channels)


def small_ins(pair):
    return {"own_small": (pair[0], "v"), "near_small": (pair[1], "v")}


def small_scratch(pair):
    return {"small": pltpu.VMEM((2,) + pair[0].shape, jnp.float32)}


def weight_ins(pair):
    return {k: (v, "h") for k, v in zip(("own_in", "near_in", "own_out", "near_out"), pair)}


def weight_scratch(blocks, channels, hidden):
    return {
        "w_in": pltpu.VMEM((blocks, channels, hidden), jnp.bfloat16),
        "w_out": pltpu.VMEM((blocks, hidden, channels), jnp.bfloat16),
        "w_sem": pltpu.SemaphoreType.DMA((2, blocks)),
    }


def start_weights(r, slot, block, out_first=False):
    def start(k, own, near, target):
        return copy_chosen(r.sel[block], (own, near), target.at[slot], r.w_sem.at[k, slot])

    if out_first:
        wait_out = start(1, r.own_out, r.near_out, r.w_out)
        return start(0, r.own_in, r.near_in, r.w_in), wait_out
    return start(0, r.own_in, r.near_in, r.w_in), start(1, r.own_out, r.near_out, r.w_out)


def pair_forward(sel, x, first, small, weights):
    rows, cols, channels = x.shape
    n, hidden = rows * cols, weights[0].shape[1]
    bf16, f32 = jnp.bfloat16, jnp.float32

    def body(r):
        @pl.when(r.sel[4] == 0)
        def _():
            low, high = start_weights(r, 0, 0), start_weights(r, 1, 1)
            choose_small(r)
            zero_borders(r.pad)
            mlp_body(r.normed0, *low, r.w_in.at[0], r.w_out.at[0], r.pre0, r.hid, r.acc)
            residual_body(r.x, r.small.at[0], r.acc, r.branch0, r.x1)
            conv_norm_body(r.x1, r.small.at[1], r.xhat1, r.normed, r.inv1, r.pad, r.conv)
            mlp_body(r.normed, *high, r.w_in.at[1], r.w_out.at[1], r.pre1, r.hid, r.acc)
            residual_body(r.x1, r.small.at[1], r.acc, r.branch1, r.y)

    return named_call(
        "pair_forward", body,
        {"sel": (sel, "s"), "x": (x, "v"), "normed0": (first[1], "v"), **small_ins(small), **weight_ins(weights)},
        {"y": (x.shape, bf16), "x1": (x.shape, bf16), "xhat1": ((n, channels), bf16), "inv1": ((n, LANES), f32),
         "pre0": ((n, hidden), bf16), "pre1": ((n, hidden), bf16),
         "branch0": ((n, channels), bf16), "branch1": ((n, channels), bf16)},
        {"normed": pltpu.VMEM((n, channels), bf16), "hid": pltpu.VMEM((n, 256), bf16), "acc": pltpu.VMEM((n, channels), f32),
         "pad": pad_shape(rows, cols, channels), "conv": pltpu.VMEM((rows, cols, channels), f32),
         **weight_scratch(2, channels, hidden), **small_scratch(small)},
        7.5,
    )


def back_scratch(n, channels):
    bf16, f32 = jnp.bfloat16, jnp.float32
    return {"gb": pltpu.VMEM((n, channels), bf16), "nm": pltpu.VMEM((n, channels), bf16),
            "hid": pltpu.VMEM((n, 256), bf16), "gp": pltpu.VMEM((n, 256), bf16), "acc": pltpu.VMEM((n, channels), f32)}


def back_temps(r):
    return r.gb, r.nm, r.hid, r.gp, r.acc


GRADS = ("keep0", "send0", "keep1", "send1")
FACTORS = ("gb", "nm", "hid", "gp", "gconv", "sums")


def factor_shapes(n, channels, hidden):
    bf16, f32 = jnp.bfloat16, jnp.float32
    one = {"gb": ((n, channels), bf16), "nm": ((n, channels), bf16), "hid": ((n, hidden), bf16), "gp": ((n, hidden), bf16),
           "gconv": ((n, channels), f32), "sums": ((8, channels), f32)}
    return {name + str(k): one[name] for k in (0, 1) for name in FACTORS}


def pair_map(sel, x, g, small, weights):
    rows, cols, channels = x.shape
    n, hidden = rows * cols, weights[0].shape[1]
    bf16, f32 = jnp.bfloat16, jnp.float32
    shapes = factor_shapes(n, channels, hidden)
    saved = {**shapes, "x1": (x.shape, bf16)}
    order = list(saved)

    def body(r):
        @pl.when(r.sel[2] == 1)
        def _():
            def copy_out(name):
                return pltpu.make_async_copy(getattr(r, "v_" + name), getattr(r, name), r.s_sem.at[order.index(name)])

            low, high = start_weights(r, 0, 0), start_weights(r, 1, 1)
            choose_small(r)
            zero_borders(r.pad)
            s0, s1 = r.small.at[0], r.small.at[1]
            conv_norm_body(r.x, s0, r.xhat0, r.normed, r.inv0, r.pad, r.conv)
            mlp_body(r.normed, *low, r.w_in.at[0], r.w_out.at[0], r.pre0, r.hid, r.acc)
            residual_body(r.x, s0, r.acc, r.branch0, r.v_x1)
            copy_out("x1").start()
            conv_norm_body(r.v_x1, s1, r.xhat1, r.normed, r.inv1, r.pad, r.conv)
            mlp_body(r.normed, *high, r.w_in.at[1], r.w_out.at[1], r.pre1, r.hid, r.acc)
            residual_body(r.v_x1, s1, r.acc, r.branch1, None)

            def ready(k):
                def start(*names):
                    for name in names:
                        copy_out(name + str(k)).start()

                return start

            mlp_back_map_body(r.g, r.branch1, r.pre1, r.xhat1, r.inv1, s1, r.w_in.at[1], r.w_out.at[1],
                              r.v_sums1, r.v_gconv1, r.v_gb1, r.v_nm1, r.v_hid1, r.v_gp1, r.acc, ready(1))
            conv_map_body(r.v_gconv1, r.g, s1, r.g1, r.pad, r.conv)
            mlp_back_map_body(r.g1, r.branch0, r.pre0, r.xhat0, r.inv0, s0, r.w_in.at[0], r.w_out.at[0],
                              r.v_sums0, r.v_gconv0, r.v_gb0, r.v_nm0, r.v_hid0, r.v_gp0, r.acc, ready(0))
            conv_map_body(r.v_gconv0, r.g1, s0, r.g0, r.pad, r.conv)
            for name in order:
                copy_out(name).wait()

    return named_call(
        "pair_map", body,
        {"sel": (sel, "s"), "x": (x, "v"), "g": (g, "v"), **small_ins(small), **weight_ins(weights)},
        {"g0": (x.shape, bf16), **{name: shape + (True,) for name, shape in saved.items()}},
        {**{"v_" + name: pltpu.VMEM(*shape) for name, shape in saved.items()},
         "s_sem": pltpu.SemaphoreType.DMA((len(order),)),
         "g1": pltpu.VMEM(x.shape, bf16),
         "xhat0": pltpu.VMEM((n, channels), bf16), "xhat1": pltpu.VMEM((n, channels), bf16),
         "inv0": pltpu.VMEM((n, LANES), f32), "inv1": pltpu.VMEM((n, LANES), f32),
         "pre0": pltpu.VMEM((n, hidden), bf16), "pre1": pltpu.VMEM((n, hidden), bf16),
         "branch0": pltpu.VMEM((n, channels), bf16), "branch1": pltpu.VMEM((n, channels), bf16),
         "normed": pltpu.VMEM((n, channels), bf16), "hid": pltpu.VMEM((n, 256), bf16), "acc": pltpu.VMEM((n, channels), f32),
         "pad": pad_shape(rows, cols, channels), "conv": pltpu.VMEM((rows, cols, channels), f32),
         **weight_scratch(2, channels, hidden), **small_scratch(small)},
        12,
    )


def pair_grads(sel, xs, parts):
    rows, cols, channels = xs[0].shape
    n, hidden = rows * cols, parts[0].hid0.shape[1]
    bf16, f32 = jnp.bfloat16, jnp.float32
    shapes = factor_shapes(n, channels, hidden)
    order = list(shapes) + ["x1"]

    def body(r):
        @pl.when(r.sel[2] == 1)
        def _():
            def copy_out(k):
                return pltpu.make_async_copy(r.grads.at[k], getattr(r, GRADS[k]), r.o_sem.at[k])

            copies = {}
            for k in (1, 0):
                for name in FACTORS + (("x1",) if k else ()):
                    full = name + str(k) if name != "x1" else name
                    for i in range(2):
                        copies[full, i] = pltpu.make_async_copy(
                            getattr(r, "i%d_%s" % (i, full)), getattr(r, "v_" + full).at[i], r.s_sem.at[i, order.index(full)]
                        )
                        copies[full, i].start()
            first = r.sel[3] == 0
            for k in (1, 0):
                gb, nm, hid, gp = (getattr(r, "v_%s%d" % (name, k)) for name in FACTORS[:4])
                keep, send = r.grads.at[2 * k], r.grads.at[2 * k + 1]
                for name in FACTORS + (("x1",) if k else ()):
                    for i in range(2):
                        copies[name + str(k) if name != "x1" else name, i].wait()
                gb_t = gb[...].reshape(2 * n, channels).T
                nm_t = nm[...].reshape(2 * n, channels).T
                for j in range(hidden // 256):
                    cut = slice(j * 256, (j + 1) * 256)
                    t_out = jnp.dot(gb_t, hid[:, :, cut].reshape(2 * n, 256), preferred_element_type=f32)
                    t_in = jnp.dot(nm_t, gp[:, :, cut].reshape(2 * n, 256), preferred_element_type=f32)
                    keep[:, cut] = jnp.where(first, t_in, t_out).astype(bf16)
                    send[:, cut] = jnp.where(first, t_out, t_in).astype(bf16)
                copy_out(2 * k).start()
                copy_out(2 * k + 1).start()
                out = getattr(r, "small%d" % k)
                for i in range(2):
                    x = r.v_x1.at[i] if k else getattr(r, "x_%d" % i)
                    gconv, sums = getattr(r, "v_gconv%d" % k).at[i], getattr(r, "v_sums%d" % k).at[i]
                    target = out if i == 0 else r.tk
                    conv_back_body(gconv, x, None, None, sums, None, target, r.pad, r.sum, r.wide, None)
                out[...] += r.tk[...]
            for k in range(4):
                copy_out(k).wait()

    ins = {"sel": (sel, "s")}
    for i in range(2):
        ins["x_%d" % i] = (xs[i], "v")
        ins.update({"i%d_%s" % (i, name): (getattr(parts[i], name), "h") for name in order})
    grad = ((channels, hidden), bf16)
    small_out = ((SMALL_ROWS, channels), f32)
    scratch = {"v_" + name: pltpu.VMEM((2,) + shape, dtype) for name, (shape, dtype) in shapes.items()}
    return named_call(
        "pair_grads", body, ins,
        {**{name: grad + (True,) for name in GRADS}, "small0": small_out, "small1": small_out},
        {**scratch, "grads": pltpu.VMEM((4, channels, hidden), bf16), "o_sem": pltpu.SemaphoreType.DMA((4,)), "v_x1": pltpu.VMEM((2,) + xs[0].shape, bf16), "s_sem": pltpu.SemaphoreType.DMA((2, len(order))),
         "pad": pad_shape(rows, cols, channels), "sum": pltpu.VMEM((cols // 8, TAPS, 8, LANES), f32),
         "wide": pltpu.VMEM(xs[0].shape, f32), "tk": pltpu.VMEM((SMALL_ROWS, channels), f32)},
        10,
    )


def pair_back(sel, g, x, first, kept, small, weights, before=None, after=()):
    rows, cols, channels = g.shape
    n, hidden = rows * cols, weights[0].shape[1]
    bf16, f32 = jnp.bfloat16, jnp.float32

    def body(r):
        def copy_old(k):
            return copy_chosen(r.sel[2], (getattr(r, "a_" + GRADS[k]), getattr(r, "p_" + GRADS[k])), r.olds.at[k], r.o_sem.at[k])

        def copy_out(k, source):
            return pltpu.make_async_copy(source, getattr(r, GRADS[k]), r.s_sem.at[k])

        @pl.when(r.sel[2] == 0)
        def _():
            core = r.sel[3] == 0
            high, waits = start_weights(r, 1, 1, True), {}
            if before is not None:
                waits = {k: copy_old(k) for k in (2, 3)}
            low = start_weights(r, 0, 0, True)
            if before is not None:
                waits.update({k: copy_old(k) for k in (0, 1)})
            choose_small(r)
            s0, s1 = r.small.at[0], r.small.at[1]

            def old(k):
                def both():
                    waits[2 * k]()
                    waits[2 * k + 1]()
                    return r.olds.at[2 * k], r.olds.at[2 * k + 1]

                return both if waits else None

            mlp_back_body(core, r.g, r.branch1, r.pre1, r.xhat1, r.inv1, s1, *high, r.w_in.at[1], r.w_out.at[1],
                          r.grads.at[2], r.grads.at[3], r.sums8, r.gconv, *back_temps(r), before=old(1))
            copy_out(2, r.grads.at[2]).start()
            copy_out(3, r.grads.at[3]).start()
            conv_back_body(r.gconv, r.x1, r.g, s1, r.sums8, r.g1, r.small1, r.pad, r.sum, r.wide, r.map)
            mlp_back_body(core, r.g1, r.branch0, r.pre0, r.xhat0, r.inv0, s0, *low, r.w_in.at[0], r.w_out.at[0],
                          r.grads.at[0], r.grads.at[1], r.sums8, r.gconv, *back_temps(r), before=old(0))
            copy_out(0, r.grads.at[0]).start()
            copy_out(1, r.grads.at[1]).start()
            conv_back_body(r.gconv, r.x, None, None, r.sums8, None, r.small0, r.pad, r.sum, r.wide, None)
            if before is not None:
                r.small0[...] += r.a_small0[...]
                r.small1[...] += r.a_small1[...]
                r.packed[...] = jnp.concatenate([r.small0[...], r.small1[...]], axis=0).T.astype(bf16)
            for k in range(4):
                copy_out(k, r.grads.at[k]).wait()

        if before is not None:

            @pl.when(r.sel[2] == 1)
            def _():
                waits = [copy_old(k) for k in range(4)]
                r.packed[...] = jnp.concatenate([r.p_small0[...], r.p_small1[...]], axis=0).T.astype(bf16)
                for k, wait in enumerate(waits):
                    wait()
                    copy_out(k, r.olds.at[k]).start()
                for k in range(4):
                    copy_out(k, r.olds.at[k]).wait()

    ins = {"sel": (sel, "s"), "g": (g, "v"), "x": (x, "v"), "x1": (kept.x1, "v"),
           "branch1": (kept.branch1, "v"), "pre1": (kept.pre1, "v"), "xhat1": (kept.xhat1, "v"), "inv1": (kept.inv1, "v"),
           "branch0": (kept.branch0, "v"), "pre0": (kept.pre0, "v"), "xhat0": (first[0], "v"), "inv0": (first[2], "v"),
           **small_ins(small), **weight_ins(weights)}
    grad = ((channels, hidden), bf16)
    small_out = ((SMALL_ROWS, channels), f32)
    outs = {name: grad + (True,) for name in GRADS}
    scratch = {"grads": pltpu.VMEM((4, channels, hidden), bf16), "s_sem": pltpu.SemaphoreType.DMA((4,)), "g1": pltpu.VMEM(g.shape, bf16), "sums8": pltpu.VMEM((8, channels), f32), "gconv": pltpu.VMEM((n, channels), f32),
               "pad": pad_shape(rows, cols, channels), "sum": pltpu.VMEM((cols // 8, TAPS, 8, LANES), f32),
               "wide": pltpu.VMEM(x.shape, f32), "map": pltpu.VMEM(x.shape, f32),
               **back_scratch(n, channels), **weight_scratch(2, channels, hidden), **small_scratch(small)}
    if before is None:
        outs.update({"small0": small_out, "small1": small_out})
    else:
        for prefix, part in zip("ap", before):
            ins.update({prefix + "_" + name: (getattr(part, name), "h") for name in GRADS})
            ins.update({prefix + "_" + name: (getattr(part, name), "v") for name in ("small0", "small1")})
        outs["packed"] = ((channels, 2 * SMALL_ROWS), bf16)
        scratch.update({"small0": pltpu.VMEM(*small_out), "small1": pltpu.VMEM(*small_out),
                        "olds": pltpu.VMEM((4, channels, hidden), bf16), "o_sem": pltpu.SemaphoreType.DMA((4,))})
    ins.update({"after%d" % k: (v, "a") for k, v in enumerate(after)})
    return named_call("pair_back", body, ins, outs, scratch, 9)


def add(a, b):
    return a.astype(jnp.float32) + b.astype(jnp.float32)


def side_kernel(sel_ref, keep_ref, got_ref, *refs):
    *small_ref, across_ref, mine_ref = refs
    side = sel_ref[0]
    levels, _, _, hidden = keep_ref.shape
    for level in range(levels):
        for out_ref, which in ((across_ref, 1 - side), (mine_ref, side)):
            out_ref[level, :, :hidden] = add(keep_ref[level, which], got_ref[level, which]).astype(jnp.bfloat16)
            if small_ref:
                out_ref[level, :, hidden:] = small_ref[0][level, which]


def to_side(side, *arrays):
    arrays = [v.reshape(4, 2, v.shape[0] // 8, v.shape[1]) for v in arrays]
    width = sum(v.shape[3] for v in arrays[1:])
    out = ((4, arrays[0].shape[2], width), jnp.bfloat16)
    return small_call(side_kernel, "to_side", (out, out), side, *arrays)


def depth_kernel(sel_ref, mine_ref, got_ref, *out_refs):
    for k, out_ref in enumerate(out_refs):
        out_ref[...] = add(mine_ref[sel_ref[k]], got_ref[sel_ref[k]]).astype(jnp.bfloat16)


def to_depths(levels, mine, got, after=()):
    return small_call(depth_kernel, "to_depths", ((mine.shape[1:], jnp.bfloat16),) * 4, levels, mine, got, after=after)


def split_kernel(sel_ref, keep_ref, got_ref, *out_refs):
    for k, out_ref in enumerate(out_refs):
        for side in range(2):
            out_ref[side] = add(keep_ref[sel_ref[k], side], got_ref[sel_ref[k], side]).astype(jnp.bfloat16)


def split_depths(levels, keep, got, after=()):
    keep, got = (v.reshape(4, 2, v.shape[0] // 8, v.shape[1]) for v in (keep, got))
    outs = ((keep.shape[1:], jnp.bfloat16),) * 4
    return small_call(split_kernel, "split_depths", outs, levels, keep, got, after=after)


def join_kernel(sel_ref, a_ref, b_ref, c_ref, d_ref, across_ref, mine_ref):
    side = sel_ref[0]
    for out_ref, which in ((across_ref, 1 - side), (mine_ref, side)):
        out_ref[...] = (add(a_ref[which], b_ref[which]) + add(c_ref[which], d_ref[which])).astype(out_ref.dtype)


def join_depths(side, parts):
    shape = parts[0].shape[1:]
    return small_call(join_kernel, "join_depths", ((shape, jnp.bfloat16), (shape, jnp.float32)), side, *parts)


def core_kernel(sel_ref, *refs):
    *parts, own_ref, send_ref = refs
    hidden = parts[-1].shape[1]
    a, b, c, d, e, f = parts
    low, high = add(a[...], b[...]) + add(c[...], d[...]), add(e[...], f[...])
    first = sel_ref[0] == 0
    small = low[:, hidden:]
    turned = pltpu.roll(small, SMALL_ROWS, 1)
    low = low[:, :hidden]
    own_ref[:, :hidden] = jnp.where(first, low, high)
    own_ref[:, hidden:] = jnp.where(first, small, turned)
    send_ref[:, :hidden] = jnp.where(first, high, low).astype(jnp.bfloat16)
    send_ref[:, hidden:] = jnp.where(first, turned, small).astype(jnp.bfloat16)


def to_core(core, parts):
    shape = (parts[-1].shape[0], parts[-1].shape[1] + 2 * SMALL_ROWS)
    return small_call(core_kernel, "to_core", ((shape, jnp.float32), (shape, jnp.bfloat16)), core, *parts)


def final_kernel(sel_ref, own_ref, got_ref, k_ref, gain_ref, in_ref, out_ref, scale_ref, pad_ref):
    share, hidden = own_ref.shape[0], in_ref.shape[2]
    taps = k_ref.shape[2]
    first = sel_ref[0] == 0
    own, got = own_ref[:, :hidden], got_ref[:, :hidden].astype(jnp.float32)
    in_ref[0] = jnp.where(first, own, got)
    out_ref[0] = jnp.where(first, got, own)
    small = add(own_ref[:, hidden:], got_ref[:, hidden:])
    k_ref[0] = small[:, :taps]
    pad_ref[0:share, :] = small
    turned = pad_ref[...].T
    gain_ref[...] = turned[taps : taps + 1, :share]
    scale_ref[...] = turned[taps + 1 : taps + 2, :share]


def final(core, own, got, taps):
    share, hidden = own.shape[0], own.shape[1] - 2 * SMALL_ROWS
    outs = (
        ((1, share, taps), jnp.float32),
        ((1, share), jnp.float32),
        ((1, share, hidden), jnp.float32),
        ((1, share, hidden), jnp.float32),
        ((1, share), jnp.float32),
    )
    t_kernel, t_gain, t_in, t_out, t_scale = small_call(
        final_kernel, "final", outs, core, own, got, scratch=[pltpu.VMEM((LANES, 2 * SMALL_ROWS), jnp.float32)]
    )
    return t_kernel.transpose(0, 2, 1), t_gain, t_in, t_out.transpose(0, 2, 1), t_scale


BF16 = jnp.bfloat16
F32 = jnp.float32


def one_image(x, g, small, sels, w_ins, w_outs, first, passing):
    blocks = small.shape[0]
    rows, cols, channels = x.shape
    which = jnp.stack([sel[0] for sel in sels])
    xs, xhats, invs, pres, branches = forward(which, x, first[1], small, w_ins, w_outs)
    xs, xhats, invs = (x,) + tuple(xs), first[:1] + tuple(xhats), first[2:] + tuple(invs)
    smalls = [None] * blocks
    for s in reversed(range(blocks)):
        keep, send, sums8, gconv = mlp_back(
            sels[s], g.reshape(rows * cols, channels), branches[s], pres[s], xhats[s], invs[s],
            small[s, TAPS : TAPS + 1], small[s, TAPS + 1 : TAPS + 2], w_ins, w_outs, passing.before("mlp", s),
        )
        passing.done(s, keep, send)
        *g_next, smalls[s] = conv_back(
            gconv, xs[s], g, small[s, :TAPS], sums8, s > 0, passing.before("conv", s)
        )
        g = g_next[0] if g_next else None
    return smalls


def finish(t_kernel, t_gain, t_scale, t_in, t_out):
    return t_kernel[None], t_gain[None], t_in[None], t_out[None], t_scale[None]


def any_mesh(images, cotangent, kernels, norm_gains, w_in, w_out, scales):
    segments = lax.axis_size("segment")
    rank = lax.axis_index("segment")
    count = images.shape[0] // segments
    taps = kernels.shape[1]
    small = lax.all_gather(parameters(kernels, norm_gains, scales), "segment")
    all_in = lax.all_gather(w_in[0], "segment")
    all_out = lax.all_gather(w_out[0], "segment")
    sels = [jnp.array([s, 0], jnp.int32) for s in range(segments)]
    pieces = [[None] * 3 for _ in range(segments)]

    class Sums:
        def before(self, part, s):
            return ()

        def done(self, s, keep, send):
            self.add(s, 0, keep.astype(F32))
            self.add(s, 1, send.astype(F32))

        def add(self, s, k, value):
            pieces[s][k] = value if pieces[s][k] is None else pieces[s][k] + value

    sums = Sums()
    w_ins = [all_in[s] for s in range(segments)]
    w_outs = [all_out[s] for s in range(segments)]
    for i in range(count):
        x = lax.dynamic_index_in_dim(images, rank * count + i, 0, keepdims=False)
        g = lax.dynamic_index_in_dim(cotangent, rank * count + i, 0, keepdims=False)
        smalls = one_image(x, g, small, sels, w_ins, w_outs, conv_norm(sels[0] * 0, x, [small[0]]), sums)
        for s in range(segments):
            sums.add(s, 2, smalls[s])

    def summed(values, dim):
        mine = lax.psum_scatter(jnp.stack(values), "segment", scatter_dimension=0, tiled=False)
        return lax.psum_scatter(mine, "dp", scatter_dimension=dim, tiled=True)

    t_in = summed([p[0] for p in pieces], 0)
    t_out = summed([p[1] for p in pieces], 0).T
    t_small = summed([p[2] for p in pieces], 1)
    return finish(t_small[:taps], t_small[taps], t_small[taps + 1], t_in, t_out)


def partners(flip, extent=(4, 2, 2, 2)):
    pairs = []
    for index in range(32):
        z, y, x, c = index >> 3, (index >> 2) & 1, (index >> 1) & 1, index & 1
        other = ((z ^ flip[0]) << 3) | ((y ^ flip[1]) << 2) | ((x ^ flip[2]) << 1) | (c ^ flip[3])
        pairs.append((index, other))
    return pairs


def swap(value, z=0, y=0, x=0, c=0):
    return lax.ppermute(value, ("dp", "segment"), partners((z, y, x, c)))


def along_x(value, to_last):
    pairs = [(i, j) for i, j in partners((0, 0, 1, 0)) if (i >> 1) & 1 == (0 if to_last else 1)]
    return lax.ppermute(value, ("dp", "segment"), pairs)


def this_mesh(images, cotangent, kernels, norm_gains, w_in, w_out, scales):
    rank = lax.axis_index("segment")
    core = rank % 2
    chip = rank // 2
    depth = lax.axis_index("dp") // 2
    side = lax.axis_index("dp") % 2
    own_small = parameters(kernels, norm_gains, scales)
    near_small = swap(own_small, c=1)
    near_in, near_out = swap(w_in[0], c=1), swap(w_out[0], c=1)
    small = (own_small, near_small)
    weights = (w_in[0], near_in, w_out[0], near_out)
    zero = jnp.zeros_like(chip)
    sel = jnp.stack([core, 1 - core, chip, core, zero]).astype(jnp.int32)
    sel_first = jnp.stack([core, 1 - core, chip, core, chip]).astype(jnp.int32)
    sel_conv = (jnp.stack([core, zero]).astype(jnp.int32), jnp.stack([core, chip]).astype(jnp.int32))
    cores = core[None].astype(jnp.int32)
    sides = side[None].astype(jnp.int32)
    levels = jnp.stack([depth, depth ^ 1, depth ^ 2, depth ^ 3]).astype(jnp.int32)

    maps = [lax.dynamic_index_in_dim(images, 2 * core + i, 0, keepdims=False) for i in range(2)]
    ends = [lax.dynamic_index_in_dim(cotangent, 2 * core + i, 0, keepdims=False) for i in range(2)]
    firsts, kept = [], []
    for x, chosen in zip(maps, sel_conv):
        firsts.append(conv_norm(chosen, x, small, tuple(k.inv1 for k in kept)))
        kept.append(pair_forward(sel_first if kept else sel, x, firsts[-1], small, weights))
    passed = [along_x(k.y, True) for k in kept]
    parts, starts = [], []
    for x, g in zip(passed, ends):
        parts.append(pair_map(sel, x, g, small, weights))
        starts.append(along_x(parts[-1].g0, False))
    totals = pair_grads(sel, passed, parts)
    grads = pair_back(sel, starts[0], maps[0], firsts[0], kept[0], small, weights)
    grads = pair_back(sel, starts[1], maps[1], firsts[1], kept[1], small, weights, (grads, totals))
    core0, core1 = swap(grads.send0, c=1), swap(grads.send1, c=1)

    def along_y(*pairs):
        across, mine = to_side(sides, *pairs)
        return mine, swap(across, y=1)

    def along_z(mine, got):
        own, *others = to_depths(levels, mine, got)
        return [own] + [swap(v, z=flip) for v, flip in zip(others, (1, 2, 3))]

    low = along_y(grads.keep0, core0, grads.packed)
    own, *others = split_depths(levels, grads.keep1, core1, low[:1])
    parts = [own] + [swap(v, z=flip) for v, flip in zip(others, (1, 2, 3))]
    across, mine = join_depths(sides, parts)
    high = [mine, swap(across, y=1)]
    low = along_z(*low)
    own, send = to_core(cores, low + high)
    return final(cores, own, swap(send, c=1), kernels.shape[1])


def solution(mesh):
    in_specs = (
        P("dp", None, None, None),
        P("dp", None, None, None),
        P("segment", None, None),
        P("segment", None),
        P("segment", None, None),
        P("segment", None, None),
        P("segment", None),
    )
    out_specs = (
        P("segment", None, "dp"),
        P("segment", "dp"),
        P("segment", "dp", None),
        P("segment", None, "dp"),
        P("segment", "dp"),
    )
    fits = dict(mesh.shape) == {"dp": 8, "segment": 4}

    def whole(images, *rest):
        local = this_mesh if fits and images.shape[0] == 32 else any_mesh
        return jax.shard_map(local, mesh=mesh, in_specs=in_specs, out_specs=out_specs, check_vma=False)(images, *rest)

    return whole
```

```python
import functools
import types
import jax
import jax.numpy as jnp
from jax import lax
from jax.sharding import PartitionSpec as P
from jax.experimental import pallas as pl
from jax.experimental.pallas import tpu as pltpu

EPS = 1e-06
GELU_C = 0.7978845608028654
GELU_A = 0.044715
LANES = 128
def estimate(microseconds):
    return pl.CostEstimate(flops=int(microseconds * 1.1e9), bytes_accessed=int(microseconds * 3.6e6), transcendentals=0)


LIMIT = 40


def vmem(mebibytes):
    return pltpu.CompilerParams(vmem_limit_bytes=mebibytes * 1024 * 1024)


def zero_borders(pad_ref):
    tiles, rows, width, _ = pad_ref.shape
    for c in range(tiles):
        pad_ref[c, :, 0:8] = jnp.zeros((rows, 8, LANES), jnp.float32)
        pad_ref[c, :, width - 8 :] = jnp.zeros((rows, 8, LANES), jnp.float32)


def conv_norm_body(x_ref, small_ref, xhat_ref, normed_ref, inv_ref, pad_ref, conv_ref):
    rows, cols, channels = x_ref.shape
    tiles = channels // LANES
    for c in range(tiles):
        pad_ref[c, :, 8 : cols + 8] = x_ref[:, :, c * LANES : (c + 1) * LANES].astype(jnp.float32)

    def tile(c, carry):
        lanes = pl.ds(pl.multiple_of(c * LANES, LANES), LANES)

        def strip(w, carry):
            base = pl.multiple_of(w * 8, 8)
            window = pad_ref.at[c, :, pl.ds(base, 24), :]
            acc = [None] * rows
            for q in range(7):
                col = [window[h, 5 + q : 13 + q, :] for h in range(rows)]
                for r in range(7):
                    weight = small_ref[r * 7 + q : r * 7 + q + 1, lanes]
                    for h in range(max(0, 3 - r), min(rows, rows + 3 - r)):
                        term = weight * col[h + r - 3]
                        acc[h] = term if acc[h] is None else acc[h] + term
            for h in range(rows):
                conv_ref[h, pl.ds(base, 8), lanes] = acc[h]
            return carry

        return lax.fori_loop(0, cols // 8, strip, carry)

    lax.fori_loop(0, tiles, tile, 0)

    def norm(h, carry):
        value = conv_ref[pl.ds(h * 2, 2)].reshape(2 * cols, channels)
        mean = jnp.mean(value, axis=1, keepdims=True)
        center = value - mean
        inv = lax.rsqrt(jnp.mean(center * center, axis=1, keepdims=True) + EPS)
        xhat = center * inv
        at = pl.ds(pl.multiple_of(h * 2 * cols, 2 * cols), 2 * cols)
        xhat_ref[at, :] = xhat.astype(jnp.bfloat16)
        normed_ref[at, :] = (xhat * small_ref[TAPS : TAPS + 1, :]).astype(jnp.bfloat16)
        inv_ref[at, :] = jnp.broadcast_to(inv, (2 * cols, LANES))
        return carry

    lax.fori_loop(0, rows // 2, norm, 0, unroll=True)


def pad_shape(rows, cols, channels):
    return pltpu.VMEM((channels // LANES, rows, cols + 16, LANES), jnp.float32)


def in_hbm(arrays):
    return [pltpu.with_memory_space_constraint(a, pltpu.HBM) for a in arrays]


def parameters_kernel(k_ref, gain_ref, scale_ref, out_ref, taps_ref, rows_ref, sems):
    copies = [
        pltpu.make_async_copy(source, target, sems.at[i])
        for i, (source, target) in enumerate(((k_ref, taps_ref), (gain_ref, rows_ref.at[0]), (scale_ref, rows_ref.at[1])))
    ]
    for copy in copies:
        copy.start()
    taps = taps_ref.shape[0]
    out_ref[taps + 2 :, :] = jnp.zeros((out_ref.shape[0] - taps - 2, out_ref.shape[1]), jnp.float32)
    for copy in copies:
        copy.wait()
    for t in range(taps):
        out_ref[t : t + 1, :] = taps_ref[t]
    out_ref[taps : taps + 1, :] = rows_ref[0]
    out_ref[taps + 1 : taps + 2, :] = rows_ref[1]


def parameters(kernels, norm_gains, scales):
    taps, channels = kernels.shape[1:]
    return pl.pallas_call(
        parameters_kernel,
        in_specs=[pl.BlockSpec(memory_space=pl.ANY)] * 3,
        out_shape=jax.ShapeDtypeStruct((56, channels), jnp.float32),
        scratch_shapes=[
            pltpu.VMEM((taps, 1, channels), jnp.float32),
            pltpu.VMEM((2, 1, channels), jnp.float32),
            pltpu.SemaphoreType.DMA((3,)),
        ],
        compiler_params=vmem(LIMIT),
        name="parameters",
        cost_estimate=estimate(0.5),
    )(*in_hbm([kernels.transpose(1, 0, 2), norm_gains, scales]))


def choose_small(r):
    first = r.sel[0] == 0
    own, near = r.own_small[...], r.near_small[...]
    r.small[0] = jnp.where(first, own, near)
    r.small[1] = jnp.where(first, near, own)


def conv_norm_kernel(choices, sel_ref, x_ref, *rest):
    smalls, rest = rest[:choices], rest[choices:]
    xhat_ref, normed_ref, inv_ref, pad_ref, conv_ref, small_ref = rest[-6:]
    active = sel_ref[1] == 0

    @pl.when(active)
    def _():
        zero_borders(pad_ref)
        small_ref[...] = smalls[0][...]
        for k in range(1, choices):

            @pl.when(sel_ref[0] == k)
            def _():
                small_ref[...] = smalls[k][...]

        conv_norm_body(x_ref, small_ref, xhat_ref, normed_ref, inv_ref, pad_ref, conv_ref)


def conv_norm(sel, x, smalls, after=()):
    rows, cols, channels = x.shape
    n = rows * cols
    return pl.pallas_call(
        functools.partial(conv_norm_kernel, len(smalls)),
        in_specs=[pl.BlockSpec(memory_space=pltpu.SMEM)]
        + [pl.BlockSpec(memory_space=pltpu.VMEM)] * (1 + len(smalls))
        + [pl.BlockSpec(memory_space=pl.ANY)] * len(after),
        out_shape=(
            jax.ShapeDtypeStruct((n, channels), jnp.bfloat16),
            jax.ShapeDtypeStruct((n, channels), jnp.bfloat16),
            jax.ShapeDtypeStruct((n, LANES), jnp.float32),
        ),
        scratch_shapes=[
            pad_shape(rows, cols, channels),
            pltpu.VMEM((rows, cols, channels), jnp.float32),
            pltpu.VMEM(smalls[0].shape, jnp.float32),
        ],
        compiler_params=vmem(LIMIT),
        name="conv_norm",
        cost_estimate=estimate(2.0),
    )(sel, x, *smalls, *after)


def copy_chosen(which, sources, target, sem):
    for m, source in enumerate(sources):

        @pl.when(which == m)
        def _():
            pltpu.make_async_copy(source, target, sem).start()

    return lambda: pltpu.make_async_copy(sources[0], target, sem).wait()


def forward_kernel(choices, blocks, sel_ref, x_ref, normed0_ref, small_ref, *rest):
    w_ins, w_outs, rest = rest[:choices], rest[choices : 2 * choices], rest[2 * choices :]
    xs = [x_ref] + list(rest[: blocks - 1])
    xhats, invs, rest = rest[blocks - 1 : 2 * blocks - 2], rest[2 * blocks - 2 : 3 * blocks - 3], rest[3 * blocks - 3 :]
    pres, branches, rest = rest[:blocks], rest[blocks : 2 * blocks], rest[2 * blocks :]
    normed_ref, hid_ref, acc_ref, pad_ref, conv_ref, w_in_ref, w_out_ref, sems = rest
    rows, cols, channels = x_ref.shape
    n = rows * cols
    hidden = w_in_ref.shape[2]
    waits = []
    for s in range(blocks):
        waits.append((
            copy_chosen(sel_ref[s], w_ins, w_in_ref.at[s], sems.at[0, s]),
            copy_chosen(sel_ref[s], w_outs, w_out_ref.at[s], sems.at[1, s]),
        ))
    zero_borders(pad_ref)
    step, sub = 256, 2 * cols
    for s in range(blocks):
        normed = normed0_ref if s == 0 else normed_ref
        waits[s][0]()
        for j in range(hidden // step):
            cut = slice(j * step, (j + 1) * step)
            pre = jnp.dot(normed[...], w_in_ref[s, :, cut], preferred_element_type=jnp.float32)
            for i in range(n // sub):
                p = pre[i * sub : (i + 1) * sub]
                half = 0.5 * p
                hid_ref[i * sub : (i + 1) * sub, :] = (half + half * tanh_arg(p)).astype(jnp.bfloat16)
                pres[s][i * sub : (i + 1) * sub, cut] = p.astype(jnp.bfloat16)
            if j == 0:
                waits[s][1]()
            part = jnp.dot(hid_ref[...], w_out_ref[s, cut, :], preferred_element_type=jnp.float32)
            if j == 0:
                acc_ref[...] = part
            else:
                acc_ref[...] += part
        scale = small_ref[s, TAPS + 1 : TAPS + 2, :]
        for i in range(n // sub):
            branch = acc_ref[i * sub : (i + 1) * sub, :]
            branches[s][i * sub : (i + 1) * sub, :] = branch.astype(jnp.bfloat16)
            if s < blocks - 1:
                x_old = xs[s][2 * i : 2 * i + 2].astype(jnp.float32).reshape(sub, channels)
                xs[s + 1][2 * i : 2 * i + 2] = (x_old + scale * branch).astype(jnp.bfloat16).reshape(2, cols, channels)
        if s < blocks - 1:
            conv_norm_body(xs[s + 1], small_ref.at[s + 1], xhats[s], normed_ref, invs[s], pad_ref, conv_ref)


def forward(sel, x, normed0, small, w_ins, w_outs):
    blocks = small.shape[0]
    rows, cols, channels = x.shape
    n = rows * cols
    hidden = w_ins[0].shape[1]
    out = pl.pallas_call(
        functools.partial(forward_kernel, len(w_ins), blocks),
        in_specs=[pl.BlockSpec(memory_space=pltpu.SMEM)]
        + [pl.BlockSpec(memory_space=pltpu.VMEM)] * 3
        + [pl.BlockSpec(memory_space=pl.ANY)] * (2 * len(w_ins)),
        out_shape=(jax.ShapeDtypeStruct((rows, cols, channels), jnp.bfloat16),) * (blocks - 1)
        + (jax.ShapeDtypeStruct((n, channels), jnp.bfloat16),) * (blocks - 1)
        + (jax.ShapeDtypeStruct((n, LANES), jnp.float32),) * (blocks - 1)
        + (jax.ShapeDtypeStruct((n, hidden), jnp.bfloat16),) * blocks
        + (jax.ShapeDtypeStruct((n, channels), jnp.bfloat16),) * blocks,
        scratch_shapes=[
            pltpu.VMEM((n, channels), jnp.bfloat16),
            pltpu.VMEM((n, 256), jnp.bfloat16),
            pltpu.VMEM((n, channels), jnp.float32),
            pad_shape(rows, cols, channels),
            pltpu.VMEM((rows, cols, channels), jnp.float32),
            pltpu.VMEM((blocks, channels, hidden), jnp.bfloat16),
            pltpu.VMEM((blocks, hidden, channels), jnp.bfloat16),
            pltpu.SemaphoreType.DMA((2, blocks)),
        ],
        compiler_params=vmem(LIMIT),
        name="forward",
        cost_estimate=estimate(15),
    )(sel, x, normed0, small, *in_hbm(w_ins), *in_hbm(w_outs))
    k = blocks - 1
    return out[:k], out[k : 2 * k], out[2 * k : 3 * k], out[3 * k : 3 * k + blocks], out[3 * k + blocks :]


def tanh_arg(x):
    return jnp.tanh(x * (GELU_C + (GELU_C * GELU_A) * (x * x)))


def load_weights(sel_ref, w_ins, w_outs, w_in_ref, w_out_ref, sems):
    for m in range(len(w_ins)):

        @pl.when(sel_ref[0] == m)
        def _():
            pltpu.make_async_copy(w_ins[m], w_in_ref, sems.at[0]).start()
            pltpu.make_async_copy(w_outs[m], w_out_ref, sems.at[1]).start()

    return (
        pltpu.make_async_copy(w_ins[0], w_in_ref, sems.at[0]).wait,
        pltpu.make_async_copy(w_outs[0], w_out_ref, sems.at[1]).wait,
    )


def specs(sel, arrays, choices, after=0):
    return (
        [pl.BlockSpec(memory_space=pltpu.SMEM)]
        + [pl.BlockSpec(memory_space=pltpu.VMEM)] * arrays
        + [pl.BlockSpec(memory_space=pl.ANY)] * (2 * choices + after)
    )


def mlp_back_kernel(choices, after, sel_ref, g_ref, branch_ref, pre_ref, xhat_ref, inv_ref, gain_ref, scale_ref, *rest):
    w_ins, w_outs = rest[:choices], rest[choices : 2 * choices]
    (keep_ref, send_ref, small_ref, gconv_ref,
     gb_ref, nm_ref, hid_ref, gp_ref, acc_ref, w_in_ref, w_out_ref, sems) = rest[2 * choices + after :]
    wait_in, wait_out = load_weights(sel_ref, w_ins, w_outs, w_in_ref, w_out_ref, sems)
    first = sel_ref[1] == 0
    n, channels = g_ref.shape
    hidden = w_in_ref.shape[1]
    step = 256
    sub = 32
    scale_sum = jnp.zeros((8, channels), jnp.float32)
    for i in range(n // sub):
        at = slice(i * sub, (i + 1) * sub)
        g = g_ref[at, :].astype(jnp.float32)
        scale_sum = scale_sum + jnp.sum((g * branch_ref[at, :].astype(jnp.float32)).reshape(sub // 8, 8, channels), axis=0)
        gb_ref[at, :] = (g * scale_ref[...]).astype(jnp.bfloat16)
        nm_ref[at, :] = (xhat_ref[at, :].astype(jnp.float32) * gain_ref[...]).astype(jnp.bfloat16)
    gb_t = gb_ref[...].T
    nm_t = nm_ref[...].T
    wait_in()
    wait_out()
    for j in range(hidden // step):
        cut = slice(j * step, (j + 1) * step)
        gh = lax.dot_general(gb_ref[...], w_out_ref[cut, :], (((1,), (1,)), ((), ())), preferred_element_type=jnp.float32)
        for i in range(n // sub):
            at = slice(i * sub, (i + 1) * sub)
            p = pre_ref[at, cut].astype(jnp.float32)
            sq = p * p
            t = jnp.tanh(p * (GELU_C + (GELU_C * GELU_A) * sq))
            cdf = 0.5 + 0.5 * t
            hid_ref[at, :] = (p * cdf).astype(jnp.bfloat16)
            slope = cdf + (0.5 * p) * (1.0 - t * t) * (GELU_C + (3.0 * GELU_C * GELU_A) * sq)
            gp_ref[at, :] = (gh[at, :] * slope).astype(jnp.bfloat16)
        t_out = jnp.dot(gb_t, hid_ref[...], preferred_element_type=jnp.float32)
        t_in = jnp.dot(nm_t, gp_ref[...], preferred_element_type=jnp.float32)
        keep_ref[:, cut] = jnp.where(first, t_in, t_out).astype(jnp.bfloat16)
        send_ref[:, cut] = jnp.where(first, t_out, t_in).astype(jnp.bfloat16)
        part = lax.dot_general(gp_ref[...], w_in_ref[:, cut], (((1,), (1,)), ((), ())), preferred_element_type=jnp.float32)
        if j == 0:
            acc_ref[...] = part
        else:
            acc_ref[...] += part
    gain_sum = jnp.zeros((8, channels), jnp.float32)
    for i in range(n // sub):
        at = slice(i * sub, (i + 1) * sub)
        gn = acc_ref[at, :]
        xhat = xhat_ref[at, :].astype(jnp.float32)
        gain_sum = gain_sum + jnp.sum((gn * xhat).reshape(sub // 8, 8, channels), axis=0)
        gx = gn * gain_ref[...]
        m1 = jnp.mean(gx, axis=1, keepdims=True)
        m2 = jnp.mean(gx * xhat, axis=1, keepdims=True)
        inv = inv_ref[at, 0:1]
        gconv_ref[at, :] = inv * (gx - m1 - xhat * m2)
    small_ref[0:1, :] = jnp.sum(gain_sum, axis=0, keepdims=True)
    small_ref[1:2, :] = jnp.sum(scale_sum, axis=0, keepdims=True)
    small_ref[2:8, :] = jnp.zeros((6, channels), jnp.float32)


def mlp_back(sel, g, branch, pre, xhat, inv, gain, scale, w_ins, w_outs, after=()):
    n, channels = g.shape
    hidden = w_ins[0].shape[1]
    return pl.pallas_call(
        functools.partial(mlp_back_kernel, len(w_ins), len(after)),
        in_specs=specs(sel, 7, len(w_ins), len(after)),
        out_shape=(
            jax.ShapeDtypeStruct((channels, hidden), jnp.bfloat16),
            jax.ShapeDtypeStruct((channels, hidden), jnp.bfloat16),
            jax.ShapeDtypeStruct((8, channels), jnp.float32),
            jax.ShapeDtypeStruct((n, channels), jnp.float32),
        ),
        scratch_shapes=[
            pltpu.VMEM((n, channels), jnp.bfloat16),
            pltpu.VMEM((n, channels), jnp.bfloat16),
            pltpu.VMEM((n, 256), jnp.bfloat16),
            pltpu.VMEM((n, 256), jnp.bfloat16),
            pltpu.VMEM((n, channels), jnp.float32),
            pltpu.VMEM((channels, hidden), jnp.bfloat16),
            pltpu.VMEM((hidden, channels), jnp.bfloat16),
            pltpu.SemaphoreType.DMA((2,)),
        ],
        compiler_params=vmem(LIMIT),
        name="mlp_back",
        cost_estimate=estimate(2.5),
    )(sel, g, branch, pre, xhat, inv, gain, scale, *in_hbm(w_ins), *in_hbm(w_outs), *after)


SMALL_ROWS = 64
TAPS = 49


def conv_back_kernel(need_map, after, gconv_ref, x_ref, g_ref, k_ref, small_ref, *rest):
    *out_ref, tk_ref, pad_ref, sum_ref, wide_ref, map_ref = rest[after:]
    conv_back_body(gconv_ref, x_ref, g_ref, k_ref, small_ref, out_ref[0] if need_map else None, tk_ref,
                   pad_ref, sum_ref, wide_ref, map_ref)


def conv_back(gconv, x, g, kernel, small, need_map=True, after=()):
    rows, cols, channels = x.shape
    out = (jax.ShapeDtypeStruct((SMALL_ROWS, channels), jnp.float32),)
    if need_map:
        out = (jax.ShapeDtypeStruct((rows, cols, channels), jnp.bfloat16),) + out
    return pl.pallas_call(
        functools.partial(conv_back_kernel, need_map, len(after)),
        in_specs=[pl.BlockSpec(memory_space=pltpu.VMEM)] * 5 + [pl.BlockSpec(memory_space=pl.ANY)] * len(after),
        out_shape=out,
        scratch_shapes=[
            pad_shape(rows, cols, channels),
            pltpu.VMEM((cols // 8, TAPS, 8, LANES), jnp.float32),
            pltpu.VMEM((rows, cols, channels), jnp.float32),
            pltpu.VMEM((rows, cols, channels), jnp.float32),
        ],
        compiler_params=vmem(LIMIT),
        name="conv_back",
        cost_estimate=estimate(3.4 if need_map else 1.6),
    )(gconv, x, g, kernel, small, *after)


def small_call(kernel, name, outs, *args, scratch=(), after=()):
    used = len(args)

    def body(*refs):
        kernel(*refs[:used], *refs[used + len(after) :])

    return pl.pallas_call(
        body,
        in_specs=[pl.BlockSpec(memory_space=pltpu.SMEM)]
        + [pl.BlockSpec(memory_space=pltpu.VMEM)] * (used - 1)
        + [pl.BlockSpec(memory_space=pl.ANY)] * len(after),
        out_shape=tuple(out_struct(*o) for o in outs),
        scratch_shapes=list(scratch),
        compiler_params=vmem(LIMIT),
        name=name,
        cost_estimate=estimate(0.7),
    )(*args, *after)


def conv_back_body(gconv_ref, x_ref, g_ref, small_ref, sums8_ref, out_ref, tk_ref, pad_ref, sum_ref, wide_ref, map_ref):
    rows, cols, channels = x_ref.shape
    tiles = channels // LANES
    zero_borders(pad_ref)
    for c in range(tiles):
        pad_ref[c, :, 8 : cols + 8] = gconv_ref[:, c * LANES : (c + 1) * LANES].reshape(rows, cols, LANES)

    for h in range(rows):
        wide_ref[h] = x_ref[h].astype(jnp.float32)

    def tile(c, carry):
        lanes = pl.ds(pl.multiple_of(c * LANES, LANES), LANES)

        def strip(w, carry):
            base = pl.multiple_of(w * 8, 8)
            window = pad_ref.at[c, :, pl.ds(base, 24), :]
            xs = [wide_ref[h, pl.ds(base, 8), lanes] for h in range(rows)]
            acc = [None] * rows
            for q in range(7):
                col = [window[h, 11 - q : 19 - q, :] for h in range(rows)]
                for r in range(7):
                    tap = r * 7 + q
                    if out_ref is not None:
                        weight = small_ref[tap : tap + 1, lanes]
                    total = None
                    for h in range(max(0, r - 3), min(rows, rows + r - 3)):
                        shifted = col[h + 3 - r]
                        term = xs[h] * shifted
                        total = term if total is None else total + term
                        if out_ref is not None:
                            moved = weight * shifted
                            acc[h] = moved if acc[h] is None else acc[h] + moved
                    sum_ref[w, tap] = total
            if out_ref is not None:
                for h in range(rows):
                    map_ref[h, pl.ds(base, 8), lanes] = acc[h]
            return carry

        lax.fori_loop(0, cols // 8, strip, 0)
        tk_ref[0:TAPS, lanes] = jnp.sum(sum_ref[0] + sum_ref[1], axis=1)
        return carry

    lax.fori_loop(0, tiles, tile, 0)
    if out_ref is not None:
        for h in range(rows):
            out_ref[h] = (g_ref[h].astype(jnp.float32) + map_ref[h]).astype(jnp.bfloat16)
    tk_ref[TAPS : TAPS + 2, :] = sums8_ref[0:2, :]
    tk_ref[TAPS + 2 :, :] = jnp.zeros((SMALL_ROWS - TAPS - 2, channels), jnp.float32)


def conv_map_body(gconv_ref, g_ref, small_ref, out_ref, pad_ref, map_ref):
    rows, cols, channels = g_ref.shape
    tiles = channels // LANES
    zero_borders(pad_ref)
    for c in range(tiles):
        pad_ref[c, :, 8 : cols + 8] = gconv_ref[:, c * LANES : (c + 1) * LANES].reshape(rows, cols, LANES)

    def tile(c, carry):
        lanes = pl.ds(pl.multiple_of(c * LANES, LANES), LANES)

        def strip(w, carry):
            base = pl.multiple_of(w * 8, 8)
            window = pad_ref.at[c, :, pl.ds(base, 24), :]
            acc = [None] * rows
            for q in range(7):
                col = [window[h, 11 - q : 19 - q, :] for h in range(rows)]
                for r in range(7):
                    weight = small_ref[r * 7 + q : r * 7 + q + 1, lanes]
                    for h in range(max(0, r - 3), min(rows, rows + r - 3)):
                        term = weight * col[h + 3 - r]
                        acc[h] = term if acc[h] is None else acc[h] + term
            for h in range(rows):
                map_ref[h, pl.ds(base, 8), lanes] = acc[h]
            return carry

        return lax.fori_loop(0, cols // 8, strip, carry)

    lax.fori_loop(0, tiles, tile, 0)
    for h in range(rows):
        out_ref[h] = (g_ref[h].astype(jnp.float32) + map_ref[h]).astype(jnp.bfloat16)


def mlp_back_map_body(g_ref, branch_ref, pre_ref, xhat_ref, inv_ref, small_ref, w_in_ref, w_out_ref,
                      sums8_ref, gconv_ref, gb_ref, nm_ref, hid_ref, gp_ref, acc_ref, ready):
    rows, cols, channels = g_ref.shape
    n = rows * cols
    hidden = w_in_ref.shape[1]
    step = 256
    sub = 2 * cols
    gain = small_ref[TAPS : TAPS + 1, :]
    scale = small_ref[TAPS + 1 : TAPS + 2, :]
    scale_sum = jnp.zeros((8, channels), jnp.float32)
    for i in range(n // sub):
        at = slice(i * sub, (i + 1) * sub)
        g = g_ref[2 * i : 2 * i + 2].astype(jnp.float32).reshape(sub, channels)
        scale_sum = scale_sum + jnp.sum((g * branch_ref[at, :].astype(jnp.float32)).reshape(sub // 8, 8, channels), axis=0)
        gb_ref[at, :] = (g * scale).astype(jnp.bfloat16)
        nm_ref[at, :] = (xhat_ref[at, :].astype(jnp.float32) * gain).astype(jnp.bfloat16)
    ready("gb", "nm")
    for j in range(hidden // step):
        cut = slice(j * step, (j + 1) * step)
        gh = lax.dot_general(gb_ref[...], w_out_ref[cut, :], (((1,), (1,)), ((), ())), preferred_element_type=jnp.float32)
        for i in range(n // sub):
            at = slice(i * sub, (i + 1) * sub)
            p = pre_ref[at, cut].astype(jnp.float32)
            sq = p * p
            t = jnp.tanh(p * (GELU_C + (GELU_C * GELU_A) * sq))
            cdf = 0.5 + 0.5 * t
            hid_ref[at, cut] = (p * cdf).astype(jnp.bfloat16)
            slope = cdf + (0.5 * p) * (1.0 - t * t) * (GELU_C + (3.0 * GELU_C * GELU_A) * sq)
            gp_ref[at, cut] = (gh[at, :] * slope).astype(jnp.bfloat16)
        part = lax.dot_general(gp_ref[:, cut], w_in_ref[:, cut], (((1,), (1,)), ((), ())), preferred_element_type=jnp.float32)
        if j == 0:
            acc_ref[...] = part
        else:
            acc_ref[...] += part
    ready("hid", "gp")
    gain_sum = jnp.zeros((8, channels), jnp.float32)
    for i in range(n // sub):
        at = slice(i * sub, (i + 1) * sub)
        gn = acc_ref[at, :]
        xhat = xhat_ref[at, :].astype(jnp.float32)
        gain_sum = gain_sum + jnp.sum((gn * xhat).reshape(sub // 8, 8, channels), axis=0)
        gx = gn * gain
        m1 = jnp.mean(gx, axis=1, keepdims=True)
        m2 = jnp.mean(gx * xhat, axis=1, keepdims=True)
        gconv_ref[at, :] = inv_ref[at, 0:1] * (gx - m1 - xhat * m2)
    sums8_ref[0:1, :] = jnp.sum(gain_sum, axis=0, keepdims=True)
    sums8_ref[1:2, :] = jnp.sum(scale_sum, axis=0, keepdims=True)
    sums8_ref[2:8, :] = jnp.zeros((6, channels), jnp.float32)
    ready("gconv", "sums")


def mlp_back_body(first, g_ref, branch_ref, pre_ref, xhat_ref, inv_ref, small_ref, wait_in, wait_out, w_in_ref, w_out_ref,
                  keep_ref, send_ref, sums8_ref, gconv_ref, gb_ref, nm_ref, hid_ref, gp_ref, acc_ref, before=None):
    rows, cols, channels = g_ref.shape
    n = rows * cols
    hidden = w_in_ref.shape[1]
    step = 256
    sub = 2 * cols
    gain = small_ref[TAPS : TAPS + 1, :]
    scale = small_ref[TAPS + 1 : TAPS + 2, :]
    scale_sum = jnp.zeros((8, channels), jnp.float32)
    for i in range(n // sub):
        at = slice(i * sub, (i + 1) * sub)
        g = g_ref[2 * i : 2 * i + 2].astype(jnp.float32).reshape(sub, channels)
        scale_sum = scale_sum + jnp.sum((g * branch_ref[at, :].astype(jnp.float32)).reshape(sub // 8, 8, channels), axis=0)
        gb_ref[at, :] = (g * scale).astype(jnp.bfloat16)
        nm_ref[at, :] = (xhat_ref[at, :].astype(jnp.float32) * gain).astype(jnp.bfloat16)
    gb_t = gb_ref[...].T
    nm_t = nm_ref[...].T
    wait_out()
    for j in range(hidden // step):
        cut = slice(j * step, (j + 1) * step)
        gh = lax.dot_general(gb_ref[...], w_out_ref[cut, :], (((1,), (1,)), ((), ())), preferred_element_type=jnp.float32)
        for i in range(n // sub):
            at = slice(i * sub, (i + 1) * sub)
            p = pre_ref[at, cut].astype(jnp.float32)
            sq = p * p
            t = jnp.tanh(p * (GELU_C + (GELU_C * GELU_A) * sq))
            cdf = 0.5 + 0.5 * t
            hid_ref[at, :] = (p * cdf).astype(jnp.bfloat16)
            slope = cdf + (0.5 * p) * (1.0 - t * t) * (GELU_C + (3.0 * GELU_C * GELU_A) * sq)
            gp_ref[at, :] = (gh[at, :] * slope).astype(jnp.bfloat16)
        t_out = jnp.dot(gb_t, hid_ref[...], preferred_element_type=jnp.float32)
        t_in = jnp.dot(nm_t, gp_ref[...], preferred_element_type=jnp.float32)
        t_keep = jnp.where(first, t_in, t_out)
        t_send = jnp.where(first, t_out, t_in)
        if before is not None:
            if j == 0:
                old_keep, old_send = before()
            t_keep = t_keep + old_keep[:, cut].astype(jnp.float32)
            t_send = t_send + old_send[:, cut].astype(jnp.float32)
        keep_ref[:, cut] = t_keep.astype(jnp.bfloat16)
        send_ref[:, cut] = t_send.astype(jnp.bfloat16)
        if j == 0:
            wait_in()
        part = lax.dot_general(gp_ref[...], w_in_ref[:, cut], (((1,), (1,)), ((), ())), preferred_element_type=jnp.float32)
        if j == 0:
            acc_ref[...] = part
        else:
            acc_ref[...] += part
    gain_sum = jnp.zeros((8, channels), jnp.float32)
    for i in range(n // sub):
        at = slice(i * sub, (i + 1) * sub)
        gn = acc_ref[at, :]
        xhat = xhat_ref[at, :].astype(jnp.float32)
        gain_sum = gain_sum + jnp.sum((gn * xhat).reshape(sub // 8, 8, channels), axis=0)
        gx = gn * gain
        m1 = jnp.mean(gx, axis=1, keepdims=True)
        m2 = jnp.mean(gx * xhat, axis=1, keepdims=True)
        gconv_ref[at, :] = inv_ref[at, 0:1] * (gx - m1 - xhat * m2)
    sums8_ref[0:1, :] = jnp.sum(gain_sum, axis=0, keepdims=True)
    sums8_ref[1:2, :] = jnp.sum(scale_sum, axis=0, keepdims=True)
    sums8_ref[2:8, :] = jnp.zeros((6, channels), jnp.float32)


def out_struct(shape, dtype, by_hand=False):
    return pltpu.HBM(shape, dtype) if by_hand else jax.ShapeDtypeStruct(shape, dtype)


def named_call(name, body, ins, outs, scratch, cost):
    names = list(ins) + list(outs) + list(scratch)
    spaces = {"v": pltpu.VMEM, "s": pltpu.SMEM, "a": pl.ANY, "h": pl.ANY}

    def kernel(*refs):
        body(types.SimpleNamespace(**dict(zip(names, refs))))

    args = [pltpu.with_memory_space_constraint(a, pltpu.HBM) if kind == "h" else a for a, kind in ins.values()]
    result = pl.pallas_call(
        kernel,
        in_specs=[pl.BlockSpec(memory_space=spaces[kind]) for _, kind in ins.values()],
        out_specs=tuple(pl.BlockSpec(memory_space=pl.ANY if len(o) > 2 else pltpu.VMEM) for o in outs.values()),
        out_shape=tuple(out_struct(*o) for o in outs.values()),
        scratch_shapes=list(scratch.values()),
        compiler_params=vmem(LIMIT),
        name=name,
        cost_estimate=estimate(cost),
    )(*args)
    return types.SimpleNamespace(**dict(zip(outs, result)))


def mlp_body(normed_ref, wait_in, wait_out, w_in_ref, w_out_ref, pre_ref, hid_ref, acc_ref):
    n = normed_ref.shape[0]
    hidden = w_in_ref.shape[1]
    step, sub = 256, 32
    wait_in()
    for j in range(hidden // step):
        cut = slice(j * step, (j + 1) * step)
        pre = jnp.dot(normed_ref[...], w_in_ref[:, cut], preferred_element_type=jnp.float32)
        for i in range(n // sub):
            p = pre[i * sub : (i + 1) * sub]
            half = 0.5 * p
            hid_ref[i * sub : (i + 1) * sub, :] = (half + half * tanh_arg(p)).astype(jnp.bfloat16)
            pre_ref[i * sub : (i + 1) * sub, cut] = p.astype(jnp.bfloat16)
        if j == 0:
            wait_out()
        part = jnp.dot(hid_ref[...], w_out_ref[cut, :], preferred_element_type=jnp.float32)
        if j == 0:
            acc_ref[...] = part
        else:
            acc_ref[...] += part


def residual_body(x_ref, small_ref, acc_ref, branch_ref, y_ref):
    rows, cols, channels = x_ref.shape
    scale = small_ref[TAPS + 1 : TAPS + 2, :]
    sub = 2 * cols
    for i in range(rows // 2):
        branch = acc_ref[i * sub : (i + 1) * sub, :]
        branch_ref[i * sub : (i + 1) * sub, :] = branch.astype(jnp.bfloat16)
        if y_ref is not None:
            old = x_ref[2 * i : 2 * i + 2].astype(jnp.float32).reshape(sub, channels)
            y_ref[2 * i : 2 * i + 2] = (old + scale * branch).astype(jnp.bfloat16).reshape(2, cols, channels)


def small_ins(pair):
    return {"own_small": (pair[0], "v"), "near_small": (pair[1], "v")}


def small_scratch(pair):
    return {"small": pltpu.VMEM((2,) + pair[0].shape, jnp.float32)}


def weight_ins(pair):
    return {k: (v, "h") for k, v in zip(("own_in", "near_in", "own_out", "near_out"), pair)}


def weight_scratch(blocks, channels, hidden):
    return {
        "w_in": pltpu.VMEM((blocks, channels, hidden), jnp.bfloat16),
        "w_out": pltpu.VMEM((blocks, hidden, channels), jnp.bfloat16),
        "w_sem": pltpu.SemaphoreType.DMA((2, blocks)),
    }


def start_weights(r, slot, block, out_first=False):
    def start(k, own, near, target):
        return copy_chosen(r.sel[block], (own, near), target.at[slot], r.w_sem.at[k, slot])

    if out_first:
        wait_out = start(1, r.own_out, r.near_out, r.w_out)
        return start(0, r.own_in, r.near_in, r.w_in), wait_out
    return start(0, r.own_in, r.near_in, r.w_in), start(1, r.own_out, r.near_out, r.w_out)


def pair_forward(sel, x, first, small, weights):
    rows, cols, channels = x.shape
    n, hidden = rows * cols, weights[0].shape[1]
    bf16, f32 = jnp.bfloat16, jnp.float32

    def body(r):
        @pl.when(r.sel[4] == 0)
        def _():
            low, high = start_weights(r, 0, 0), start_weights(r, 1, 1)
            choose_small(r)
            zero_borders(r.pad)
            mlp_body(r.normed0, *low, r.w_in.at[0], r.w_out.at[0], r.pre0, r.hid, r.acc)
            residual_body(r.x, r.small.at[0], r.acc, r.branch0, r.x1)
            conv_norm_body(r.x1, r.small.at[1], r.xhat1, r.normed, r.inv1, r.pad, r.conv)
            mlp_body(r.normed, *high, r.w_in.at[1], r.w_out.at[1], r.pre1, r.hid, r.acc)
            residual_body(r.x1, r.small.at[1], r.acc, r.branch1, r.y)

    return named_call(
        "pair_forward", body,
        {"sel": (sel, "s"), "x": (x, "v"), "normed0": (first[1], "v"), **small_ins(small), **weight_ins(weights)},
        {"y": (x.shape, bf16), "x1": (x.shape, bf16), "xhat1": ((n, channels), bf16), "inv1": ((n, LANES), f32),
         "pre0": ((n, hidden), bf16), "pre1": ((n, hidden), bf16),
         "branch0": ((n, channels), bf16), "branch1": ((n, channels), bf16)},
        {"normed": pltpu.VMEM((n, channels), bf16), "hid": pltpu.VMEM((n, 256), bf16), "acc": pltpu.VMEM((n, channels), f32),
         "pad": pad_shape(rows, cols, channels), "conv": pltpu.VMEM((rows, cols, channels), f32),
         **weight_scratch(2, channels, hidden), **small_scratch(small)},
        7.5,
    )


def back_scratch(n, channels):
    bf16, f32 = jnp.bfloat16, jnp.float32
    return {"gb": pltpu.VMEM((n, channels), bf16), "nm": pltpu.VMEM((n, channels), bf16),
            "hid": pltpu.VMEM((n, 256), bf16), "gp": pltpu.VMEM((n, 256), bf16), "acc": pltpu.VMEM((n, channels), f32)}


def back_temps(r):
    return r.gb, r.nm, r.hid, r.gp, r.acc


GRADS = ("keep0", "send0", "keep1", "send1")
FACTORS = ("gb", "nm", "hid", "gp", "gconv", "sums")


def factor_shapes(n, channels, hidden):
    bf16, f32 = jnp.bfloat16, jnp.float32
    one = {"gb": ((n, channels), bf16), "nm": ((n, channels), bf16), "hid": ((n, hidden), bf16), "gp": ((n, hidden), bf16),
           "gconv": ((n, channels), f32), "sums": ((8, channels), f32)}
    return {name + str(k): one[name] for k in (0, 1) for name in FACTORS}


def pair_map(sel, x, g, small, weights):
    rows, cols, channels = x.shape
    n, hidden = rows * cols, weights[0].shape[1]
    bf16, f32 = jnp.bfloat16, jnp.float32
    shapes = factor_shapes(n, channels, hidden)
    saved = {**shapes, "x1": (x.shape, bf16)}
    order = list(saved)

    def body(r):
        @pl.when(r.sel[2] == 1)
        def _():
            def copy_out(name):
                return pltpu.make_async_copy(getattr(r, "v_" + name), getattr(r, name), r.s_sem.at[order.index(name)])

            low, high = start_weights(r, 0, 0), start_weights(r, 1, 1)
            choose_small(r)
            zero_borders(r.pad)
            s0, s1 = r.small.at[0], r.small.at[1]
            conv_norm_body(r.x, s0, r.xhat0, r.normed, r.inv0, r.pad, r.conv)
            mlp_body(r.normed, *low, r.w_in.at[0], r.w_out.at[0], r.pre0, r.hid, r.acc)
            residual_body(r.x, s0, r.acc, r.branch0, r.v_x1)
            copy_out("x1").start()
            conv_norm_body(r.v_x1, s1, r.xhat1, r.normed, r.inv1, r.pad, r.conv)
            mlp_body(r.normed, *high, r.w_in.at[1], r.w_out.at[1], r.pre1, r.hid, r.acc)
            residual_body(r.v_x1, s1, r.acc, r.branch1, None)

            def ready(k):
                def start(*names):
                    for name in names:
                        copy_out(name + str(k)).start()

                return start

            mlp_back_map_body(r.g, r.branch1, r.pre1, r.xhat1, r.inv1, s1, r.w_in.at[1], r.w_out.at[1],
                              r.v_sums1, r.v_gconv1, r.v_gb1, r.v_nm1, r.v_hid1, r.v_gp1, r.acc, ready(1))
            conv_map_body(r.v_gconv1, r.g, s1, r.g1, r.pad, r.conv)
            mlp_back_map_body(r.g1, r.branch0, r.pre0, r.xhat0, r.inv0, s0, r.w_in.at[0], r.w_out.at[0],
                              r.v_sums0, r.v_gconv0, r.v_gb0, r.v_nm0, r.v_hid0, r.v_gp0, r.acc, ready(0))
            conv_map_body(r.v_gconv0, r.g1, s0, r.g0, r.pad, r.conv)
            for name in order:
                copy_out(name).wait()

    return named_call(
        "pair_map", body,
        {"sel": (sel, "s"), "x": (x, "v"), "g": (g, "v"), **small_ins(small), **weight_ins(weights)},
        {"g0": (x.shape, bf16), **{name: shape + (True,) for name, shape in saved.items()}},
        {**{"v_" + name: pltpu.VMEM(*shape) for name, shape in saved.items()},
         "s_sem": pltpu.SemaphoreType.DMA((len(order),)),
         "g1": pltpu.VMEM(x.shape, bf16),
         "xhat0": pltpu.VMEM((n, channels), bf16), "xhat1": pltpu.VMEM((n, channels), bf16),
         "inv0": pltpu.VMEM((n, LANES), f32), "inv1": pltpu.VMEM((n, LANES), f32),
         "pre0": pltpu.VMEM((n, hidden), bf16), "pre1": pltpu.VMEM((n, hidden), bf16),
         "branch0": pltpu.VMEM((n, channels), bf16), "branch1": pltpu.VMEM((n, channels), bf16),
         "normed": pltpu.VMEM((n, channels), bf16), "hid": pltpu.VMEM((n, 256), bf16), "acc": pltpu.VMEM((n, channels), f32),
         "pad": pad_shape(rows, cols, channels), "conv": pltpu.VMEM((rows, cols, channels), f32),
         **weight_scratch(2, channels, hidden), **small_scratch(small)},
        12,
    )


def pair_grads(sel, xs, parts):
    rows, cols, channels = xs[0].shape
    n, hidden = rows * cols, parts[0].hid0.shape[1]
    bf16, f32 = jnp.bfloat16, jnp.float32
    shapes = factor_shapes(n, channels, hidden)
    order = list(shapes) + ["x1"]

    def body(r):
        @pl.when(r.sel[2] == 1)
        def _():
            def copy_out(k):
                return pltpu.make_async_copy(r.grads.at[k], getattr(r, GRADS[k]), r.o_sem.at[k])

            copies = {}
            for k in (1, 0):
                for name in FACTORS + (("x1",) if k else ()):
                    full = name + str(k) if name != "x1" else name
                    for i in range(2):
                        copies[full, i] = pltpu.make_async_copy(
                            getattr(r, "i%d_%s" % (i, full)), getattr(r, "v_" + full).at[i], r.s_sem.at[i, order.index(full)]
                        )
                        copies[full, i].start()
            first = r.sel[3] == 0
            for k in (1, 0):
                gb, nm, hid, gp = (getattr(r, "v_%s%d" % (name, k)) for name in FACTORS[:4])
                keep, send = r.grads.at[2 * k], r.grads.at[2 * k + 1]
                for name in FACTORS + (("x1",) if k else ()):
                    for i in range(2):
                        copies[name + str(k) if name != "x1" else name, i].wait()
                gb_t = gb[...].reshape(2 * n, channels).T
                nm_t = nm[...].reshape(2 * n, channels).T
                for j in range(hidden // 256):
                    cut = slice(j * 256, (j + 1) * 256)
                    t_out = jnp.dot(gb_t, hid[:, :, cut].reshape(2 * n, 256), preferred_element_type=f32)
                    t_in = jnp.dot(nm_t, gp[:, :, cut].reshape(2 * n, 256), preferred_element_type=f32)
                    keep[:, cut] = jnp.where(first, t_in, t_out).astype(bf16)
                    send[:, cut] = jnp.where(first, t_out, t_in).astype(bf16)
                copy_out(2 * k).start()
                copy_out(2 * k + 1).start()
                out = getattr(r, "small%d" % k)
                for i in range(2):
                    x = r.v_x1.at[i] if k else getattr(r, "x_%d" % i)
                    gconv, sums = getattr(r, "v_gconv%d" % k).at[i], getattr(r, "v_sums%d" % k).at[i]
                    target = out if i == 0 else r.tk
                    conv_back_body(gconv, x, None, None, sums, None, target, r.pad, r.sum, r.wide, None)
                out[...] += r.tk[...]
            for k in range(4):
                copy_out(k).wait()

    ins = {"sel": (sel, "s")}
    for i in range(2):
        ins["x_%d" % i] = (xs[i], "v")
        ins.update({"i%d_%s" % (i, name): (getattr(parts[i], name), "h") for name in order})
    grad = ((channels, hidden), bf16)
    small_out = ((SMALL_ROWS, channels), f32)
    scratch = {"v_" + name: pltpu.VMEM((2,) + shape, dtype) for name, (shape, dtype) in shapes.items()}
    return named_call(
        "pair_grads", body, ins,
        {**{name: grad + (True,) for name in GRADS}, "small0": small_out, "small1": small_out},
        {**scratch, "grads": pltpu.VMEM((4, channels, hidden), bf16), "o_sem": pltpu.SemaphoreType.DMA((4,)), "v_x1": pltpu.VMEM((2,) + xs[0].shape, bf16), "s_sem": pltpu.SemaphoreType.DMA((2, len(order))),
         "pad": pad_shape(rows, cols, channels), "sum": pltpu.VMEM((cols // 8, TAPS, 8, LANES), f32),
         "wide": pltpu.VMEM(xs[0].shape, f32), "tk": pltpu.VMEM((SMALL_ROWS, channels), f32)},
        10,
    )


def pair_back(sel, g, x, first, kept, small, weights, before=None, after=()):
    rows, cols, channels = g.shape
    n, hidden = rows * cols, weights[0].shape[1]
    bf16, f32 = jnp.bfloat16, jnp.float32

    def body(r):
        def copy_old(k):
            return copy_chosen(r.sel[2], (getattr(r, "a_" + GRADS[k]), getattr(r, "p_" + GRADS[k])), r.olds.at[k], r.o_sem.at[k])

        def copy_out(k, source):
            return pltpu.make_async_copy(source, getattr(r, GRADS[k]), r.s_sem.at[k])

        @pl.when(r.sel[2] == 0)
        def _():
            core = r.sel[3] == 0
            high, waits = start_weights(r, 1, 1, True), {}
            if before is not None:
                waits = {k: copy_old(k) for k in (2, 3)}
            low = start_weights(r, 0, 0, True)
            if before is not None:
                waits.update({k: copy_old(k) for k in (0, 1)})
            choose_small(r)
            s0, s1 = r.small.at[0], r.small.at[1]

            def old(k):
                def both():
                    waits[2 * k]()
                    waits[2 * k + 1]()
                    return r.olds.at[2 * k], r.olds.at[2 * k + 1]

                return both if waits else None

            mlp_back_body(core, r.g, r.branch1, r.pre1, r.xhat1, r.inv1, s1, *high, r.w_in.at[1], r.w_out.at[1],
                          r.grads.at[2], r.grads.at[3], r.sums8, r.gconv, *back_temps(r), before=old(1))
            copy_out(2, r.grads.at[2]).start()
            copy_out(3, r.grads.at[3]).start()
            conv_back_body(r.gconv, r.x1, r.g, s1, r.sums8, r.g1, r.small1, r.pad, r.sum, r.wide, r.map)
            mlp_back_body(core, r.g1, r.branch0, r.pre0, r.xhat0, r.inv0, s0, *low, r.w_in.at[0], r.w_out.at[0],
                          r.grads.at[0], r.grads.at[1], r.sums8, r.gconv, *back_temps(r), before=old(0))
            copy_out(0, r.grads.at[0]).start()
            copy_out(1, r.grads.at[1]).start()
            conv_back_body(r.gconv, r.x, None, None, r.sums8, None, r.small0, r.pad, r.sum, r.wide, None)
            if before is not None:
                r.small0[...] += r.a_small0[...]
                r.small1[...] += r.a_small1[...]
                r.packed[...] = jnp.concatenate([r.small0[...], r.small1[...]], axis=0).T.astype(bf16)
            for k in range(4):
                copy_out(k, r.grads.at[k]).wait()

        if before is not None:

            @pl.when(r.sel[2] == 1)
            def _():
                waits = [copy_old(k) for k in range(4)]
                r.packed[...] = jnp.concatenate([r.p_small0[...], r.p_small1[...]], axis=0).T.astype(bf16)
                for k, wait in enumerate(waits):
                    wait()
                    copy_out(k, r.olds.at[k]).start()
                for k in range(4):
                    copy_out(k, r.olds.at[k]).wait()

    ins = {"sel": (sel, "s"), "g": (g, "v"), "x": (x, "v"), "x1": (kept.x1, "v"),
           "branch1": (kept.branch1, "v"), "pre1": (kept.pre1, "v"), "xhat1": (kept.xhat1, "v"), "inv1": (kept.inv1, "v"),
           "branch0": (kept.branch0, "v"), "pre0": (kept.pre0, "v"), "xhat0": (first[0], "v"), "inv0": (first[2], "v"),
           **small_ins(small), **weight_ins(weights)}
    grad = ((channels, hidden), bf16)
    small_out = ((SMALL_ROWS, channels), f32)
    outs = {name: grad + (True,) for name in GRADS}
    scratch = {"grads": pltpu.VMEM((4, channels, hidden), bf16), "s_sem": pltpu.SemaphoreType.DMA((4,)), "g1": pltpu.VMEM(g.shape, bf16), "sums8": pltpu.VMEM((8, channels), f32), "gconv": pltpu.VMEM((n, channels), f32),
               "pad": pad_shape(rows, cols, channels), "sum": pltpu.VMEM((cols // 8, TAPS, 8, LANES), f32),
               "wide": pltpu.VMEM(x.shape, f32), "map": pltpu.VMEM(x.shape, f32),
               **back_scratch(n, channels), **weight_scratch(2, channels, hidden), **small_scratch(small)}
    if before is None:
        outs.update({"small0": small_out, "small1": small_out})
    else:
        for prefix, part in zip("ap", before):
            ins.update({prefix + "_" + name: (getattr(part, name), "h") for name in GRADS})
            ins.update({prefix + "_" + name: (getattr(part, name), "v") for name in ("small0", "small1")})
        outs["packed"] = ((channels, 2 * SMALL_ROWS), bf16)
        scratch.update({"small0": pltpu.VMEM(*small_out), "small1": pltpu.VMEM(*small_out),
                        "olds": pltpu.VMEM((4, channels, hidden), bf16), "o_sem": pltpu.SemaphoreType.DMA((4,))})
    ins.update({"after%d" % k: (v, "a") for k, v in enumerate(after)})
    return named_call("pair_back", body, ins, outs, scratch, 9)


def brought_kernel(source_ref, out_ref, sem):
    copy = pltpu.make_async_copy(source_ref, out_ref, sem)
    copy.start()
    copy.wait()


def brought(value):
    return pl.pallas_call(
        brought_kernel,
        in_specs=[pl.BlockSpec(memory_space=pl.ANY)],
        out_shape=jax.ShapeDtypeStruct(value.shape, value.dtype),
        scratch_shapes=[pltpu.SemaphoreType.DMA(())],
        compiler_params=vmem(LIMIT),
        name="brought",
        cost_estimate=estimate(1.1),
    )(pltpu.with_memory_space_constraint(value, pltpu.HBM))


def add(a, b):
    return a.astype(jnp.float32) + b.astype(jnp.float32)


def side_kernel(sel_ref, keep_ref, got_ref, *refs):
    *small_ref, across_ref, mine_ref = refs
    side = sel_ref[0]
    levels, _, _, hidden = keep_ref.shape
    for level in range(levels):
        for out_ref, which in ((across_ref, 1 - side), (mine_ref, side)):
            out_ref[level, :, :hidden] = add(keep_ref[level, which], got_ref[level, which]).astype(jnp.bfloat16)
            if small_ref:
                out_ref[level, :, hidden:] = small_ref[0][level, which]


def to_side(side, *arrays):
    arrays = [v.reshape(4, 2, v.shape[0] // 8, v.shape[1]) for v in arrays]
    width = sum(v.shape[3] for v in arrays[1:])
    out = ((4, arrays[0].shape[2], width), jnp.bfloat16)
    return small_call(side_kernel, "to_side", (out, out), side, *arrays)


def depth_kernel(sel_ref, mine_ref, got_ref, *out_refs):
    for k, out_ref in enumerate(out_refs):
        out_ref[...] = add(mine_ref[sel_ref[k]], got_ref[sel_ref[k]]).astype(jnp.bfloat16)


def to_depths(levels, mine, got, after=()):
    return small_call(depth_kernel, "to_depths", ((mine.shape[1:], jnp.bfloat16),) * 4, levels, mine, got, after=after)


def split_kernel(sel_ref, keep_ref, got_ref, *out_refs):
    for k, out_ref in enumerate(out_refs):
        for side in range(2):
            out_ref[side] = add(keep_ref[sel_ref[k], side], got_ref[sel_ref[k], side]).astype(jnp.bfloat16)


def split_depths(levels, keep, got, after=()):
    keep, got = (v.reshape(4, 2, v.shape[0] // 8, v.shape[1]) for v in (keep, got))
    outs = ((keep.shape[1:], jnp.bfloat16),) * 4
    return small_call(split_kernel, "split_depths", outs, levels, keep, got, after=after)


def join_kernel(sel_ref, a_ref, b_ref, c_ref, d_ref, across_ref, mine_ref):
    side = sel_ref[0]
    for out_ref, which in ((across_ref, 1 - side), (mine_ref, side)):
        out_ref[...] = (add(a_ref[which], b_ref[which]) + add(c_ref[which], d_ref[which])).astype(out_ref.dtype)


def join_depths(side, parts):
    shape = parts[0].shape[1:]
    return small_call(join_kernel, "join_depths", ((shape, jnp.bfloat16), (shape, jnp.float32)), side, *parts)


def core_kernel(sel_ref, *refs):
    *parts, own_ref, send_ref = refs
    hidden = parts[-1].shape[1]
    a, b, c, d, e, f = parts
    low, high = add(a[...], b[...]) + add(c[...], d[...]), add(e[...], f[...])
    first = sel_ref[0] == 0
    small = low[:, hidden:]
    turned = pltpu.roll(small, SMALL_ROWS, 1)
    low = low[:, :hidden]
    own_ref[:, :hidden] = jnp.where(first, low, high)
    own_ref[:, hidden:] = jnp.where(first, small, turned)
    send_ref[:, :hidden] = jnp.where(first, high, low).astype(jnp.bfloat16)
    send_ref[:, hidden:] = jnp.where(first, turned, small).astype(jnp.bfloat16)


def to_core(core, parts):
    shape = (parts[-1].shape[0], parts[-1].shape[1] + 2 * SMALL_ROWS)
    return small_call(core_kernel, "to_core", ((shape, jnp.float32), (shape, jnp.bfloat16)), core, *parts)


def final_kernel(sel_ref, own_ref, got_ref, k_ref, gain_ref, in_ref, out_ref, scale_ref, pad_ref):
    share, hidden = own_ref.shape[0], in_ref.shape[2]
    taps = k_ref.shape[2]
    first = sel_ref[0] == 0
    own, got = own_ref[:, :hidden], got_ref[:, :hidden].astype(jnp.float32)
    in_ref[0] = jnp.where(first, own, got)
    out_ref[0] = jnp.where(first, got, own)
    small = add(own_ref[:, hidden:], got_ref[:, hidden:])
    k_ref[0] = small[:, :taps]
    pad_ref[0:share, :] = small
    turned = pad_ref[...].T
    gain_ref[...] = turned[taps : taps + 1, :share]
    scale_ref[...] = turned[taps + 1 : taps + 2, :share]


def final(core, own, got, taps):
    share, hidden = own.shape[0], own.shape[1] - 2 * SMALL_ROWS
    outs = (
        ((1, share, taps), jnp.float32),
        ((1, share), jnp.float32),
        ((1, share, hidden), jnp.float32),
        ((1, share, hidden), jnp.float32),
        ((1, share), jnp.float32),
    )
    t_kernel, t_gain, t_in, t_out, t_scale = small_call(
        final_kernel, "final", outs, core, own, got, scratch=[pltpu.VMEM((LANES, 2 * SMALL_ROWS), jnp.float32)]
    )
    return t_kernel.transpose(0, 2, 1), t_gain, t_in, t_out.transpose(0, 2, 1), t_scale


BF16 = jnp.bfloat16
F32 = jnp.float32


def one_image(x, g, small, sels, w_ins, w_outs, first, passing):
    blocks = small.shape[0]
    rows, cols, channels = x.shape
    which = jnp.stack([sel[0] for sel in sels])
    xs, xhats, invs, pres, branches = forward(which, x, first[1], small, w_ins, w_outs)
    xs, xhats, invs = (x,) + tuple(xs), first[:1] + tuple(xhats), first[2:] + tuple(invs)
    smalls = [None] * blocks
    for s in reversed(range(blocks)):
        keep, send, sums8, gconv = mlp_back(
            sels[s], g.reshape(rows * cols, channels), branches[s], pres[s], xhats[s], invs[s],
            small[s, TAPS : TAPS + 1], small[s, TAPS + 1 : TAPS + 2], w_ins, w_outs, passing.before("mlp", s),
        )
        passing.done(s, keep, send)
        *g_next, smalls[s] = conv_back(
            gconv, xs[s], g, small[s, :TAPS], sums8, s > 0, passing.before("conv", s)
        )
        g = g_next[0] if g_next else None
    return smalls


def finish(t_kernel, t_gain, t_scale, t_in, t_out):
    return t_kernel[None], t_gain[None], t_in[None], t_out[None], t_scale[None]


def any_mesh(images, cotangent, kernels, norm_gains, w_in, w_out, scales):
    segments = lax.axis_size("segment")
    rank = lax.axis_index("segment")
    count = images.shape[0] // segments
    taps = kernels.shape[1]
    small = lax.all_gather(parameters(kernels, norm_gains, scales), "segment")
    all_in = lax.all_gather(w_in[0], "segment")
    all_out = lax.all_gather(w_out[0], "segment")
    sels = [jnp.array([s, 0], jnp.int32) for s in range(segments)]
    pieces = [[None] * 3 for _ in range(segments)]

    class Sums:
        def before(self, part, s):
            return ()

        def done(self, s, keep, send):
            self.add(s, 0, keep.astype(F32))
            self.add(s, 1, send.astype(F32))

        def add(self, s, k, value):
            pieces[s][k] = value if pieces[s][k] is None else pieces[s][k] + value

    sums = Sums()
    w_ins = [all_in[s] for s in range(segments)]
    w_outs = [all_out[s] for s in range(segments)]
    for i in range(count):
        x = lax.dynamic_index_in_dim(images, rank * count + i, 0, keepdims=False)
        g = lax.dynamic_index_in_dim(cotangent, rank * count + i, 0, keepdims=False)
        smalls = one_image(x, g, small, sels, w_ins, w_outs, conv_norm(sels[0] * 0, x, [small[0]]), sums)
        for s in range(segments):
            sums.add(s, 2, smalls[s])

    def summed(values, dim):
        mine = lax.psum_scatter(jnp.stack(values), "segment", scatter_dimension=0, tiled=False)
        return lax.psum_scatter(mine, "dp", scatter_dimension=dim, tiled=True)

    t_in = summed([p[0] for p in pieces], 0)
    t_out = summed([p[1] for p in pieces], 0).T
    t_small = summed([p[2] for p in pieces], 1)
    return finish(t_small[:taps], t_small[taps], t_small[taps + 1], t_in, t_out)


def partners(flip, extent=(4, 2, 2, 2)):
    pairs = []
    for index in range(32):
        z, y, x, c = index >> 3, (index >> 2) & 1, (index >> 1) & 1, index & 1
        other = ((z ^ flip[0]) << 3) | ((y ^ flip[1]) << 2) | ((x ^ flip[2]) << 1) | (c ^ flip[3])
        pairs.append((index, other))
    return pairs


def swap(value, z=0, y=0, x=0, c=0):
    return lax.ppermute(value, ("dp", "segment"), partners((z, y, x, c)))


def along_x(value, to_last):
    pairs = [(i, j) for i, j in partners((0, 0, 1, 0)) if (i >> 1) & 1 == (0 if to_last else 1)]
    return lax.ppermute(value, ("dp", "segment"), pairs)


def this_mesh(images, cotangent, kernels, norm_gains, w_in, w_out, scales):
    rank = lax.axis_index("segment")
    core = rank % 2
    chip = rank // 2
    depth = lax.axis_index("dp") // 2
    side = lax.axis_index("dp") % 2
    own_small = parameters(kernels, norm_gains, scales)
    near_small = swap(own_small, c=1)
    near_in, near_out = swap(w_in[0], c=1), swap(w_out[0], c=1)
    small = (own_small, near_small)
    weights = (w_in[0], near_in, w_out[0], near_out)
    zero = jnp.zeros_like(chip)
    sel = jnp.stack([core, 1 - core, chip, core, zero]).astype(jnp.int32)
    sel_first = jnp.stack([core, 1 - core, chip, core, chip]).astype(jnp.int32)
    sel_conv = (jnp.stack([core, zero]).astype(jnp.int32), jnp.stack([core, chip]).astype(jnp.int32))
    cores = core[None].astype(jnp.int32)
    sides = side[None].astype(jnp.int32)
    levels = jnp.stack([depth, depth ^ 1, depth ^ 2, depth ^ 3]).astype(jnp.int32)

    maps = [lax.dynamic_index_in_dim(images, 2 * core + i, 0, keepdims=False) for i in range(2)]
    ends = [lax.dynamic_index_in_dim(cotangent, 2 * core + i, 0, keepdims=False) for i in range(2)]
    firsts, kept = [], []
    for x, chosen in zip(maps, sel_conv):
        firsts.append(conv_norm(chosen, x, small, tuple(k.inv1 for k in kept)))
        kept.append(pair_forward(sel_first if kept else sel, x, firsts[-1], small, weights))
    passed = [along_x(k.y, True) for k in kept]
    parts, starts = [], []
    for x, g in zip(passed, ends):
        parts.append(pair_map(sel, x, g, small, weights))
        starts.append(along_x(parts[-1].g0, False))
    totals = pair_grads(sel, passed, parts)
    grads = pair_back(sel, starts[0], maps[0], firsts[0], kept[0], small, weights)
    grads = pair_back(sel, starts[1], maps[1], firsts[1], kept[1], small, weights, (grads, totals))
    core0, core1 = swap(grads.send0, c=1), swap(grads.send1, c=1)

    def along_y(*pairs):
        across, mine = to_side(sides, *pairs)
        return mine, swap(across, y=1)

    def along_z(mine, got):
        own, *others = to_depths(levels, mine, got)
        return [own] + [swap(v, z=flip) for v, flip in zip(others, (1, 2, 3))]

    low = along_y(brought(grads.keep0), core0, grads.packed)
    own, *others = split_depths(levels, grads.keep1, core1, low[:1])
    parts = [own] + [swap(v, z=flip) for v, flip in zip(others, (1, 2, 3))]
    across, mine = join_depths(sides, parts)
    high = [mine, swap(across, y=1)]
    low = along_z(*low)
    own, send = to_core(cores, low + high)
    return final(cores, own, swap(send, c=1), kernels.shape[1])


def solution(mesh):
    in_specs = (
        P("dp", None, None, None),
        P("dp", None, None, None),
        P("segment", None, None),
        P("segment", None),
        P("segment", None, None),
        P("segment", None, None),
        P("segment", None),
    )
    out_specs = (
        P("segment", None, "dp"),
        P("segment", "dp"),
        P("segment", "dp", None),
        P("segment", None, "dp"),
        P("segment", "dp"),
    )
    fits = dict(mesh.shape) == {"dp": 8, "segment": 4}

    def whole(images, *rest):
        local = this_mesh if fits and images.shape[0] == 32 else any_mesh
        return jax.shard_map(local, mesh=mesh, in_specs=in_specs, out_specs=out_specs, check_vma=False)(images, *rest)

    return whole
```

```python
import functools
import types
import jax
import jax.numpy as jnp
from jax import lax
from jax.sharding import PartitionSpec as P
from jax.experimental import pallas as pl
from jax.experimental.pallas import tpu as pltpu

EPS = 1e-06
GELU_C = 0.7978845608028654
GELU_A = 0.044715
LANES = 128
def estimate(microseconds):
    return pl.CostEstimate(flops=int(microseconds * 1.1e9), bytes_accessed=int(microseconds * 3.6e6), transcendentals=0)


LIMIT = 40


def vmem(mebibytes):
    return pltpu.CompilerParams(vmem_limit_bytes=mebibytes * 1024 * 1024)


def zero_borders(pad_ref):
    tiles, rows, width, _ = pad_ref.shape
    for c in range(tiles):
        pad_ref[c, :, 0:8] = jnp.zeros((rows, 8, LANES), jnp.float32)
        pad_ref[c, :, width - 8 :] = jnp.zeros((rows, 8, LANES), jnp.float32)


def conv_norm_body(x_ref, small_ref, xhat_ref, normed_ref, inv_ref, pad_ref, conv_ref):
    rows, cols, channels = x_ref.shape
    tiles = channels // LANES
    for c in range(tiles):
        pad_ref[c, :, 8 : cols + 8] = x_ref[:, :, c * LANES : (c + 1) * LANES].astype(jnp.float32)

    def tile(c, carry):
        lanes = pl.ds(pl.multiple_of(c * LANES, LANES), LANES)

        def strip(w, carry):
            base = pl.multiple_of(w * 8, 8)
            window = pad_ref.at[c, :, pl.ds(base, 24), :]
            acc = [None] * rows
            for q in range(7):
                col = [window[h, 5 + q : 13 + q, :] for h in range(rows)]
                for r in range(7):
                    weight = small_ref[r * 7 + q : r * 7 + q + 1, lanes]
                    for h in range(max(0, 3 - r), min(rows, rows + 3 - r)):
                        term = weight * col[h + r - 3]
                        acc[h] = term if acc[h] is None else acc[h] + term
            for h in range(rows):
                conv_ref[h, pl.ds(base, 8), lanes] = acc[h]
            return carry

        return lax.fori_loop(0, cols // 8, strip, carry)

    lax.fori_loop(0, tiles, tile, 0)

    def norm(h, carry):
        value = conv_ref[pl.ds(h * 2, 2)].reshape(2 * cols, channels)
        mean = jnp.mean(value, axis=1, keepdims=True)
        center = value - mean
        inv = lax.rsqrt(jnp.mean(center * center, axis=1, keepdims=True) + EPS)
        xhat = center * inv
        at = pl.ds(pl.multiple_of(h * 2 * cols, 2 * cols), 2 * cols)
        xhat_ref[at, :] = xhat.astype(jnp.bfloat16)
        normed_ref[at, :] = (xhat * small_ref[TAPS : TAPS + 1, :]).astype(jnp.bfloat16)
        inv_ref[at, :] = jnp.broadcast_to(inv, (2 * cols, LANES))
        return carry

    lax.fori_loop(0, rows // 2, norm, 0, unroll=True)


def pad_shape(rows, cols, channels):
    return pltpu.VMEM((channels // LANES, rows, cols + 16, LANES), jnp.float32)


def in_hbm(arrays):
    return [pltpu.with_memory_space_constraint(a, pltpu.HBM) for a in arrays]


def parameters_kernel(k_ref, gain_ref, scale_ref, out_ref, taps_ref, rows_ref, sems):
    copies = [
        pltpu.make_async_copy(source, target, sems.at[i])
        for i, (source, target) in enumerate(((k_ref, taps_ref), (gain_ref, rows_ref.at[0]), (scale_ref, rows_ref.at[1])))
    ]
    for copy in copies:
        copy.start()
    taps = taps_ref.shape[0]
    out_ref[taps + 2 :, :] = jnp.zeros((out_ref.shape[0] - taps - 2, out_ref.shape[1]), jnp.float32)
    for copy in copies:
        copy.wait()
    for t in range(taps):
        out_ref[t : t + 1, :] = taps_ref[t]
    out_ref[taps : taps + 1, :] = rows_ref[0]
    out_ref[taps + 1 : taps + 2, :] = rows_ref[1]


def parameters(kernels, norm_gains, scales):
    taps, channels = kernels.shape[1:]
    return pl.pallas_call(
        parameters_kernel,
        in_specs=[pl.BlockSpec(memory_space=pl.ANY)] * 3,
        out_shape=jax.ShapeDtypeStruct((56, channels), jnp.float32),
        scratch_shapes=[
            pltpu.VMEM((taps, 1, channels), jnp.float32),
            pltpu.VMEM((2, 1, channels), jnp.float32),
            pltpu.SemaphoreType.DMA((3,)),
        ],
        compiler_params=vmem(LIMIT),
        name="parameters",
        cost_estimate=estimate(0.5),
    )(*in_hbm([kernels.transpose(1, 0, 2), norm_gains, scales]))


def choose_small(r):
    first = r.sel[0] == 0
    own, near = r.own_small[...], r.near_small[...]
    r.small[0] = jnp.where(first, own, near)
    r.small[1] = jnp.where(first, near, own)


def conv_norm_kernel(choices, sel_ref, x_ref, *rest):
    smalls, rest = rest[:choices], rest[choices:]
    xhat_ref, normed_ref, inv_ref, pad_ref, conv_ref, small_ref = rest[-6:]
    active = sel_ref[1] == 0

    @pl.when(active)
    def _():
        zero_borders(pad_ref)
        small_ref[...] = smalls[0][...]
        for k in range(1, choices):

            @pl.when(sel_ref[0] == k)
            def _():
                small_ref[...] = smalls[k][...]

        conv_norm_body(x_ref, small_ref, xhat_ref, normed_ref, inv_ref, pad_ref, conv_ref)


def conv_norm(sel, x, smalls, after=()):
    rows, cols, channels = x.shape
    n = rows * cols
    return pl.pallas_call(
        functools.partial(conv_norm_kernel, len(smalls)),
        in_specs=[pl.BlockSpec(memory_space=pltpu.SMEM)]
        + [pl.BlockSpec(memory_space=pltpu.VMEM)] * (1 + len(smalls))
        + [pl.BlockSpec(memory_space=pl.ANY)] * len(after),
        out_shape=(
            jax.ShapeDtypeStruct((n, channels), jnp.bfloat16),
            jax.ShapeDtypeStruct((n, channels), jnp.bfloat16),
            jax.ShapeDtypeStruct((n, LANES), jnp.float32),
        ),
        scratch_shapes=[
            pad_shape(rows, cols, channels),
            pltpu.VMEM((rows, cols, channels), jnp.float32),
            pltpu.VMEM(smalls[0].shape, jnp.float32),
        ],
        compiler_params=vmem(LIMIT),
        name="conv_norm",
        cost_estimate=estimate(2.0),
    )(sel, x, *smalls, *after)


def copy_chosen(which, sources, target, sem):
    for m, source in enumerate(sources):

        @pl.when(which == m)
        def _():
            pltpu.make_async_copy(source, target, sem).start()

    return lambda: pltpu.make_async_copy(sources[0], target, sem).wait()


def forward_kernel(choices, blocks, sel_ref, x_ref, normed0_ref, small_ref, *rest):
    w_ins, w_outs, rest = rest[:choices], rest[choices : 2 * choices], rest[2 * choices :]
    xs = [x_ref] + list(rest[: blocks - 1])
    xhats, invs, rest = rest[blocks - 1 : 2 * blocks - 2], rest[2 * blocks - 2 : 3 * blocks - 3], rest[3 * blocks - 3 :]
    pres, branches, rest = rest[:blocks], rest[blocks : 2 * blocks], rest[2 * blocks :]
    normed_ref, hid_ref, acc_ref, pad_ref, conv_ref, w_in_ref, w_out_ref, sems = rest
    rows, cols, channels = x_ref.shape
    n = rows * cols
    hidden = w_in_ref.shape[2]
    waits = []
    for s in range(blocks):
        waits.append((
            copy_chosen(sel_ref[s], w_ins, w_in_ref.at[s], sems.at[0, s]),
            copy_chosen(sel_ref[s], w_outs, w_out_ref.at[s], sems.at[1, s]),
        ))
    zero_borders(pad_ref)
    step, sub = 256, 2 * cols
    for s in range(blocks):
        normed = normed0_ref if s == 0 else normed_ref
        waits[s][0]()
        for j in range(hidden // step):
            cut = slice(j * step, (j + 1) * step)
            pre = jnp.dot(normed[...], w_in_ref[s, :, cut], preferred_element_type=jnp.float32)
            for i in range(n // sub):
                p = pre[i * sub : (i + 1) * sub]
                half = 0.5 * p
                hid_ref[i * sub : (i + 1) * sub, :] = (half + half * tanh_arg(p)).astype(jnp.bfloat16)
                pres[s][i * sub : (i + 1) * sub, cut] = p.astype(jnp.bfloat16)
            if j == 0:
                waits[s][1]()
            part = jnp.dot(hid_ref[...], w_out_ref[s, cut, :], preferred_element_type=jnp.float32)
            if j == 0:
                acc_ref[...] = part
            else:
                acc_ref[...] += part
        scale = small_ref[s, TAPS + 1 : TAPS + 2, :]
        for i in range(n // sub):
            branch = acc_ref[i * sub : (i + 1) * sub, :]
            branches[s][i * sub : (i + 1) * sub, :] = branch.astype(jnp.bfloat16)
            if s < blocks - 1:
                x_old = xs[s][2 * i : 2 * i + 2].astype(jnp.float32).reshape(sub, channels)
                xs[s + 1][2 * i : 2 * i + 2] = (x_old + scale * branch).astype(jnp.bfloat16).reshape(2, cols, channels)
        if s < blocks - 1:
            conv_norm_body(xs[s + 1], small_ref.at[s + 1], xhats[s], normed_ref, invs[s], pad_ref, conv_ref)


def forward(sel, x, normed0, small, w_ins, w_outs):
    blocks = small.shape[0]
    rows, cols, channels = x.shape
    n = rows * cols
    hidden = w_ins[0].shape[1]
    out = pl.pallas_call(
        functools.partial(forward_kernel, len(w_ins), blocks),
        in_specs=[pl.BlockSpec(memory_space=pltpu.SMEM)]
        + [pl.BlockSpec(memory_space=pltpu.VMEM)] * 3
        + [pl.BlockSpec(memory_space=pl.ANY)] * (2 * len(w_ins)),
        out_shape=(jax.ShapeDtypeStruct((rows, cols, channels), jnp.bfloat16),) * (blocks - 1)
        + (jax.ShapeDtypeStruct((n, channels), jnp.bfloat16),) * (blocks - 1)
        + (jax.ShapeDtypeStruct((n, LANES), jnp.float32),) * (blocks - 1)
        + (jax.ShapeDtypeStruct((n, hidden), jnp.bfloat16),) * blocks
        + (jax.ShapeDtypeStruct((n, channels), jnp.bfloat16),) * blocks,
        scratch_shapes=[
            pltpu.VMEM((n, channels), jnp.bfloat16),
            pltpu.VMEM((n, 256), jnp.bfloat16),
            pltpu.VMEM((n, channels), jnp.float32),
            pad_shape(rows, cols, channels),
            pltpu.VMEM((rows, cols, channels), jnp.float32),
            pltpu.VMEM((blocks, channels, hidden), jnp.bfloat16),
            pltpu.VMEM((blocks, hidden, channels), jnp.bfloat16),
            pltpu.SemaphoreType.DMA((2, blocks)),
        ],
        compiler_params=vmem(LIMIT),
        name="forward",
        cost_estimate=estimate(15),
    )(sel, x, normed0, small, *in_hbm(w_ins), *in_hbm(w_outs))
    k = blocks - 1
    return out[:k], out[k : 2 * k], out[2 * k : 3 * k], out[3 * k : 3 * k + blocks], out[3 * k + blocks :]


def tanh_arg(x):
    return jnp.tanh(x * (GELU_C + (GELU_C * GELU_A) * (x * x)))


def load_weights(sel_ref, w_ins, w_outs, w_in_ref, w_out_ref, sems):
    for m in range(len(w_ins)):

        @pl.when(sel_ref[0] == m)
        def _():
            pltpu.make_async_copy(w_ins[m], w_in_ref, sems.at[0]).start()
            pltpu.make_async_copy(w_outs[m], w_out_ref, sems.at[1]).start()

    return (
        pltpu.make_async_copy(w_ins[0], w_in_ref, sems.at[0]).wait,
        pltpu.make_async_copy(w_outs[0], w_out_ref, sems.at[1]).wait,
    )


def specs(sel, arrays, choices, after=0):
    return (
        [pl.BlockSpec(memory_space=pltpu.SMEM)]
        + [pl.BlockSpec(memory_space=pltpu.VMEM)] * arrays
        + [pl.BlockSpec(memory_space=pl.ANY)] * (2 * choices + after)
    )


def mlp_back_kernel(choices, after, sel_ref, g_ref, branch_ref, pre_ref, xhat_ref, inv_ref, gain_ref, scale_ref, *rest):
    w_ins, w_outs = rest[:choices], rest[choices : 2 * choices]
    (keep_ref, send_ref, small_ref, gconv_ref,
     gb_ref, nm_ref, hid_ref, gp_ref, acc_ref, w_in_ref, w_out_ref, sems) = rest[2 * choices + after :]
    wait_in, wait_out = load_weights(sel_ref, w_ins, w_outs, w_in_ref, w_out_ref, sems)
    first = sel_ref[1] == 0
    n, channels = g_ref.shape
    hidden = w_in_ref.shape[1]
    step = 256
    sub = 32
    scale_sum = jnp.zeros((8, channels), jnp.float32)
    for i in range(n // sub):
        at = slice(i * sub, (i + 1) * sub)
        g = g_ref[at, :].astype(jnp.float32)
        scale_sum = scale_sum + jnp.sum((g * branch_ref[at, :].astype(jnp.float32)).reshape(sub // 8, 8, channels), axis=0)
        gb_ref[at, :] = (g * scale_ref[...]).astype(jnp.bfloat16)
        nm_ref[at, :] = (xhat_ref[at, :].astype(jnp.float32) * gain_ref[...]).astype(jnp.bfloat16)
    gb_t = gb_ref[...].T
    nm_t = nm_ref[...].T
    wait_in()
    wait_out()
    for j in range(hidden // step):
        cut = slice(j * step, (j + 1) * step)
        gh = lax.dot_general(gb_ref[...], w_out_ref[cut, :], (((1,), (1,)), ((), ())), preferred_element_type=jnp.float32)
        for i in range(n // sub):
            at = slice(i * sub, (i + 1) * sub)
            p = pre_ref[at, cut].astype(jnp.float32)
            sq = p * p
            t = jnp.tanh(p * (GELU_C + (GELU_C * GELU_A) * sq))
            cdf = 0.5 + 0.5 * t
            hid_ref[at, :] = (p * cdf).astype(jnp.bfloat16)
            slope = cdf + (0.5 * p) * (1.0 - t * t) * (GELU_C + (3.0 * GELU_C * GELU_A) * sq)
            gp_ref[at, :] = (gh[at, :] * slope).astype(jnp.bfloat16)
        t_out = jnp.dot(gb_t, hid_ref[...], preferred_element_type=jnp.float32)
        t_in = jnp.dot(nm_t, gp_ref[...], preferred_element_type=jnp.float32)
        keep_ref[:, cut] = jnp.where(first, t_in, t_out).astype(jnp.bfloat16)
        send_ref[:, cut] = jnp.where(first, t_out, t_in).astype(jnp.bfloat16)
        part = lax.dot_general(gp_ref[...], w_in_ref[:, cut], (((1,), (1,)), ((), ())), preferred_element_type=jnp.float32)
        if j == 0:
            acc_ref[...] = part
        else:
            acc_ref[...] += part
    gain_sum = jnp.zeros((8, channels), jnp.float32)
    for i in range(n // sub):
        at = slice(i * sub, (i + 1) * sub)
        gn = acc_ref[at, :]
        xhat = xhat_ref[at, :].astype(jnp.float32)
        gain_sum = gain_sum + jnp.sum((gn * xhat).reshape(sub // 8, 8, channels), axis=0)
        gx = gn * gain_ref[...]
        m1 = jnp.mean(gx, axis=1, keepdims=True)
        m2 = jnp.mean(gx * xhat, axis=1, keepdims=True)
        inv = inv_ref[at, 0:1]
        gconv_ref[at, :] = inv * (gx - m1 - xhat * m2)
    small_ref[0:1, :] = jnp.sum(gain_sum, axis=0, keepdims=True)
    small_ref[1:2, :] = jnp.sum(scale_sum, axis=0, keepdims=True)
    small_ref[2:8, :] = jnp.zeros((6, channels), jnp.float32)


def mlp_back(sel, g, branch, pre, xhat, inv, gain, scale, w_ins, w_outs, after=()):
    n, channels = g.shape
    hidden = w_ins[0].shape[1]
    return pl.pallas_call(
        functools.partial(mlp_back_kernel, len(w_ins), len(after)),
        in_specs=specs(sel, 7, len(w_ins), len(after)),
        out_shape=(
            jax.ShapeDtypeStruct((channels, hidden), jnp.bfloat16),
            jax.ShapeDtypeStruct((channels, hidden), jnp.bfloat16),
            jax.ShapeDtypeStruct((8, channels), jnp.float32),
            jax.ShapeDtypeStruct((n, channels), jnp.float32),
        ),
        scratch_shapes=[
            pltpu.VMEM((n, channels), jnp.bfloat16),
            pltpu.VMEM((n, channels), jnp.bfloat16),
            pltpu.VMEM((n, 256), jnp.bfloat16),
            pltpu.VMEM((n, 256), jnp.bfloat16),
            pltpu.VMEM((n, channels), jnp.float32),
            pltpu.VMEM((channels, hidden), jnp.bfloat16),
            pltpu.VMEM((hidden, channels), jnp.bfloat16),
            pltpu.SemaphoreType.DMA((2,)),
        ],
        compiler_params=vmem(LIMIT),
        name="mlp_back",
        cost_estimate=estimate(2.5),
    )(sel, g, branch, pre, xhat, inv, gain, scale, *in_hbm(w_ins), *in_hbm(w_outs), *after)


SMALL_ROWS = 64
TAPS = 49


def conv_back_kernel(need_map, after, gconv_ref, x_ref, g_ref, k_ref, small_ref, *rest):
    *out_ref, tk_ref, pad_ref, sum_ref, wide_ref, map_ref = rest[after:]
    conv_back_body(gconv_ref, x_ref, g_ref, k_ref, small_ref, out_ref[0] if need_map else None, tk_ref,
                   pad_ref, sum_ref, wide_ref, map_ref)


def conv_back(gconv, x, g, kernel, small, need_map=True, after=()):
    rows, cols, channels = x.shape
    out = (jax.ShapeDtypeStruct((SMALL_ROWS, channels), jnp.float32),)
    if need_map:
        out = (jax.ShapeDtypeStruct((rows, cols, channels), jnp.bfloat16),) + out
    return pl.pallas_call(
        functools.partial(conv_back_kernel, need_map, len(after)),
        in_specs=[pl.BlockSpec(memory_space=pltpu.VMEM)] * 5 + [pl.BlockSpec(memory_space=pl.ANY)] * len(after),
        out_shape=out,
        scratch_shapes=[
            pad_shape(rows, cols, channels),
            pltpu.VMEM((cols // 8, TAPS, 8, LANES), jnp.float32),
            pltpu.VMEM((rows, cols, channels), jnp.float32),
            pltpu.VMEM((rows, cols, channels), jnp.float32),
        ],
        compiler_params=vmem(LIMIT),
        name="conv_back",
        cost_estimate=estimate(3.4 if need_map else 1.6),
    )(gconv, x, g, kernel, small, *after)


def small_call(kernel, name, outs, *args, scratch=(), after=()):
    used = len(args)

    def body(*refs):
        kernel(*refs[:used], *refs[used + len(after) :])

    return pl.pallas_call(
        body,
        in_specs=[pl.BlockSpec(memory_space=pltpu.SMEM)]
        + [pl.BlockSpec(memory_space=pltpu.VMEM)] * (used - 1)
        + [pl.BlockSpec(memory_space=pl.ANY)] * len(after),
        out_shape=tuple(out_struct(*o) for o in outs),
        scratch_shapes=list(scratch),
        compiler_params=vmem(LIMIT),
        name=name,
        cost_estimate=estimate(0.7),
    )(*args, *after)


def conv_back_body(gconv_ref, x_ref, g_ref, small_ref, sums8_ref, out_ref, tk_ref, pad_ref, sum_ref, wide_ref, map_ref):
    rows, cols, channels = x_ref.shape
    tiles = channels // LANES
    zero_borders(pad_ref)
    for c in range(tiles):
        pad_ref[c, :, 8 : cols + 8] = gconv_ref[:, c * LANES : (c + 1) * LANES].reshape(rows, cols, LANES)

    for h in range(rows):
        wide_ref[h] = x_ref[h].astype(jnp.float32)

    def tile(c, carry):
        lanes = pl.ds(pl.multiple_of(c * LANES, LANES), LANES)

        def strip(w, carry):
            base = pl.multiple_of(w * 8, 8)
            window = pad_ref.at[c, :, pl.ds(base, 24), :]
            xs = [wide_ref[h, pl.ds(base, 8), lanes] for h in range(rows)]
            acc = [None] * rows
            for q in range(7):
                col = [window[h, 11 - q : 19 - q, :] for h in range(rows)]
                for r in range(7):
                    tap = r * 7 + q
                    if out_ref is not None:
                        weight = small_ref[tap : tap + 1, lanes]
                    total = None
                    for h in range(max(0, r - 3), min(rows, rows + r - 3)):
                        shifted = col[h + 3 - r]
                        term = xs[h] * shifted
                        total = term if total is None else total + term
                        if out_ref is not None:
                            moved = weight * shifted
                            acc[h] = moved if acc[h] is None else acc[h] + moved
                    sum_ref[w, tap] = total
            if out_ref is not None:
                for h in range(rows):
                    map_ref[h, pl.ds(base, 8), lanes] = acc[h]
            return carry

        lax.fori_loop(0, cols // 8, strip, 0)
        tk_ref[0:TAPS, lanes] = jnp.sum(sum_ref[0] + sum_ref[1], axis=1)
        return carry

    lax.fori_loop(0, tiles, tile, 0)
    if out_ref is not None:
        for h in range(rows):
            out_ref[h] = (g_ref[h].astype(jnp.float32) + map_ref[h]).astype(jnp.bfloat16)
    tk_ref[TAPS : TAPS + 2, :] = sums8_ref[0:2, :]
    tk_ref[TAPS + 2 :, :] = jnp.zeros((SMALL_ROWS - TAPS - 2, channels), jnp.float32)


def conv_map_body(gconv_ref, g_ref, small_ref, out_ref, pad_ref, map_ref):
    rows, cols, channels = g_ref.shape
    tiles = channels // LANES
    zero_borders(pad_ref)
    for c in range(tiles):
        pad_ref[c, :, 8 : cols + 8] = gconv_ref[:, c * LANES : (c + 1) * LANES].reshape(rows, cols, LANES)

    def tile(c, carry):
        lanes = pl.ds(pl.multiple_of(c * LANES, LANES), LANES)

        def strip(w, carry):
            base = pl.multiple_of(w * 8, 8)
            window = pad_ref.at[c, :, pl.ds(base, 24), :]
            acc = [None] * rows
            for q in range(7):
                col = [window[h, 11 - q : 19 - q, :] for h in range(rows)]
                for r in range(7):
                    weight = small_ref[r * 7 + q : r * 7 + q + 1, lanes]
                    for h in range(max(0, r - 3), min(rows, rows + r - 3)):
                        term = weight * col[h + 3 - r]
                        acc[h] = term if acc[h] is None else acc[h] + term
            for h in range(rows):
                map_ref[h, pl.ds(base, 8), lanes] = acc[h]
            return carry

        return lax.fori_loop(0, cols // 8, strip, carry)

    lax.fori_loop(0, tiles, tile, 0)
    for h in range(rows):
        out_ref[h] = (g_ref[h].astype(jnp.float32) + map_ref[h]).astype(jnp.bfloat16)


def mlp_back_map_body(g_ref, branch_ref, pre_ref, xhat_ref, inv_ref, small_ref, w_in_ref, w_out_ref,
                      sums8_ref, gconv_ref, gb_ref, nm_ref, hid_ref, gp_ref, acc_ref, ready):
    rows, cols, channels = g_ref.shape
    n = rows * cols
    hidden = w_in_ref.shape[1]
    step = 256
    sub = 2 * cols
    gain = small_ref[TAPS : TAPS + 1, :]
    scale = small_ref[TAPS + 1 : TAPS + 2, :]
    scale_sum = jnp.zeros((8, channels), jnp.float32)
    for i in range(n // sub):
        at = slice(i * sub, (i + 1) * sub)
        g = g_ref[2 * i : 2 * i + 2].astype(jnp.float32).reshape(sub, channels)
        scale_sum = scale_sum + jnp.sum((g * branch_ref[at, :].astype(jnp.float32)).reshape(sub // 8, 8, channels), axis=0)
        gb_ref[at, :] = (g * scale).astype(jnp.bfloat16)
        nm_ref[at, :] = (xhat_ref[at, :].astype(jnp.float32) * gain).astype(jnp.bfloat16)
    ready("gb", "nm")
    for j in range(hidden // step):
        cut = slice(j * step, (j + 1) * step)
        gh = lax.dot_general(gb_ref[...], w_out_ref[cut, :], (((1,), (1,)), ((), ())), preferred_element_type=jnp.float32)
        for i in range(n // sub):
            at = slice(i * sub, (i + 1) * sub)
            p = pre_ref[at, cut].astype(jnp.float32)
            sq = p * p
            t = jnp.tanh(p * (GELU_C + (GELU_C * GELU_A) * sq))
            cdf = 0.5 + 0.5 * t
            hid_ref[at, cut] = (p * cdf).astype(jnp.bfloat16)
            slope = cdf + (0.5 * p) * (1.0 - t * t) * (GELU_C + (3.0 * GELU_C * GELU_A) * sq)
            gp_ref[at, cut] = (gh[at, :] * slope).astype(jnp.bfloat16)
        part = lax.dot_general(gp_ref[:, cut], w_in_ref[:, cut], (((1,), (1,)), ((), ())), preferred_element_type=jnp.float32)
        if j == 0:
            acc_ref[...] = part
        else:
            acc_ref[...] += part
    ready("hid", "gp")
    gain_sum = jnp.zeros((8, channels), jnp.float32)
    for i in range(n // sub):
        at = slice(i * sub, (i + 1) * sub)
        gn = acc_ref[at, :]
        xhat = xhat_ref[at, :].astype(jnp.float32)
        gain_sum = gain_sum + jnp.sum((gn * xhat).reshape(sub // 8, 8, channels), axis=0)
        gx = gn * gain
        m1 = jnp.mean(gx, axis=1, keepdims=True)
        m2 = jnp.mean(gx * xhat, axis=1, keepdims=True)
        gconv_ref[at, :] = inv_ref[at, 0:1] * (gx - m1 - xhat * m2)
    sums8_ref[0:1, :] = jnp.sum(gain_sum, axis=0, keepdims=True)
    sums8_ref[1:2, :] = jnp.sum(scale_sum, axis=0, keepdims=True)
    sums8_ref[2:8, :] = jnp.zeros((6, channels), jnp.float32)
    ready("gconv", "sums")


def mlp_back_body(first, g_ref, branch_ref, pre_ref, xhat_ref, inv_ref, small_ref, wait_in, wait_out, w_in_ref, w_out_ref,
                  keep_ref, send_ref, sums8_ref, gconv_ref, gb_ref, nm_ref, hid_ref, gp_ref, acc_ref, before=None):
    rows, cols, channels = g_ref.shape
    n = rows * cols
    hidden = w_in_ref.shape[1]
    step = 256
    sub = 2 * cols
    gain = small_ref[TAPS : TAPS + 1, :]
    scale = small_ref[TAPS + 1 : TAPS + 2, :]
    scale_sum = jnp.zeros((8, channels), jnp.float32)
    for i in range(n // sub):
        at = slice(i * sub, (i + 1) * sub)
        g = g_ref[2 * i : 2 * i + 2].astype(jnp.float32).reshape(sub, channels)
        scale_sum = scale_sum + jnp.sum((g * branch_ref[at, :].astype(jnp.float32)).reshape(sub // 8, 8, channels), axis=0)
        gb_ref[at, :] = (g * scale).astype(jnp.bfloat16)
        nm_ref[at, :] = (xhat_ref[at, :].astype(jnp.float32) * gain).astype(jnp.bfloat16)
    gb_t = gb_ref[...].T
    nm_t = nm_ref[...].T
    wait_out()
    for j in range(hidden // step):
        cut = slice(j * step, (j + 1) * step)
        gh = lax.dot_general(gb_ref[...], w_out_ref[cut, :], (((1,), (1,)), ((), ())), preferred_element_type=jnp.float32)
        for i in range(n // sub):
            at = slice(i * sub, (i + 1) * sub)
            p = pre_ref[at, cut].astype(jnp.float32)
            sq = p * p
            t = jnp.tanh(p * (GELU_C + (GELU_C * GELU_A) * sq))
            cdf = 0.5 + 0.5 * t
            hid_ref[at, :] = (p * cdf).astype(jnp.bfloat16)
            slope = cdf + (0.5 * p) * (1.0 - t * t) * (GELU_C + (3.0 * GELU_C * GELU_A) * sq)
            gp_ref[at, :] = (gh[at, :] * slope).astype(jnp.bfloat16)
        t_out = jnp.dot(gb_t, hid_ref[...], preferred_element_type=jnp.float32)
        t_in = jnp.dot(nm_t, gp_ref[...], preferred_element_type=jnp.float32)
        t_keep = jnp.where(first, t_in, t_out)
        t_send = jnp.where(first, t_out, t_in)
        if before is not None:
            if j == 0:
                old_keep, old_send = before()
            t_keep = t_keep + old_keep[:, cut].astype(jnp.float32)
            t_send = t_send + old_send[:, cut].astype(jnp.float32)
        keep_ref[:, cut] = t_keep.astype(jnp.bfloat16)
        send_ref[:, cut] = t_send.astype(jnp.bfloat16)
        if j == 0:
            wait_in()
        part = lax.dot_general(gp_ref[...], w_in_ref[:, cut], (((1,), (1,)), ((), ())), preferred_element_type=jnp.float32)
        if j == 0:
            acc_ref[...] = part
        else:
            acc_ref[...] += part
    gain_sum = jnp.zeros((8, channels), jnp.float32)
    for i in range(n // sub):
        at = slice(i * sub, (i + 1) * sub)
        gn = acc_ref[at, :]
        xhat = xhat_ref[at, :].astype(jnp.float32)
        gain_sum = gain_sum + jnp.sum((gn * xhat).reshape(sub // 8, 8, channels), axis=0)
        gx = gn * gain
        m1 = jnp.mean(gx, axis=1, keepdims=True)
        m2 = jnp.mean(gx * xhat, axis=1, keepdims=True)
        gconv_ref[at, :] = inv_ref[at, 0:1] * (gx - m1 - xhat * m2)
    sums8_ref[0:1, :] = jnp.sum(gain_sum, axis=0, keepdims=True)
    sums8_ref[1:2, :] = jnp.sum(scale_sum, axis=0, keepdims=True)
    sums8_ref[2:8, :] = jnp.zeros((6, channels), jnp.float32)


def out_struct(shape, dtype, by_hand=False):
    return pltpu.HBM(shape, dtype) if by_hand else jax.ShapeDtypeStruct(shape, dtype)


def named_call(name, body, ins, outs, scratch, cost):
    names = list(ins) + list(outs) + list(scratch)
    spaces = {"v": pltpu.VMEM, "s": pltpu.SMEM, "a": pl.ANY, "h": pl.ANY}

    def kernel(*refs):
        body(types.SimpleNamespace(**dict(zip(names, refs))))

    args = [pltpu.with_memory_space_constraint(a, pltpu.HBM) if kind == "h" else a for a, kind in ins.values()]
    result = pl.pallas_call(
        kernel,
        in_specs=[pl.BlockSpec(memory_space=spaces[kind]) for _, kind in ins.values()],
        out_specs=tuple(pl.BlockSpec(memory_space=pl.ANY if len(o) > 2 else pltpu.VMEM) for o in outs.values()),
        out_shape=tuple(out_struct(*o) for o in outs.values()),
        scratch_shapes=list(scratch.values()),
        compiler_params=vmem(LIMIT),
        name=name,
        cost_estimate=estimate(cost),
    )(*args)
    return types.SimpleNamespace(**dict(zip(outs, result)))


def mlp_body(normed_ref, wait_in, wait_out, w_in_ref, w_out_ref, pre_ref, hid_ref, acc_ref):
    n = normed_ref.shape[0]
    hidden = w_in_ref.shape[1]
    step, sub = 256, 32
    wait_in()
    for j in range(hidden // step):
        cut = slice(j * step, (j + 1) * step)
        pre = jnp.dot(normed_ref[...], w_in_ref[:, cut], preferred_element_type=jnp.float32)
        for i in range(n // sub):
            p = pre[i * sub : (i + 1) * sub]
            half = 0.5 * p
            hid_ref[i * sub : (i + 1) * sub, :] = (half + half * tanh_arg(p)).astype(jnp.bfloat16)
            pre_ref[i * sub : (i + 1) * sub, cut] = p.astype(jnp.bfloat16)
        if j == 0:
            wait_out()
        part = jnp.dot(hid_ref[...], w_out_ref[cut, :], preferred_element_type=jnp.float32)
        if j == 0:
            acc_ref[...] = part
        else:
            acc_ref[...] += part


def residual_body(x_ref, small_ref, acc_ref, branch_ref, y_ref):
    rows, cols, channels = x_ref.shape
    scale = small_ref[TAPS + 1 : TAPS + 2, :]
    sub = 2 * cols
    for i in range(rows // 2):
        branch = acc_ref[i * sub : (i + 1) * sub, :]
        branch_ref[i * sub : (i + 1) * sub, :] = branch.astype(jnp.bfloat16)
        if y_ref is not None:
            old = x_ref[2 * i : 2 * i + 2].astype(jnp.float32).reshape(sub, channels)
            y_ref[2 * i : 2 * i + 2] = (old + scale * branch).astype(jnp.bfloat16).reshape(2, cols, channels)


def small_ins(pair):
    return {"own_small": (pair[0], "v"), "near_small": (pair[1], "v")}


def small_scratch(pair):
    return {"small": pltpu.VMEM((2,) + pair[0].shape, jnp.float32)}


def weight_ins(pair):
    return {k: (v, "h") for k, v in zip(("own_in", "near_in", "own_out", "near_out"), pair)}


def weight_scratch(blocks, channels, hidden):
    return {
        "w_in": pltpu.VMEM((blocks, channels, hidden), jnp.bfloat16),
        "w_out": pltpu.VMEM((blocks, hidden, channels), jnp.bfloat16),
        "w_sem": pltpu.SemaphoreType.DMA((2, blocks)),
    }


def start_weights(r, slot, block, out_first=False):
    def start(k, own, near, target):
        return copy_chosen(r.sel[block], (own, near), target.at[slot], r.w_sem.at[k, slot])

    if out_first:
        wait_out = start(1, r.own_out, r.near_out, r.w_out)
        return start(0, r.own_in, r.near_in, r.w_in), wait_out
    return start(0, r.own_in, r.near_in, r.w_in), start(1, r.own_out, r.near_out, r.w_out)


def pair_forward(sel, x, first, small, weights):
    rows, cols, channels = x.shape
    n, hidden = rows * cols, weights[0].shape[1]
    bf16, f32 = jnp.bfloat16, jnp.float32

    def body(r):
        @pl.when(r.sel[4] == 0)
        def _():
            low, high = start_weights(r, 0, 0), start_weights(r, 1, 1)
            choose_small(r)
            zero_borders(r.pad)
            mlp_body(r.normed0, *low, r.w_in.at[0], r.w_out.at[0], r.pre0, r.hid, r.acc)
            residual_body(r.x, r.small.at[0], r.acc, r.branch0, r.x1)
            conv_norm_body(r.x1, r.small.at[1], r.xhat1, r.normed, r.inv1, r.pad, r.conv)
            mlp_body(r.normed, *high, r.w_in.at[1], r.w_out.at[1], r.pre1, r.hid, r.acc)
            residual_body(r.x1, r.small.at[1], r.acc, r.branch1, r.y)

    return named_call(
        "pair_forward", body,
        {"sel": (sel, "s"), "x": (x, "v"), "normed0": (first[1], "v"), **small_ins(small), **weight_ins(weights)},
        {"y": (x.shape, bf16), "x1": (x.shape, bf16), "xhat1": ((n, channels), bf16), "inv1": ((n, LANES), f32),
         "pre0": ((n, hidden), bf16), "pre1": ((n, hidden), bf16),
         "branch0": ((n, channels), bf16), "branch1": ((n, channels), bf16)},
        {"normed": pltpu.VMEM((n, channels), bf16), "hid": pltpu.VMEM((n, 256), bf16), "acc": pltpu.VMEM((n, channels), f32),
         "pad": pad_shape(rows, cols, channels), "conv": pltpu.VMEM((rows, cols, channels), f32),
         **weight_scratch(2, channels, hidden), **small_scratch(small)},
        7.5,
    )


def back_scratch(n, channels):
    bf16, f32 = jnp.bfloat16, jnp.float32
    return {"gb": pltpu.VMEM((n, channels), bf16), "nm": pltpu.VMEM((n, channels), bf16),
            "hid": pltpu.VMEM((n, 256), bf16), "gp": pltpu.VMEM((n, 256), bf16), "acc": pltpu.VMEM((n, channels), f32)}


def back_temps(r):
    return r.gb, r.nm, r.hid, r.gp, r.acc


GRADS = ("keep0", "send0", "keep1", "send1")
FACTORS = ("gb", "nm", "hid", "gp", "gconv", "sums")


def factor_shapes(n, channels, hidden):
    bf16, f32 = jnp.bfloat16, jnp.float32
    one = {"gb": ((n, channels), bf16), "nm": ((n, channels), bf16), "hid": ((n, hidden), bf16), "gp": ((n, hidden), bf16),
           "gconv": ((n, channels), f32), "sums": ((8, channels), f32)}
    return {name + str(k): one[name] for k in (0, 1) for name in FACTORS}


def pair_map(sel, x, g, small, weights):
    rows, cols, channels = x.shape
    n, hidden = rows * cols, weights[0].shape[1]
    bf16, f32 = jnp.bfloat16, jnp.float32
    shapes = factor_shapes(n, channels, hidden)
    saved = {**shapes, "x1": (x.shape, bf16)}
    order = list(saved)

    def body(r):
        @pl.when(r.sel[2] == 1)
        def _():
            def copy_out(name):
                return pltpu.make_async_copy(getattr(r, "v_" + name), getattr(r, name), r.s_sem.at[order.index(name)])

            low, high = start_weights(r, 0, 0), start_weights(r, 1, 1)
            choose_small(r)
            zero_borders(r.pad)
            s0, s1 = r.small.at[0], r.small.at[1]
            conv_norm_body(r.x, s0, r.xhat0, r.normed, r.inv0, r.pad, r.conv)
            mlp_body(r.normed, *low, r.w_in.at[0], r.w_out.at[0], r.pre0, r.hid, r.acc)
            residual_body(r.x, s0, r.acc, r.branch0, r.v_x1)
            copy_out("x1").start()
            conv_norm_body(r.v_x1, s1, r.xhat1, r.normed, r.inv1, r.pad, r.conv)
            mlp_body(r.normed, *high, r.w_in.at[1], r.w_out.at[1], r.pre1, r.hid, r.acc)
            residual_body(r.v_x1, s1, r.acc, r.branch1, None)

            def ready(k):
                def start(*names):
                    for name in names:
                        copy_out(name + str(k)).start()

                return start

            mlp_back_map_body(r.g, r.branch1, r.pre1, r.xhat1, r.inv1, s1, r.w_in.at[1], r.w_out.at[1],
                              r.v_sums1, r.v_gconv1, r.v_gb1, r.v_nm1, r.v_hid1, r.v_gp1, r.acc, ready(1))
            conv_map_body(r.v_gconv1, r.g, s1, r.g1, r.pad, r.conv)
            mlp_back_map_body(r.g1, r.branch0, r.pre0, r.xhat0, r.inv0, s0, r.w_in.at[0], r.w_out.at[0],
                              r.v_sums0, r.v_gconv0, r.v_gb0, r.v_nm0, r.v_hid0, r.v_gp0, r.acc, ready(0))
            conv_map_body(r.v_gconv0, r.g1, s0, r.g0, r.pad, r.conv)
            for name in order:
                copy_out(name).wait()

    return named_call(
        "pair_map", body,
        {"sel": (sel, "s"), "x": (x, "v"), "g": (g, "v"), **small_ins(small), **weight_ins(weights)},
        {"g0": (x.shape, bf16), **{name: shape + (True,) for name, shape in saved.items()}},
        {**{"v_" + name: pltpu.VMEM(*shape) for name, shape in saved.items()},
         "s_sem": pltpu.SemaphoreType.DMA((len(order),)),
         "g1": pltpu.VMEM(x.shape, bf16),
         "xhat0": pltpu.VMEM((n, channels), bf16), "xhat1": pltpu.VMEM((n, channels), bf16),
         "inv0": pltpu.VMEM((n, LANES), f32), "inv1": pltpu.VMEM((n, LANES), f32),
         "pre0": pltpu.VMEM((n, hidden), bf16), "pre1": pltpu.VMEM((n, hidden), bf16),
         "branch0": pltpu.VMEM((n, channels), bf16), "branch1": pltpu.VMEM((n, channels), bf16),
         "normed": pltpu.VMEM((n, channels), bf16), "hid": pltpu.VMEM((n, 256), bf16), "acc": pltpu.VMEM((n, channels), f32),
         "pad": pad_shape(rows, cols, channels), "conv": pltpu.VMEM((rows, cols, channels), f32),
         **weight_scratch(2, channels, hidden), **small_scratch(small)},
        12,
    )


def pair_grads(sel, xs, parts):
    rows, cols, channels = xs[0].shape
    n, hidden = rows * cols, parts[0].hid0.shape[1]
    bf16, f32 = jnp.bfloat16, jnp.float32
    shapes = factor_shapes(n, channels, hidden)
    order = list(shapes) + ["x1"]

    def body(r):
        @pl.when(r.sel[2] == 1)
        def _():
            def copy_out(k):
                return pltpu.make_async_copy(r.grads.at[k], getattr(r, GRADS[k]), r.o_sem.at[k])

            copies = {}
            for k in (1, 0):
                for name in FACTORS + (("x1",) if k else ()):
                    full = name + str(k) if name != "x1" else name
                    for i in range(2):
                        copies[full, i] = pltpu.make_async_copy(
                            getattr(r, "i%d_%s" % (i, full)), getattr(r, "v_" + full).at[i], r.s_sem.at[i, order.index(full)]
                        )
                        copies[full, i].start()
            first = r.sel[3] == 0
            for k in (1, 0):
                gb, nm, hid, gp = (getattr(r, "v_%s%d" % (name, k)) for name in FACTORS[:4])
                keep, send = r.grads.at[2 * k], r.grads.at[2 * k + 1]
                for name in FACTORS + (("x1",) if k else ()):
                    for i in range(2):
                        copies[name + str(k) if name != "x1" else name, i].wait()
                gb_t = gb[...].reshape(2 * n, channels).T
                nm_t = nm[...].reshape(2 * n, channels).T
                for j in range(hidden // 256):
                    cut = slice(j * 256, (j + 1) * 256)
                    t_out = jnp.dot(gb_t, hid[:, :, cut].reshape(2 * n, 256), preferred_element_type=f32)
                    t_in = jnp.dot(nm_t, gp[:, :, cut].reshape(2 * n, 256), preferred_element_type=f32)
                    keep[:, cut] = jnp.where(first, t_in, t_out).astype(bf16)
                    send[:, cut] = jnp.where(first, t_out, t_in).astype(bf16)
                copy_out(2 * k).start()
                copy_out(2 * k + 1).start()
                out = getattr(r, "small%d" % k)
                for i in range(2):
                    x = r.v_x1.at[i] if k else getattr(r, "x_%d" % i)
                    gconv, sums = getattr(r, "v_gconv%d" % k).at[i], getattr(r, "v_sums%d" % k).at[i]
                    target = out if i == 0 else r.tk
                    conv_back_body(gconv, x, None, None, sums, None, target, r.pad, r.sum, r.wide, None)
                out[...] += r.tk[...]
            for k in range(4):
                copy_out(k).wait()

    ins = {"sel": (sel, "s")}
    for i in range(2):
        ins["x_%d" % i] = (xs[i], "v")
        ins.update({"i%d_%s" % (i, name): (getattr(parts[i], name), "h") for name in order})
    grad = ((channels, hidden), bf16)
    small_out = ((SMALL_ROWS, channels), f32)
    scratch = {"v_" + name: pltpu.VMEM((2,) + shape, dtype) for name, (shape, dtype) in shapes.items()}
    return named_call(
        "pair_grads", body, ins,
        {**{name: grad + (True,) for name in GRADS}, "small0": small_out, "small1": small_out},
        {**scratch, "grads": pltpu.VMEM((4, channels, hidden), bf16), "o_sem": pltpu.SemaphoreType.DMA((4,)), "v_x1": pltpu.VMEM((2,) + xs[0].shape, bf16), "s_sem": pltpu.SemaphoreType.DMA((2, len(order))),
         "pad": pad_shape(rows, cols, channels), "sum": pltpu.VMEM((cols // 8, TAPS, 8, LANES), f32),
         "wide": pltpu.VMEM(xs[0].shape, f32), "tk": pltpu.VMEM((SMALL_ROWS, channels), f32)},
        10,
    )


def pair_back(sel, g, x, first, kept, small, weights, before=None, after=()):
    rows, cols, channels = g.shape
    n, hidden = rows * cols, weights[0].shape[1]
    bf16, f32 = jnp.bfloat16, jnp.float32

    def body(r):
        def copy_old(k):
            return copy_chosen(r.sel[2], (getattr(r, "a_" + GRADS[k]), getattr(r, "p_" + GRADS[k])), r.olds.at[k], r.o_sem.at[k])

        def copy_out(k, source):
            return pltpu.make_async_copy(source, getattr(r, GRADS[k]), r.s_sem.at[k])

        @pl.when(r.sel[2] == 0)
        def _():
            core = r.sel[3] == 0
            high, waits = start_weights(r, 1, 1, True), {}
            if before is not None:
                waits = {k: copy_old(k) for k in (2, 3)}
            low = start_weights(r, 0, 0, True)
            if before is not None:
                waits.update({k: copy_old(k) for k in (0, 1)})
            choose_small(r)
            s0, s1 = r.small.at[0], r.small.at[1]

            def old(k):
                def both():
                    waits[2 * k]()
                    waits[2 * k + 1]()
                    return r.olds.at[2 * k], r.olds.at[2 * k + 1]

                return both if waits else None

            mlp_back_body(core, r.g, r.branch1, r.pre1, r.xhat1, r.inv1, s1, *high, r.w_in.at[1], r.w_out.at[1],
                          r.grads.at[2], r.grads.at[3], r.sums8, r.gconv, *back_temps(r), before=old(1))
            copy_out(2, r.grads.at[2]).start()
            copy_out(3, r.grads.at[3]).start()
            conv_back_body(r.gconv, r.x1, r.g, s1, r.sums8, r.g1, r.small1, r.pad, r.sum, r.wide, r.map)
            mlp_back_body(core, r.g1, r.branch0, r.pre0, r.xhat0, r.inv0, s0, *low, r.w_in.at[0], r.w_out.at[0],
                          r.grads.at[0], r.grads.at[1], r.sums8, r.gconv, *back_temps(r), before=old(0))
            copy_out(0, r.grads.at[0]).start()
            copy_out(1, r.grads.at[1]).start()
            conv_back_body(r.gconv, r.x, None, None, r.sums8, None, r.small0, r.pad, r.sum, r.wide, None)
            if before is not None:
                r.small0[...] += r.a_small0[...]
                r.small1[...] += r.a_small1[...]
                r.packed[...] = jnp.concatenate([r.small0[...], r.small1[...]], axis=0).T.astype(bf16)
            for k in range(4):
                copy_out(k, r.grads.at[k]).wait()

        if before is not None:

            @pl.when(r.sel[2] == 1)
            def _():
                waits = [copy_old(k) for k in range(4)]
                r.packed[...] = jnp.concatenate([r.p_small0[...], r.p_small1[...]], axis=0).T.astype(bf16)
                for k, wait in enumerate(waits):
                    wait()
                    copy_out(k, r.olds.at[k]).start()
                for k in range(4):
                    copy_out(k, r.olds.at[k]).wait()

    ins = {"sel": (sel, "s"), "g": (g, "v"), "x": (x, "v"), "x1": (kept.x1, "v"),
           "branch1": (kept.branch1, "v"), "pre1": (kept.pre1, "v"), "xhat1": (kept.xhat1, "v"), "inv1": (kept.inv1, "v"),
           "branch0": (kept.branch0, "v"), "pre0": (kept.pre0, "v"), "xhat0": (first[0], "v"), "inv0": (first[2], "v"),
           **small_ins(small), **weight_ins(weights)}
    grad = ((channels, hidden), bf16)
    small_out = ((SMALL_ROWS, channels), f32)
    outs = {name: grad + (True,) for name in GRADS}
    scratch = {"grads": pltpu.VMEM((4, channels, hidden), bf16), "s_sem": pltpu.SemaphoreType.DMA((4,)), "g1": pltpu.VMEM(g.shape, bf16), "sums8": pltpu.VMEM((8, channels), f32), "gconv": pltpu.VMEM((n, channels), f32),
               "pad": pad_shape(rows, cols, channels), "sum": pltpu.VMEM((cols // 8, TAPS, 8, LANES), f32),
               "wide": pltpu.VMEM(x.shape, f32), "map": pltpu.VMEM(x.shape, f32),
               **back_scratch(n, channels), **weight_scratch(2, channels, hidden), **small_scratch(small)}
    if before is None:
        outs.update({"small0": small_out, "small1": small_out})
    else:
        for prefix, part in zip("ap", before):
            ins.update({prefix + "_" + name: (getattr(part, name), "h") for name in GRADS})
            ins.update({prefix + "_" + name: (getattr(part, name), "v") for name in ("small0", "small1")})
        outs["packed"] = ((channels, 2 * SMALL_ROWS), bf16)
        scratch.update({"small0": pltpu.VMEM(*small_out), "small1": pltpu.VMEM(*small_out),
                        "olds": pltpu.VMEM((4, channels, hidden), bf16), "o_sem": pltpu.SemaphoreType.DMA((4,))})
    ins.update({"after%d" % k: (v, "a") for k, v in enumerate(after)})
    return named_call("pair_back", body, ins, outs, scratch, 9)


def brought_kernel(source_ref, out_ref, sem):
    copy = pltpu.make_async_copy(source_ref, out_ref, sem)
    copy.start()
    copy.wait()


def brought(value):
    return pl.pallas_call(
        brought_kernel,
        in_specs=[pl.BlockSpec(memory_space=pl.ANY)],
        out_shape=jax.ShapeDtypeStruct(value.shape, value.dtype),
        scratch_shapes=[pltpu.SemaphoreType.DMA(())],
        compiler_params=vmem(LIMIT),
        name="brought",
        cost_estimate=estimate(1.1),
    )(pltpu.with_memory_space_constraint(value, pltpu.HBM))


def add(a, b):
    return a.astype(jnp.float32) + b.astype(jnp.float32)


def side_kernel(sel_ref, keep_ref, got_ref, *refs):
    *small_ref, across_ref, mine_ref = refs
    side = sel_ref[0]
    levels, _, _, hidden = keep_ref.shape
    for level in range(levels):
        for out_ref, which in ((across_ref, 1 - side), (mine_ref, side)):
            out_ref[level, :, :hidden] = add(keep_ref[level, which], got_ref[level, which]).astype(jnp.bfloat16)
            if small_ref:
                out_ref[level, :, hidden:] = small_ref[0][level, which]


def to_side(side, *arrays):
    arrays = [v.reshape(4, 2, v.shape[0] // 8, v.shape[1]) for v in arrays]
    width = sum(v.shape[3] for v in arrays[1:])
    out = ((4, arrays[0].shape[2], width), jnp.bfloat16)
    return small_call(side_kernel, "to_side", (out, out), side, *arrays)


def depth_kernel(sel_ref, mine_ref, got_ref, *out_refs):
    for k, out_ref in enumerate(out_refs):
        out_ref[...] = add(mine_ref[sel_ref[k]], got_ref[sel_ref[k]]).astype(jnp.bfloat16)


def to_depths(levels, mine, got, after=()):
    return small_call(depth_kernel, "to_depths", ((mine.shape[1:], jnp.bfloat16),) * 4, levels, mine, got, after=after)


def split_kernel(sel_ref, keep_ref, got_ref, *out_refs):
    for k, out_ref in enumerate(out_refs):
        for side in range(2):
            out_ref[side] = add(keep_ref[sel_ref[k], side], got_ref[sel_ref[k], side]).astype(jnp.bfloat16)


def split_depths(levels, keep, got, after=()):
    keep, got = (v.reshape(4, 2, v.shape[0] // 8, v.shape[1]) for v in (keep, got))
    outs = ((keep.shape[1:], jnp.bfloat16),) * 4
    return small_call(split_kernel, "split_depths", outs, levels, keep, got, after=after)


def join_kernel(sel_ref, a_ref, b_ref, c_ref, d_ref, across_ref, mine_ref):
    side = sel_ref[0]
    for out_ref, which in ((across_ref, 1 - side), (mine_ref, side)):
        out_ref[...] = (add(a_ref[which], b_ref[which]) + add(c_ref[which], d_ref[which])).astype(out_ref.dtype)


def join_depths(side, parts):
    shape = parts[0].shape[1:]
    return small_call(join_kernel, "join_depths", ((shape, jnp.bfloat16), (shape, jnp.float32)), side, *parts)


def core_kernel(sel_ref, *refs):
    *parts, own_ref, send_ref = refs
    hidden = parts[-1].shape[1]
    a, b, c, d, e, f = parts
    low, high = add(a[...], b[...]) + add(c[...], d[...]), add(e[...], f[...])
    first = sel_ref[0] == 0
    small = low[:, hidden:]
    turned = pltpu.roll(small, SMALL_ROWS, 1)
    low = low[:, :hidden]
    own_ref[:, :hidden] = jnp.where(first, low, high)
    own_ref[:, hidden:] = jnp.where(first, small, turned)
    send_ref[:, :hidden] = jnp.where(first, high, low).astype(jnp.bfloat16)
    send_ref[:, hidden:] = jnp.where(first, turned, small).astype(jnp.bfloat16)


def to_core(core, parts):
    shape = (parts[-1].shape[0], parts[-1].shape[1] + 2 * SMALL_ROWS)
    return small_call(core_kernel, "to_core", ((shape, jnp.float32), (shape, jnp.bfloat16)), core, *parts)


def final_kernel(sel_ref, own_ref, got_ref, k_ref, gain_ref, in_ref, out_ref, scale_ref, pad_ref):
    share, hidden = own_ref.shape[0], in_ref.shape[2]
    taps = k_ref.shape[2]
    first = sel_ref[0] == 0
    own, got = own_ref[:, :hidden], got_ref[:, :hidden].astype(jnp.float32)
    in_ref[0] = jnp.where(first, own, got)
    out_ref[0] = jnp.where(first, got, own)
    small = add(own_ref[:, hidden:], got_ref[:, hidden:])
    k_ref[0] = small[:, :taps]
    pad_ref[0:share, :] = small
    turned = pad_ref[...].T
    gain_ref[...] = turned[taps : taps + 1, :share]
    scale_ref[...] = turned[taps + 1 : taps + 2, :share]


def final(core, own, got, taps):
    share, hidden = own.shape[0], own.shape[1] - 2 * SMALL_ROWS
    outs = (
        ((1, share, taps), jnp.float32),
        ((1, share), jnp.float32),
        ((1, share, hidden), jnp.float32),
        ((1, share, hidden), jnp.float32),
        ((1, share), jnp.float32),
    )
    t_kernel, t_gain, t_in, t_out, t_scale = small_call(
        final_kernel, "final", outs, core, own, got, scratch=[pltpu.VMEM((LANES, 2 * SMALL_ROWS), jnp.float32)]
    )
    return t_kernel.transpose(0, 2, 1), t_gain, t_in, t_out.transpose(0, 2, 1), t_scale


BF16 = jnp.bfloat16
F32 = jnp.float32


def one_image(x, g, small, sels, w_ins, w_outs, first, passing):
    blocks = small.shape[0]
    rows, cols, channels = x.shape
    which = jnp.stack([sel[0] for sel in sels])
    xs, xhats, invs, pres, branches = forward(which, x, first[1], small, w_ins, w_outs)
    xs, xhats, invs = (x,) + tuple(xs), first[:1] + tuple(xhats), first[2:] + tuple(invs)
    smalls = [None] * blocks
    for s in reversed(range(blocks)):
        keep, send, sums8, gconv = mlp_back(
            sels[s], g.reshape(rows * cols, channels), branches[s], pres[s], xhats[s], invs[s],
            small[s, TAPS : TAPS + 1], small[s, TAPS + 1 : TAPS + 2], w_ins, w_outs, passing.before("mlp", s),
        )
        passing.done(s, keep, send)
        *g_next, smalls[s] = conv_back(
            gconv, xs[s], g, small[s, :TAPS], sums8, s > 0, passing.before("conv", s)
        )
        g = g_next[0] if g_next else None
    return smalls


def finish(t_kernel, t_gain, t_scale, t_in, t_out):
    return t_kernel[None], t_gain[None], t_in[None], t_out[None], t_scale[None]


def any_mesh(images, cotangent, kernels, norm_gains, w_in, w_out, scales):
    segments = lax.axis_size("segment")
    rank = lax.axis_index("segment")
    count = images.shape[0] // segments
    taps = kernels.shape[1]
    small = lax.all_gather(parameters(kernels, norm_gains, scales), "segment")
    all_in = lax.all_gather(w_in[0], "segment")
    all_out = lax.all_gather(w_out[0], "segment")
    sels = [jnp.array([s, 0], jnp.int32) for s in range(segments)]
    pieces = [[None] * 3 for _ in range(segments)]

    class Sums:
        def before(self, part, s):
            return ()

        def done(self, s, keep, send):
            self.add(s, 0, keep.astype(F32))
            self.add(s, 1, send.astype(F32))

        def add(self, s, k, value):
            pieces[s][k] = value if pieces[s][k] is None else pieces[s][k] + value

    sums = Sums()
    w_ins = [all_in[s] for s in range(segments)]
    w_outs = [all_out[s] for s in range(segments)]
    for i in range(count):
        x = lax.dynamic_index_in_dim(images, rank * count + i, 0, keepdims=False)
        g = lax.dynamic_index_in_dim(cotangent, rank * count + i, 0, keepdims=False)
        smalls = one_image(x, g, small, sels, w_ins, w_outs, conv_norm(sels[0] * 0, x, [small[0]]), sums)
        for s in range(segments):
            sums.add(s, 2, smalls[s])

    def summed(values, dim):
        mine = lax.psum_scatter(jnp.stack(values), "segment", scatter_dimension=0, tiled=False)
        return lax.psum_scatter(mine, "dp", scatter_dimension=dim, tiled=True)

    t_in = summed([p[0] for p in pieces], 0)
    t_out = summed([p[1] for p in pieces], 0).T
    t_small = summed([p[2] for p in pieces], 1)
    return finish(t_small[:taps], t_small[taps], t_small[taps + 1], t_in, t_out)


def partners(flip, extent=(4, 2, 2, 2)):
    pairs = []
    for index in range(32):
        z, y, x, c = index >> 3, (index >> 2) & 1, (index >> 1) & 1, index & 1
        other = ((z ^ flip[0]) << 3) | ((y ^ flip[1]) << 2) | ((x ^ flip[2]) << 1) | (c ^ flip[3])
        pairs.append((index, other))
    return pairs


def swap(value, z=0, y=0, x=0, c=0):
    return lax.ppermute(value, ("dp", "segment"), partners((z, y, x, c)))


def along_x(value, to_last):
    pairs = [(i, j) for i, j in partners((0, 0, 1, 0)) if (i >> 1) & 1 == (0 if to_last else 1)]
    return lax.ppermute(value, ("dp", "segment"), pairs)


def this_mesh(images, cotangent, kernels, norm_gains, w_in, w_out, scales):
    rank = lax.axis_index("segment")
    core = rank % 2
    chip = rank // 2
    depth = lax.axis_index("dp") // 2
    side = lax.axis_index("dp") % 2
    own_small = parameters(kernels, norm_gains, scales)
    near_small = swap(own_small, c=1)
    near_in, near_out = swap(w_in[0], c=1), swap(w_out[0], c=1)
    small = (own_small, near_small)
    weights = (w_in[0], near_in, w_out[0], near_out)
    zero = jnp.zeros_like(chip)
    sel = jnp.stack([core, 1 - core, chip, core, zero]).astype(jnp.int32)
    sel_first = jnp.stack([core, 1 - core, chip, core, chip]).astype(jnp.int32)
    sel_conv = (jnp.stack([core, zero]).astype(jnp.int32), jnp.stack([core, chip]).astype(jnp.int32))
    cores = core[None].astype(jnp.int32)
    sides = side[None].astype(jnp.int32)
    levels = jnp.stack([depth, depth ^ 1, depth ^ 2, depth ^ 3]).astype(jnp.int32)

    maps = [lax.dynamic_index_in_dim(images, 2 * core + i, 0, keepdims=False) for i in range(2)]
    ends = [lax.dynamic_index_in_dim(cotangent, 2 * core + i, 0, keepdims=False) for i in range(2)]
    firsts, kept = [], []
    for x, chosen in zip(maps, sel_conv):
        firsts.append(conv_norm(chosen, x, small, tuple(k.inv1 for k in kept)))
        kept.append(pair_forward(sel_first if kept else sel, x, firsts[-1], small, weights))
    passed = [along_x(k.y, True) for k in kept]
    parts, starts = [], []
    for x, g in zip(passed, ends):
        parts.append(pair_map(sel, x, g, small, weights))
        starts.append(along_x(parts[-1].g0, False))
    totals = pair_grads(sel, passed, parts)
    grads = pair_back(sel, starts[0], maps[0], firsts[0], kept[0], small, weights)
    grads = pair_back(sel, starts[1], maps[1], firsts[1], kept[1], small, weights, (grads, totals))
    core0, core1 = swap(grads.send0, c=1), swap(grads.send1, c=1)

    def along_y(*pairs):
        across, mine = to_side(sides, *pairs)
        return mine, swap(across, y=1)

    def along_z(mine, got):
        own, *others = to_depths(levels, mine, got)
        return [own] + [swap(v, z=flip) for v, flip in zip(others, (1, 2, 3))]

    low = along_y(brought(grads.keep0), core0, grads.packed)
    own, *others = split_depths(levels, grads.keep1, core1, low[:1])
    parts = [own] + [swap(others[flip - 1], z=flip) for flip in (2, 3, 1)]
    across, mine = join_depths(sides, parts)
    high = [mine, swap(across, y=1)]
    low = along_z(*low)
    own, send = to_core(cores, low + high)
    return final(cores, own, swap(send, c=1), kernels.shape[1])


def solution(mesh):
    in_specs = (
        P("dp", None, None, None),
        P("dp", None, None, None),
        P("segment", None, None),
        P("segment", None),
        P("segment", None, None),
        P("segment", None, None),
        P("segment", None),
    )
    out_specs = (
        P("segment", None, "dp"),
        P("segment", "dp"),
        P("segment", "dp", None),
        P("segment", None, "dp"),
        P("segment", "dp"),
    )
    fits = dict(mesh.shape) == {"dp": 8, "segment": 4}

    def whole(images, *rest):
        local = this_mesh if fits and images.shape[0] == 32 else any_mesh
        return jax.shard_map(local, mesh=mesh, in_specs=in_specs, out_specs=out_specs, check_vma=False)(images, *rest)

    return whole
```

```python
import functools
import types
import jax
import jax.numpy as jnp
from jax import lax
from jax.sharding import PartitionSpec as P
from jax.experimental import pallas as pl
from jax.experimental.pallas import tpu as pltpu

EPS = 1e-06
GELU_C = 0.7978845608028654
GELU_A = 0.044715
LANES = 128
def estimate(microseconds):
    return pl.CostEstimate(flops=int(microseconds * 1.1e9), bytes_accessed=int(microseconds * 3.6e6), transcendentals=0)


LIMIT = 40


def vmem(mebibytes):
    return pltpu.CompilerParams(vmem_limit_bytes=mebibytes * 1024 * 1024)


def zero_borders(pad_ref):
    tiles, rows, width, _ = pad_ref.shape
    for c in range(tiles):
        pad_ref[c, :, 0:8] = jnp.zeros((rows, 8, LANES), jnp.float32)
        pad_ref[c, :, width - 8 :] = jnp.zeros((rows, 8, LANES), jnp.float32)


def conv_norm_body(x_ref, small_ref, xhat_ref, normed_ref, inv_ref, pad_ref, conv_ref):
    rows, cols, channels = x_ref.shape
    tiles = channels // LANES
    for c in range(tiles):
        pad_ref[c, :, 8 : cols + 8] = x_ref[:, :, c * LANES : (c + 1) * LANES].astype(jnp.float32)

    def tile(c, carry):
        lanes = pl.ds(pl.multiple_of(c * LANES, LANES), LANES)

        def strip(w, carry):
            base = pl.multiple_of(w * 8, 8)
            window = pad_ref.at[c, :, pl.ds(base, 24), :]
            acc = [None] * rows
            for q in range(7):
                col = [window[h, 5 + q : 13 + q, :] for h in range(rows)]
                for r in range(7):
                    weight = small_ref[r * 7 + q : r * 7 + q + 1, lanes]
                    for h in range(max(0, 3 - r), min(rows, rows + 3 - r)):
                        term = weight * col[h + r - 3]
                        acc[h] = term if acc[h] is None else acc[h] + term
            for h in range(rows):
                conv_ref[h, pl.ds(base, 8), lanes] = acc[h]
            return carry

        return lax.fori_loop(0, cols // 8, strip, carry)

    lax.fori_loop(0, tiles, tile, 0)

    def norm(h, carry):
        value = conv_ref[pl.ds(h * 2, 2)].reshape(2 * cols, channels)
        mean = jnp.mean(value, axis=1, keepdims=True)
        center = value - mean
        inv = lax.rsqrt(jnp.mean(center * center, axis=1, keepdims=True) + EPS)
        xhat = center * inv
        at = pl.ds(pl.multiple_of(h * 2 * cols, 2 * cols), 2 * cols)
        xhat_ref[at, :] = xhat.astype(jnp.bfloat16)
        normed_ref[at, :] = (xhat * small_ref[TAPS : TAPS + 1, :]).astype(jnp.bfloat16)
        inv_ref[at, :] = jnp.broadcast_to(inv, (2 * cols, LANES))
        return carry

    lax.fori_loop(0, rows // 2, norm, 0, unroll=True)


def pad_shape(rows, cols, channels):
    return pltpu.VMEM((channels // LANES, rows, cols + 16, LANES), jnp.float32)


def in_hbm(arrays):
    return [pltpu.with_memory_space_constraint(a, pltpu.HBM) for a in arrays]


def parameters_kernel(k_ref, gain_ref, scale_ref, out_ref, taps_ref, rows_ref, sems):
    copies = [
        pltpu.make_async_copy(source, target, sems.at[i])
        for i, (source, target) in enumerate(((k_ref, taps_ref), (gain_ref, rows_ref.at[0]), (scale_ref, rows_ref.at[1])))
    ]
    for copy in copies:
        copy.start()
    taps = taps_ref.shape[0]
    out_ref[taps + 2 :, :] = jnp.zeros((out_ref.shape[0] - taps - 2, out_ref.shape[1]), jnp.float32)
    for copy in copies:
        copy.wait()
    for t in range(taps):
        out_ref[t : t + 1, :] = taps_ref[t]
    out_ref[taps : taps + 1, :] = rows_ref[0]
    out_ref[taps + 1 : taps + 2, :] = rows_ref[1]


def parameters(kernels, norm_gains, scales):
    taps, channels = kernels.shape[1:]
    return pl.pallas_call(
        parameters_kernel,
        in_specs=[pl.BlockSpec(memory_space=pl.ANY)] * 3,
        out_shape=jax.ShapeDtypeStruct((56, channels), jnp.float32),
        scratch_shapes=[
            pltpu.VMEM((taps, 1, channels), jnp.float32),
            pltpu.VMEM((2, 1, channels), jnp.float32),
            pltpu.SemaphoreType.DMA((3,)),
        ],
        compiler_params=vmem(LIMIT),
        name="parameters",
        cost_estimate=estimate(0.5),
    )(*in_hbm([kernels.transpose(1, 0, 2), norm_gains, scales]))


def choose_small(r):
    first = r.sel[0] == 0
    own, near = r.own_small[...], r.near_small[...]
    r.small[0] = jnp.where(first, own, near)
    r.small[1] = jnp.where(first, near, own)


def conv_norm_kernel(choices, sel_ref, x_ref, *rest):
    smalls, rest = rest[:choices], rest[choices:]
    xhat_ref, normed_ref, inv_ref, pad_ref, conv_ref, small_ref = rest[-6:]
    active = sel_ref[1] == 0

    @pl.when(active)
    def _():
        zero_borders(pad_ref)
        small_ref[...] = smalls[0][...]
        for k in range(1, choices):

            @pl.when(sel_ref[0] == k)
            def _():
                small_ref[...] = smalls[k][...]

        conv_norm_body(x_ref, small_ref, xhat_ref, normed_ref, inv_ref, pad_ref, conv_ref)


def conv_norm(sel, x, smalls, after=()):
    rows, cols, channels = x.shape
    n = rows * cols
    return pl.pallas_call(
        functools.partial(conv_norm_kernel, len(smalls)),
        in_specs=[pl.BlockSpec(memory_space=pltpu.SMEM)]
        + [pl.BlockSpec(memory_space=pltpu.VMEM)] * (1 + len(smalls))
        + [pl.BlockSpec(memory_space=pl.ANY)] * len(after),
        out_shape=(
            jax.ShapeDtypeStruct((n, channels), jnp.bfloat16),
            jax.ShapeDtypeStruct((n, channels), jnp.bfloat16),
            jax.ShapeDtypeStruct((n, LANES), jnp.float32),
        ),
        scratch_shapes=[
            pad_shape(rows, cols, channels),
            pltpu.VMEM((rows, cols, channels), jnp.float32),
            pltpu.VMEM(smalls[0].shape, jnp.float32),
        ],
        compiler_params=vmem(LIMIT),
        name="conv_norm",
        cost_estimate=estimate(2.0),
    )(sel, x, *smalls, *after)


def copy_chosen(which, sources, target, sem):
    for m, source in enumerate(sources):

        @pl.when(which == m)
        def _():
            pltpu.make_async_copy(source, target, sem).start()

    return lambda: pltpu.make_async_copy(sources[0], target, sem).wait()


def forward_kernel(choices, blocks, sel_ref, x_ref, normed0_ref, small_ref, *rest):
    w_ins, w_outs, rest = rest[:choices], rest[choices : 2 * choices], rest[2 * choices :]
    xs = [x_ref] + list(rest[: blocks - 1])
    xhats, invs, rest = rest[blocks - 1 : 2 * blocks - 2], rest[2 * blocks - 2 : 3 * blocks - 3], rest[3 * blocks - 3 :]
    pres, branches, rest = rest[:blocks], rest[blocks : 2 * blocks], rest[2 * blocks :]
    normed_ref, hid_ref, acc_ref, pad_ref, conv_ref, w_in_ref, w_out_ref, sems = rest
    rows, cols, channels = x_ref.shape
    n = rows * cols
    hidden = w_in_ref.shape[2]
    waits = []
    for s in range(blocks):
        waits.append((
            copy_chosen(sel_ref[s], w_ins, w_in_ref.at[s], sems.at[0, s]),
            copy_chosen(sel_ref[s], w_outs, w_out_ref.at[s], sems.at[1, s]),
        ))
    zero_borders(pad_ref)
    step, sub = 256, 2 * cols
    for s in range(blocks):
        normed = normed0_ref if s == 0 else normed_ref
        waits[s][0]()
        for j in range(hidden // step):
            cut = slice(j * step, (j + 1) * step)
            pre = jnp.dot(normed[...], w_in_ref[s, :, cut], preferred_element_type=jnp.float32)
            for i in range(n // sub):
                p = pre[i * sub : (i + 1) * sub]
                half = 0.5 * p
                hid_ref[i * sub : (i + 1) * sub, :] = (half + half * tanh_arg(p)).astype(jnp.bfloat16)
                pres[s][i * sub : (i + 1) * sub, cut] = p.astype(jnp.bfloat16)
            if j == 0:
                waits[s][1]()
            part = jnp.dot(hid_ref[...], w_out_ref[s, cut, :], preferred_element_type=jnp.float32)
            if j == 0:
                acc_ref[...] = part
            else:
                acc_ref[...] += part
        scale = small_ref[s, TAPS + 1 : TAPS + 2, :]
        for i in range(n // sub):
            branch = acc_ref[i * sub : (i + 1) * sub, :]
            branches[s][i * sub : (i + 1) * sub, :] = branch.astype(jnp.bfloat16)
            if s < blocks - 1:
                x_old = xs[s][2 * i : 2 * i + 2].astype(jnp.float32).reshape(sub, channels)
                xs[s + 1][2 * i : 2 * i + 2] = (x_old + scale * branch).astype(jnp.bfloat16).reshape(2, cols, channels)
        if s < blocks - 1:
            conv_norm_body(xs[s + 1], small_ref.at[s + 1], xhats[s], normed_ref, invs[s], pad_ref, conv_ref)


def forward(sel, x, normed0, small, w_ins, w_outs):
    blocks = small.shape[0]
    rows, cols, channels = x.shape
    n = rows * cols
    hidden = w_ins[0].shape[1]
    out = pl.pallas_call(
        functools.partial(forward_kernel, len(w_ins), blocks),
        in_specs=[pl.BlockSpec(memory_space=pltpu.SMEM)]
        + [pl.BlockSpec(memory_space=pltpu.VMEM)] * 3
        + [pl.BlockSpec(memory_space=pl.ANY)] * (2 * len(w_ins)),
        out_shape=(jax.ShapeDtypeStruct((rows, cols, channels), jnp.bfloat16),) * (blocks - 1)
        + (jax.ShapeDtypeStruct((n, channels), jnp.bfloat16),) * (blocks - 1)
        + (jax.ShapeDtypeStruct((n, LANES), jnp.float32),) * (blocks - 1)
        + (jax.ShapeDtypeStruct((n, hidden), jnp.bfloat16),) * blocks
        + (jax.ShapeDtypeStruct((n, channels), jnp.bfloat16),) * blocks,
        scratch_shapes=[
            pltpu.VMEM((n, channels), jnp.bfloat16),
            pltpu.VMEM((n, 256), jnp.bfloat16),
            pltpu.VMEM((n, channels), jnp.float32),
            pad_shape(rows, cols, channels),
            pltpu.VMEM((rows, cols, channels), jnp.float32),
            pltpu.VMEM((blocks, channels, hidden), jnp.bfloat16),
            pltpu.VMEM((blocks, hidden, channels), jnp.bfloat16),
            pltpu.SemaphoreType.DMA((2, blocks)),
        ],
        compiler_params=vmem(LIMIT),
        name="forward",
        cost_estimate=estimate(15),
    )(sel, x, normed0, small, *in_hbm(w_ins), *in_hbm(w_outs))
    k = blocks - 1
    return out[:k], out[k : 2 * k], out[2 * k : 3 * k], out[3 * k : 3 * k + blocks], out[3 * k + blocks :]


def tanh_arg(x):
    return jnp.tanh(x * (GELU_C + (GELU_C * GELU_A) * (x * x)))


def load_weights(sel_ref, w_ins, w_outs, w_in_ref, w_out_ref, sems):
    for m in range(len(w_ins)):

        @pl.when(sel_ref[0] == m)
        def _():
            pltpu.make_async_copy(w_ins[m], w_in_ref, sems.at[0]).start()
            pltpu.make_async_copy(w_outs[m], w_out_ref, sems.at[1]).start()

    return (
        pltpu.make_async_copy(w_ins[0], w_in_ref, sems.at[0]).wait,
        pltpu.make_async_copy(w_outs[0], w_out_ref, sems.at[1]).wait,
    )


def specs(sel, arrays, choices, after=0):
    return (
        [pl.BlockSpec(memory_space=pltpu.SMEM)]
        + [pl.BlockSpec(memory_space=pltpu.VMEM)] * arrays
        + [pl.BlockSpec(memory_space=pl.ANY)] * (2 * choices + after)
    )


def mlp_back_kernel(choices, after, sel_ref, g_ref, branch_ref, pre_ref, xhat_ref, inv_ref, gain_ref, scale_ref, *rest):
    w_ins, w_outs = rest[:choices], rest[choices : 2 * choices]
    (keep_ref, send_ref, small_ref, gconv_ref,
     gb_ref, nm_ref, hid_ref, gp_ref, acc_ref, w_in_ref, w_out_ref, sems) = rest[2 * choices + after :]
    wait_in, wait_out = load_weights(sel_ref, w_ins, w_outs, w_in_ref, w_out_ref, sems)
    first = sel_ref[1] == 0
    n, channels = g_ref.shape
    hidden = w_in_ref.shape[1]
    step = 256
    sub = 32
    scale_sum = jnp.zeros((8, channels), jnp.float32)
    for i in range(n // sub):
        at = slice(i * sub, (i + 1) * sub)
        g = g_ref[at, :].astype(jnp.float32)
        scale_sum = scale_sum + jnp.sum((g * branch_ref[at, :].astype(jnp.float32)).reshape(sub // 8, 8, channels), axis=0)
        gb_ref[at, :] = (g * scale_ref[...]).astype(jnp.bfloat16)
        nm_ref[at, :] = (xhat_ref[at, :].astype(jnp.float32) * gain_ref[...]).astype(jnp.bfloat16)
    gb_t = gb_ref[...].T
    nm_t = nm_ref[...].T
    wait_in()
    wait_out()
    for j in range(hidden // step):
        cut = slice(j * step, (j + 1) * step)
        gh = lax.dot_general(gb_ref[...], w_out_ref[cut, :], (((1,), (1,)), ((), ())), preferred_element_type=jnp.float32)
        for i in range(n // sub):
            at = slice(i * sub, (i + 1) * sub)
            p = pre_ref[at, cut].astype(jnp.float32)
            sq = p * p
            t = jnp.tanh(p * (GELU_C + (GELU_C * GELU_A) * sq))
            cdf = 0.5 + 0.5 * t
            hid_ref[at, :] = (p * cdf).astype(jnp.bfloat16)
            slope = cdf + (0.5 * p) * (1.0 - t * t) * (GELU_C + (3.0 * GELU_C * GELU_A) * sq)
            gp_ref[at, :] = (gh[at, :] * slope).astype(jnp.bfloat16)
        t_out = jnp.dot(gb_t, hid_ref[...], preferred_element_type=jnp.float32)
        t_in = jnp.dot(nm_t, gp_ref[...], preferred_element_type=jnp.float32)
        keep_ref[:, cut] = jnp.where(first, t_in, t_out).astype(jnp.bfloat16)
        send_ref[:, cut] = jnp.where(first, t_out, t_in).astype(jnp.bfloat16)
        part = lax.dot_general(gp_ref[...], w_in_ref[:, cut], (((1,), (1,)), ((), ())), preferred_element_type=jnp.float32)
        if j == 0:
            acc_ref[...] = part
        else:
            acc_ref[...] += part
    gain_sum = jnp.zeros((8, channels), jnp.float32)
    for i in range(n // sub):
        at = slice(i * sub, (i + 1) * sub)
        gn = acc_ref[at, :]
        xhat = xhat_ref[at, :].astype(jnp.float32)
        gain_sum = gain_sum + jnp.sum((gn * xhat).reshape(sub // 8, 8, channels), axis=0)
        gx = gn * gain_ref[...]
        m1 = jnp.mean(gx, axis=1, keepdims=True)
        m2 = jnp.mean(gx * xhat, axis=1, keepdims=True)
        inv = inv_ref[at, 0:1]
        gconv_ref[at, :] = inv * (gx - m1 - xhat * m2)
    small_ref[0:1, :] = jnp.sum(gain_sum, axis=0, keepdims=True)
    small_ref[1:2, :] = jnp.sum(scale_sum, axis=0, keepdims=True)
    small_ref[2:8, :] = jnp.zeros((6, channels), jnp.float32)


def mlp_back(sel, g, branch, pre, xhat, inv, gain, scale, w_ins, w_outs, after=()):
    n, channels = g.shape
    hidden = w_ins[0].shape[1]
    return pl.pallas_call(
        functools.partial(mlp_back_kernel, len(w_ins), len(after)),
        in_specs=specs(sel, 7, len(w_ins), len(after)),
        out_shape=(
            jax.ShapeDtypeStruct((channels, hidden), jnp.bfloat16),
            jax.ShapeDtypeStruct((channels, hidden), jnp.bfloat16),
            jax.ShapeDtypeStruct((8, channels), jnp.float32),
            jax.ShapeDtypeStruct((n, channels), jnp.float32),
        ),
        scratch_shapes=[
            pltpu.VMEM((n, channels), jnp.bfloat16),
            pltpu.VMEM((n, channels), jnp.bfloat16),
            pltpu.VMEM((n, 256), jnp.bfloat16),
            pltpu.VMEM((n, 256), jnp.bfloat16),
            pltpu.VMEM((n, channels), jnp.float32),
            pltpu.VMEM((channels, hidden), jnp.bfloat16),
            pltpu.VMEM((hidden, channels), jnp.bfloat16),
            pltpu.SemaphoreType.DMA((2,)),
        ],
        compiler_params=vmem(LIMIT),
        name="mlp_back",
        cost_estimate=estimate(2.5),
    )(sel, g, branch, pre, xhat, inv, gain, scale, *in_hbm(w_ins), *in_hbm(w_outs), *after)


SMALL_ROWS = 64
TAPS = 49


def conv_back_kernel(need_map, after, gconv_ref, x_ref, g_ref, k_ref, small_ref, *rest):
    *out_ref, tk_ref, pad_ref, sum_ref, wide_ref, map_ref = rest[after:]
    conv_back_body(gconv_ref, x_ref, g_ref, k_ref, small_ref, out_ref[0] if need_map else None, tk_ref,
                   pad_ref, sum_ref, wide_ref, map_ref)


def conv_back(gconv, x, g, kernel, small, need_map=True, after=()):
    rows, cols, channels = x.shape
    out = (jax.ShapeDtypeStruct((SMALL_ROWS, channels), jnp.float32),)
    if need_map:
        out = (jax.ShapeDtypeStruct((rows, cols, channels), jnp.bfloat16),) + out
    return pl.pallas_call(
        functools.partial(conv_back_kernel, need_map, len(after)),
        in_specs=[pl.BlockSpec(memory_space=pltpu.VMEM)] * 5 + [pl.BlockSpec(memory_space=pl.ANY)] * len(after),
        out_shape=out,
        scratch_shapes=[
            pad_shape(rows, cols, channels),
            pltpu.VMEM((cols // 8, TAPS, 8, LANES), jnp.float32),
            pltpu.VMEM((rows, cols, channels), jnp.float32),
            pltpu.VMEM((rows, cols, channels), jnp.float32),
        ],
        compiler_params=vmem(LIMIT),
        name="conv_back",
        cost_estimate=estimate(3.4 if need_map else 1.6),
    )(gconv, x, g, kernel, small, *after)


def small_call(kernel, name, outs, *args, scratch=(), after=()):
    used = len(args)

    def body(*refs):
        kernel(*refs[:used], *refs[used + len(after) :])

    return pl.pallas_call(
        body,
        in_specs=[pl.BlockSpec(memory_space=pltpu.SMEM)]
        + [pl.BlockSpec(memory_space=pltpu.VMEM)] * (used - 1)
        + [pl.BlockSpec(memory_space=pl.ANY)] * len(after),
        out_shape=tuple(out_struct(*o) for o in outs),
        scratch_shapes=list(scratch),
        compiler_params=vmem(LIMIT),
        name=name,
        cost_estimate=estimate(0.7),
    )(*args, *after)


def conv_back_body(gconv_ref, x_ref, g_ref, small_ref, sums8_ref, out_ref, tk_ref, pad_ref, sum_ref, wide_ref, map_ref):
    rows, cols, channels = x_ref.shape
    tiles = channels // LANES
    zero_borders(pad_ref)
    for c in range(tiles):
        pad_ref[c, :, 8 : cols + 8] = gconv_ref[:, c * LANES : (c + 1) * LANES].reshape(rows, cols, LANES)

    for h in range(rows):
        wide_ref[h] = x_ref[h].astype(jnp.float32)

    def tile(c, carry):
        lanes = pl.ds(pl.multiple_of(c * LANES, LANES), LANES)

        def strip(w, carry):
            base = pl.multiple_of(w * 8, 8)
            window = pad_ref.at[c, :, pl.ds(base, 24), :]
            xs = [wide_ref[h, pl.ds(base, 8), lanes] for h in range(rows)]
            acc = [None] * rows
            for q in range(7):
                col = [window[h, 11 - q : 19 - q, :] for h in range(rows)]
                for r in range(7):
                    tap = r * 7 + q
                    if out_ref is not None:
                        weight = small_ref[tap : tap + 1, lanes]
                    total = None
                    for h in range(max(0, r - 3), min(rows, rows + r - 3)):
                        shifted = col[h + 3 - r]
                        term = xs[h] * shifted
                        total = term if total is None else total + term
                        if out_ref is not None:
                            moved = weight * shifted
                            acc[h] = moved if acc[h] is None else acc[h] + moved
                    sum_ref[w, tap] = total
            if out_ref is not None:
                for h in range(rows):
                    map_ref[h, pl.ds(base, 8), lanes] = acc[h]
            return carry

        lax.fori_loop(0, cols // 8, strip, 0)
        tk_ref[0:TAPS, lanes] = jnp.sum(sum_ref[0] + sum_ref[1], axis=1)
        return carry

    lax.fori_loop(0, tiles, tile, 0)
    if out_ref is not None:
        for h in range(rows):
            out_ref[h] = (g_ref[h].astype(jnp.float32) + map_ref[h]).astype(jnp.bfloat16)
    tk_ref[TAPS : TAPS + 2, :] = sums8_ref[0:2, :]
    tk_ref[TAPS + 2 :, :] = jnp.zeros((SMALL_ROWS - TAPS - 2, channels), jnp.float32)


def conv_map_body(gconv_ref, g_ref, small_ref, out_ref, pad_ref, map_ref):
    rows, cols, channels = g_ref.shape
    tiles = channels // LANES
    zero_borders(pad_ref)
    for c in range(tiles):
        pad_ref[c, :, 8 : cols + 8] = gconv_ref[:, c * LANES : (c + 1) * LANES].reshape(rows, cols, LANES)

    def tile(c, carry):
        lanes = pl.ds(pl.multiple_of(c * LANES, LANES), LANES)

        def strip(w, carry):
            base = pl.multiple_of(w * 8, 8)
            window = pad_ref.at[c, :, pl.ds(base, 24), :]
            acc = [None] * rows
            for q in range(7):
                col = [window[h, 11 - q : 19 - q, :] for h in range(rows)]
                for r in range(7):
                    weight = small_ref[r * 7 + q : r * 7 + q + 1, lanes]
                    for h in range(max(0, r - 3), min(rows, rows + r - 3)):
                        term = weight * col[h + 3 - r]
                        acc[h] = term if acc[h] is None else acc[h] + term
            for h in range(rows):
                map_ref[h, pl.ds(base, 8), lanes] = acc[h]
            return carry

        return lax.fori_loop(0, cols // 8, strip, carry)

    lax.fori_loop(0, tiles, tile, 0)
    for h in range(rows):
        out_ref[h] = (g_ref[h].astype(jnp.float32) + map_ref[h]).astype(jnp.bfloat16)


def mlp_back_map_body(g_ref, branch_ref, pre_ref, xhat_ref, inv_ref, small_ref, w_in_ref, w_out_ref,
                      sums8_ref, gconv_ref, gb_ref, nm_ref, hid_ref, gp_ref, acc_ref, ready):
    rows, cols, channels = g_ref.shape
    n = rows * cols
    hidden = w_in_ref.shape[1]
    step = 256
    sub = 2 * cols
    gain = small_ref[TAPS : TAPS + 1, :]
    scale = small_ref[TAPS + 1 : TAPS + 2, :]
    scale_sum = jnp.zeros((8, channels), jnp.float32)
    for i in range(n // sub):
        at = slice(i * sub, (i + 1) * sub)
        g = g_ref[2 * i : 2 * i + 2].astype(jnp.float32).reshape(sub, channels)
        scale_sum = scale_sum + jnp.sum((g * branch_ref[at, :].astype(jnp.float32)).reshape(sub // 8, 8, channels), axis=0)
        gb_ref[at, :] = (g * scale).astype(jnp.bfloat16)
        nm_ref[at, :] = (xhat_ref[at, :].astype(jnp.float32) * gain).astype(jnp.bfloat16)
    ready("gb", "nm")
    for j in range(hidden // step):
        cut = slice(j * step, (j + 1) * step)
        gh = lax.dot_general(gb_ref[...], w_out_ref[cut, :], (((1,), (1,)), ((), ())), preferred_element_type=jnp.float32)
        for i in range(n // sub):
            at = slice(i * sub, (i + 1) * sub)
            p = pre_ref[at, cut].astype(jnp.float32)
            sq = p * p
            t = jnp.tanh(p * (GELU_C + (GELU_C * GELU_A) * sq))
            cdf = 0.5 + 0.5 * t
            hid_ref[at, cut] = (p * cdf).astype(jnp.bfloat16)
            slope = cdf + (0.5 * p) * (1.0 - t * t) * (GELU_C + (3.0 * GELU_C * GELU_A) * sq)
            gp_ref[at, cut] = (gh[at, :] * slope).astype(jnp.bfloat16)
        part = lax.dot_general(gp_ref[:, cut], w_in_ref[:, cut], (((1,), (1,)), ((), ())), preferred_element_type=jnp.float32)
        if j == 0:
            acc_ref[...] = part
        else:
            acc_ref[...] += part
    ready("hid", "gp")
    gain_sum = jnp.zeros((8, channels), jnp.float32)
    for i in range(n // sub):
        at = slice(i * sub, (i + 1) * sub)
        gn = acc_ref[at, :]
        xhat = xhat_ref[at, :].astype(jnp.float32)
        gain_sum = gain_sum + jnp.sum((gn * xhat).reshape(sub // 8, 8, channels), axis=0)
        gx = gn * gain
        m1 = jnp.mean(gx, axis=1, keepdims=True)
        m2 = jnp.mean(gx * xhat, axis=1, keepdims=True)
        gconv_ref[at, :] = inv_ref[at, 0:1] * (gx - m1 - xhat * m2)
    sums8_ref[0:1, :] = jnp.sum(gain_sum, axis=0, keepdims=True)
    sums8_ref[1:2, :] = jnp.sum(scale_sum, axis=0, keepdims=True)
    sums8_ref[2:8, :] = jnp.zeros((6, channels), jnp.float32)
    ready("gconv", "sums")


def mlp_back_body(first, g_ref, branch_ref, pre_ref, xhat_ref, inv_ref, small_ref, wait_in, wait_out, w_in_ref, w_out_ref,
                  keep_ref, send_ref, sums8_ref, gconv_ref, gb_ref, nm_ref, hid_ref, gp_ref, acc_ref, before=None):
    rows, cols, channels = g_ref.shape
    n = rows * cols
    hidden = w_in_ref.shape[1]
    step = 256
    sub = 2 * cols
    gain = small_ref[TAPS : TAPS + 1, :]
    scale = small_ref[TAPS + 1 : TAPS + 2, :]
    scale_sum = jnp.zeros((8, channels), jnp.float32)
    for i in range(n // sub):
        at = slice(i * sub, (i + 1) * sub)
        g = g_ref[2 * i : 2 * i + 2].astype(jnp.float32).reshape(sub, channels)
        scale_sum = scale_sum + jnp.sum((g * branch_ref[at, :].astype(jnp.float32)).reshape(sub // 8, 8, channels), axis=0)
        gb_ref[at, :] = (g * scale).astype(jnp.bfloat16)
        nm_ref[at, :] = (xhat_ref[at, :].astype(jnp.float32) * gain).astype(jnp.bfloat16)
    gb_t = gb_ref[...].T
    nm_t = nm_ref[...].T
    wait_out()
    for j in range(hidden // step):
        cut = slice(j * step, (j + 1) * step)
        gh = lax.dot_general(gb_ref[...], w_out_ref[cut, :], (((1,), (1,)), ((), ())), preferred_element_type=jnp.float32)
        for i in range(n // sub):
            at = slice(i * sub, (i + 1) * sub)
            p = pre_ref[at, cut].astype(jnp.float32)
            sq = p * p
            t = jnp.tanh(p * (GELU_C + (GELU_C * GELU_A) * sq))
            cdf = 0.5 + 0.5 * t
            hid_ref[at, :] = (p * cdf).astype(jnp.bfloat16)
            slope = cdf + (0.5 * p) * (1.0 - t * t) * (GELU_C + (3.0 * GELU_C * GELU_A) * sq)
            gp_ref[at, :] = (gh[at, :] * slope).astype(jnp.bfloat16)
        t_out = jnp.dot(gb_t, hid_ref[...], preferred_element_type=jnp.float32)
        t_in = jnp.dot(nm_t, gp_ref[...], preferred_element_type=jnp.float32)
        t_keep = jnp.where(first, t_in, t_out)
        t_send = jnp.where(first, t_out, t_in)
        if before is not None:
            if j == 0:
                old_keep, old_send = before()
            t_keep = t_keep + old_keep[:, cut].astype(jnp.float32)
            t_send = t_send + old_send[:, cut].astype(jnp.float32)
        keep_ref[:, cut] = t_keep.astype(jnp.bfloat16)
        send_ref[:, cut] = t_send.astype(jnp.bfloat16)
        if j == 0:
            wait_in()
        part = lax.dot_general(gp_ref[...], w_in_ref[:, cut], (((1,), (1,)), ((), ())), preferred_element_type=jnp.float32)
        if j == 0:
            acc_ref[...] = part
        else:
            acc_ref[...] += part
    gain_sum = jnp.zeros((8, channels), jnp.float32)
    for i in range(n // sub):
        at = slice(i * sub, (i + 1) * sub)
        gn = acc_ref[at, :]
        xhat = xhat_ref[at, :].astype(jnp.float32)
        gain_sum = gain_sum + jnp.sum((gn * xhat).reshape(sub // 8, 8, channels), axis=0)
        gx = gn * gain
        m1 = jnp.mean(gx, axis=1, keepdims=True)
        m2 = jnp.mean(gx * xhat, axis=1, keepdims=True)
        gconv_ref[at, :] = inv_ref[at, 0:1] * (gx - m1 - xhat * m2)
    sums8_ref[0:1, :] = jnp.sum(gain_sum, axis=0, keepdims=True)
    sums8_ref[1:2, :] = jnp.sum(scale_sum, axis=0, keepdims=True)
    sums8_ref[2:8, :] = jnp.zeros((6, channels), jnp.float32)


def out_struct(shape, dtype, by_hand=False):
    return pltpu.HBM(shape, dtype) if by_hand else jax.ShapeDtypeStruct(shape, dtype)


def named_call(name, body, ins, outs, scratch, cost):
    names = list(ins) + list(outs) + list(scratch)
    spaces = {"v": pltpu.VMEM, "s": pltpu.SMEM, "a": pl.ANY, "h": pl.ANY}

    def kernel(*refs):
        body(types.SimpleNamespace(**dict(zip(names, refs))))

    args = [pltpu.with_memory_space_constraint(a, pltpu.HBM) if kind == "h" else a for a, kind in ins.values()]
    result = pl.pallas_call(
        kernel,
        in_specs=[pl.BlockSpec(memory_space=spaces[kind]) for _, kind in ins.values()],
        out_specs=tuple(pl.BlockSpec(memory_space=pl.ANY if len(o) > 2 else pltpu.VMEM) for o in outs.values()),
        out_shape=tuple(out_struct(*o) for o in outs.values()),
        scratch_shapes=list(scratch.values()),
        compiler_params=vmem(LIMIT),
        name=name,
        cost_estimate=estimate(cost),
    )(*args)
    return types.SimpleNamespace(**dict(zip(outs, result)))


def mlp_body(normed_ref, wait_in, wait_out, w_in_ref, w_out_ref, pre_ref, hid_ref, acc_ref):
    n = normed_ref.shape[0]
    hidden = w_in_ref.shape[1]
    step, sub = 256, 32
    wait_in()
    for j in range(hidden // step):
        cut = slice(j * step, (j + 1) * step)
        pre = jnp.dot(normed_ref[...], w_in_ref[:, cut], preferred_element_type=jnp.float32)
        for i in range(n // sub):
            p = pre[i * sub : (i + 1) * sub]
            half = 0.5 * p
            hid_ref[i * sub : (i + 1) * sub, :] = (half + half * tanh_arg(p)).astype(jnp.bfloat16)
            pre_ref[i * sub : (i + 1) * sub, cut] = p.astype(jnp.bfloat16)
        if j == 0:
            wait_out()
        part = jnp.dot(hid_ref[...], w_out_ref[cut, :], preferred_element_type=jnp.float32)
        if j == 0:
            acc_ref[...] = part
        else:
            acc_ref[...] += part


def residual_body(x_ref, small_ref, acc_ref, branch_ref, y_ref):
    rows, cols, channels = x_ref.shape
    scale = small_ref[TAPS + 1 : TAPS + 2, :]
    sub = 2 * cols
    for i in range(rows // 2):
        branch = acc_ref[i * sub : (i + 1) * sub, :]
        branch_ref[i * sub : (i + 1) * sub, :] = branch.astype(jnp.bfloat16)
        if y_ref is not None:
            old = x_ref[2 * i : 2 * i + 2].astype(jnp.float32).reshape(sub, channels)
            y_ref[2 * i : 2 * i + 2] = (old + scale * branch).astype(jnp.bfloat16).reshape(2, cols, channels)


def small_ins(pair):
    return {"own_small": (pair[0], "v"), "near_small": (pair[1], "v")}


def small_scratch(pair):
    return {"small": pltpu.VMEM((2,) + pair[0].shape, jnp.float32)}


def weight_ins(pair):
    return {k: (v, "h") for k, v in zip(("own_in", "near_in", "own_out", "near_out"), pair)}


def weight_scratch(blocks, channels, hidden):
    return {
        "w_in": pltpu.VMEM((blocks, channels, hidden), jnp.bfloat16),
        "w_out": pltpu.VMEM((blocks, hidden, channels), jnp.bfloat16),
        "w_sem": pltpu.SemaphoreType.DMA((2, blocks)),
    }


def start_weights(r, slot, block, out_first=False):
    def start(k, own, near, target):
        return copy_chosen(r.sel[block], (own, near), target.at[slot], r.w_sem.at[k, slot])

    if out_first:
        wait_out = start(1, r.own_out, r.near_out, r.w_out)
        return start(0, r.own_in, r.near_in, r.w_in), wait_out
    return start(0, r.own_in, r.near_in, r.w_in), start(1, r.own_out, r.near_out, r.w_out)


def pair_forward(sel, x, first, small, weights):
    rows, cols, channels = x.shape
    n, hidden = rows * cols, weights[0].shape[1]
    bf16, f32 = jnp.bfloat16, jnp.float32

    def body(r):
        @pl.when(r.sel[4] == 0)
        def _():
            low, high = start_weights(r, 0, 0), []

            def low_in():
                low[0]()
                high.extend(start_weights(r, 1, 1))

            choose_small(r)
            zero_borders(r.pad)
            mlp_body(r.normed0, low_in, low[1], r.w_in.at[0], r.w_out.at[0], r.pre0, r.hid, r.acc)
            residual_body(r.x, r.small.at[0], r.acc, r.branch0, r.x1)
            conv_norm_body(r.x1, r.small.at[1], r.xhat1, r.normed, r.inv1, r.pad, r.conv)
            mlp_body(r.normed, *high, r.w_in.at[1], r.w_out.at[1], r.pre1, r.hid, r.acc)
            residual_body(r.x1, r.small.at[1], r.acc, r.branch1, r.y)

    return named_call(
        "pair_forward", body,
        {"sel": (sel, "s"), "x": (x, "v"), "normed0": (first[1], "v"), **small_ins(small), **weight_ins(weights)},
        {"y": (x.shape, bf16), "x1": (x.shape, bf16), "xhat1": ((n, channels), bf16), "inv1": ((n, LANES), f32),
         "pre0": ((n, hidden), bf16), "pre1": ((n, hidden), bf16),
         "branch0": ((n, channels), bf16), "branch1": ((n, channels), bf16)},
        {"normed": pltpu.VMEM((n, channels), bf16), "hid": pltpu.VMEM((n, 256), bf16), "acc": pltpu.VMEM((n, channels), f32),
         "pad": pad_shape(rows, cols, channels), "conv": pltpu.VMEM((rows, cols, channels), f32),
         **weight_scratch(2, channels, hidden), **small_scratch(small)},
        7.5,
    )


def back_scratch(n, channels):
    bf16, f32 = jnp.bfloat16, jnp.float32
    return {"gb": pltpu.VMEM((n, channels), bf16), "nm": pltpu.VMEM((n, channels), bf16),
            "hid": pltpu.VMEM((n, 256), bf16), "gp": pltpu.VMEM((n, 256), bf16), "acc": pltpu.VMEM((n, channels), f32)}


def back_temps(r):
    return r.gb, r.nm, r.hid, r.gp, r.acc


GRADS = ("keep0", "send0", "keep1", "send1")
FACTORS = ("gb", "nm", "hid", "gp", "gconv", "sums")


def factor_shapes(n, channels, hidden):
    bf16, f32 = jnp.bfloat16, jnp.float32
    one = {"gb": ((n, channels), bf16), "nm": ((n, channels), bf16), "hid": ((n, hidden), bf16), "gp": ((n, hidden), bf16),
           "gconv": ((n, channels), f32), "sums": ((8, channels), f32)}
    return {name + str(k): one[name] for k in (0, 1) for name in FACTORS}


def pair_map(sel, x, g, small, weights):
    rows, cols, channels = x.shape
    n, hidden = rows * cols, weights[0].shape[1]
    bf16, f32 = jnp.bfloat16, jnp.float32
    shapes = factor_shapes(n, channels, hidden)
    saved = {**shapes, "x1": (x.shape, bf16)}
    order = list(saved)

    def body(r):
        @pl.when(r.sel[2] == 1)
        def _():
            def copy_out(name):
                return pltpu.make_async_copy(getattr(r, "v_" + name), getattr(r, name), r.s_sem.at[order.index(name)])

            low, high = start_weights(r, 0, 0), start_weights(r, 1, 1)
            choose_small(r)
            zero_borders(r.pad)
            s0, s1 = r.small.at[0], r.small.at[1]
            conv_norm_body(r.x, s0, r.xhat0, r.normed, r.inv0, r.pad, r.conv)
            mlp_body(r.normed, *low, r.w_in.at[0], r.w_out.at[0], r.pre0, r.hid, r.acc)
            residual_body(r.x, s0, r.acc, r.branch0, r.v_x1)
            copy_out("x1").start()
            conv_norm_body(r.v_x1, s1, r.xhat1, r.normed, r.inv1, r.pad, r.conv)
            mlp_body(r.normed, *high, r.w_in.at[1], r.w_out.at[1], r.pre1, r.hid, r.acc)
            residual_body(r.v_x1, s1, r.acc, r.branch1, None)

            def ready(k):
                def start(*names):
                    for name in names:
                        copy_out(name + str(k)).start()

                return start

            mlp_back_map_body(r.g, r.branch1, r.pre1, r.xhat1, r.inv1, s1, r.w_in.at[1], r.w_out.at[1],
                              r.v_sums1, r.v_gconv1, r.v_gb1, r.v_nm1, r.v_hid1, r.v_gp1, r.acc, ready(1))
            conv_map_body(r.v_gconv1, r.g, s1, r.g1, r.pad, r.conv)
            mlp_back_map_body(r.g1, r.branch0, r.pre0, r.xhat0, r.inv0, s0, r.w_in.at[0], r.w_out.at[0],
                              r.v_sums0, r.v_gconv0, r.v_gb0, r.v_nm0, r.v_hid0, r.v_gp0, r.acc, ready(0))
            conv_map_body(r.v_gconv0, r.g1, s0, r.g0, r.pad, r.conv)
            for name in order:
                copy_out(name).wait()

    return named_call(
        "pair_map", body,
        {"sel": (sel, "s"), "x": (x, "v"), "g": (g, "v"), **small_ins(small), **weight_ins(weights)},
        {"g0": (x.shape, bf16), **{name: shape + (True,) for name, shape in saved.items()}},
        {**{"v_" + name: pltpu.VMEM(*shape) for name, shape in saved.items()},
         "s_sem": pltpu.SemaphoreType.DMA((len(order),)),
         "g1": pltpu.VMEM(x.shape, bf16),
         "xhat0": pltpu.VMEM((n, channels), bf16), "xhat1": pltpu.VMEM((n, channels), bf16),
         "inv0": pltpu.VMEM((n, LANES), f32), "inv1": pltpu.VMEM((n, LANES), f32),
         "pre0": pltpu.VMEM((n, hidden), bf16), "pre1": pltpu.VMEM((n, hidden), bf16),
         "branch0": pltpu.VMEM((n, channels), bf16), "branch1": pltpu.VMEM((n, channels), bf16),
         "normed": pltpu.VMEM((n, channels), bf16), "hid": pltpu.VMEM((n, 256), bf16), "acc": pltpu.VMEM((n, channels), f32),
         "pad": pad_shape(rows, cols, channels), "conv": pltpu.VMEM((rows, cols, channels), f32),
         **weight_scratch(2, channels, hidden), **small_scratch(small)},
        12,
    )


def pair_grads(sel, xs, parts):
    rows, cols, channels = xs[0].shape
    n, hidden = rows * cols, parts[0].hid0.shape[1]
    bf16, f32 = jnp.bfloat16, jnp.float32
    shapes = factor_shapes(n, channels, hidden)
    order = list(shapes) + ["x1"]

    def body(r):
        @pl.when(r.sel[2] == 1)
        def _():
            def copy_out(k):
                return pltpu.make_async_copy(r.grads.at[k], getattr(r, GRADS[k]), r.o_sem.at[k])

            copies = {}
            for k in (1, 0):
                for name in FACTORS + (("x1",) if k else ()):
                    full = name + str(k) if name != "x1" else name
                    for i in range(2):
                        copies[full, i] = pltpu.make_async_copy(
                            getattr(r, "i%d_%s" % (i, full)), getattr(r, "v_" + full).at[i], r.s_sem.at[i, order.index(full)]
                        )
                        copies[full, i].start()
            first = r.sel[3] == 0
            for k in (1, 0):
                gb, nm, hid, gp = (getattr(r, "v_%s%d" % (name, k)) for name in FACTORS[:4])
                keep, send = r.grads.at[2 * k], r.grads.at[2 * k + 1]
                for name in FACTORS + (("x1",) if k else ()):
                    for i in range(2):
                        copies[name + str(k) if name != "x1" else name, i].wait()
                gb_t = gb[...].reshape(2 * n, channels).T
                nm_t = nm[...].reshape(2 * n, channels).T
                for j in range(hidden // 256):
                    cut = slice(j * 256, (j + 1) * 256)
                    t_out = jnp.dot(gb_t, hid[:, :, cut].reshape(2 * n, 256), preferred_element_type=f32)
                    t_in = jnp.dot(nm_t, gp[:, :, cut].reshape(2 * n, 256), preferred_element_type=f32)
                    keep[:, cut] = jnp.where(first, t_in, t_out).astype(bf16)
                    send[:, cut] = jnp.where(first, t_out, t_in).astype(bf16)
                copy_out(2 * k).start()
                copy_out(2 * k + 1).start()
                out = getattr(r, "small%d" % k)
                for i in range(2):
                    x = r.v_x1.at[i] if k else getattr(r, "x_%d" % i)
                    gconv, sums = getattr(r, "v_gconv%d" % k).at[i], getattr(r, "v_sums%d" % k).at[i]
                    target = out if i == 0 else r.tk
                    conv_back_body(gconv, x, None, None, sums, None, target, r.pad, r.sum, r.wide, None)
                out[...] += r.tk[...]
            for k in range(4):
                copy_out(k).wait()

    ins = {"sel": (sel, "s")}
    for i in range(2):
        ins["x_%d" % i] = (xs[i], "v")
        ins.update({"i%d_%s" % (i, name): (getattr(parts[i], name), "h") for name in order})
    grad = ((channels, hidden), bf16)
    small_out = ((SMALL_ROWS, channels), f32)
    scratch = {"v_" + name: pltpu.VMEM((2,) + shape, dtype) for name, (shape, dtype) in shapes.items()}
    return named_call(
        "pair_grads", body, ins,
        {**{name: grad + (True,) for name in GRADS}, "small0": small_out, "small1": small_out},
        {**scratch, "grads": pltpu.VMEM((4, channels, hidden), bf16), "o_sem": pltpu.SemaphoreType.DMA((4,)), "v_x1": pltpu.VMEM((2,) + xs[0].shape, bf16), "s_sem": pltpu.SemaphoreType.DMA((2, len(order))),
         "pad": pad_shape(rows, cols, channels), "sum": pltpu.VMEM((cols // 8, TAPS, 8, LANES), f32),
         "wide": pltpu.VMEM(xs[0].shape, f32), "tk": pltpu.VMEM((SMALL_ROWS, channels), f32)},
        10,
    )


def pair_back(sel, g, x, first, kept, small, weights, before=None, after=()):
    rows, cols, channels = g.shape
    n, hidden = rows * cols, weights[0].shape[1]
    bf16, f32 = jnp.bfloat16, jnp.float32

    def body(r):
        def copy_old(k):
            return copy_chosen(r.sel[2], (getattr(r, "a_" + GRADS[k]), getattr(r, "p_" + GRADS[k])), r.olds.at[k], r.o_sem.at[k])

        def copy_out(k, source):
            return pltpu.make_async_copy(source, getattr(r, GRADS[k]), r.s_sem.at[k])

        @pl.when(r.sel[2] == 0)
        def _():
            core = r.sel[3] == 0
            high, waits = start_weights(r, 1, 1, True), {}
            if before is not None:
                waits = {k: copy_old(k) for k in (2, 3)}
            low = []

            def high_out():
                high[1]()
                low.extend(start_weights(r, 0, 0, True))
                if before is not None:
                    waits.update({k: copy_old(k) for k in (0, 1)})

            choose_small(r)
            s0, s1 = r.small.at[0], r.small.at[1]

            def old(k):
                def both():
                    waits[2 * k]()
                    waits[2 * k + 1]()
                    return r.olds.at[2 * k], r.olds.at[2 * k + 1]

                return both if before is not None else None

            mlp_back_body(core, r.g, r.branch1, r.pre1, r.xhat1, r.inv1, s1, high[0], high_out, r.w_in.at[1], r.w_out.at[1],
                          r.grads.at[2], r.grads.at[3], r.sums8, r.gconv, *back_temps(r), before=old(1))
            copy_out(2, r.grads.at[2]).start()
            copy_out(3, r.grads.at[3]).start()
            conv_back_body(r.gconv, r.x1, r.g, s1, r.sums8, r.g1, r.small1, r.pad, r.sum, r.wide, r.map)
            mlp_back_body(core, r.g1, r.branch0, r.pre0, r.xhat0, r.inv0, s0, *low, r.w_in.at[0], r.w_out.at[0],
                          r.grads.at[0], r.grads.at[1], r.sums8, r.gconv, *back_temps(r), before=old(0))
            copy_out(0, r.grads.at[0]).start()
            copy_out(1, r.grads.at[1]).start()
            conv_back_body(r.gconv, r.x, None, None, r.sums8, None, r.small0, r.pad, r.sum, r.wide, None)
            if before is not None:
                r.small0[...] += r.a_small0[...]
                r.small1[...] += r.a_small1[...]
                r.packed[...] = jnp.concatenate([r.small0[...], r.small1[...]], axis=0).T.astype(bf16)
            for k in range(4):
                copy_out(k, r.grads.at[k]).wait()

        if before is not None:

            @pl.when(r.sel[2] == 1)
            def _():
                waits = [copy_old(k) for k in range(4)]
                r.packed[...] = jnp.concatenate([r.p_small0[...], r.p_small1[...]], axis=0).T.astype(bf16)
                for k, wait in enumerate(waits):
                    wait()
                    copy_out(k, r.olds.at[k]).start()
                for k in range(4):
                    copy_out(k, r.olds.at[k]).wait()

    ins = {"sel": (sel, "s"), "g": (g, "v"), "x": (x, "v"), "x1": (kept.x1, "v"),
           "branch1": (kept.branch1, "v"), "pre1": (kept.pre1, "v"), "xhat1": (kept.xhat1, "v"), "inv1": (kept.inv1, "v"),
           "branch0": (kept.branch0, "v"), "pre0": (kept.pre0, "v"), "xhat0": (first[0], "v"), "inv0": (first[2], "v"),
           **small_ins(small), **weight_ins(weights)}
    grad = ((channels, hidden), bf16)
    small_out = ((SMALL_ROWS, channels), f32)
    outs = {name: grad + (True,) for name in GRADS}
    scratch = {"grads": pltpu.VMEM((4, channels, hidden), bf16), "s_sem": pltpu.SemaphoreType.DMA((4,)), "g1": pltpu.VMEM(g.shape, bf16), "sums8": pltpu.VMEM((8, channels), f32), "gconv": pltpu.VMEM((n, channels), f32),
               "pad": pad_shape(rows, cols, channels), "sum": pltpu.VMEM((cols // 8, TAPS, 8, LANES), f32),
               "wide": pltpu.VMEM(x.shape, f32), "map": pltpu.VMEM(x.shape, f32),
               **back_scratch(n, channels), **weight_scratch(2, channels, hidden), **small_scratch(small)}
    if before is None:
        outs.update({"small0": small_out, "small1": small_out})
    else:
        for prefix, part in zip("ap", before):
            ins.update({prefix + "_" + name: (getattr(part, name), "h") for name in GRADS})
            ins.update({prefix + "_" + name: (getattr(part, name), "v") for name in ("small0", "small1")})
        outs["packed"] = ((channels, 2 * SMALL_ROWS), bf16)
        scratch.update({"small0": pltpu.VMEM(*small_out), "small1": pltpu.VMEM(*small_out),
                        "olds": pltpu.VMEM((4, channels, hidden), bf16), "o_sem": pltpu.SemaphoreType.DMA((4,))})
    ins.update({"after%d" % k: (v, "a") for k, v in enumerate(after)})
    return named_call("pair_back", body, ins, outs, scratch, 9)


def brought_kernel(source_ref, out_ref, sem):
    copy = pltpu.make_async_copy(source_ref, out_ref, sem)
    copy.start()
    copy.wait()


def brought(value):
    return pl.pallas_call(
        brought_kernel,
        in_specs=[pl.BlockSpec(memory_space=pl.ANY)],
        out_shape=jax.ShapeDtypeStruct(value.shape, value.dtype),
        scratch_shapes=[pltpu.SemaphoreType.DMA(())],
        compiler_params=vmem(LIMIT),
        name="brought",
        cost_estimate=estimate(1.1),
    )(pltpu.with_memory_space_constraint(value, pltpu.HBM))


def add(a, b):
    return a.astype(jnp.float32) + b.astype(jnp.float32)


def side_kernel(sel_ref, keep_ref, got_ref, *refs):
    *small_ref, across_ref, mine_ref = refs
    side = sel_ref[0]
    levels, _, _, hidden = keep_ref.shape
    for level in range(levels):
        for out_ref, which in ((across_ref, 1 - side), (mine_ref, side)):
            out_ref[level, :, :hidden] = add(keep_ref[level, which], got_ref[level, which]).astype(jnp.bfloat16)
            if small_ref:
                out_ref[level, :, hidden:] = small_ref[0][level, which]


def to_side(side, *arrays):
    arrays = [v.reshape(4, 2, v.shape[0] // 8, v.shape[1]) for v in arrays]
    width = sum(v.shape[3] for v in arrays[1:])
    out = ((4, arrays[0].shape[2], width), jnp.bfloat16)
    return small_call(side_kernel, "to_side", (out, out), side, *arrays)


def depth_kernel(sel_ref, mine_ref, got_ref, *out_refs):
    for k, out_ref in enumerate(out_refs):
        out_ref[...] = add(mine_ref[sel_ref[k]], got_ref[sel_ref[k]]).astype(jnp.bfloat16)


def to_depths(levels, mine, got, after=()):
    return small_call(depth_kernel, "to_depths", ((mine.shape[1:], jnp.bfloat16),) * 4, levels, mine, got, after=after)


def split_kernel(sel_ref, keep_ref, got_ref, *out_refs):
    for k, out_ref in enumerate(out_refs):
        for side in range(2):
            out_ref[side] = add(keep_ref[sel_ref[k], side], got_ref[sel_ref[k], side]).astype(jnp.bfloat16)


def split_depths(levels, keep, got, after=()):
    keep, got = (v.reshape(4, 2, v.shape[0] // 8, v.shape[1]) for v in (keep, got))
    outs = ((keep.shape[1:], jnp.bfloat16),) * 4
    return small_call(split_kernel, "split_depths", outs, levels, keep, got, after=after)


def join_kernel(sel_ref, a_ref, b_ref, c_ref, d_ref, across_ref, mine_ref):
    side = sel_ref[0]
    for out_ref, which in ((across_ref, 1 - side), (mine_ref, side)):
        out_ref[...] = (add(a_ref[which], b_ref[which]) + add(c_ref[which], d_ref[which])).astype(out_ref.dtype)


def join_depths(side, parts):
    shape = parts[0].shape[1:]
    return small_call(join_kernel, "join_depths", ((shape, jnp.bfloat16), (shape, jnp.float32)), side, *parts)


def core_kernel(sel_ref, *refs):
    *parts, own_ref, send_ref = refs
    hidden = parts[-1].shape[1]
    a, b, c, d, e, f = parts
    low, high = add(a[...], b[...]) + add(c[...], d[...]), add(e[...], f[...])
    first = sel_ref[0] == 0
    small = low[:, hidden:]
    turned = pltpu.roll(small, SMALL_ROWS, 1)
    low = low[:, :hidden]
    own_ref[:, :hidden] = jnp.where(first, low, high)
    own_ref[:, hidden:] = jnp.where(first, small, turned)
    send_ref[:, :hidden] = jnp.where(first, high, low).astype(jnp.bfloat16)
    send_ref[:, hidden:] = jnp.where(first, turned, small).astype(jnp.bfloat16)


def to_core(core, parts):
    shape = (parts[-1].shape[0], parts[-1].shape[1] + 2 * SMALL_ROWS)
    return small_call(core_kernel, "to_core", ((shape, jnp.float32), (shape, jnp.bfloat16)), core, *parts)


def final_kernel(sel_ref, own_ref, got_ref, k_ref, gain_ref, in_ref, out_ref, scale_ref, pad_ref):
    share, hidden = own_ref.shape[0], in_ref.shape[2]
    taps = k_ref.shape[2]
    first = sel_ref[0] == 0
    own, got = own_ref[:, :hidden], got_ref[:, :hidden].astype(jnp.float32)
    in_ref[0] = jnp.where(first, own, got)
    out_ref[0] = jnp.where(first, got, own)
    small = add(own_ref[:, hidden:], got_ref[:, hidden:])
    k_ref[0] = small[:, :taps]
    pad_ref[0:share, :] = small
    turned = pad_ref[...].T
    gain_ref[...] = turned[taps : taps + 1, :share]
    scale_ref[...] = turned[taps + 1 : taps + 2, :share]


def final(core, own, got, taps):
    share, hidden = own.shape[0], own.shape[1] - 2 * SMALL_ROWS
    outs = (
        ((1, share, taps), jnp.float32),
        ((1, share), jnp.float32),
        ((1, share, hidden), jnp.float32),
        ((1, share, hidden), jnp.float32),
        ((1, share), jnp.float32),
    )
    t_kernel, t_gain, t_in, t_out, t_scale = small_call(
        final_kernel, "final", outs, core, own, got, scratch=[pltpu.VMEM((LANES, 2 * SMALL_ROWS), jnp.float32)]
    )
    return t_kernel.transpose(0, 2, 1), t_gain, t_in, t_out.transpose(0, 2, 1), t_scale


BF16 = jnp.bfloat16
F32 = jnp.float32


def one_image(x, g, small, sels, w_ins, w_outs, first, passing):
    blocks = small.shape[0]
    rows, cols, channels = x.shape
    which = jnp.stack([sel[0] for sel in sels])
    xs, xhats, invs, pres, branches = forward(which, x, first[1], small, w_ins, w_outs)
    xs, xhats, invs = (x,) + tuple(xs), first[:1] + tuple(xhats), first[2:] + tuple(invs)
    smalls = [None] * blocks
    for s in reversed(range(blocks)):
        keep, send, sums8, gconv = mlp_back(
            sels[s], g.reshape(rows * cols, channels), branches[s], pres[s], xhats[s], invs[s],
            small[s, TAPS : TAPS + 1], small[s, TAPS + 1 : TAPS + 2], w_ins, w_outs, passing.before("mlp", s),
        )
        passing.done(s, keep, send)
        *g_next, smalls[s] = conv_back(
            gconv, xs[s], g, small[s, :TAPS], sums8, s > 0, passing.before("conv", s)
        )
        g = g_next[0] if g_next else None
    return smalls


def finish(t_kernel, t_gain, t_scale, t_in, t_out):
    return t_kernel[None], t_gain[None], t_in[None], t_out[None], t_scale[None]


def any_mesh(images, cotangent, kernels, norm_gains, w_in, w_out, scales):
    segments = lax.axis_size("segment")
    rank = lax.axis_index("segment")
    count = images.shape[0] // segments
    taps = kernels.shape[1]
    small = lax.all_gather(parameters(kernels, norm_gains, scales), "segment")
    all_in = lax.all_gather(w_in[0], "segment")
    all_out = lax.all_gather(w_out[0], "segment")
    sels = [jnp.array([s, 0], jnp.int32) for s in range(segments)]
    pieces = [[None] * 3 for _ in range(segments)]

    class Sums:
        def before(self, part, s):
            return ()

        def done(self, s, keep, send):
            self.add(s, 0, keep.astype(F32))
            self.add(s, 1, send.astype(F32))

        def add(self, s, k, value):
            pieces[s][k] = value if pieces[s][k] is None else pieces[s][k] + value

    sums = Sums()
    w_ins = [all_in[s] for s in range(segments)]
    w_outs = [all_out[s] for s in range(segments)]
    for i in range(count):
        x = lax.dynamic_index_in_dim(images, rank * count + i, 0, keepdims=False)
        g = lax.dynamic_index_in_dim(cotangent, rank * count + i, 0, keepdims=False)
        smalls = one_image(x, g, small, sels, w_ins, w_outs, conv_norm(sels[0] * 0, x, [small[0]]), sums)
        for s in range(segments):
            sums.add(s, 2, smalls[s])

    def summed(values, dim):
        mine = lax.psum_scatter(jnp.stack(values), "segment", scatter_dimension=0, tiled=False)
        return lax.psum_scatter(mine, "dp", scatter_dimension=dim, tiled=True)

    t_in = summed([p[0] for p in pieces], 0)
    t_out = summed([p[1] for p in pieces], 0).T
    t_small = summed([p[2] for p in pieces], 1)
    return finish(t_small[:taps], t_small[taps], t_small[taps + 1], t_in, t_out)


def partners(flip, extent=(4, 2, 2, 2)):
    pairs = []
    for index in range(32):
        z, y, x, c = index >> 3, (index >> 2) & 1, (index >> 1) & 1, index & 1
        other = ((z ^ flip[0]) << 3) | ((y ^ flip[1]) << 2) | ((x ^ flip[2]) << 1) | (c ^ flip[3])
        pairs.append((index, other))
    return pairs


def swap(value, z=0, y=0, x=0, c=0):
    return lax.ppermute(value, ("dp", "segment"), partners((z, y, x, c)))


def along_x(value, to_last):
    pairs = [(i, j) for i, j in partners((0, 0, 1, 0)) if (i >> 1) & 1 == (0 if to_last else 1)]
    return lax.ppermute(value, ("dp", "segment"), pairs)


def this_mesh(images, cotangent, kernels, norm_gains, w_in, w_out, scales):
    rank = lax.axis_index("segment")
    core = rank % 2
    chip = rank // 2
    depth = lax.axis_index("dp") // 2
    side = lax.axis_index("dp") % 2
    own_small = parameters(kernels, norm_gains, scales)
    near_small = swap(own_small, c=1)
    near_in, near_out = swap(w_in[0], c=1), swap(w_out[0], c=1)
    small = (own_small, near_small)
    weights = (w_in[0], near_in, w_out[0], near_out)
    zero = jnp.zeros_like(chip)
    sel = jnp.stack([core, 1 - core, chip, core, zero]).astype(jnp.int32)
    sel_first = jnp.stack([core, 1 - core, chip, core, chip]).astype(jnp.int32)
    sel_conv = (jnp.stack([core, zero]).astype(jnp.int32), jnp.stack([core, chip]).astype(jnp.int32))
    cores = core[None].astype(jnp.int32)
    sides = side[None].astype(jnp.int32)
    levels = jnp.stack([depth, depth ^ 1, depth ^ 2, depth ^ 3]).astype(jnp.int32)

    maps = [lax.dynamic_index_in_dim(images, 2 * core + i, 0, keepdims=False) for i in range(2)]
    ends = [lax.dynamic_index_in_dim(cotangent, 2 * core + i, 0, keepdims=False) for i in range(2)]
    firsts, kept = [], []
    for x, chosen in zip(maps, sel_conv):
        firsts.append(conv_norm(chosen, x, small, tuple(k.inv1 for k in kept)))
        kept.append(pair_forward(sel_first if kept else sel, x, firsts[-1], small, weights))
    passed = [along_x(k.y, True) for k in kept]
    parts, starts = [], []
    for x, g in zip(passed, ends):
        parts.append(pair_map(sel, x, g, small, weights))
        starts.append(along_x(parts[-1].g0, False))
    totals = pair_grads(sel, passed, parts)
    grads = pair_back(sel, starts[0], maps[0], firsts[0], kept[0], small, weights)
    grads = pair_back(sel, starts[1], maps[1], firsts[1], kept[1], small, weights, (grads, totals))
    core0, core1 = swap(grads.send0, c=1), swap(grads.send1, c=1)

    def along_y(*pairs):
        across, mine = to_side(sides, *pairs)
        return mine, swap(across, y=1)

    def along_z(mine, got):
        own, *others = to_depths(levels, mine, got)
        return [own] + [swap(v, z=flip) for v, flip in zip(others, (1, 2, 3))]

    low = along_y(brought(grads.keep0), core0, grads.packed)
    own, *others = split_depths(levels, grads.keep1, core1, low[:1])
    parts = [own] + [swap(others[flip - 1], z=flip) for flip in (2, 3, 1)]
    across, mine = join_depths(sides, parts)
    high = [mine, swap(across, y=1)]
    low = along_z(*low)
    own, send = to_core(cores, low + high)
    return final(cores, own, swap(send, c=1), kernels.shape[1])


def solution(mesh):
    in_specs = (
        P("dp", None, None, None),
        P("dp", None, None, None),
        P("segment", None, None),
        P("segment", None),
        P("segment", None, None),
        P("segment", None, None),
        P("segment", None),
    )
    out_specs = (
        P("segment", None, "dp"),
        P("segment", "dp"),
        P("segment", "dp", None),
        P("segment", None, "dp"),
        P("segment", "dp"),
    )
    fits = dict(mesh.shape) == {"dp": 8, "segment": 4}

    def whole(images, *rest):
        local = this_mesh if fits and images.shape[0] == 32 else any_mesh
        return jax.shard_map(local, mesh=mesh, in_specs=in_specs, out_specs=out_specs, check_vma=False)(images, *rest)

    return whole
```

```python
import functools
import types
import jax
import jax.numpy as jnp
from jax import lax
from jax.sharding import PartitionSpec as P
from jax.experimental import pallas as pl
from jax.experimental.pallas import tpu as pltpu

EPS = 1e-06
GELU_C = 0.7978845608028654
GELU_A = 0.044715
LANES = 128
def estimate(microseconds):
    return pl.CostEstimate(flops=int(microseconds * 1.1e9), bytes_accessed=int(microseconds * 3.6e6), transcendentals=0)


LIMIT = 40


def vmem(mebibytes):
    return pltpu.CompilerParams(vmem_limit_bytes=mebibytes * 1024 * 1024)


def zero_borders(pad_ref):
    tiles, rows, width, _ = pad_ref.shape
    for c in range(tiles):
        pad_ref[c, :, 0:8] = jnp.zeros((rows, 8, LANES), jnp.float32)
        pad_ref[c, :, width - 8 :] = jnp.zeros((rows, 8, LANES), jnp.float32)


def conv_norm_body(x_ref, small_ref, xhat_ref, normed_ref, inv_ref, pad_ref, conv_ref):
    rows, cols, channels = x_ref.shape
    tiles = channels // LANES
    for c in range(tiles):
        pad_ref[c, :, 8 : cols + 8] = x_ref[:, :, c * LANES : (c + 1) * LANES].astype(jnp.float32)

    def tile(c, carry):
        lanes = pl.ds(pl.multiple_of(c * LANES, LANES), LANES)

        def strip(w, carry):
            base = pl.multiple_of(w * 8, 8)
            window = pad_ref.at[c, :, pl.ds(base, 24), :]
            acc = [None] * rows
            for q in range(7):
                col = [window[h, 5 + q : 13 + q, :] for h in range(rows)]
                for r in range(7):
                    weight = small_ref[r * 7 + q : r * 7 + q + 1, lanes]
                    for h in range(max(0, 3 - r), min(rows, rows + 3 - r)):
                        term = weight * col[h + r - 3]
                        acc[h] = term if acc[h] is None else acc[h] + term
            for h in range(rows):
                conv_ref[h, pl.ds(base, 8), lanes] = acc[h]
            return carry

        return lax.fori_loop(0, cols // 8, strip, carry)

    lax.fori_loop(0, tiles, tile, 0)

    def norm(h, carry):
        value = conv_ref[pl.ds(h * 2, 2)].reshape(2 * cols, channels)
        mean = jnp.mean(value, axis=1, keepdims=True)
        center = value - mean
        inv = lax.rsqrt(jnp.mean(center * center, axis=1, keepdims=True) + EPS)
        xhat = center * inv
        at = pl.ds(pl.multiple_of(h * 2 * cols, 2 * cols), 2 * cols)
        xhat_ref[at, :] = xhat.astype(jnp.bfloat16)
        normed_ref[at, :] = (xhat * small_ref[TAPS : TAPS + 1, :]).astype(jnp.bfloat16)
        inv_ref[at, :] = jnp.broadcast_to(inv, (2 * cols, LANES))
        return carry

    lax.fori_loop(0, rows // 2, norm, 0, unroll=True)


def pad_shape(rows, cols, channels):
    return pltpu.VMEM((channels // LANES, rows, cols + 16, LANES), jnp.float32)


def in_hbm(arrays):
    return [pltpu.with_memory_space_constraint(a, pltpu.HBM) for a in arrays]


def parameters_kernel(k_ref, gain_ref, scale_ref, out_ref, taps_ref, rows_ref, sems):
    copies = [
        pltpu.make_async_copy(source, target, sems.at[i])
        for i, (source, target) in enumerate(((k_ref, taps_ref), (gain_ref, rows_ref.at[0]), (scale_ref, rows_ref.at[1])))
    ]
    for copy in copies:
        copy.start()
    taps = taps_ref.shape[0]
    out_ref[taps + 2 :, :] = jnp.zeros((out_ref.shape[0] - taps - 2, out_ref.shape[1]), jnp.float32)
    for copy in copies:
        copy.wait()
    for t in range(taps):
        out_ref[t : t + 1, :] = taps_ref[t]
    out_ref[taps : taps + 1, :] = rows_ref[0]
    out_ref[taps + 1 : taps + 2, :] = rows_ref[1]


def parameters(kernels, norm_gains, scales):
    taps, channels = kernels.shape[1:]
    return pl.pallas_call(
        parameters_kernel,
        in_specs=[pl.BlockSpec(memory_space=pl.ANY)] * 3,
        out_shape=jax.ShapeDtypeStruct((56, channels), jnp.float32),
        scratch_shapes=[
            pltpu.VMEM((taps, 1, channels), jnp.float32),
            pltpu.VMEM((2, 1, channels), jnp.float32),
            pltpu.SemaphoreType.DMA((3,)),
        ],
        compiler_params=vmem(LIMIT),
        name="parameters",
        cost_estimate=estimate(0.5),
    )(*in_hbm([kernels.transpose(1, 0, 2), norm_gains, scales]))


def choose_small(r):
    first = r.sel[0] == 0
    own, near = r.own_small[...], r.near_small[...]
    r.small[0] = jnp.where(first, own, near)
    r.small[1] = jnp.where(first, near, own)


def conv_norm_kernel(choices, sel_ref, x_ref, *rest):
    smalls, rest = rest[:choices], rest[choices:]
    xhat_ref, normed_ref, inv_ref, pad_ref, conv_ref, small_ref = rest[-6:]
    active = sel_ref[1] == 0

    @pl.when(active)
    def _():
        zero_borders(pad_ref)
        small_ref[...] = smalls[0][...]
        for k in range(1, choices):

            @pl.when(sel_ref[0] == k)
            def _():
                small_ref[...] = smalls[k][...]

        conv_norm_body(x_ref, small_ref, xhat_ref, normed_ref, inv_ref, pad_ref, conv_ref)


def conv_norm(sel, x, smalls, after=()):
    rows, cols, channels = x.shape
    n = rows * cols
    return pl.pallas_call(
        functools.partial(conv_norm_kernel, len(smalls)),
        in_specs=[pl.BlockSpec(memory_space=pltpu.SMEM)]
        + [pl.BlockSpec(memory_space=pltpu.VMEM)] * (1 + len(smalls))
        + [pl.BlockSpec(memory_space=pl.ANY)] * len(after),
        out_shape=(
            jax.ShapeDtypeStruct((n, channels), jnp.bfloat16),
            jax.ShapeDtypeStruct((n, channels), jnp.bfloat16),
            jax.ShapeDtypeStruct((n, LANES), jnp.float32),
        ),
        scratch_shapes=[
            pad_shape(rows, cols, channels),
            pltpu.VMEM((rows, cols, channels), jnp.float32),
            pltpu.VMEM(smalls[0].shape, jnp.float32),
        ],
        compiler_params=vmem(LIMIT),
        name="conv_norm",
        cost_estimate=estimate(2.0),
    )(sel, x, *smalls, *after)


def copy_chosen(which, sources, target, sem):
    for m, source in enumerate(sources):

        @pl.when(which == m)
        def _():
            pltpu.make_async_copy(source, target, sem).start()

    return lambda: pltpu.make_async_copy(sources[0], target, sem).wait()


def forward_kernel(choices, blocks, sel_ref, x_ref, normed0_ref, small_ref, *rest):
    w_ins, w_outs, rest = rest[:choices], rest[choices : 2 * choices], rest[2 * choices :]
    xs = [x_ref] + list(rest[: blocks - 1])
    xhats, invs, rest = rest[blocks - 1 : 2 * blocks - 2], rest[2 * blocks - 2 : 3 * blocks - 3], rest[3 * blocks - 3 :]
    pres, branches, rest = rest[:blocks], rest[blocks : 2 * blocks], rest[2 * blocks :]
    normed_ref, hid_ref, acc_ref, pad_ref, conv_ref, w_in_ref, w_out_ref, sems = rest
    rows, cols, channels = x_ref.shape
    n = rows * cols
    hidden = w_in_ref.shape[2]
    waits = []
    for s in range(blocks):
        waits.append((
            copy_chosen(sel_ref[s], w_ins, w_in_ref.at[s], sems.at[0, s]),
            copy_chosen(sel_ref[s], w_outs, w_out_ref.at[s], sems.at[1, s]),
        ))
    zero_borders(pad_ref)
    step, sub = 256, 2 * cols
    for s in range(blocks):
        normed = normed0_ref if s == 0 else normed_ref
        waits[s][0]()
        for j in range(hidden // step):
            cut = slice(j * step, (j + 1) * step)
            pre = jnp.dot(normed[...], w_in_ref[s, :, cut], preferred_element_type=jnp.float32)
            for i in range(n // sub):
                p = pre[i * sub : (i + 1) * sub]
                half = 0.5 * p
                hid_ref[i * sub : (i + 1) * sub, :] = (half + half * tanh_arg(p)).astype(jnp.bfloat16)
                pres[s][i * sub : (i + 1) * sub, cut] = p.astype(jnp.bfloat16)
            if j == 0:
                waits[s][1]()
            part = jnp.dot(hid_ref[...], w_out_ref[s, cut, :], preferred_element_type=jnp.float32)
            if j == 0:
                acc_ref[...] = part
            else:
                acc_ref[...] += part
        scale = small_ref[s, TAPS + 1 : TAPS + 2, :]
        for i in range(n // sub):
            branch = acc_ref[i * sub : (i + 1) * sub, :]
            branches[s][i * sub : (i + 1) * sub, :] = branch.astype(jnp.bfloat16)
            if s < blocks - 1:
                x_old = xs[s][2 * i : 2 * i + 2].astype(jnp.float32).reshape(sub, channels)
                xs[s + 1][2 * i : 2 * i + 2] = (x_old + scale * branch).astype(jnp.bfloat16).reshape(2, cols, channels)
        if s < blocks - 1:
            conv_norm_body(xs[s + 1], small_ref.at[s + 1], xhats[s], normed_ref, invs[s], pad_ref, conv_ref)


def forward(sel, x, normed0, small, w_ins, w_outs):
    blocks = small.shape[0]
    rows, cols, channels = x.shape
    n = rows * cols
    hidden = w_ins[0].shape[1]
    out = pl.pallas_call(
        functools.partial(forward_kernel, len(w_ins), blocks),
        in_specs=[pl.BlockSpec(memory_space=pltpu.SMEM)]
        + [pl.BlockSpec(memory_space=pltpu.VMEM)] * 3
        + [pl.BlockSpec(memory_space=pl.ANY)] * (2 * len(w_ins)),
        out_shape=(jax.ShapeDtypeStruct((rows, cols, channels), jnp.bfloat16),) * (blocks - 1)
        + (jax.ShapeDtypeStruct((n, channels), jnp.bfloat16),) * (blocks - 1)
        + (jax.ShapeDtypeStruct((n, LANES), jnp.float32),) * (blocks - 1)
        + (jax.ShapeDtypeStruct((n, hidden), jnp.bfloat16),) * blocks
        + (jax.ShapeDtypeStruct((n, channels), jnp.bfloat16),) * blocks,
        scratch_shapes=[
            pltpu.VMEM((n, channels), jnp.bfloat16),
            pltpu.VMEM((n, 256), jnp.bfloat16),
            pltpu.VMEM((n, channels), jnp.float32),
            pad_shape(rows, cols, channels),
            pltpu.VMEM((rows, cols, channels), jnp.float32),
            pltpu.VMEM((blocks, channels, hidden), jnp.bfloat16),
            pltpu.VMEM((blocks, hidden, channels), jnp.bfloat16),
            pltpu.SemaphoreType.DMA((2, blocks)),
        ],
        compiler_params=vmem(LIMIT),
        name="forward",
        cost_estimate=estimate(15),
    )(sel, x, normed0, small, *in_hbm(w_ins), *in_hbm(w_outs))
    k = blocks - 1
    return out[:k], out[k : 2 * k], out[2 * k : 3 * k], out[3 * k : 3 * k + blocks], out[3 * k + blocks :]


def tanh_arg(x):
    return jnp.tanh(x * (GELU_C + (GELU_C * GELU_A) * (x * x)))


def load_weights(sel_ref, w_ins, w_outs, w_in_ref, w_out_ref, sems):
    for m in range(len(w_ins)):

        @pl.when(sel_ref[0] == m)
        def _():
            pltpu.make_async_copy(w_ins[m], w_in_ref, sems.at[0]).start()
            pltpu.make_async_copy(w_outs[m], w_out_ref, sems.at[1]).start()

    return (
        pltpu.make_async_copy(w_ins[0], w_in_ref, sems.at[0]).wait,
        pltpu.make_async_copy(w_outs[0], w_out_ref, sems.at[1]).wait,
    )


def specs(sel, arrays, choices, after=0):
    return (
        [pl.BlockSpec(memory_space=pltpu.SMEM)]
        + [pl.BlockSpec(memory_space=pltpu.VMEM)] * arrays
        + [pl.BlockSpec(memory_space=pl.ANY)] * (2 * choices + after)
    )


def mlp_back_kernel(choices, after, sel_ref, g_ref, branch_ref, pre_ref, xhat_ref, inv_ref, gain_ref, scale_ref, *rest):
    w_ins, w_outs = rest[:choices], rest[choices : 2 * choices]
    (keep_ref, send_ref, small_ref, gconv_ref,
     gb_ref, nm_ref, hid_ref, gp_ref, acc_ref, w_in_ref, w_out_ref, sems) = rest[2 * choices + after :]
    wait_in, wait_out = load_weights(sel_ref, w_ins, w_outs, w_in_ref, w_out_ref, sems)
    first = sel_ref[1] == 0
    n, channels = g_ref.shape
    hidden = w_in_ref.shape[1]
    step = 256
    sub = 32
    scale_sum = jnp.zeros((8, channels), jnp.float32)
    for i in range(n // sub):
        at = slice(i * sub, (i + 1) * sub)
        g = g_ref[at, :].astype(jnp.float32)
        scale_sum = scale_sum + jnp.sum((g * branch_ref[at, :].astype(jnp.float32)).reshape(sub // 8, 8, channels), axis=0)
        gb_ref[at, :] = (g * scale_ref[...]).astype(jnp.bfloat16)
        nm_ref[at, :] = (xhat_ref[at, :].astype(jnp.float32) * gain_ref[...]).astype(jnp.bfloat16)
    gb_t = gb_ref[...].T
    nm_t = nm_ref[...].T
    wait_in()
    wait_out()
    for j in range(hidden // step):
        cut = slice(j * step, (j + 1) * step)
        gh = lax.dot_general(gb_ref[...], w_out_ref[cut, :], (((1,), (1,)), ((), ())), preferred_element_type=jnp.float32)
        for i in range(n // sub):
            at = slice(i * sub, (i + 1) * sub)
            p = pre_ref[at, cut].astype(jnp.float32)
            sq = p * p
            t = jnp.tanh(p * (GELU_C + (GELU_C * GELU_A) * sq))
            cdf = 0.5 + 0.5 * t
            hid_ref[at, :] = (p * cdf).astype(jnp.bfloat16)
            slope = cdf + (0.5 * p) * (1.0 - t * t) * (GELU_C + (3.0 * GELU_C * GELU_A) * sq)
            gp_ref[at, :] = (gh[at, :] * slope).astype(jnp.bfloat16)
        t_out = jnp.dot(gb_t, hid_ref[...], preferred_element_type=jnp.float32)
        t_in = jnp.dot(nm_t, gp_ref[...], preferred_element_type=jnp.float32)
        keep_ref[:, cut] = jnp.where(first, t_in, t_out).astype(jnp.bfloat16)
        send_ref[:, cut] = jnp.where(first, t_out, t_in).astype(jnp.bfloat16)
        part = lax.dot_general(gp_ref[...], w_in_ref[:, cut], (((1,), (1,)), ((), ())), preferred_element_type=jnp.float32)
        if j == 0:
            acc_ref[...] = part
        else:
            acc_ref[...] += part
    gain_sum = jnp.zeros((8, channels), jnp.float32)
    for i in range(n // sub):
        at = slice(i * sub, (i + 1) * sub)
        gn = acc_ref[at, :]
        xhat = xhat_ref[at, :].astype(jnp.float32)
        gain_sum = gain_sum + jnp.sum((gn * xhat).reshape(sub // 8, 8, channels), axis=0)
        gx = gn * gain_ref[...]
        m1 = jnp.mean(gx, axis=1, keepdims=True)
        m2 = jnp.mean(gx * xhat, axis=1, keepdims=True)
        inv = inv_ref[at, 0:1]
        gconv_ref[at, :] = inv * (gx - m1 - xhat * m2)
    small_ref[0:1, :] = jnp.sum(gain_sum, axis=0, keepdims=True)
    small_ref[1:2, :] = jnp.sum(scale_sum, axis=0, keepdims=True)
    small_ref[2:8, :] = jnp.zeros((6, channels), jnp.float32)


def mlp_back(sel, g, branch, pre, xhat, inv, gain, scale, w_ins, w_outs, after=()):
    n, channels = g.shape
    hidden = w_ins[0].shape[1]
    return pl.pallas_call(
        functools.partial(mlp_back_kernel, len(w_ins), len(after)),
        in_specs=specs(sel, 7, len(w_ins), len(after)),
        out_shape=(
            jax.ShapeDtypeStruct((channels, hidden), jnp.bfloat16),
            jax.ShapeDtypeStruct((channels, hidden), jnp.bfloat16),
            jax.ShapeDtypeStruct((8, channels), jnp.float32),
            jax.ShapeDtypeStruct((n, channels), jnp.float32),
        ),
        scratch_shapes=[
            pltpu.VMEM((n, channels), jnp.bfloat16),
            pltpu.VMEM((n, channels), jnp.bfloat16),
            pltpu.VMEM((n, 256), jnp.bfloat16),
            pltpu.VMEM((n, 256), jnp.bfloat16),
            pltpu.VMEM((n, channels), jnp.float32),
            pltpu.VMEM((channels, hidden), jnp.bfloat16),
            pltpu.VMEM((hidden, channels), jnp.bfloat16),
            pltpu.SemaphoreType.DMA((2,)),
        ],
        compiler_params=vmem(LIMIT),
        name="mlp_back",
        cost_estimate=estimate(2.5),
    )(sel, g, branch, pre, xhat, inv, gain, scale, *in_hbm(w_ins), *in_hbm(w_outs), *after)


SMALL_ROWS = 64
TAPS = 49


def conv_back_kernel(need_map, after, gconv_ref, x_ref, g_ref, k_ref, small_ref, *rest):
    *out_ref, tk_ref, pad_ref, sum_ref, wide_ref, map_ref = rest[after:]
    conv_back_body(gconv_ref, x_ref, g_ref, k_ref, small_ref, out_ref[0] if need_map else None, tk_ref,
                   pad_ref, sum_ref, wide_ref, map_ref)


def conv_back(gconv, x, g, kernel, small, need_map=True, after=()):
    rows, cols, channels = x.shape
    out = (jax.ShapeDtypeStruct((SMALL_ROWS, channels), jnp.float32),)
    if need_map:
        out = (jax.ShapeDtypeStruct((rows, cols, channels), jnp.bfloat16),) + out
    return pl.pallas_call(
        functools.partial(conv_back_kernel, need_map, len(after)),
        in_specs=[pl.BlockSpec(memory_space=pltpu.VMEM)] * 5 + [pl.BlockSpec(memory_space=pl.ANY)] * len(after),
        out_shape=out,
        scratch_shapes=[
            pad_shape(rows, cols, channels),
            pltpu.VMEM((cols // 8, TAPS, 8, LANES), jnp.float32),
            pltpu.VMEM((rows, cols, channels), jnp.float32),
            pltpu.VMEM((rows, cols, channels), jnp.float32),
        ],
        compiler_params=vmem(LIMIT),
        name="conv_back",
        cost_estimate=estimate(3.4 if need_map else 1.6),
    )(gconv, x, g, kernel, small, *after)


def small_call(kernel, name, outs, *args, scratch=(), after=()):
    used = len(args)

    def body(*refs):
        kernel(*refs[:used], *refs[used + len(after) :])

    return pl.pallas_call(
        body,
        in_specs=[pl.BlockSpec(memory_space=pltpu.SMEM)]
        + [pl.BlockSpec(memory_space=pltpu.VMEM)] * (used - 1)
        + [pl.BlockSpec(memory_space=pl.ANY)] * len(after),
        out_shape=tuple(out_struct(*o) for o in outs),
        scratch_shapes=list(scratch),
        compiler_params=vmem(LIMIT),
        name=name,
        cost_estimate=estimate(0.7),
    )(*args, *after)


def conv_back_body(gconv_ref, x_ref, g_ref, small_ref, sums8_ref, out_ref, tk_ref, pad_ref, sum_ref, wide_ref, map_ref):
    rows, cols, channels = x_ref.shape
    tiles = channels // LANES
    zero_borders(pad_ref)
    for c in range(tiles):
        pad_ref[c, :, 8 : cols + 8] = gconv_ref[:, c * LANES : (c + 1) * LANES].reshape(rows, cols, LANES)

    for h in range(rows):
        wide_ref[h] = x_ref[h].astype(jnp.float32)

    def tile(c, carry):
        lanes = pl.ds(pl.multiple_of(c * LANES, LANES), LANES)

        def strip(w, carry):
            base = pl.multiple_of(w * 8, 8)
            window = pad_ref.at[c, :, pl.ds(base, 24), :]
            xs = [wide_ref[h, pl.ds(base, 8), lanes] for h in range(rows)]
            acc = [None] * rows
            for q in range(7):
                col = [window[h, 11 - q : 19 - q, :] for h in range(rows)]
                for r in range(7):
                    tap = r * 7 + q
                    if out_ref is not None:
                        weight = small_ref[tap : tap + 1, lanes]
                    total = None
                    for h in range(max(0, r - 3), min(rows, rows + r - 3)):
                        shifted = col[h + 3 - r]
                        term = xs[h] * shifted
                        total = term if total is None else total + term
                        if out_ref is not None:
                            moved = weight * shifted
                            acc[h] = moved if acc[h] is None else acc[h] + moved
                    sum_ref[w, tap] = total
            if out_ref is not None:
                for h in range(rows):
                    map_ref[h, pl.ds(base, 8), lanes] = acc[h]
            return carry

        lax.fori_loop(0, cols // 8, strip, 0)
        tk_ref[0:TAPS, lanes] = jnp.sum(sum_ref[0] + sum_ref[1], axis=1)
        return carry

    lax.fori_loop(0, tiles, tile, 0)
    if out_ref is not None:
        for h in range(rows):
            out_ref[h] = (g_ref[h].astype(jnp.float32) + map_ref[h]).astype(jnp.bfloat16)
    tk_ref[TAPS : TAPS + 2, :] = sums8_ref[0:2, :]
    tk_ref[TAPS + 2 :, :] = jnp.zeros((SMALL_ROWS - TAPS - 2, channels), jnp.float32)


def conv_map_body(gconv_ref, g_ref, small_ref, out_ref, pad_ref, map_ref):
    rows, cols, channels = g_ref.shape
    tiles = channels // LANES
    for c in range(tiles):
        pad_ref[c, :, 8 : cols + 8] = gconv_ref[:, c * LANES : (c + 1) * LANES].reshape(rows, cols, LANES)

    def tile(c, carry):
        lanes = pl.ds(pl.multiple_of(c * LANES, LANES), LANES)

        def strip(w, carry):
            base = pl.multiple_of(w * 8, 8)
            window = pad_ref.at[c, :, pl.ds(base, 24), :]
            acc = [None] * rows
            for q in range(7):
                col = [window[h, 11 - q : 19 - q, :] for h in range(rows)]
                for r in range(7):
                    weight = small_ref[r * 7 + q : r * 7 + q + 1, lanes]
                    for h in range(max(0, r - 3), min(rows, rows + r - 3)):
                        term = weight * col[h + 3 - r]
                        acc[h] = term if acc[h] is None else acc[h] + term
            for h in range(rows):
                map_ref[h, pl.ds(base, 8), lanes] = acc[h]
            return carry

        return lax.fori_loop(0, cols // 8, strip, carry)

    lax.fori_loop(0, tiles, tile, 0)
    for h in range(rows):
        out_ref[h] = (g_ref[h].astype(jnp.float32) + map_ref[h]).astype(jnp.bfloat16)


def mlp_back_map_body(g_ref, branch_ref, pre_ref, xhat_ref, inv_ref, small_ref, w_in_ref, w_out_ref,
                      sums8_ref, gconv_ref, gb_ref, nm_ref, hid_ref, gp_ref, acc_ref, ready):
    rows, cols, channels = g_ref.shape
    n = rows * cols
    hidden = w_in_ref.shape[1]
    step = 256
    sub = 2 * cols
    gain = small_ref[TAPS : TAPS + 1, :]
    scale = small_ref[TAPS + 1 : TAPS + 2, :]
    scale_sum = jnp.zeros((8, channels), jnp.float32)
    for i in range(n // sub):
        at = slice(i * sub, (i + 1) * sub)
        g = g_ref[2 * i : 2 * i + 2].astype(jnp.float32).reshape(sub, channels)
        scale_sum = scale_sum + jnp.sum((g * branch_ref[at, :].astype(jnp.float32)).reshape(sub // 8, 8, channels), axis=0)
        gb_ref[at, :] = (g * scale).astype(jnp.bfloat16)
        nm_ref[at, :] = (xhat_ref[at, :].astype(jnp.float32) * gain).astype(jnp.bfloat16)
    ready("gb", "nm")
    for j in range(hidden // step):
        cut = slice(j * step, (j + 1) * step)
        gh = lax.dot_general(gb_ref[...], w_out_ref[cut, :], (((1,), (1,)), ((), ())), preferred_element_type=jnp.float32)
        for i in range(n // sub):
            at = slice(i * sub, (i + 1) * sub)
            p = pre_ref[at, cut].astype(jnp.float32)
            sq = p * p
            t = jnp.tanh(p * (GELU_C + (GELU_C * GELU_A) * sq))
            cdf = 0.5 + 0.5 * t
            hid_ref[at, cut] = (p * cdf).astype(jnp.bfloat16)
            slope = cdf + (0.5 * p) * (1.0 - t * t) * (GELU_C + (3.0 * GELU_C * GELU_A) * sq)
            gp_ref[at, cut] = (gh[at, :] * slope).astype(jnp.bfloat16)
        part = lax.dot_general(gp_ref[:, cut], w_in_ref[:, cut], (((1,), (1,)), ((), ())), preferred_element_type=jnp.float32)
        if j == 0:
            acc_ref[...] = part
        else:
            acc_ref[...] += part
    ready("hid", "gp")
    gain_sum = jnp.zeros((8, channels), jnp.float32)
    for i in range(n // sub):
        at = slice(i * sub, (i + 1) * sub)
        gn = acc_ref[at, :]
        xhat = xhat_ref[at, :].astype(jnp.float32)
        gain_sum = gain_sum + jnp.sum((gn * xhat).reshape(sub // 8, 8, channels), axis=0)
        gx = gn * gain
        m1 = jnp.mean(gx, axis=1, keepdims=True)
        m2 = jnp.mean(gx * xhat, axis=1, keepdims=True)
        gconv_ref[at, :] = inv_ref[at, 0:1] * (gx - m1 - xhat * m2)
    sums8_ref[0:1, :] = jnp.sum(gain_sum, axis=0, keepdims=True)
    sums8_ref[1:2, :] = jnp.sum(scale_sum, axis=0, keepdims=True)
    sums8_ref[2:8, :] = jnp.zeros((6, channels), jnp.float32)
    ready("gconv", "sums")


def mlp_back_body(first, g_ref, branch_ref, pre_ref, xhat_ref, inv_ref, small_ref, wait_in, wait_out, w_in_ref, w_out_ref,
                  keep_ref, send_ref, sums8_ref, gconv_ref, gb_ref, nm_ref, hid_ref, gp_ref, acc_ref, before=None):
    rows, cols, channels = g_ref.shape
    n = rows * cols
    hidden = w_in_ref.shape[1]
    step = 256
    sub = 2 * cols
    gain = small_ref[TAPS : TAPS + 1, :]
    scale = small_ref[TAPS + 1 : TAPS + 2, :]
    scale_sum = jnp.zeros((8, channels), jnp.float32)
    for i in range(n // sub):
        at = slice(i * sub, (i + 1) * sub)
        g = g_ref[2 * i : 2 * i + 2].astype(jnp.float32).reshape(sub, channels)
        scale_sum = scale_sum + jnp.sum((g * branch_ref[at, :].astype(jnp.float32)).reshape(sub // 8, 8, channels), axis=0)
        gb_ref[at, :] = (g * scale).astype(jnp.bfloat16)
        nm_ref[at, :] = (xhat_ref[at, :].astype(jnp.float32) * gain).astype(jnp.bfloat16)
    gb_t = gb_ref[...].T
    nm_t = nm_ref[...].T
    wait_out()
    for j in range(hidden // step):
        cut = slice(j * step, (j + 1) * step)
        gh = lax.dot_general(gb_ref[...], w_out_ref[cut, :], (((1,), (1,)), ((), ())), preferred_element_type=jnp.float32)
        for i in range(n // sub):
            at = slice(i * sub, (i + 1) * sub)
            p = pre_ref[at, cut].astype(jnp.float32)
            sq = p * p
            t = jnp.tanh(p * (GELU_C + (GELU_C * GELU_A) * sq))
            cdf = 0.5 + 0.5 * t
            hid_ref[at, :] = (p * cdf).astype(jnp.bfloat16)
            slope = cdf + (0.5 * p) * (1.0 - t * t) * (GELU_C + (3.0 * GELU_C * GELU_A) * sq)
            gp_ref[at, :] = (gh[at, :] * slope).astype(jnp.bfloat16)
        t_out = jnp.dot(gb_t, hid_ref[...], preferred_element_type=jnp.float32)
        t_in = jnp.dot(nm_t, gp_ref[...], preferred_element_type=jnp.float32)
        t_keep = jnp.where(first, t_in, t_out)
        t_send = jnp.where(first, t_out, t_in)
        if before is not None:
            if j == 0:
                old_keep, old_send = before()
            t_keep = t_keep + old_keep[:, cut].astype(jnp.float32)
            t_send = t_send + old_send[:, cut].astype(jnp.float32)
        keep_ref[:, cut] = t_keep.astype(jnp.bfloat16)
        send_ref[:, cut] = t_send.astype(jnp.bfloat16)
        if j == 0:
            wait_in()
        part = lax.dot_general(gp_ref[...], w_in_ref[:, cut], (((1,), (1,)), ((), ())), preferred_element_type=jnp.float32)
        if j == 0:
            acc_ref[...] = part
        else:
            acc_ref[...] += part
    gain_sum = jnp.zeros((8, channels), jnp.float32)
    for i in range(n // sub):
        at = slice(i * sub, (i + 1) * sub)
        gn = acc_ref[at, :]
        xhat = xhat_ref[at, :].astype(jnp.float32)
        gain_sum = gain_sum + jnp.sum((gn * xhat).reshape(sub // 8, 8, channels), axis=0)
        gx = gn * gain
        m1 = jnp.mean(gx, axis=1, keepdims=True)
        m2 = jnp.mean(gx * xhat, axis=1, keepdims=True)
        gconv_ref[at, :] = inv_ref[at, 0:1] * (gx - m1 - xhat * m2)
    sums8_ref[0:1, :] = jnp.sum(gain_sum, axis=0, keepdims=True)
    sums8_ref[1:2, :] = jnp.sum(scale_sum, axis=0, keepdims=True)
    sums8_ref[2:8, :] = jnp.zeros((6, channels), jnp.float32)


def out_struct(shape, dtype, by_hand=False):
    return pltpu.HBM(shape, dtype) if by_hand else jax.ShapeDtypeStruct(shape, dtype)


def named_call(name, body, ins, outs, scratch, cost):
    names = list(ins) + list(outs) + list(scratch)
    spaces = {"v": pltpu.VMEM, "s": pltpu.SMEM, "a": pl.ANY, "h": pl.ANY}

    def kernel(*refs):
        body(types.SimpleNamespace(**dict(zip(names, refs))))

    args = [pltpu.with_memory_space_constraint(a, pltpu.HBM) if kind == "h" else a for a, kind in ins.values()]
    result = pl.pallas_call(
        kernel,
        in_specs=[pl.BlockSpec(memory_space=spaces[kind]) for _, kind in ins.values()],
        out_specs=tuple(pl.BlockSpec(memory_space=pl.ANY if len(o) > 2 else pltpu.VMEM) for o in outs.values()),
        out_shape=tuple(out_struct(*o) for o in outs.values()),
        scratch_shapes=list(scratch.values()),
        compiler_params=vmem(LIMIT),
        name=name,
        cost_estimate=estimate(cost),
    )(*args)
    return types.SimpleNamespace(**dict(zip(outs, result)))


def mlp_body(normed_ref, wait_in, wait_out, w_in_ref, w_out_ref, pre_ref, hid_ref, acc_ref):
    n = normed_ref.shape[0]
    hidden = w_in_ref.shape[1]
    step, sub = 256, 32
    wait_in()
    for j in range(hidden // step):
        cut = slice(j * step, (j + 1) * step)
        pre = jnp.dot(normed_ref[...], w_in_ref[:, cut], preferred_element_type=jnp.float32)
        for i in range(n // sub):
            p = pre[i * sub : (i + 1) * sub]
            half = 0.5 * p
            hid_ref[i * sub : (i + 1) * sub, :] = (half + half * tanh_arg(p)).astype(jnp.bfloat16)
            pre_ref[i * sub : (i + 1) * sub, cut] = p.astype(jnp.bfloat16)
        if j == 0:
            wait_out()
        part = jnp.dot(hid_ref[...], w_out_ref[cut, :], preferred_element_type=jnp.float32)
        if j == 0:
            acc_ref[...] = part
        else:
            acc_ref[...] += part


def residual_body(x_ref, small_ref, acc_ref, branch_ref, y_ref):
    rows, cols, channels = x_ref.shape
    scale = small_ref[TAPS + 1 : TAPS + 2, :]
    sub = 2 * cols
    for i in range(rows // 2):
        branch = acc_ref[i * sub : (i + 1) * sub, :]
        branch_ref[i * sub : (i + 1) * sub, :] = branch.astype(jnp.bfloat16)
        if y_ref is not None:
            old = x_ref[2 * i : 2 * i + 2].astype(jnp.float32).reshape(sub, channels)
            y_ref[2 * i : 2 * i + 2] = (old + scale * branch).astype(jnp.bfloat16).reshape(2, cols, channels)


def small_ins(pair):
    return {"own_small": (pair[0], "v"), "near_small": (pair[1], "v")}


def small_scratch(pair):
    return {"small": pltpu.VMEM((2,) + pair[0].shape, jnp.float32)}


def weight_ins(pair):
    return {k: (v, "h") for k, v in zip(("own_in", "near_in", "own_out", "near_out"), pair)}


def weight_scratch(blocks, channels, hidden):
    return {
        "w_in": pltpu.VMEM((blocks, channels, hidden), jnp.bfloat16),
        "w_out": pltpu.VMEM((blocks, hidden, channels), jnp.bfloat16),
        "w_sem": pltpu.SemaphoreType.DMA((2, blocks)),
    }


def start_weights(r, slot, block, out_first=False):
    def start(k, own, near, target):
        return copy_chosen(r.sel[block], (own, near), target.at[slot], r.w_sem.at[k, slot])

    if out_first:
        wait_out = start(1, r.own_out, r.near_out, r.w_out)
        return start(0, r.own_in, r.near_in, r.w_in), wait_out
    return start(0, r.own_in, r.near_in, r.w_in), start(1, r.own_out, r.near_out, r.w_out)


def pair_forward(sel, x, first, small, weights):
    rows, cols, channels = x.shape
    n, hidden = rows * cols, weights[0].shape[1]
    bf16, f32 = jnp.bfloat16, jnp.float32

    def body(r):
        @pl.when(r.sel[4] == 0)
        def _():
            low, high = start_weights(r, 0, 0), start_weights(r, 1, 1)
            choose_small(r)
            zero_borders(r.pad)
            mlp_body(r.normed0, *low, r.w_in.at[0], r.w_out.at[0], r.pre0, r.hid, r.acc)
            residual_body(r.x, r.small.at[0], r.acc, r.branch0, r.x1)
            conv_norm_body(r.x1, r.small.at[1], r.xhat1, r.normed, r.inv1, r.pad, r.conv)
            mlp_body(r.normed, *high, r.w_in.at[1], r.w_out.at[1], r.pre1, r.hid, r.acc)
            residual_body(r.x1, r.small.at[1], r.acc, r.branch1, r.y)

    return named_call(
        "pair_forward", body,
        {"sel": (sel, "s"), "x": (x, "v"), "normed0": (first[1], "v"), **small_ins(small), **weight_ins(weights)},
        {"y": (x.shape, bf16), "x1": (x.shape, bf16), "xhat1": ((n, channels), bf16), "inv1": ((n, LANES), f32),
         "pre0": ((n, hidden), bf16), "pre1": ((n, hidden), bf16),
         "branch0": ((n, channels), bf16), "branch1": ((n, channels), bf16)},
        {"normed": pltpu.VMEM((n, channels), bf16), "hid": pltpu.VMEM((n, 256), bf16), "acc": pltpu.VMEM((n, channels), f32),
         "pad": pad_shape(rows, cols, channels), "conv": pltpu.VMEM((rows, cols, channels), f32),
         **weight_scratch(2, channels, hidden), **small_scratch(small)},
        7.5,
    )


def back_scratch(n, channels):
    bf16, f32 = jnp.bfloat16, jnp.float32
    return {"gb": pltpu.VMEM((n, channels), bf16), "nm": pltpu.VMEM((n, channels), bf16),
            "hid": pltpu.VMEM((n, 256), bf16), "gp": pltpu.VMEM((n, 256), bf16), "acc": pltpu.VMEM((n, channels), f32)}


def back_temps(r):
    return r.gb, r.nm, r.hid, r.gp, r.acc


GRADS = ("keep0", "send0", "keep1", "send1")
FACTORS = ("gb", "nm", "hid", "gp", "gconv", "sums")


def factor_shapes(n, channels, hidden):
    bf16, f32 = jnp.bfloat16, jnp.float32
    one = {"gb": ((n, channels), bf16), "nm": ((n, channels), bf16), "hid": ((n, hidden), bf16), "gp": ((n, hidden), bf16),
           "gconv": ((n, channels), f32), "sums": ((8, channels), f32)}
    return {name + str(k): one[name] for k in (0, 1) for name in FACTORS}


def pair_map(sel, x, g, small, weights):
    rows, cols, channels = x.shape
    n, hidden = rows * cols, weights[0].shape[1]
    bf16, f32 = jnp.bfloat16, jnp.float32
    shapes = factor_shapes(n, channels, hidden)
    saved = {**shapes, "x1": (x.shape, bf16)}
    order = list(saved)

    def body(r):
        @pl.when(r.sel[2] == 1)
        def _():
            def copy_out(name):
                return pltpu.make_async_copy(getattr(r, "v_" + name), getattr(r, name), r.s_sem.at[order.index(name)])

            low, high = start_weights(r, 0, 0), start_weights(r, 1, 1)
            choose_small(r)
            zero_borders(r.pad)
            s0, s1 = r.small.at[0], r.small.at[1]
            conv_norm_body(r.x, s0, r.xhat0, r.normed, r.inv0, r.pad, r.conv)
            mlp_body(r.normed, *low, r.w_in.at[0], r.w_out.at[0], r.pre0, r.hid, r.acc)
            residual_body(r.x, s0, r.acc, r.branch0, r.v_x1)
            copy_out("x1").start()
            conv_norm_body(r.v_x1, s1, r.xhat1, r.normed, r.inv1, r.pad, r.conv)
            mlp_body(r.normed, *high, r.w_in.at[1], r.w_out.at[1], r.pre1, r.hid, r.acc)
            residual_body(r.v_x1, s1, r.acc, r.branch1, None)

            def ready(k):
                def start(*names):
                    for name in names:
                        copy_out(name + str(k)).start()

                return start

            mlp_back_map_body(r.g, r.branch1, r.pre1, r.xhat1, r.inv1, s1, r.w_in.at[1], r.w_out.at[1],
                              r.v_sums1, r.v_gconv1, r.v_gb1, r.v_nm1, r.v_hid1, r.v_gp1, r.acc, ready(1))
            conv_map_body(r.v_gconv1, r.g, s1, r.g1, r.pad, r.conv)
            mlp_back_map_body(r.g1, r.branch0, r.pre0, r.xhat0, r.inv0, s0, r.w_in.at[0], r.w_out.at[0],
                              r.v_sums0, r.v_gconv0, r.v_gb0, r.v_nm0, r.v_hid0, r.v_gp0, r.acc, ready(0))
            conv_map_body(r.v_gconv0, r.g1, s0, r.g0, r.pad, r.conv)
            for name in order:
                copy_out(name).wait()

    return named_call(
        "pair_map", body,
        {"sel": (sel, "s"), "x": (x, "v"), "g": (g, "v"), **small_ins(small), **weight_ins(weights)},
        {"g0": (x.shape, bf16), **{name: shape + (True,) for name, shape in saved.items()}},
        {**{"v_" + name: pltpu.VMEM(*shape) for name, shape in saved.items()},
         "s_sem": pltpu.SemaphoreType.DMA((len(order),)),
         "g1": pltpu.VMEM(x.shape, bf16),
         "xhat0": pltpu.VMEM((n, channels), bf16), "xhat1": pltpu.VMEM((n, channels), bf16),
         "inv0": pltpu.VMEM((n, LANES), f32), "inv1": pltpu.VMEM((n, LANES), f32),
         "pre0": pltpu.VMEM((n, hidden), bf16), "pre1": pltpu.VMEM((n, hidden), bf16),
         "branch0": pltpu.VMEM((n, channels), bf16), "branch1": pltpu.VMEM((n, channels), bf16),
         "normed": pltpu.VMEM((n, channels), bf16), "hid": pltpu.VMEM((n, 256), bf16), "acc": pltpu.VMEM((n, channels), f32),
         "pad": pad_shape(rows, cols, channels), "conv": pltpu.VMEM((rows, cols, channels), f32),
         **weight_scratch(2, channels, hidden), **small_scratch(small)},
        12,
    )


def pair_grads(sel, xs, parts):
    rows, cols, channels = xs[0].shape
    n, hidden = rows * cols, parts[0].hid0.shape[1]
    bf16, f32 = jnp.bfloat16, jnp.float32
    shapes = factor_shapes(n, channels, hidden)
    order = list(shapes) + ["x1"]

    def body(r):
        @pl.when(r.sel[2] == 1)
        def _():
            def copy_out(k):
                return pltpu.make_async_copy(r.grads.at[k], getattr(r, GRADS[k]), r.o_sem.at[k])

            copies = {}
            for k in (1, 0):
                for name in FACTORS + (("x1",) if k else ()):
                    full = name + str(k) if name != "x1" else name
                    for i in range(2):
                        copies[full, i] = pltpu.make_async_copy(
                            getattr(r, "i%d_%s" % (i, full)), getattr(r, "v_" + full).at[i], r.s_sem.at[i, order.index(full)]
                        )
                        copies[full, i].start()
            first = r.sel[3] == 0
            for k in (1, 0):
                gb, nm, hid, gp = (getattr(r, "v_%s%d" % (name, k)) for name in FACTORS[:4])
                keep, send = r.grads.at[2 * k], r.grads.at[2 * k + 1]
                for name in FACTORS + (("x1",) if k else ()):
                    for i in range(2):
                        copies[name + str(k) if name != "x1" else name, i].wait()
                gb_t = gb[...].reshape(2 * n, channels).T
                nm_t = nm[...].reshape(2 * n, channels).T
                for j in range(hidden // 256):
                    cut = slice(j * 256, (j + 1) * 256)
                    t_out = jnp.dot(gb_t, hid[:, :, cut].reshape(2 * n, 256), preferred_element_type=f32)
                    t_in = jnp.dot(nm_t, gp[:, :, cut].reshape(2 * n, 256), preferred_element_type=f32)
                    keep[:, cut] = jnp.where(first, t_in, t_out).astype(bf16)
                    send[:, cut] = jnp.where(first, t_out, t_in).astype(bf16)
                copy_out(2 * k).start()
                copy_out(2 * k + 1).start()
                out = getattr(r, "small%d" % k)
                for i in range(2):
                    x = r.v_x1.at[i] if k else getattr(r, "x_%d" % i)
                    gconv, sums = getattr(r, "v_gconv%d" % k).at[i], getattr(r, "v_sums%d" % k).at[i]
                    target = out if i == 0 else r.tk
                    conv_back_body(gconv, x, None, None, sums, None, target, r.pad, r.sum, r.wide, None)
                out[...] += r.tk[...]
            for k in range(4):
                copy_out(k).wait()

    ins = {"sel": (sel, "s")}
    for i in range(2):
        ins["x_%d" % i] = (xs[i], "v")
        ins.update({"i%d_%s" % (i, name): (getattr(parts[i], name), "h") for name in order})
    grad = ((channels, hidden), bf16)
    small_out = ((SMALL_ROWS, channels), f32)
    scratch = {"v_" + name: pltpu.VMEM((2,) + shape, dtype) for name, (shape, dtype) in shapes.items()}
    return named_call(
        "pair_grads", body, ins,
        {**{name: grad + (True,) for name in GRADS}, "small0": small_out, "small1": small_out},
        {**scratch, "grads": pltpu.VMEM((4, channels, hidden), bf16), "o_sem": pltpu.SemaphoreType.DMA((4,)), "v_x1": pltpu.VMEM((2,) + xs[0].shape, bf16), "s_sem": pltpu.SemaphoreType.DMA((2, len(order))),
         "pad": pad_shape(rows, cols, channels), "sum": pltpu.VMEM((cols // 8, TAPS, 8, LANES), f32),
         "wide": pltpu.VMEM(xs[0].shape, f32), "tk": pltpu.VMEM((SMALL_ROWS, channels), f32)},
        10,
    )


def pair_back(sel, g, x, first, kept, small, weights, before=None, after=()):
    rows, cols, channels = g.shape
    n, hidden = rows * cols, weights[0].shape[1]
    bf16, f32 = jnp.bfloat16, jnp.float32

    def body(r):
        def copy_old(k):
            return copy_chosen(r.sel[2], (getattr(r, "a_" + GRADS[k]), getattr(r, "p_" + GRADS[k])), r.olds.at[k], r.o_sem.at[k])

        def copy_out(k, source):
            return pltpu.make_async_copy(source, getattr(r, GRADS[k]), r.s_sem.at[k])

        @pl.when(r.sel[2] == 0)
        def _():
            core = r.sel[3] == 0
            high, waits = start_weights(r, 1, 1, True), {}
            if before is not None:
                waits = {k: copy_old(k) for k in (2, 3)}
            low = start_weights(r, 0, 0, True)
            if before is not None:
                waits.update({k: copy_old(k) for k in (0, 1)})
            choose_small(r)
            s0, s1 = r.small.at[0], r.small.at[1]

            def old(k):
                def both():
                    waits[2 * k]()
                    waits[2 * k + 1]()
                    return r.olds.at[2 * k], r.olds.at[2 * k + 1]

                return both if waits else None

            mlp_back_body(core, r.g, r.branch1, r.pre1, r.xhat1, r.inv1, s1, *high, r.w_in.at[1], r.w_out.at[1],
                          r.grads.at[2], r.grads.at[3], r.sums8, r.gconv, *back_temps(r), before=old(1))
            copy_out(2, r.grads.at[2]).start()
            copy_out(3, r.grads.at[3]).start()
            conv_back_body(r.gconv, r.x1, r.g, s1, r.sums8, r.g1, r.small1, r.pad, r.sum, r.wide, r.map)
            mlp_back_body(core, r.g1, r.branch0, r.pre0, r.xhat0, r.inv0, s0, *low, r.w_in.at[0], r.w_out.at[0],
                          r.grads.at[0], r.grads.at[1], r.sums8, r.gconv, *back_temps(r), before=old(0))
            copy_out(0, r.grads.at[0]).start()
            copy_out(1, r.grads.at[1]).start()
            conv_back_body(r.gconv, r.x, None, None, r.sums8, None, r.small0, r.pad, r.sum, r.wide, None)
            if before is not None:
                r.small0[...] += r.a_small0[...]
                r.small1[...] += r.a_small1[...]
                r.packed[...] = jnp.concatenate([r.small0[...], r.small1[...]], axis=0).T.astype(bf16)
            for k in range(4):
                copy_out(k, r.grads.at[k]).wait()

        if before is not None:

            @pl.when(r.sel[2] == 1)
            def _():
                waits = [copy_old(k) for k in range(4)]
                r.packed[...] = jnp.concatenate([r.p_small0[...], r.p_small1[...]], axis=0).T.astype(bf16)
                for k, wait in enumerate(waits):
                    wait()
                    copy_out(k, r.olds.at[k]).start()
                for k in range(4):
                    copy_out(k, r.olds.at[k]).wait()

    ins = {"sel": (sel, "s"), "g": (g, "v"), "x": (x, "v"), "x1": (kept.x1, "v"),
           "branch1": (kept.branch1, "v"), "pre1": (kept.pre1, "v"), "xhat1": (kept.xhat1, "v"), "inv1": (kept.inv1, "v"),
           "branch0": (kept.branch0, "v"), "pre0": (kept.pre0, "v"), "xhat0": (first[0], "v"), "inv0": (first[2], "v"),
           **small_ins(small), **weight_ins(weights)}
    grad = ((channels, hidden), bf16)
    small_out = ((SMALL_ROWS, channels), f32)
    outs = {name: grad + (True,) for name in GRADS}
    scratch = {"grads": pltpu.VMEM((4, channels, hidden), bf16), "s_sem": pltpu.SemaphoreType.DMA((4,)), "g1": pltpu.VMEM(g.shape, bf16), "sums8": pltpu.VMEM((8, channels), f32), "gconv": pltpu.VMEM((n, channels), f32),
               "pad": pad_shape(rows, cols, channels), "sum": pltpu.VMEM((cols // 8, TAPS, 8, LANES), f32),
               "wide": pltpu.VMEM(x.shape, f32), "map": pltpu.VMEM(x.shape, f32),
               **back_scratch(n, channels), **weight_scratch(2, channels, hidden), **small_scratch(small)}
    if before is None:
        outs.update({"small0": small_out, "small1": small_out})
    else:
        for prefix, part in zip("ap", before):
            ins.update({prefix + "_" + name: (getattr(part, name), "h") for name in GRADS})
            ins.update({prefix + "_" + name: (getattr(part, name), "v") for name in ("small0", "small1")})
        outs["packed"] = ((channels, 2 * SMALL_ROWS), bf16)
        scratch.update({"small0": pltpu.VMEM(*small_out), "small1": pltpu.VMEM(*small_out),
                        "olds": pltpu.VMEM((4, channels, hidden), bf16), "o_sem": pltpu.SemaphoreType.DMA((4,))})
    ins.update({"after%d" % k: (v, "a") for k, v in enumerate(after)})
    return named_call("pair_back", body, ins, outs, scratch, 9)


def brought_kernel(source_ref, out_ref, sem):
    copy = pltpu.make_async_copy(source_ref, out_ref, sem)
    copy.start()
    copy.wait()


def brought(value):
    return pl.pallas_call(
        brought_kernel,
        in_specs=[pl.BlockSpec(memory_space=pl.ANY)],
        out_shape=jax.ShapeDtypeStruct(value.shape, value.dtype),
        scratch_shapes=[pltpu.SemaphoreType.DMA(())],
        compiler_params=vmem(LIMIT),
        name="brought",
        cost_estimate=estimate(1.1),
    )(pltpu.with_memory_space_constraint(value, pltpu.HBM))


def add(a, b):
    return a.astype(jnp.float32) + b.astype(jnp.float32)


def side_kernel(sel_ref, keep_ref, got_ref, *refs):
    *small_ref, across_ref, mine_ref = refs
    side = sel_ref[0]
    levels, _, _, hidden = keep_ref.shape
    for level in range(levels):
        for out_ref, which in ((across_ref, 1 - side), (mine_ref, side)):
            out_ref[level, :, :hidden] = add(keep_ref[level, which], got_ref[level, which]).astype(jnp.bfloat16)
            if small_ref:
                out_ref[level, :, hidden:] = small_ref[0][level, which]


def to_side(side, *arrays):
    arrays = [v.reshape(4, 2, v.shape[0] // 8, v.shape[1]) for v in arrays]
    width = sum(v.shape[3] for v in arrays[1:])
    out = ((4, arrays[0].shape[2], width), jnp.bfloat16)
    return small_call(side_kernel, "to_side", (out, out), side, *arrays)


def depth_kernel(sel_ref, mine_ref, got_ref, *out_refs):
    for k, out_ref in enumerate(out_refs):
        out_ref[...] = add(mine_ref[sel_ref[k]], got_ref[sel_ref[k]]).astype(jnp.bfloat16)


def to_depths(levels, mine, got, after=()):
    return small_call(depth_kernel, "to_depths", ((mine.shape[1:], jnp.bfloat16),) * 4, levels, mine, got, after=after)


def split_kernel(sel_ref, keep_ref, got_ref, *out_refs):
    for k, out_ref in enumerate(out_refs):
        for side in range(2):
            out_ref[side] = add(keep_ref[sel_ref[k], side], got_ref[sel_ref[k], side]).astype(jnp.bfloat16)


def split_depths(levels, keep, got, after=()):
    keep, got = (v.reshape(4, 2, v.shape[0] // 8, v.shape[1]) for v in (keep, got))
    outs = ((keep.shape[1:], jnp.bfloat16),) * 4
    return small_call(split_kernel, "split_depths", outs, levels, keep, got, after=after)


def join_kernel(sel_ref, a_ref, b_ref, c_ref, d_ref, across_ref, mine_ref):
    side = sel_ref[0]
    for out_ref, which in ((across_ref, 1 - side), (mine_ref, side)):
        out_ref[...] = (add(a_ref[which], b_ref[which]) + add(c_ref[which], d_ref[which])).astype(out_ref.dtype)


def join_depths(side, parts):
    shape = parts[0].shape[1:]
    return small_call(join_kernel, "join_depths", ((shape, jnp.bfloat16), (shape, jnp.float32)), side, *parts)


def core_kernel(sel_ref, *refs):
    *parts, own_ref, send_ref = refs
    hidden = parts[-1].shape[1]
    a, b, c, d, e, f = parts
    low, high = add(a[...], b[...]) + add(c[...], d[...]), add(e[...], f[...])
    first = sel_ref[0] == 0
    small = low[:, hidden:]
    turned = pltpu.roll(small, SMALL_ROWS, 1)
    low = low[:, :hidden]
    own_ref[:, :hidden] = jnp.where(first, low, high)
    own_ref[:, hidden:] = jnp.where(first, small, turned)
    send_ref[:, :hidden] = jnp.where(first, high, low).astype(jnp.bfloat16)
    send_ref[:, hidden:] = jnp.where(first, turned, small).astype(jnp.bfloat16)


def to_core(core, parts):
    shape = (parts[-1].shape[0], parts[-1].shape[1] + 2 * SMALL_ROWS)
    return small_call(core_kernel, "to_core", ((shape, jnp.float32), (shape, jnp.bfloat16)), core, *parts)


def final_kernel(sel_ref, own_ref, got_ref, k_ref, gain_ref, in_ref, out_ref, scale_ref, pad_ref):
    share, hidden = own_ref.shape[0], in_ref.shape[2]
    taps = k_ref.shape[2]
    first = sel_ref[0] == 0
    own, got = own_ref[:, :hidden], got_ref[:, :hidden].astype(jnp.float32)
    in_ref[0] = jnp.where(first, own, got)
    out_ref[0] = jnp.where(first, got, own)
    small = add(own_ref[:, hidden:], got_ref[:, hidden:])
    k_ref[0] = small[:, :taps]
    pad_ref[0:share, :] = small
    turned = pad_ref[...].T
    gain_ref[...] = turned[taps : taps + 1, :share]
    scale_ref[...] = turned[taps + 1 : taps + 2, :share]


def final(core, own, got, taps):
    share, hidden = own.shape[0], own.shape[1] - 2 * SMALL_ROWS
    outs = (
        ((1, share, taps), jnp.float32),
        ((1, share), jnp.float32),
        ((1, share, hidden), jnp.float32),
        ((1, share, hidden), jnp.float32),
        ((1, share), jnp.float32),
    )
    t_kernel, t_gain, t_in, t_out, t_scale = small_call(
        final_kernel, "final", outs, core, own, got, scratch=[pltpu.VMEM((LANES, 2 * SMALL_ROWS), jnp.float32)]
    )
    return t_kernel.transpose(0, 2, 1), t_gain, t_in, t_out.transpose(0, 2, 1), t_scale


BF16 = jnp.bfloat16
F32 = jnp.float32


def one_image(x, g, small, sels, w_ins, w_outs, first, passing):
    blocks = small.shape[0]
    rows, cols, channels = x.shape
    which = jnp.stack([sel[0] for sel in sels])
    xs, xhats, invs, pres, branches = forward(which, x, first[1], small, w_ins, w_outs)
    xs, xhats, invs = (x,) + tuple(xs), first[:1] + tuple(xhats), first[2:] + tuple(invs)
    smalls = [None] * blocks
    for s in reversed(range(blocks)):
        keep, send, sums8, gconv = mlp_back(
            sels[s], g.reshape(rows * cols, channels), branches[s], pres[s], xhats[s], invs[s],
            small[s, TAPS : TAPS + 1], small[s, TAPS + 1 : TAPS + 2], w_ins, w_outs, passing.before("mlp", s),
        )
        passing.done(s, keep, send)
        *g_next, smalls[s] = conv_back(
            gconv, xs[s], g, small[s, :TAPS], sums8, s > 0, passing.before("conv", s)
        )
        g = g_next[0] if g_next else None
    return smalls


def finish(t_kernel, t_gain, t_scale, t_in, t_out):
    return t_kernel[None], t_gain[None], t_in[None], t_out[None], t_scale[None]


def any_mesh(images, cotangent, kernels, norm_gains, w_in, w_out, scales):
    segments = lax.axis_size("segment")
    rank = lax.axis_index("segment")
    count = images.shape[0] // segments
    taps = kernels.shape[1]
    small = lax.all_gather(parameters(kernels, norm_gains, scales), "segment")
    all_in = lax.all_gather(w_in[0], "segment")
    all_out = lax.all_gather(w_out[0], "segment")
    sels = [jnp.array([s, 0], jnp.int32) for s in range(segments)]
    pieces = [[None] * 3 for _ in range(segments)]

    class Sums:
        def before(self, part, s):
            return ()

        def done(self, s, keep, send):
            self.add(s, 0, keep.astype(F32))
            self.add(s, 1, send.astype(F32))

        def add(self, s, k, value):
            pieces[s][k] = value if pieces[s][k] is None else pieces[s][k] + value

    sums = Sums()
    w_ins = [all_in[s] for s in range(segments)]
    w_outs = [all_out[s] for s in range(segments)]
    for i in range(count):
        x = lax.dynamic_index_in_dim(images, rank * count + i, 0, keepdims=False)
        g = lax.dynamic_index_in_dim(cotangent, rank * count + i, 0, keepdims=False)
        smalls = one_image(x, g, small, sels, w_ins, w_outs, conv_norm(sels[0] * 0, x, [small[0]]), sums)
        for s in range(segments):
            sums.add(s, 2, smalls[s])

    def summed(values, dim):
        mine = lax.psum_scatter(jnp.stack(values), "segment", scatter_dimension=0, tiled=False)
        return lax.psum_scatter(mine, "dp", scatter_dimension=dim, tiled=True)

    t_in = summed([p[0] for p in pieces], 0)
    t_out = summed([p[1] for p in pieces], 0).T
    t_small = summed([p[2] for p in pieces], 1)
    return finish(t_small[:taps], t_small[taps], t_small[taps + 1], t_in, t_out)


def partners(flip, extent=(4, 2, 2, 2)):
    pairs = []
    for index in range(32):
        z, y, x, c = index >> 3, (index >> 2) & 1, (index >> 1) & 1, index & 1
        other = ((z ^ flip[0]) << 3) | ((y ^ flip[1]) << 2) | ((x ^ flip[2]) << 1) | (c ^ flip[3])
        pairs.append((index, other))
    return pairs


def swap(value, z=0, y=0, x=0, c=0):
    return lax.ppermute(value, ("dp", "segment"), partners((z, y, x, c)))


def along_x(value, to_last):
    pairs = [(i, j) for i, j in partners((0, 0, 1, 0)) if (i >> 1) & 1 == (0 if to_last else 1)]
    return lax.ppermute(value, ("dp", "segment"), pairs)


def this_mesh(images, cotangent, kernels, norm_gains, w_in, w_out, scales):
    rank = lax.axis_index("segment")
    core = rank % 2
    chip = rank // 2
    depth = lax.axis_index("dp") // 2
    side = lax.axis_index("dp") % 2
    own_small = parameters(kernels, norm_gains, scales)
    near_small = swap(own_small, c=1)
    near_in, near_out = swap(w_in[0], c=1), swap(w_out[0], c=1)
    small = (own_small, near_small)
    weights = (w_in[0], near_in, w_out[0], near_out)
    zero = jnp.zeros_like(chip)
    sel = jnp.stack([core, 1 - core, chip, core, zero]).astype(jnp.int32)
    sel_first = jnp.stack([core, 1 - core, chip, core, chip]).astype(jnp.int32)
    sel_conv = (jnp.stack([core, zero]).astype(jnp.int32), jnp.stack([core, chip]).astype(jnp.int32))
    cores = core[None].astype(jnp.int32)
    sides = side[None].astype(jnp.int32)
    levels = jnp.stack([depth, depth ^ 1, depth ^ 2, depth ^ 3]).astype(jnp.int32)

    maps = [lax.dynamic_index_in_dim(images, 2 * core + i, 0, keepdims=False) for i in range(2)]
    ends = [lax.dynamic_index_in_dim(cotangent, 2 * core + i, 0, keepdims=False) for i in range(2)]
    firsts, kept = [], []
    for x, chosen in zip(maps, sel_conv):
        firsts.append(conv_norm(chosen, x, small, tuple(k.inv1 for k in kept)))
        kept.append(pair_forward(sel_first if kept else sel, x, firsts[-1], small, weights))
    passed = [along_x(k.y, True) for k in kept]
    parts, starts = [], []
    for x, g in zip(passed, ends):
        parts.append(pair_map(sel, x, g, small, weights))
        starts.append(along_x(parts[-1].g0, False))
    totals = pair_grads(sel, passed, parts)
    grads = pair_back(sel, starts[0], maps[0], firsts[0], kept[0], small, weights)
    grads = pair_back(sel, starts[1], maps[1], firsts[1], kept[1], small, weights, (grads, totals))
    core0, core1 = swap(grads.send0, c=1), swap(grads.send1, c=1)

    def along_y(*pairs):
        across, mine = to_side(sides, *pairs)
        return mine, swap(across, y=1)

    def along_z(mine, got):
        own, *others = to_depths(levels, mine, got)
        return [own] + [swap(v, z=flip) for v, flip in zip(others, (1, 2, 3))]

    low = along_y(brought(grads.keep0), core0, grads.packed)
    own, *others = split_depths(levels, grads.keep1, core1, low[:1])
    parts = [own] + [swap(others[flip - 1], z=flip) for flip in (2, 3, 1)]
    across, mine = join_depths(sides, parts)
    high = [mine, swap(across, y=1)]
    low = along_z(*low)
    own, send = to_core(cores, low + high)
    return final(cores, own, swap(send, c=1), kernels.shape[1])


def solution(mesh):
    in_specs = (
        P("dp", None, None, None),
        P("dp", None, None, None),
        P("segment", None, None),
        P("segment", None),
        P("segment", None, None),
        P("segment", None, None),
        P("segment", None),
    )
    out_specs = (
        P("segment", None, "dp"),
        P("segment", "dp"),
        P("segment", "dp", None),
        P("segment", None, "dp"),
        P("segment", "dp"),
    )
    fits = dict(mesh.shape) == {"dp": 8, "segment": 4}

    def whole(images, *rest):
        local = this_mesh if fits and images.shape[0] == 32 else any_mesh
        return jax.shard_map(local, mesh=mesh, in_specs=in_specs, out_specs=out_specs, check_vma=False)(images, *rest)

    return whole
```
